32 devices in a mesh: col: 8 (over y, x, core), seq: 4 (over z).
Axes of the slice: x: 2, y: 2, z: 4, core: 2. Of those that a mesh axis runs over, the one named last changes fastest.
Arguments:
- tokens: bfloat16 [8192, 768], P(('col', 'seq')), may hold values from -6 to 6
- table_ids: int32 [8192], P(('col', 'seq')), may hold values from 0 to 2, as said below
- w_query: bfloat16 [768, 768], P(('col', 'seq')), may hold values from -0.21875 to 0.21875
- w_key: bfloat16 [768, 768], P(('col', 'seq')), may hold values from -0.21875 to 0.21875
- w_value: bfloat16 [768, 768], P(('col', 'seq')), may hold values from -0.21875 to 0.21875
- w_out: bfloat16 [768, 768], P(('col', 'seq')), may hold values from -1.75 to 1.75
- w_up: bfloat16 [768, 3072], P(('col', 'seq')), may hold values from -0.21875 to 0.21875
- w_down: bfloat16 [3072, 768], P(('col', 'seq')), may hold values from -0.109375 to 0.109375
- b_query: bfloat16 [768], P(('col', 'seq')), may hold values from -3 to 3
- b_value: bfloat16 [768], P(('col', 'seq')), may hold values from -3 to 3
- b_out: bfloat16 [768], P(('col', 'seq')), may hold values from -3 to 3
- b_up: bfloat16 [3072], P(('col', 'seq')), may hold values from -3 to 3
- b_down: bfloat16 [768], P(('col', 'seq')), may hold values from -3 to 3
- gain_attn: bfloat16 [768], P(('col', 'seq')), may hold values from 0.099609375 to 1.8984375
- shift_attn: bfloat16 [768], P(('col', 'seq')), may hold values from -3 to 3
- gain_ffn: bfloat16 [768], P(('col', 'seq')), may hold values from 0.099609375 to 1.8984375
- shift_ffn: bfloat16 [768], P(('col', 'seq')), may hold values from -3 to 3
- cotangent: bfloat16 [8192, 768], P(('col', 'seq')), may hold values from -6 to 6
Outputs:
- layer_out: bfloat16 [8192, 768], P(('col', 'seq'))
- grad_tokens: float32 [8192, 768], P(('col', 'seq'))
- grad_w_query: float32 [768, 768], P(('col', 'seq'))
- grad_w_key: float32 [768, 768], P(('col', 'seq'))
- grad_w_value: float32 [768, 768], P(('col', 'seq'))
- grad_w_out: float32 [768, 768], P(('col', 'seq'))
- grad_w_up: float32 [768, 3072], P(('col', 'seq'))
- grad_w_down: float32 [3072, 768], P(('col', 'seq'))
- grad_b_query: float32 [768], P(('col', 'seq'))
- grad_b_value: float32 [768], P(('col', 'seq'))
- grad_b_out: float32 [768], P(('col', 'seq'))
- grad_b_up: float32 [3072], P(('col', 'seq'))
- grad_b_down: float32 [768], P(('col', 'seq'))
- grad_gain_attn: float32 [768], P(('col', 'seq'))
- grad_shift_attn: float32 [768], P(('col', 'seq'))
- grad_gain_ffn: float32 [768], P(('col', 'seq'))
- grad_shift_ffn: float32 [768], P(('col', 'seq'))
The draws below stay inside these ranges and needn't reach their ends.
Inputs may be any that keep to these rules, and one draw needn't show every extreme that they name: `table_ids`: each seq group holds 3 whole tables, 1 of 1024 tokens and the others of 512 tokens; every table's tokens are dealt evenly over the col devices of its group, 512 / (the number of col devices) tokens of a short table and 1024 / (the number of col devices) of a long one on each, in any order within a device.
All inputs are finite; a program needn't handle non-finite values.
Results may differ from the reference program's by a relative error of at most 0.02.
Values may be sent and summed in bfloat16 or wider, within the bound.
No kernel may reach another device: no remote copies, remote signals or barrier semaphores. Data moves between devices by JAX's collectives and lax.ppermute only.
A program may use at most 192 MiB of HBM per device.

```python
import jax
import jax.numpy as jnp
import numpy as np
from jax import lax

D = 768
H = 12
HD = 64
FF = 3072
SHORT = 512
LONG_ROWS = 64
TOK_DEV = 256
TOKENS = 8192
N_COL = 8
N_SEQ = 4


def table_layout():
    long_units = max(2 * SHORT, LONG_ROWS * N_COL) // SHORT
    unit_count = TOK_DEV * N_COL // SHORT
    long_count = max(1, unit_count // (2 * long_units))
    table_count = unit_count - long_count * (long_units - 1)
    return (long_units, long_count, table_count)


def shuffle_labels(piece_key):
    long_units, long_count, table_count = table_layout()
    return jax.random.permutation(piece_key, table_count).astype(jnp.int32)


def shuffle_places(piece_key):
    return jax.random.permutation(piece_key, TOK_DEV).astype(jnp.int32)


def draw_table_ids(key, part):
    key = jax.random.fold_in(key, 7)
    label_key, place_key = jax.random.split(key)
    long_units, long_count, table_count = table_layout()
    unit_rows = SHORT // N_COL
    unit_table = np.concatenate([np.repeat(np.arange(long_count), long_units), np.arange(long_count, table_count)])
    base_ids = jnp.asarray(np.repeat(unit_table, unit_rows), jnp.int32)
    labels = jax.vmap(shuffle_labels)(jax.random.split(label_key, N_SEQ))
    blocks = N_COL * N_SEQ
    group_of = jnp.arange(blocks, dtype=jnp.int32) % N_SEQ
    named_ids = labels[group_of][:, base_ids]
    orders = jax.vmap(shuffle_places)(jax.random.split(place_key, blocks))
    placed = jnp.take_along_axis(named_ids, orders, axis=1)
    return placed.reshape(TOKENS).astype(jnp.int32)


def strengthened(values, stream_key, source, target, shards_of, factor):
    def block_of(dim):
        return (jnp.arange(values.shape[dim]) // (values.shape[dim] // shards_of)).reshape((-1,) + (1,) * (values.ndim - 1 - dim))

    first = jax.random.permutation(stream_key, shards_of)[block_of(target)]
    far = (block_of(target) + shards_of // 2) % shards_of
    return jnp.where((block_of(source) == first) | (block_of(source) == far), factor * values, values)


def steps_of(stream_key, shape, cuts, low, high):
    def one(position, blocks):
        steps = jax.random.uniform(jax.random.fold_in(jax.random.fold_in(stream_key, 6), position), (blocks,), jnp.float32, low / len(cuts), high / len(cuts))
        return jnp.repeat(jnp.exp(steps), shape[position] // blocks).reshape((-1,) + (1,) * (len(shape) - position - 1))

    level = one(*cuts[0])
    for cut in cuts[1:]:
        level = level * one(*cut)
    return level


def gaussian(rng, dims, scale, most, cuts=(), kind=jnp.bfloat16):
    drawn = jax.random.normal(rng, dims, jnp.float32) * scale
    if len(cuts) > 0:
        drawn = steps_of(rng, dims, cuts, -0.22, 0.18) * drawn
    return jnp.clip(drawn, min=-most, max=most).astype(kind)


def noise_with(rng, dims, deviation, most, cuts, heavy, kind=jnp.bfloat16):
    entries = deviation * jax.random.normal(rng, dims, jnp.float32)
    if cuts:
        entries = entries * steps_of(rng, dims, cuts, -0.22, 0.18)
    return jnp.clip(strengthened(entries, jax.random.fold_in(rng, 3), *heavy), -most, most).astype(kind)


def setup_inputs(seed: int = 0) -> dict:
    key_of = jax.random.split(jax.random.key(seed), 19)
    return {
        "tokens": noise_with(key_of[0], (TOKENS, D), 1.0, 6.0, ((0, 32),), (0, 1, 32, 2.75)),
        "table_ids": draw_table_ids(jax.random.fold_in(key_of[18], 71), 0),
        "w_query": gaussian(key_of[2], (D, D), D ** -0.5, 0.21875, ((0, 32),)),
        "w_key": gaussian(key_of[3], (D, D), D ** -0.5, 0.21875, ((0, 32),)),
        "w_value": gaussian(key_of[4], (D, D), D ** -0.5, 0.21875, ((0, 32),)),
        "w_out": gaussian(key_of[5], (D, D), (D // 64) ** -0.5, 1.75, ((0, 32),)),
        "w_up": gaussian(key_of[6], (D, FF), D ** -0.5, 0.21875, ((0, 32),)),
        "w_down": gaussian(key_of[7], (FF, D), FF ** -0.5, 0.109375, ((0, 32),)),
        "b_query": gaussian(key_of[8], (D,), 0.5, 3.0, ((0, 32),)),
        "b_value": gaussian(key_of[9], (D,), 0.5, 3.0, ((0, 32),)),
        "b_out": gaussian(key_of[10], (D,), 0.5, 3.0, ((0, 32),)),
        "b_up": gaussian(key_of[11], (FF,), 0.5, 3.0, ((0, 32),)),
        "b_down": gaussian(key_of[12], (D,), 0.5, 3.0, ((0, 32),)),
        "gain_attn": jnp.clip(1.0 + 0.18 * jax.random.normal(key_of[13], (D,), jnp.float32), 0.099609375, 1.8984375).astype(jnp.bfloat16),
        "shift_attn": gaussian(key_of[14], (D,), 0.5, 3.0, ((0, 32),)),
        "gain_ffn": jnp.clip(1.0 + 0.18 * jax.random.normal(key_of[15], (D,), jnp.float32), 0.099609375, 1.8984375).astype(jnp.bfloat16),
        "shift_ffn": gaussian(key_of[16], (D,), 0.5, 3.0, ((0, 32),)),
        "cotangent": gaussian(key_of[17], (TOKENS, D), 1.0, 6.0, ((0, 32),)),
    }


HIGH = lax.Precision.HIGHEST
NEG_BIG = -1e+30
NORM_EPS = 1e-12

@jax.custom_vjp
def low(v):
    return lax.optimization_barrier(v.astype(jnp.bfloat16)).astype(jnp.float32)

@jax.custom_vjp
def low_back(v):
    return v

def low_keep(v):
    return (low(v), None)

def low_pass(kept, grad):
    return (grad,)

def back_keep(v):
    return (v, None)

def back_low(kept, grad):
    return (low(grad),)
low.defvjp(low_keep, low_pass)
low_back.defvjp(back_keep, back_low)

def matmul_high(left, right):
    return jnp.dot(left, right, precision=HIGH)

def layer_norm(values, gain, shift):
    center = values - lax.optimization_barrier(jnp.mean(values, axis=-1, keepdims=True))
    spread = lax.optimization_barrier(jnp.mean(center * center, axis=-1, keepdims=True))
    return center * lax.rsqrt(spread + NORM_EPS) * gain + shift

def regroup(values):
    width = values.shape[-1]
    return values.reshape(N_COL, N_SEQ, TOK_DEV, width).transpose(1, 0, 2, 3).reshape(N_SEQ, N_COL * TOK_DEV, width)

def ungroup(values):
    width = values.shape[-1]
    return values.reshape(N_SEQ, N_COL, TOK_DEV, width).transpose(1, 0, 2, 3).reshape(N_COL * N_SEQ * TOK_DEV, width)

def attend_block(query_rows, query_ids, key_rows, value_rows, key_ids):
    row_count = query_rows.shape[0]
    query_heads = query_rows.reshape(row_count, H, HD)
    key_heads = key_rows.reshape(key_rows.shape[0], H, HD)
    value_heads = value_rows.reshape(value_rows.shape[0], H, HD)
    raw = low_back(jnp.einsum('thd,shd->hts', query_heads, key_heads, precision=HIGH) * 0.125)
    visible = (query_ids[:, None] == key_ids[None, :])[None]
    probabilities = low(jax.nn.softmax(jnp.where(visible, raw, NEG_BIG), axis=-1))
    mixed = jnp.einsum('hts,shd->thd', probabilities, value_heads, precision=HIGH)
    return mixed.reshape(row_count, H * HD)

def attend_group(group):
    queries, keys, values, group_ids = group
    query_blocks = queries.reshape(N_COL, TOK_DEV, H * HD)
    id_blocks = group_ids.reshape(N_COL, TOK_DEV)

    def one_block(pieces):
        return attend_block(pieces[0], pieces[1], keys, values, group_ids)
    mixed = lax.map(jax.checkpoint(one_block), (query_blocks, id_blocks))
    return mixed.reshape(N_COL * TOK_DEV, H * HD)

def attention(queries, keys, values, table_ids):
    group_ids = table_ids.reshape(N_COL, N_SEQ, TOK_DEV).transpose(1, 0, 2).reshape(N_SEQ, N_COL * TOK_DEV)
    mixed = lax.map(attend_group, (regroup(queries), regroup(keys), regroup(values), group_ids))
    return ungroup(mixed)

def block_layer(tokens, w_query, w_key, w_value, w_out, w_up, w_down, b_query, b_value, b_out, b_up, b_down, gain_attn, shift_attn, gain_ffn, shift_ffn, table_ids):
    queries = low(low_back(matmul_high(tokens, w_query) + b_query))
    keys = low(low_back(matmul_high(tokens, w_key)))
    values = low(low_back(matmul_high(tokens, w_value) + b_value))
    mixed = low(low_back(attention(queries, keys, values, table_ids)))
    hidden = tokens + low_back(matmul_high(mixed, w_out) + b_out)
    normed = layer_norm(hidden, gain_attn, shift_attn)
    upper = low_back(matmul_high(low(normed), w_up) + b_up)
    active = low(jax.nn.gelu(upper, approximate=False))
    summed = normed + low_back(matmul_high(active, w_down) + b_down)
    return layer_norm(summed, gain_ffn, shift_ffn)

def reference(tokens, table_ids, w_query, w_key, w_value, w_out, w_up, w_down, b_query, b_value, b_out, b_up, b_down, gain_attn, shift_attn, gain_ffn, shift_ffn, cotangent):
    floats = [array.astype(jnp.float32) for array in (tokens, w_query, w_key, w_value, w_out, w_up, w_down, b_query, b_value, b_out, b_up, b_down, gain_attn, shift_attn, gain_ffn, shift_ffn)]

    def forward(*arrays):
        return block_layer(*arrays, table_ids)
    result, pullback = jax.vjp(forward, *floats)
    gradients = pullback(cotangent.astype(jnp.float32))
    return (result.astype(jnp.bfloat16), gradients[0], gradients[1], gradients[2], gradients[3], gradients[4], gradients[5], gradients[6], gradients[7], gradients[8], gradients[9], gradients[10], gradients[11], gradients[12], gradients[13], gradients[14], gradients[15])
```

```python
import functools

import jax
import jax.numpy as jnp
import numpy as np
from jax import lax
from jax.experimental import pallas as pl
from jax.experimental.pallas import tpu as pltpu
from jax.sharding import PartitionSpec as P

H = 12
HD = 64


NEG_BIG = -1e30
NORM_EPS = 1e-12
LOW_TYPE = jnp.bfloat16
FULL_TYPE = jnp.float32


def block_length(unit_rows):
    target = unit_rows * max(1, -(-512 // unit_rows))
    return target


def layer_norm(values, gain, shift):
    center = values - jnp.mean(values, axis=-1, keepdims=True)
    spread = jnp.mean(center * center, axis=-1, keepdims=True)
    return center * lax.rsqrt(spread + NORM_EPS) * gain + shift


def gelu_exact(values):
    return jax.nn.gelu(values, approximate=False)


def project(left, right, bias):
    return jnp.dot(left, right, preferred_element_type=FULL_TYPE) + bias.astype(FULL_TYPE)


def attend(running, query_heads, query_ids, key_slab, value_slab, key_ids):
    maxima, totals, weighted = running
    scores = (
        jnp.einsum("thd,shd->hts", query_heads, key_slab, preferred_element_type=FULL_TYPE) * 0.125
    )
    visible = (query_ids[:, None] == key_ids[None, :])[None]
    scores = jnp.where(visible, scores, NEG_BIG)
    new_max = jnp.maximum(maxima, jnp.max(scores, axis=2))
    rescale = jnp.exp(maxima - new_max)
    exponents = jnp.where(visible, jnp.exp(scores - new_max[:, :, None]), 0.0)
    totals = totals * rescale + jnp.sum(exponents, axis=2)
    weighted = weighted * rescale[:, :, None] + jnp.einsum(
        "hts,shd->htd", exponents.astype(LOW_TYPE), value_slab, preferred_element_type=FULL_TYPE
    )
    return (new_max, totals, weighted)


def grad_block(
    query_heads, dout_heads, log_totals, row_delta, query_ids, key_slab, value_slab, key_ids
):
    scores = (
        jnp.einsum("thd,shd->hts", query_heads, key_slab, preferred_element_type=FULL_TYPE) * 0.125
    )
    visible = (query_ids[:, None] == key_ids[None, :])[None]
    probabilities = jnp.where(visible, jnp.exp(scores - log_totals[:, :, None]), 0.0)
    grad_value = jnp.einsum(
        "hts,thd->shd", probabilities.astype(LOW_TYPE), dout_heads, preferred_element_type=FULL_TYPE
    )
    grad_probs = jnp.einsum(
        "thd,shd->hts", dout_heads, value_slab, preferred_element_type=FULL_TYPE
    )
    grad_scores = (probabilities * (grad_probs - row_delta[:, :, None])).astype(LOW_TYPE)
    grad_query = (
        jnp.einsum("hts,shd->thd", grad_scores, key_slab, preferred_element_type=FULL_TYPE) * 0.125
    )
    grad_key = (
        jnp.einsum("hts,thd->shd", grad_scores, query_heads, preferred_element_type=FULL_TYPE)
        * 0.125
    )
    return (grad_query, grad_key, grad_value)


def per_device(
    tokens,
    table_ids,
    w_query,
    w_key,
    w_value,
    w_out,
    w_up,
    w_down,
    b_query,
    b_value,
    b_out,
    b_up,
    b_down,
    gain_attn,
    shift_attn,
    gain_ffn,
    shift_ffn,
    cotangent,
):
    shards = (
        w_query,
        w_key,
        w_value,
        w_out,
        w_up,
        w_down,
        b_query,
        b_value,
        b_out,
        b_up,
        b_down,
        gain_attn,
        shift_attn,
        gain_ffn,
        shift_ffn,
    )
    gathered = (
        lax.all_gather(shards[0], ("col", "seq"), axis=0, tiled=True),
        lax.all_gather(shards[1], ("col", "seq"), axis=0, tiled=True),
        lax.all_gather(shards[2], ("col", "seq"), axis=0, tiled=True),
        lax.all_gather(shards[3], ("col", "seq"), axis=0, tiled=True),
        lax.all_gather(shards[4], ("col", "seq"), axis=0, tiled=True),
        lax.all_gather(shards[5], ("col", "seq"), axis=0, tiled=True),
        lax.all_gather(shards[6], ("col", "seq"), axis=0, tiled=True),
        lax.all_gather(shards[7], ("col", "seq"), axis=0, tiled=True),
        lax.all_gather(shards[8], ("col", "seq"), axis=0, tiled=True),
        lax.all_gather(shards[9], ("col", "seq"), axis=0, tiled=True),
        lax.all_gather(shards[10], ("col", "seq"), axis=0, tiled=True),
        lax.all_gather(shards[11], ("col", "seq"), axis=0, tiled=True),
        lax.all_gather(shards[12], ("col", "seq"), axis=0, tiled=True),
        lax.all_gather(shards[13], ("col", "seq"), axis=0, tiled=True),
        lax.all_gather(shards[14], ("col", "seq"), axis=0, tiled=True),
    )
    query_mat, key_mat, value_mat, out_mat, up_mat, down_mat = (
        gathered[0],
        gathered[1],
        gathered[2],
        gathered[3],
        gathered[4],
        gathered[5],
    )
    query_bias, value_bias, out_bias, up_bias, down_bias = (
        gathered[6],
        gathered[7],
        gathered[8],
        gathered[9],
        gathered[10],
    )
    attn_gain, attn_shift, ffn_gain, ffn_shift = (
        gathered[11],
        gathered[12],
        gathered[13],
        gathered[14],
    )
    tok_rows = tokens.shape[0]
    ids_all = lax.all_gather(table_ids, "col", axis=0, tiled=True)
    inputs = tokens.astype(FULL_TYPE)
    queries = project(tokens, query_mat, query_bias).astype(LOW_TYPE)
    keys = jnp.dot(tokens, key_mat, preferred_element_type=FULL_TYPE).astype(LOW_TYPE)
    values = project(tokens, value_mat, value_bias).astype(LOW_TYPE)
    query_heads = queries.reshape(tok_rows, H, HD)
    starting = (
        jnp.full((H, tok_rows), NEG_BIG, FULL_TYPE),
        jnp.zeros((H, tok_rows), FULL_TYPE),
        jnp.zeros((H, tok_rows, HD), FULL_TYPE),
    )
    running = starting
    key_rows = lax.all_gather(keys, "col", axis=0, tiled=True)
    value_rows = lax.all_gather(values, "col", axis=0, tiled=True)
    row_count = key_rows.shape[0]
    length = block_length(tok_rows)
    blocks = row_count // length

    def advance(current, pieces):
        return (attend(current, query_heads, table_ids, pieces[0], pieces[1], pieces[2]), None)

    running, _ = lax.scan(
        advance,
        running,
        (
            key_rows.reshape(blocks, length, H, HD),
            value_rows.reshape(blocks, length, H, HD),
            ids_all.reshape(blocks, length),
        ),
    )
    maxima, totals, weighted = running
    attn_heads = weighted / totals[:, :, None]
    log_totals = maxima + jnp.log(totals)
    attn_low = attn_heads.transpose(1, 0, 2).reshape(tok_rows, H * HD).astype(LOW_TYPE)
    hidden = inputs + project(attn_low, out_mat, out_bias)
    normed, norm_first = jax.vjp(
        layer_norm, hidden, attn_gain.astype(FULL_TYPE), attn_shift.astype(FULL_TYPE)
    )
    normed_low = normed.astype(LOW_TYPE)
    upper = project(normed_low, up_mat, up_bias)
    active, gelu_back = jax.vjp(gelu_exact, upper)
    active_low = active.astype(LOW_TYPE)
    summed = normed + project(active_low, down_mat, down_bias)
    result, norm_second = jax.vjp(
        layer_norm, summed, ffn_gain.astype(FULL_TYPE), ffn_shift.astype(FULL_TYPE)
    )
    again = (
        lax.all_gather(w_query, ("col", "seq"), axis=0, tiled=True),
        lax.all_gather(w_key, ("col", "seq"), axis=0, tiled=True),
        lax.all_gather(w_value, ("col", "seq"), axis=0, tiled=True),
        lax.all_gather(w_out, ("col", "seq"), axis=0, tiled=True),
        lax.all_gather(w_up, ("col", "seq"), axis=0, tiled=True),
        lax.all_gather(w_down, ("col", "seq"), axis=0, tiled=True),
    )
    query_mat, key_mat, value_mat, out_mat, up_mat, down_mat = (
        again[0],
        again[1],
        again[2],
        again[3],
        again[4],
        again[5],
    )
    d_summed, d_ffn_gain, d_ffn_shift = norm_second(cotangent.astype(FULL_TYPE))
    d_down = d_summed.astype(LOW_TYPE)
    grad_down = jnp.einsum("tf,td->fd", active_low, d_down, preferred_element_type=FULL_TYPE)
    d_active = jnp.einsum("td,fd->tf", d_down, down_mat, preferred_element_type=FULL_TYPE)
    d_upper = gelu_back(d_active)[0].astype(LOW_TYPE)
    grad_up = jnp.einsum("td,tf->df", normed_low, d_upper, preferred_element_type=FULL_TYPE)
    d_normed = d_summed + jnp.einsum("tf,df->td", d_upper, up_mat, preferred_element_type=FULL_TYPE)
    d_hidden, d_attn_gain, d_attn_shift = norm_first(d_normed)
    d_branch = d_hidden.astype(LOW_TYPE)
    grad_out = jnp.einsum("tc,td->cd", attn_low, d_branch, preferred_element_type=FULL_TYPE)
    d_attn = jnp.einsum("td,cd->tc", d_branch, out_mat, preferred_element_type=FULL_TYPE).astype(
        LOW_TYPE
    )
    dout_heads = d_attn.reshape(tok_rows, H, HD)
    row_delta = jnp.einsum("thd,htd->ht", dout_heads.astype(FULL_TYPE), attn_heads)
    key_all, value_all = (
        lax.all_gather(keys, "col", axis=0, tiled=True),
        lax.all_gather(values, "col", axis=0, tiled=True),
    )
    total_rows = key_all.shape[0]
    length = block_length(tok_rows)
    blocks = total_rows // length

    def key_pass(grad_sum, pieces):
        grad_query_part, grad_key_part, grad_value_part = grad_block(
            query_heads,
            dout_heads,
            log_totals,
            row_delta,
            table_ids,
            pieces[0],
            pieces[1],
            pieces[2],
        )
        return (grad_sum + grad_query_part, (grad_key_part, grad_value_part))

    query_sum, (key_parts, value_parts) = lax.scan(
        key_pass,
        jnp.zeros((tok_rows, H, HD), FULL_TYPE),
        (
            key_all.reshape(blocks, length, H, HD),
            value_all.reshape(blocks, length, H, HD),
            ids_all.reshape(blocks, length),
        ),
    )
    key_sum, value_sum = (
        lax.psum_scatter(
            key_parts.reshape(total_rows, H * HD).astype(jnp.bfloat16),
            "col",
            scatter_dimension=0,
            tiled=True,
        ).astype(jnp.float32),
        lax.psum_scatter(
            value_parts.reshape(total_rows, H * HD).astype(jnp.bfloat16),
            "col",
            scatter_dimension=0,
            tiled=True,
        ).astype(jnp.float32),
    )
    query_sum = query_sum.reshape(tok_rows, H * HD)
    query_low = query_sum.astype(LOW_TYPE)
    key_low = key_sum.astype(LOW_TYPE)
    value_low = value_sum.astype(LOW_TYPE)
    grad_query = jnp.einsum("tc,td->cd", tokens, query_low, preferred_element_type=FULL_TYPE)
    grad_key = jnp.einsum("tc,td->cd", tokens, key_low, preferred_element_type=FULL_TYPE)
    grad_value = jnp.einsum("tc,td->cd", tokens, value_low, preferred_element_type=FULL_TYPE)
    d_tokens = d_hidden + jnp.einsum(
        "td,cd->tc", query_low, query_mat, preferred_element_type=FULL_TYPE
    )
    d_tokens = d_tokens + jnp.einsum(
        "td,cd->tc", key_low, key_mat, preferred_element_type=FULL_TYPE
    )
    d_tokens = d_tokens + jnp.einsum(
        "td,cd->tc", value_low, value_mat, preferred_element_type=FULL_TYPE
    )
    sums_local = (
        grad_query,
        grad_key,
        grad_value,
        grad_out,
        grad_up,
        grad_down,
        jnp.sum(query_low.astype(FULL_TYPE), axis=0),
        jnp.sum(value_low.astype(FULL_TYPE), axis=0),
        jnp.sum(d_branch.astype(FULL_TYPE), axis=0),
        jnp.sum(d_upper.astype(FULL_TYPE), axis=0),
        jnp.sum(d_down.astype(FULL_TYPE), axis=0),
        d_attn_gain,
        d_attn_shift,
        d_ffn_gain,
        d_ffn_shift,
    )
    owned = (
        lax.psum_scatter(sums_local[0], ("col", "seq"), scatter_dimension=0, tiled=True),
        lax.psum_scatter(sums_local[1], ("col", "seq"), scatter_dimension=0, tiled=True),
        lax.psum_scatter(sums_local[2], ("col", "seq"), scatter_dimension=0, tiled=True),
        lax.psum_scatter(sums_local[3], ("col", "seq"), scatter_dimension=0, tiled=True),
        lax.psum_scatter(sums_local[4], ("col", "seq"), scatter_dimension=0, tiled=True),
        lax.psum_scatter(sums_local[5], ("col", "seq"), scatter_dimension=0, tiled=True),
        lax.psum_scatter(sums_local[6], ("col", "seq"), scatter_dimension=0, tiled=True),
        lax.psum_scatter(sums_local[7], ("col", "seq"), scatter_dimension=0, tiled=True),
        lax.psum_scatter(sums_local[8], ("col", "seq"), scatter_dimension=0, tiled=True),
        lax.psum_scatter(sums_local[9], ("col", "seq"), scatter_dimension=0, tiled=True),
        lax.psum_scatter(sums_local[10], ("col", "seq"), scatter_dimension=0, tiled=True),
        lax.psum_scatter(sums_local[11], ("col", "seq"), scatter_dimension=0, tiled=True),
        lax.psum_scatter(sums_local[12], ("col", "seq"), scatter_dimension=0, tiled=True),
        lax.psum_scatter(sums_local[13], ("col", "seq"), scatter_dimension=0, tiled=True),
        lax.psum_scatter(sums_local[14], ("col", "seq"), scatter_dimension=0, tiled=True),
    )
    return (result.astype(LOW_TYPE), d_tokens) + tuple(owned)


WIDTH = 768
HALF = WIDTH // 2
SHARD = 24
DOWN = 96
SLAB = (SHARD, HALF)
VMEM_BYTES = 60 * 2**20
F32 = jnp.float32
BF16 = jnp.bfloat16


def dot(left, right):
    return jnp.dot(left, right, preferred_element_type=F32)


def dot_nt(left, right):
    return lax.dot_general(left, right, (((1,), (1,)), ((), ())), preferred_element_type=F32)


def dot_tn(left, right):
    return lax.dot_general(left, right, (((0,), (0,)), ((), ())), preferred_element_type=F32)


def call(body, name, place, inputs, outs, scratch=(), flops=0):
    vmem = pl.BlockSpec(memory_space=pltpu.VMEM)
    moved = sum(a.size * a.dtype.itemsize for a in inputs)
    moved += sum(int(np.prod(s)) * np.dtype(t).itemsize for s, t in outs)
    return pl.pallas_call(
        body,
        name=name,
        out_shape=tuple(jax.ShapeDtypeStruct(s, t) for s, t in outs),
        in_specs=[pl.BlockSpec(memory_space=pltpu.SMEM)] + [vmem] * len(inputs),
        out_specs=tuple(vmem for _ in outs),
        scratch_shapes=list(scratch),
        compiler_params=pltpu.CompilerParams(vmem_limit_bytes=VMEM_BYTES),
        cost_estimate=pl.CostEstimate(flops=flops, bytes_accessed=moved, transcendentals=0),
    )(place, *inputs)


def iota(shape, dim):
    return lax.broadcasted_iota(jnp.int32, shape, dim)


def prep_body(place, ids, tokens, cot, wq, wk, wv, wo, wup, *rest):
    vectors, b_up = rest[:8], rest[8]
    perm_out, tok_out, cot_out, keep, send = rest[9:14]
    rows8 = rest[14]
    core, dev = place[0], place[3]
    rows = tokens.shape[0]
    id_j = jnp.broadcast_to(ids[...].astype(F32), (rows, rows))
    id_i = id_j.T
    same = jnp.where(id_i == id_j, 1.0, 0.0)
    count_i = jnp.sum(same, axis=1, keepdims=True)
    count_j = jnp.sum(same, axis=0, keepdims=True)
    i, j = iota((rows, rows), 0), iota((rows, rows), 1)
    equal = jnp.where((id_i == id_j) & (i < j), 1.0, 0.0)
    tie = jnp.where((count_i == count_j) & (id_i < id_j), 1.0, 0.0)
    larger = jnp.where(count_i > count_j, 1.0, 0.0)
    position = jnp.sum(equal + tie + larger, axis=0, keepdims=True)
    perm = jnp.where(i.astype(F32) == position, 1.0, 0.0).astype(BF16)
    perm_out[...] = perm
    tok_out[...] = dot(perm, tokens[...]).astype(BF16)
    cot_out[...] = dot(perm, cot[...]).astype(BF16)

    def split(mine, other):
        for n, w in enumerate((wq, wk, wv, wo)):
            keep[n] = w[:, mine * HALF : (mine + 1) * HALF]
            send[n] = w[:, other * HALF : (other + 1) * HALF]
        for u in range(4):
            keep[4 + u] = wup[:, u * WIDTH + mine * HALF : u * WIDTH + (mine + 1) * HALF]
            send[4 + u] = wup[:, u * WIDTH + other * HALF : u * WIDTH + (other + 1) * HALF]

    @pl.when(core == 0)
    def _():
        split(0, 1)

    @pl.when(core == 1)
    def _():
        split(1, 0)

    for n, vector in enumerate(vectors):
        rows8[n : n + 1, :] = vector[...].astype(F32)
    spread = jnp.where(iota((SHARD, WIDTH), 1) == dev * SHARD + iota((SHARD, WIDTH), 0), 1.0, 0.0)
    eight = dot(rows8[...].astype(BF16), spread.astype(BF16))
    lane = lax.rem(dev, 8) * DOWN
    spread_up = jnp.where(iota((DOWN, WIDTH), 1) == lane + iota((DOWN, WIDTH), 0), 1.0, 0.0)
    one = dot(jnp.broadcast_to(b_up[...], (8, DOWN)), spread_up.astype(BF16))
    one = jnp.where(iota((8, WIDTH), 0) == dev // 8, one, 0.0)
    block = jnp.concatenate([eight, one, jnp.zeros((8, WIDTH), F32)], axis=0).astype(BF16)
    for n in range(2):
        part = block[:, n * HALF : (n + 1) * HALF]
        keep[8 + n] = part
        send[8 + n] = part


def merge_body(place, keep, recv, chunk_q, chunk_u):
    def fill(even, odd):
        for n in range(4):
            chunk_q[n] = even[n]
            chunk_q[4 + n] = odd[n]
            chunk_u[n] = even[4 + n]
            chunk_u[4 + n] = odd[4 + n]

    @pl.when(place[0] == 0)
    def _():
        fill(keep, recv)

    @pl.when(place[0] == 1)
    def _():
        fill(recv, keep)

    for n in (8, 9):
        chunk_q[n] = (keep[n].astype(F32) + recv[n].astype(F32)).astype(BF16)


def z_slot(place, k):
    return lax.rem(place[2] + 4 - k, 4)


def zcat_q_body(place, own, r1, r2, r3, out):
    for k, part in enumerate((own, r1, r2, r3)):
        slot = z_slot(place, k) * 8
        for n in range(8):
            out[slot + n] = part[n]
    for n in (8, 9):
        total = own[n].astype(F32) + r1[n].astype(F32) + r2[n].astype(F32) + r3[n].astype(F32)
        out[24 + n] = total.astype(BF16)


def zcat_u_body(place, own, r1, r2, r3, out):
    for k, part in enumerate((own, r1, r2, r3)):
        slot = z_slot(place, k) * 8
        for n in range(8):
            out[slot + n] = part[n]


def pcat_d_body(place, own, r1, r2, r3, out):
    for r, part in enumerate((own, r1, r2, r3)):
        out[place[1] ^ r] = part[...]


def natural(place, parts, scr, n, count=8):
    for r, part in enumerate(parts):
        base = (place[1] ^ r) * (8 * SHARD)
        for z in range(4):
            for c in range(2):
                row = pl.multiple_of(base + c * 4 * SHARD + z * SHARD, 8)
                scr[pl.ds(row, SHARD), :] = part[z * count + c * 4 + n].astype(F32)


def on_core(place, action):
    @pl.when(place[0] == 0)
    def _():
        action(0)

    @pl.when(place[0] == 1)
    def _():
        action(1)


def table_rows(tok_rows, n_col):
    long_rows = max(2 * 512, 64 * n_col) // n_col
    short_rows = 512 // n_col
    units = tok_rows // short_rows
    long_count = max(1, units // (2 * (long_rows // short_rows)))
    tables, start = [], 0
    for _ in range(long_count):
        tables.append((start, long_rows))
        start += long_rows
    while start < tok_rows:
        tables.append((start, short_rows))
        start += short_rows
    return tables


def attend_body(tables, place, *refs):
    toks, parts = refs[:8], refs[8:12]
    (wqkv, wo, bias, q_out, k_out, v_out, mixed_out, mixed_low, lse_out) = refs[12:21]
    slab, tok, q3, k3, v3 = refs[21:]
    for n in range(3):
        natural(place, parts, slab, n)
        wqkv[:, n * HALF : (n + 1) * HALF] = slab[...].astype(BF16)
    natural(place, parts, slab, 3)
    wo[...] = slab[...].astype(BF16)
    for n in range(2):
        total = sum(part[32 + n].astype(F32) for part in parts)
        bias[:, n * HALF : (n + 1) * HALF] = total
    for n, ref in enumerate(toks):
        tok[n] = ref[...]
    rows = toks[0].shape[0]
    count = len(toks)
    k_all = dot(tok[...].reshape(count * rows, WIDTH), wqkv[:, HALF : 2 * HALF])
    k3[...] = k_all.astype(BF16).reshape(count, rows, HALF)

    def with_bias(c):
        q_bias = bias[0:1, c * HALF : (c + 1) * HALF]
        v_bias = bias[1:2, c * HALF : (c + 1) * HALF]
        q_all = dot(tok[0:2].reshape(2 * rows, WIDTH), wqkv[:, :HALF]) + q_bias
        q3[...] = q_all.astype(BF16).reshape(2, rows, HALF)
        v_all = dot(tok[...].reshape(count * rows, WIDTH), wqkv[:, 2 * HALF :]) + v_bias
        v3[...] = v_all.astype(BF16).reshape(count, rows, HALF)

    on_core(place, with_bias)
    q_out[...] = q3[...]
    k_out[...] = k3[...]
    v_out[...] = v3[...]
    for start, size in tables:
        lse = jnp.zeros((2 * size, 128), F32)
        for pair in range(3):
            lanes = slice(pair * 128, (pair + 1) * 128)
            qp = q3[:, start : start + size, lanes].reshape(2 * size, 128)
            kp = k3[:, start : start + size, lanes].reshape(count * size, 128)
            vp = v3[:, start : start + size, lanes].reshape(count * size, 128)
            low_half = iota(qp.shape, 1) < HD
            found = []
            for h in range(2):
                mine = low_half if h == 0 else jnp.logical_not(low_half)
                qm = jnp.where(mine, qp.astype(F32) * 0.125, 0.0).astype(BF16)
                scores = dot_nt(qm, kp)
                top = jnp.max(scores, axis=1, keepdims=True)
                expo = jnp.exp(scores - top)
                total = jnp.sum(expo, axis=1, keepdims=True)
                found.append(dot(expo.astype(BF16), vp) * (1.0 / total))
                lse = jnp.where(iota(lse.shape, 1) == pair * 2 + h, top + jnp.log(total), lse)
            mixed = jnp.where(low_half, found[0], found[1]).reshape(2, size, 128)
            mixed_out[:, start : start + size, lanes] = mixed
            mixed_low[:, start : start + size, lanes] = mixed.astype(BF16)
        lse_out[:, start : start + size, :] = lse.reshape(2, size, 128)


def norm_stats(values):
    center = values - jnp.mean(values, axis=1, keepdims=True)
    spread = jnp.mean(center * center, axis=1, keepdims=True)
    scale = lax.rsqrt(spread + NORM_EPS)
    return center * scale, scale


def norm_back(e, gain, vhat, scale):
    eg = e * gain
    mean_e = jnp.mean(eg, axis=1, keepdims=True)
    mean_ev = jnp.mean(eg * vhat, axis=1, keepdims=True)
    return scale * (eg - mean_e - vhat * mean_ev)


def flip(pair):
    return jnp.concatenate([pair[1], pair[0]], axis=0)


def forward_body(place, tok0, tok1, mine, other, wo_mine, wo_other, bias, *refs):
    u_parts, d_parts = refs[:4], refs[4:8]
    (partial, vhat_out, scale_out, normed_low, active, slope, wup, wdown, mixed, wo) = refs[8:18]
    slab, hidden = refs[18:]
    for u in range(4):
        natural(place, u_parts, slab, u)
        wup[:, u * HALF : (u + 1) * HALF] = slab[...].astype(BF16)
    for k, part in enumerate(d_parts):
        slot = z_slot(place, k)
        for y in range(4):
            wdown[y * 4 + slot] = part[y]
    rows = tok0.shape[0]

    def place_halves(c):
        mixed[:, c * HALF : (c + 1) * HALF] = mine[...].reshape(2 * rows, HALF)
        mixed[:, (1 - c) * HALF : (2 - c) * HALF] = flip(other)
        wo[:, c * HALF : (c + 1) * HALF] = wo_mine[...]
        wo[:, (1 - c) * HALF : (2 - c) * HALF] = wo_other[...]

    on_core(place, place_halves)
    hidden[...] = dot(mixed[...], wo[...]) + bias[2:3, :]
    hidden[:rows, :] += tok0[...].astype(F32)
    hidden[rows:, :] += tok1[...].astype(F32)
    vhat, scale = norm_stats(hidden[...])
    vhat_out[...] = vhat
    scale_out[...] = scale
    normed_low[...] = (vhat * bias[4:5, :] + bias[5:6, :]).astype(BF16)

    def up(c):
        for u in range(4):
            b = bias[8 + u : 9 + u, c * HALF : (c + 1) * HALF]
            upper = dot(normed_low[...], wup[:, u * HALF : (u + 1) * HALF]) + b
            cdf = 0.5 * (1.0 + lax.erf(upper * 0.7071067811865476))
            pdf = jnp.exp(-0.5 * upper * upper) * 0.3989422804014327
            active[:, u * HALF : (u + 1) * HALF] = (upper * cdf).astype(BF16)
            slope[:, u * HALF : (u + 1) * HALF] = (cdf + upper * pdf).astype(BF16)

    on_core(place, up)
    partial[...] = dot(active[...], wdown[...].reshape(4 * HALF, WIDTH)).astype(BF16).reshape(2, rows, WIDTH)


def back_ffn_body(place, perm, mine, other, vhat1, bias, cot0, cot1, slope, wup, wdown, *refs):
    layer_out, d_summed, d_down, d_upper, d_part, sums = refs
    rows = cot0.shape[0]
    summed = vhat1[...] * bias[4:5, :] + bias[5:6, :] + bias[3:4, :]
    summed = summed + mine[...].astype(F32).reshape(2 * rows, WIDTH) + flip(other).astype(F32)
    vhat, scale = norm_stats(summed)
    gain = bias[6:7, :]
    result = (vhat[:rows] * gain + bias[7:8, :]).astype(BF16)
    layer_out[...] = dot_tn(perm[...], result).astype(BF16)
    e = jnp.concatenate([cot0[...], cot1[...]], axis=0).astype(F32)
    sums[0:1, :] = jnp.sum(e * vhat, axis=0, keepdims=True)
    sums[1:2, :] = jnp.sum(e, axis=0, keepdims=True)
    grad = norm_back(e, gain, vhat, scale)
    d_summed[...] = grad
    low = grad.astype(BF16)
    d_down[...] = low
    sums[2:3, :] = jnp.sum(low.astype(F32), axis=0, keepdims=True)
    for u in range(4):
        d_active = dot_nt(d_down[...], wdown[u * 4 : (u + 1) * 4].reshape(HALF, WIDTH))
        part = (d_active * slope[:, u * HALF : (u + 1) * HALF].astype(F32)).astype(BF16)
        d_upper[:, u * HALF : (u + 1) * HALF] = part
        half = slice((u % 2) * HALF, (u % 2 + 1) * HALF)
        sums[3 + u // 2 : 4 + u // 2, half] = jnp.sum(part.astype(F32), axis=0, keepdims=True)
    sums[5:8, :] = jnp.zeros((3, WIDTH), F32)
    d_part[...] = dot_nt(d_upper[...], wup[...]).astype(BF16).reshape(2, rows, WIDTH)


def grad_down_body(place, active, d_down, *refs):
    outs, scr = refs[:4], refs[4]
    scr[...] = dot_tn(active[...], d_down[...])
    for k, out in enumerate(outs):
        z = lax.rem(place[2] + k, 4)
        for r in range(4):
            row = pl.multiple_of((place[1] ^ r) * (4 * DOWN) + z * DOWN, 8)
            out[r] = scr[pl.ds(row, DOWN), :].astype(BF16)


def cut_slabs(place, scr, outs, n, count):
    for r, out in enumerate(outs):
        base = (place[1] ^ r) * (8 * SHARD)
        for k in range(4):
            z = lax.rem(place[2] + k, 4)
            for c in range(2):
                row = pl.multiple_of(base + c * 4 * SHARD + z * SHARD, 8)
                out[k * count + c * 4 + n] = scr[pl.ds(row, SHARD), :].astype(BF16)


def grad_up_body(place, normed_low, d_upper, *refs):
    outs, scr = refs[:4], refs[4]
    for u in range(4):
        scr[...] = dot_tn(normed_low[...], d_upper[:, u * HALF : (u + 1) * HALF])
        cut_slabs(place, scr, outs, u, 8)


def back_attend_body(tables, place, d_summed, mine, other, vhat1, scale1, bias, wo, mixed, q3, k3, v3, lse, *refs):
    d_hidden_out, d_branch, dq_out, dk_out, dv_out, sums, dm3 = refs
    rows = d_hidden_out.shape[0]
    e = d_summed[...] + mine[...].astype(F32).reshape(2 * rows, WIDTH) + flip(other).astype(F32)
    vhat = vhat1[...]
    sums[0:1, :] = jnp.sum(e * vhat, axis=0, keepdims=True)
    sums[1:2, :] = jnp.sum(e, axis=0, keepdims=True)
    d_hidden = norm_back(e, bias[4:5, :], vhat, scale1[...])
    d_hidden_out[...] = d_hidden[:rows]
    low = d_hidden.astype(BF16)
    d_branch[...] = low
    sums[2:3, :] = jnp.sum(low.astype(F32), axis=0, keepdims=True)
    wo_rows = wo[pl.ds(pl.multiple_of(place[0] * HALF, HALF), HALF), :]
    dm3[...] = dot_nt(d_branch[...], wo_rows).astype(BF16).reshape(2, rows, HALF)
    count = k3.shape[0]
    for start, size in tables:
        for pair in range(3):
            lanes = slice(pair * 128, (pair + 1) * 128)
            qp = q3[:, start : start + size, lanes].reshape(2 * size, 128).astype(F32) * 0.125
            dp = dm3[:, start : start + size, lanes].reshape(2 * size, 128).astype(F32)
            mp = mixed[:, start : start + size, lanes].reshape(2 * size, 128)
            kp = k3[:, start : start + size, lanes].reshape(count * size, 128)
            vp = v3[:, start : start + size, lanes].reshape(count * size, 128)
            logs = lse[:, start : start + size, :].reshape(2 * size, 128)
            low_half = iota(qp.shape, 1) < HD
            found, d_key, d_value = [], None, None
            for h in range(2):
                mine_h = low_half if h == 0 else jnp.logical_not(low_half)
                qm = jnp.where(mine_h, qp, 0.0).astype(BF16)
                dmask = jnp.where(mine_h, dp, 0.0)
                delta = jnp.sum(dmask * mp, axis=1, keepdims=True)
                dm = dmask.astype(BF16)
                column = pair * 2 + h
                probs = jnp.exp(dot_nt(qm, kp) - logs[:, column : column + 1])
                part = dot_tn(probs.astype(BF16), dm)
                d_value = part if d_value is None else d_value + part
                d_scores = (probs * (dot_nt(dm, vp) - delta)).astype(BF16)
                found.append(dot(d_scores, kp))
                part = dot_tn(d_scores, qm)
                d_key = part if d_key is None else d_key + part
            d_query = jnp.where(low_half, found[0], found[1]) * 0.125
            dq_out[:, start : start + size, lanes] = d_query.astype(BF16).reshape(2, size, 128)
            dk_out[:, start : start + size, lanes] = d_key.astype(BF16).reshape(count, size, 128)
            dv_out[:, start : start + size, lanes] = d_value.astype(BF16).reshape(count, size, 128)
    sums[3:8, :] = jnp.zeros((5, WIDTH), F32)
    q_sum = jnp.sum(dq_out[...].reshape(2 * rows, HALF).astype(F32), axis=0, keepdims=True)
    v_sum = jnp.sum(dv_out[...].reshape(count * rows, HALF).astype(F32), axis=0, keepdims=True)

    def sides(c):
        sums[3:4, c * HALF : (c + 1) * HALF] = q_sum
        sums[4:5, c * HALF : (c + 1) * HALF] = v_sum

    on_core(place, sides)


def grad_qkvo_body(place, *refs):
    toks = refs[:8]
    dq, dk, dv, mixed, d_branch, sums_ffn, sums_attn = refs[8:15]
    outs, scr, tok, block = refs[15:19], refs[19], refs[20], refs[21]
    rows = toks[0].shape[0]
    count = len(toks)
    for n, ref in enumerate(toks):
        tok[n * rows : (n + 1) * rows, :] = ref[...]
    scr[...] = dot_tn(tok[: 2 * rows], dq[...].reshape(2 * rows, HALF))
    cut_slabs(place, scr, outs, 0, 8)
    scr[...] = dot_tn(tok[...], dk[...].reshape(count * rows, HALF))
    cut_slabs(place, scr, outs, 1, 8)
    scr[...] = dot_tn(tok[...], dv[...].reshape(count * rows, HALF))
    cut_slabs(place, scr, outs, 2, 8)

    def out_half(c):
        scr[...] = dot_tn(mixed[...], d_branch[:, c * HALF : (c + 1) * HALF])

    on_core(place, out_half)
    cut_slabs(place, scr, outs, 3, 8)
    once = jnp.where(place[0] == 0, 1.0, 0.0)
    block[...] = jnp.zeros(block.shape, F32)
    block[0:2, :] = sums_attn[3:5, :]
    block[2:3, :] = sums_attn[2:3, :] * once
    block[3:4, :] = sums_ffn[2:3, :] * once
    block[4:6, :] = sums_attn[0:2, :] * once
    block[6:8, :] = sums_ffn[0:2, :] * once

    def up_rows(c):
        for u in range(4):
            half = sums_ffn[3 + u // 2 : 4 + u // 2, (u % 2) * HALF : (u % 2 + 1) * HALF]
            block[8 + u : 9 + u, c * HALF : (c + 1) * HALF] = half

    on_core(place, up_rows)
    for out in outs:
        for n in range(2):
            out[32 + n] = block[:, n * HALF : (n + 1) * HALF].astype(BF16)


def grad_tok_body(place, dq, dk, dv, wqkv, same, sib):
    rows = same.shape[1]
    count = dk.shape[0]
    for n in range(count):
        total = dot_nt(dk[n], wqkv[:, HALF : 2 * HALF]) + dot_nt(dv[n], wqkv[:, 2 * HALF :])
        if n < 2:
            total = total + dot_nt(dq[n], wqkv[:, :HALF])
        (same if n % 2 == 0 else sib)[n // 2] = total.astype(BF16)


def sum_tok_body(place, same, recv, own, s1, s2, s3):
    for r, out in enumerate((own, s1, s2, s3)):
        out[...] = (same[r].astype(F32) + recv[r].astype(F32)).astype(BF16)


def last_tok_body(place, perm, d_hidden, own, r1, r2, r3, out):
    total = d_hidden[...]
    for part in (own, r1, r2, r3):
        total = total + part[...].astype(F32)
    high = total.astype(BF16)
    left = total - high.astype(F32)
    middle = left.astype(BF16)
    low = (left - middle.astype(F32)).astype(BF16)
    out[...] = dot_tn(perm[...], high) + dot_tn(perm[...], middle) + dot_tn(perm[...], low)


def added(parts, index):
    total = parts[0][index].astype(F32)
    for part in parts[1:]:
        total = total + part[index].astype(F32)
    return total


def sum_plane_body(extra, place, own, r1, r2, r3, *outs):
    parts = (own, r1, r2, r3)
    for k, out in enumerate(outs):
        for n in range(8):
            out[n] = added(parts, k * 8 + n).astype(BF16)
    if extra:
        for n in range(2):
            total = added(parts, 32 + n).astype(BF16)
            for out in outs:
                out[8 + n] = total


def sum_down_body(place, own, r1, r2, r3, *outs):
    for r, out in enumerate(outs):
        out[...] = added((own, r1, r2, r3), r).astype(BF16)


def last_down_body(place, own, r1, r2, r3, out):
    out[...] = added((own, r1, r2, r3), slice(None))


def sum_last_body(place, q0, q1, q2, q3, u0, u1, u2, u3, keep, send):
    q_parts, u_parts = (q0, q1, q2, q3), (u0, u1, u2, u3)

    def fill(mine):
        for n in range(4):
            keep[n] = added(q_parts, mine * 4 + n)
            send[n] = added(q_parts, (1 - mine) * 4 + n)
            keep[4 + n] = added(u_parts, mine * 4 + n)
            send[4 + n] = added(u_parts, (1 - mine) * 4 + n)

    on_core(place, fill)
    for n in (8, 9):
        total = added(q_parts, n)
        keep[n] = total
        send[n] = total


def last_body(place, keep, recv, gq, gk, gv, go, gup, vectors, ups):
    def fill(c):
        for n, out in enumerate((gq, gk, gv, go)):
            out[:, c * HALF : (c + 1) * HALF] = keep[n]
            out[:, (1 - c) * HALF : (2 - c) * HALF] = recv[n]
        for u in range(4):
            gup[:, u * WIDTH + c * HALF : u * WIDTH + (c + 1) * HALF] = keep[4 + u]
            gup[:, u * WIDTH + (1 - c) * HALF : u * WIDTH + (2 - c) * HALF] = recv[4 + u]

    on_core(place, fill)
    dev = place[3]
    total = jnp.concatenate([keep[8] + recv[8], keep[9] + recv[9]], axis=1)
    pick = jnp.where(iota((WIDTH, 128), 0) == dev * SHARD + iota((WIDTH, 128), 1), 1.0, 0.0)
    high = lax.Precision.HIGHEST
    vectors[...] = jnp.dot(total, pick, precision=high, preferred_element_type=F32)
    lane = lax.rem(dev, 8) * DOWN
    pick_up = jnp.where(iota((WIDTH, 128), 0) == lane + iota((WIDTH, 128), 1), 1.0, 0.0)
    rows = jnp.where(iota(total.shape, 0) == 8 + dev // 8, total, 0.0)
    row = jnp.broadcast_to(jnp.sum(rows, axis=0, keepdims=True), (8, WIDTH))
    ups[...] = jnp.dot(row, pick_up, precision=high, preferred_element_type=F32)


def fast_device(
    tokens,
    table_ids,
    w_query,
    w_key,
    w_value,
    w_out,
    w_up,
    w_down,
    b_query,
    b_value,
    b_out,
    b_up,
    b_down,
    gain_attn,
    shift_attn,
    gain_ffn,
    shift_ffn,
    cotangent,
):
    col, z = lax.axis_index("col"), lax.axis_index("seq")
    place = jnp.stack([col % 2, col // 2, z, col * 4 + z]).astype(jnp.int32)
    rows = tokens.shape[0]
    tables = table_rows(rows, 8)

    def swap(x):
        return lax.ppermute(x, "col", [(i, i ^ 1) for i in range(8)])

    def plane(x, r):
        return lax.ppermute(x, "col", [(i, i ^ (2 * r)) for i in range(8)])

    def shift(x, k):
        return lax.ppermute(x, "seq", [(i, (i + k) % 4) for i in range(4)])

    def planes(x):
        return (x, plane(x, 1), plane(x, 2), plane(x, 3))

    def shifts(x):
        return (x, shift(x, 1), shift(x, 2), shift(x, 3))

    down_parts = planes(w_down)
    vectors = (b_query, b_value, b_out, b_down, gain_attn, shift_attn, gain_ffn, shift_ffn)
    perm, tok_sorted, cot_sorted, keep, send = call(
        prep_body,
        "prep",
        place,
        (table_ids.reshape(1, rows), tokens, cotangent, w_query, w_key, w_value, w_out, w_up)
        + tuple(v.reshape(1, SHARD) for v in vectors)
        + (b_up.reshape(1, DOWN),),
        (
            ((rows, rows), BF16),
            ((rows, WIDTH), BF16),
            ((rows, WIDTH), BF16),
            ((10,) + SLAB, BF16),
            ((10,) + SLAB, BF16),
        ),
        (pltpu.VMEM((8, SHARD), F32),),
    )
    chunk_q, chunk_u = call(
        merge_body, "merge", place, (keep, swap(send)), (((10,) + SLAB, BF16), ((8,) + SLAB, BF16))
    )
    (plane_q,) = call(zcat_q_body, "zcat_q", place, shifts(chunk_q), (((34,) + SLAB, BF16),))
    q_parts = planes(plane_q)
    same_core = planes(tok_sorted)
    toks = tuple(t for part in same_core for t in (part, swap(part)))
    cot_other = swap(cot_sorted)
    (plane_u,) = call(zcat_u_body, "zcat_u", place, shifts(chunk_u), (((32,) + SLAB, BF16),))
    u_parts = planes(plane_u)
    (column_d,) = call(pcat_d_body, "pcat_d", place, down_parts, (((4, DOWN, WIDTH), BF16),))
    d_parts = shifts(column_d)

    heads = ((2, rows, HALF), BF16)
    heads_all = ((8, rows, HALF), BF16)
    wqkv, wo_mine, bias, q3, k3, v3, mixed3, mixed_low, lse = call(
        functools.partial(attend_body, tables),
        "attend",
        place,
        toks + q_parts,
        (
            ((WIDTH, 3 * HALF), BF16),
            ((WIDTH, HALF), BF16),
            ((SHARD, WIDTH), F32),
            heads,
            heads_all,
            heads_all,
            ((2, rows, HALF), F32),
            heads,
            ((2, rows, 128), F32),
        ),
        (
            pltpu.VMEM((WIDTH, HALF), F32),
            pltpu.VMEM((8, rows, WIDTH), BF16),
            pltpu.VMEM((2, rows, HALF), BF16),
            pltpu.VMEM((8, rows, HALF), BF16),
            pltpu.VMEM((8, rows, HALF), BF16),
        ),
    )
    pair = ((2, rows, WIDTH), BF16)
    full = (2 * rows, WIDTH)
    wide = ((2 * rows, 4 * HALF), BF16)
    partial, vhat, scale, normed_low, active, slope, wup, wdown, mixed, wo = call(
        forward_body,
        "forward",
        place,
        (toks[0], toks[1], mixed_low, swap(mixed_low), wo_mine, swap(wo_mine), bias) + u_parts + d_parts,
        (
            pair,
            (full, F32),
            ((2 * rows, 1), F32),
            (full, BF16),
            wide,
            wide,
            ((WIDTH, 4 * HALF), BF16),
            ((16, DOWN, WIDTH), BF16),
            (full, BF16),
            ((WIDTH, WIDTH), BF16),
        ),
        (pltpu.VMEM((WIDTH, HALF), F32), pltpu.VMEM(full, F32)),
    )
    layer_out, d_summed, d_down, d_upper, d_part, sums_ffn = call(
        back_ffn_body,
        "back_ffn",
        place,
        (perm, partial, swap(partial), vhat, bias, cot_sorted, cot_other, slope, wup, wdown),
        (((rows, WIDTH), BF16), (full, F32), (full, BF16), wide, pair, ((8, WIDTH), F32)),
    )
    d_part_other = swap(d_part)
    g_down = call(
        grad_down_body,
        "grad_down",
        place,
        (active, d_down),
        (((4, DOWN, WIDTH), BF16),) * 4,
        (pltpu.VMEM((4 * HALF, WIDTH), F32),),
    )
    g_down = (g_down[0],) + tuple(shift(g_down[k], k) for k in (1, 2, 3))
    g_up = call(
        grad_up_body,
        "grad_up",
        place,
        (normed_low, d_upper),
        (((32,) + SLAB, BF16),) * 4,
        (pltpu.VMEM((WIDTH, HALF), F32),),
    )
    g_up = (g_up[0],) + tuple(plane(g_up[r], r) for r in (1, 2, 3))
    d_hidden, d_branch, dq, dk, dv, sums_attn = call(
        functools.partial(back_attend_body, tables),
        "back_attend",
        place,
        (d_summed, d_part, d_part_other, vhat, scale, bias, wo, mixed3, q3, k3, v3, lse),
        (((rows, WIDTH), F32), (full, BF16), heads, heads_all, heads_all, ((8, WIDTH), F32)),
        (pltpu.VMEM((2, rows, HALF), BF16),),
    )
    g_q = call(
        grad_qkvo_body,
        "grad_qkvo",
        place,
        toks + (dq, dk, dv, mixed, d_branch, sums_ffn, sums_attn),
        (((34,) + SLAB, BF16),) * 4,
        (
            pltpu.VMEM((WIDTH, HALF), F32),
            pltpu.VMEM((8 * rows, WIDTH), BF16),
            pltpu.VMEM((SHARD, WIDTH), F32),
        ),
    )
    g_q = (g_q[0],) + tuple(plane(g_q[r], r) for r in (1, 2, 3))
    quad = ((4, rows, WIDTH), BF16)
    same, sib = call(grad_tok_body, "grad_tok", place, (dq, dk, dv, wqkv), (quad, quad))
    s_tok = call(sum_tok_body, "sum_tok", place, (same, swap(sib)), (((rows, WIDTH), BF16),) * 4)
    s_tok = (s_tok[0],) + tuple(plane(s_tok[r], r) for r in (1, 2, 3))

    s_up = call(
        functools.partial(sum_plane_body, False), "sum_up", place, g_up, (((8,) + SLAB, BF16),) * 4
    )
    s_up = (s_up[0],) + tuple(shift(s_up[k], k) for k in (1, 2, 3))
    s_down = call(sum_down_body, "sum_down", place, g_down, (((DOWN, WIDTH), BF16),) * 4)
    s_down = (s_down[0],) + tuple(plane(s_down[r], r) for r in (1, 2, 3))
    s_q = call(
        functools.partial(sum_plane_body, True), "sum_q", place, g_q, (((10,) + SLAB, BF16),) * 4
    )
    s_q = (s_q[0],) + tuple(shift(s_q[k], k) for k in (1, 2, 3))
    (grad_tokens,) = call(
        last_tok_body, "last_tok", place, (perm, d_hidden) + s_tok, (((rows, WIDTH), F32),)
    )
    (grad_down,) = call(last_down_body, "last_down", place, s_down, (((DOWN, WIDTH), F32),))
    kept, sent = call(
        sum_last_body, "sum_last", place, s_q + s_up, (((10,) + SLAB, F32), ((10,) + SLAB, F32))
    )
    row = ((SHARD, WIDTH), F32)
    gq, gk, gv, go, gup, small, ups = call(
        last_body,
        "last",
        place,
        (kept, swap(sent)),
        (row, row, row, row, ((SHARD, 4 * WIDTH), F32), ((SHARD, 128), F32), ((8, 128), F32)),
    )
    small = small[:, :SHARD]
    return (
        layer_out,
        grad_tokens,
        gq,
        gk,
        gv,
        go,
        gup,
        grad_down,
        small[0],
        small[1],
        small[2],
        ups[0, :DOWN],
        small[3],
        small[4],
        small[5],
        small[6],
        small[7],
    )


def solution(mesh):
    placed = (
        P(("col", "seq"), None),
        P(("col", "seq")),
        P(("col", "seq"), None),
        P(("col", "seq"), None),
        P(("col", "seq"), None),
        P(("col", "seq"), None),
        P(("col", "seq"), None),
        P(("col", "seq"), None),
        P(("col", "seq")),
        P(("col", "seq")),
        P(("col", "seq")),
        P(("col", "seq")),
        P(("col", "seq")),
        P(("col", "seq")),
        P(("col", "seq")),
        P(("col", "seq")),
        P(("col", "seq")),
        P(("col", "seq"), None),
    )
    fast = mesh.shape["col"] == 8 and mesh.shape["seq"] == 4
    return jax.shard_map(
        fast_device if fast else per_device,
        mesh=mesh,
        in_specs=placed,
        out_specs=(
            P(("col", "seq"), None),
            P(("col", "seq"), None),
            P(("col", "seq"), None),
            P(("col", "seq"), None),
            P(("col", "seq"), None),
            P(("col", "seq"), None),
            P(("col", "seq"), None),
            P(("col", "seq"), None),
            P(("col", "seq")),
            P(("col", "seq")),
            P(("col", "seq")),
            P(("col", "seq")),
            P(("col", "seq")),
            P(("col", "seq")),
            P(("col", "seq")),
            P(("col", "seq")),
            P(("col", "seq")),
        ),
        check_vma=False,
    )
```

```python
import functools

import jax
import jax.numpy as jnp
import numpy as np
from jax import lax
from jax.experimental import pallas as pl
from jax.experimental.pallas import tpu as pltpu
from jax.sharding import PartitionSpec as P

H = 12
HD = 64


NEG_BIG = -1e30
NORM_EPS = 1e-12
LOW_TYPE = jnp.bfloat16
FULL_TYPE = jnp.float32


def block_length(unit_rows):
    target = unit_rows * max(1, -(-512 // unit_rows))
    return target


def layer_norm(values, gain, shift):
    center = values - jnp.mean(values, axis=-1, keepdims=True)
    spread = jnp.mean(center * center, axis=-1, keepdims=True)
    return center * lax.rsqrt(spread + NORM_EPS) * gain + shift


def gelu_exact(values):
    return jax.nn.gelu(values, approximate=False)


def project(left, right, bias):
    return jnp.dot(left, right, preferred_element_type=FULL_TYPE) + bias.astype(FULL_TYPE)


def attend(running, query_heads, query_ids, key_slab, value_slab, key_ids):
    maxima, totals, weighted = running
    scores = (
        jnp.einsum("thd,shd->hts", query_heads, key_slab, preferred_element_type=FULL_TYPE) * 0.125
    )
    visible = (query_ids[:, None] == key_ids[None, :])[None]
    scores = jnp.where(visible, scores, NEG_BIG)
    new_max = jnp.maximum(maxima, jnp.max(scores, axis=2))
    rescale = jnp.exp(maxima - new_max)
    exponents = jnp.where(visible, jnp.exp(scores - new_max[:, :, None]), 0.0)
    totals = totals * rescale + jnp.sum(exponents, axis=2)
    weighted = weighted * rescale[:, :, None] + jnp.einsum(
        "hts,shd->htd", exponents.astype(LOW_TYPE), value_slab, preferred_element_type=FULL_TYPE
    )
    return (new_max, totals, weighted)


def grad_block(
    query_heads, dout_heads, log_totals, row_delta, query_ids, key_slab, value_slab, key_ids
):
    scores = (
        jnp.einsum("thd,shd->hts", query_heads, key_slab, preferred_element_type=FULL_TYPE) * 0.125
    )
    visible = (query_ids[:, None] == key_ids[None, :])[None]
    probabilities = jnp.where(visible, jnp.exp(scores - log_totals[:, :, None]), 0.0)
    grad_value = jnp.einsum(
        "hts,thd->shd", probabilities.astype(LOW_TYPE), dout_heads, preferred_element_type=FULL_TYPE
    )
    grad_probs = jnp.einsum(
        "thd,shd->hts", dout_heads, value_slab, preferred_element_type=FULL_TYPE
    )
    grad_scores = (probabilities * (grad_probs - row_delta[:, :, None])).astype(LOW_TYPE)
    grad_query = (
        jnp.einsum("hts,shd->thd", grad_scores, key_slab, preferred_element_type=FULL_TYPE) * 0.125
    )
    grad_key = (
        jnp.einsum("hts,thd->shd", grad_scores, query_heads, preferred_element_type=FULL_TYPE)
        * 0.125
    )
    return (grad_query, grad_key, grad_value)


def per_device(
    tokens,
    table_ids,
    w_query,
    w_key,
    w_value,
    w_out,
    w_up,
    w_down,
    b_query,
    b_value,
    b_out,
    b_up,
    b_down,
    gain_attn,
    shift_attn,
    gain_ffn,
    shift_ffn,
    cotangent,
):
    shards = (
        w_query,
        w_key,
        w_value,
        w_out,
        w_up,
        w_down,
        b_query,
        b_value,
        b_out,
        b_up,
        b_down,
        gain_attn,
        shift_attn,
        gain_ffn,
        shift_ffn,
    )
    gathered = (
        lax.all_gather(shards[0], ("col", "seq"), axis=0, tiled=True),
        lax.all_gather(shards[1], ("col", "seq"), axis=0, tiled=True),
        lax.all_gather(shards[2], ("col", "seq"), axis=0, tiled=True),
        lax.all_gather(shards[3], ("col", "seq"), axis=0, tiled=True),
        lax.all_gather(shards[4], ("col", "seq"), axis=0, tiled=True),
        lax.all_gather(shards[5], ("col", "seq"), axis=0, tiled=True),
        lax.all_gather(shards[6], ("col", "seq"), axis=0, tiled=True),
        lax.all_gather(shards[7], ("col", "seq"), axis=0, tiled=True),
        lax.all_gather(shards[8], ("col", "seq"), axis=0, tiled=True),
        lax.all_gather(shards[9], ("col", "seq"), axis=0, tiled=True),
        lax.all_gather(shards[10], ("col", "seq"), axis=0, tiled=True),
        lax.all_gather(shards[11], ("col", "seq"), axis=0, tiled=True),
        lax.all_gather(shards[12], ("col", "seq"), axis=0, tiled=True),
        lax.all_gather(shards[13], ("col", "seq"), axis=0, tiled=True),
        lax.all_gather(shards[14], ("col", "seq"), axis=0, tiled=True),
    )
    query_mat, key_mat, value_mat, out_mat, up_mat, down_mat = (
        gathered[0],
        gathered[1],
        gathered[2],
        gathered[3],
        gathered[4],
        gathered[5],
    )
    query_bias, value_bias, out_bias, up_bias, down_bias = (
        gathered[6],
        gathered[7],
        gathered[8],
        gathered[9],
        gathered[10],
    )
    attn_gain, attn_shift, ffn_gain, ffn_shift = (
        gathered[11],
        gathered[12],
        gathered[13],
        gathered[14],
    )
    tok_rows = tokens.shape[0]
    ids_all = lax.all_gather(table_ids, "col", axis=0, tiled=True)
    inputs = tokens.astype(FULL_TYPE)
    queries = project(tokens, query_mat, query_bias).astype(LOW_TYPE)
    keys = jnp.dot(tokens, key_mat, preferred_element_type=FULL_TYPE).astype(LOW_TYPE)
    values = project(tokens, value_mat, value_bias).astype(LOW_TYPE)
    query_heads = queries.reshape(tok_rows, H, HD)
    starting = (
        jnp.full((H, tok_rows), NEG_BIG, FULL_TYPE),
        jnp.zeros((H, tok_rows), FULL_TYPE),
        jnp.zeros((H, tok_rows, HD), FULL_TYPE),
    )
    running = starting
    key_rows = lax.all_gather(keys, "col", axis=0, tiled=True)
    value_rows = lax.all_gather(values, "col", axis=0, tiled=True)
    row_count = key_rows.shape[0]
    length = block_length(tok_rows)
    blocks = row_count // length

    def advance(current, pieces):
        return (attend(current, query_heads, table_ids, pieces[0], pieces[1], pieces[2]), None)

    running, _ = lax.scan(
        advance,
        running,
        (
            key_rows.reshape(blocks, length, H, HD),
            value_rows.reshape(blocks, length, H, HD),
            ids_all.reshape(blocks, length),
        ),
    )
    maxima, totals, weighted = running
    attn_heads = weighted / totals[:, :, None]
    log_totals = maxima + jnp.log(totals)
    attn_low = attn_heads.transpose(1, 0, 2).reshape(tok_rows, H * HD).astype(LOW_TYPE)
    hidden = inputs + project(attn_low, out_mat, out_bias)
    normed, norm_first = jax.vjp(
        layer_norm, hidden, attn_gain.astype(FULL_TYPE), attn_shift.astype(FULL_TYPE)
    )
    normed_low = normed.astype(LOW_TYPE)
    upper = project(normed_low, up_mat, up_bias)
    active, gelu_back = jax.vjp(gelu_exact, upper)
    active_low = active.astype(LOW_TYPE)
    summed = normed + project(active_low, down_mat, down_bias)
    result, norm_second = jax.vjp(
        layer_norm, summed, ffn_gain.astype(FULL_TYPE), ffn_shift.astype(FULL_TYPE)
    )
    again = (
        lax.all_gather(w_query, ("col", "seq"), axis=0, tiled=True),
        lax.all_gather(w_key, ("col", "seq"), axis=0, tiled=True),
        lax.all_gather(w_value, ("col", "seq"), axis=0, tiled=True),
        lax.all_gather(w_out, ("col", "seq"), axis=0, tiled=True),
        lax.all_gather(w_up, ("col", "seq"), axis=0, tiled=True),
        lax.all_gather(w_down, ("col", "seq"), axis=0, tiled=True),
    )
    query_mat, key_mat, value_mat, out_mat, up_mat, down_mat = (
        again[0],
        again[1],
        again[2],
        again[3],
        again[4],
        again[5],
    )
    d_summed, d_ffn_gain, d_ffn_shift = norm_second(cotangent.astype(FULL_TYPE))
    d_down = d_summed.astype(LOW_TYPE)
    grad_down = jnp.einsum("tf,td->fd", active_low, d_down, preferred_element_type=FULL_TYPE)
    d_active = jnp.einsum("td,fd->tf", d_down, down_mat, preferred_element_type=FULL_TYPE)
    d_upper = gelu_back(d_active)[0].astype(LOW_TYPE)
    grad_up = jnp.einsum("td,tf->df", normed_low, d_upper, preferred_element_type=FULL_TYPE)
    d_normed = d_summed + jnp.einsum("tf,df->td", d_upper, up_mat, preferred_element_type=FULL_TYPE)
    d_hidden, d_attn_gain, d_attn_shift = norm_first(d_normed)
    d_branch = d_hidden.astype(LOW_TYPE)
    grad_out = jnp.einsum("tc,td->cd", attn_low, d_branch, preferred_element_type=FULL_TYPE)
    d_attn = jnp.einsum("td,cd->tc", d_branch, out_mat, preferred_element_type=FULL_TYPE).astype(
        LOW_TYPE
    )
    dout_heads = d_attn.reshape(tok_rows, H, HD)
    row_delta = jnp.einsum("thd,htd->ht", dout_heads.astype(FULL_TYPE), attn_heads)
    key_all, value_all = (
        lax.all_gather(keys, "col", axis=0, tiled=True),
        lax.all_gather(values, "col", axis=0, tiled=True),
    )
    total_rows = key_all.shape[0]
    length = block_length(tok_rows)
    blocks = total_rows // length

    def key_pass(grad_sum, pieces):
        grad_query_part, grad_key_part, grad_value_part = grad_block(
            query_heads,
            dout_heads,
            log_totals,
            row_delta,
            table_ids,
            pieces[0],
            pieces[1],
            pieces[2],
        )
        return (grad_sum + grad_query_part, (grad_key_part, grad_value_part))

    query_sum, (key_parts, value_parts) = lax.scan(
        key_pass,
        jnp.zeros((tok_rows, H, HD), FULL_TYPE),
        (
            key_all.reshape(blocks, length, H, HD),
            value_all.reshape(blocks, length, H, HD),
            ids_all.reshape(blocks, length),
        ),
    )
    key_sum, value_sum = (
        lax.psum_scatter(
            key_parts.reshape(total_rows, H * HD).astype(jnp.bfloat16),
            "col",
            scatter_dimension=0,
            tiled=True,
        ).astype(jnp.float32),
        lax.psum_scatter(
            value_parts.reshape(total_rows, H * HD).astype(jnp.bfloat16),
            "col",
            scatter_dimension=0,
            tiled=True,
        ).astype(jnp.float32),
    )
    query_sum = query_sum.reshape(tok_rows, H * HD)
    query_low = query_sum.astype(LOW_TYPE)
    key_low = key_sum.astype(LOW_TYPE)
    value_low = value_sum.astype(LOW_TYPE)
    grad_query = jnp.einsum("tc,td->cd", tokens, query_low, preferred_element_type=FULL_TYPE)
    grad_key = jnp.einsum("tc,td->cd", tokens, key_low, preferred_element_type=FULL_TYPE)
    grad_value = jnp.einsum("tc,td->cd", tokens, value_low, preferred_element_type=FULL_TYPE)
    d_tokens = d_hidden + jnp.einsum(
        "td,cd->tc", query_low, query_mat, preferred_element_type=FULL_TYPE
    )
    d_tokens = d_tokens + jnp.einsum(
        "td,cd->tc", key_low, key_mat, preferred_element_type=FULL_TYPE
    )
    d_tokens = d_tokens + jnp.einsum(
        "td,cd->tc", value_low, value_mat, preferred_element_type=FULL_TYPE
    )
    sums_local = (
        grad_query,
        grad_key,
        grad_value,
        grad_out,
        grad_up,
        grad_down,
        jnp.sum(query_low.astype(FULL_TYPE), axis=0),
        jnp.sum(value_low.astype(FULL_TYPE), axis=0),
        jnp.sum(d_branch.astype(FULL_TYPE), axis=0),
        jnp.sum(d_upper.astype(FULL_TYPE), axis=0),
        jnp.sum(d_down.astype(FULL_TYPE), axis=0),
        d_attn_gain,
        d_attn_shift,
        d_ffn_gain,
        d_ffn_shift,
    )
    owned = (
        lax.psum_scatter(sums_local[0], ("col", "seq"), scatter_dimension=0, tiled=True),
        lax.psum_scatter(sums_local[1], ("col", "seq"), scatter_dimension=0, tiled=True),
        lax.psum_scatter(sums_local[2], ("col", "seq"), scatter_dimension=0, tiled=True),
        lax.psum_scatter(sums_local[3], ("col", "seq"), scatter_dimension=0, tiled=True),
        lax.psum_scatter(sums_local[4], ("col", "seq"), scatter_dimension=0, tiled=True),
        lax.psum_scatter(sums_local[5], ("col", "seq"), scatter_dimension=0, tiled=True),
        lax.psum_scatter(sums_local[6], ("col", "seq"), scatter_dimension=0, tiled=True),
        lax.psum_scatter(sums_local[7], ("col", "seq"), scatter_dimension=0, tiled=True),
        lax.psum_scatter(sums_local[8], ("col", "seq"), scatter_dimension=0, tiled=True),
        lax.psum_scatter(sums_local[9], ("col", "seq"), scatter_dimension=0, tiled=True),
        lax.psum_scatter(sums_local[10], ("col", "seq"), scatter_dimension=0, tiled=True),
        lax.psum_scatter(sums_local[11], ("col", "seq"), scatter_dimension=0, tiled=True),
        lax.psum_scatter(sums_local[12], ("col", "seq"), scatter_dimension=0, tiled=True),
        lax.psum_scatter(sums_local[13], ("col", "seq"), scatter_dimension=0, tiled=True),
        lax.psum_scatter(sums_local[14], ("col", "seq"), scatter_dimension=0, tiled=True),
    )
    return (result.astype(LOW_TYPE), d_tokens) + tuple(owned)


WIDTH = 768
HALF = WIDTH // 2
SHARD = 24
DOWN = 96
SLAB = (SHARD, HALF)
VMEM_BYTES = 60 * 2**20
F32 = jnp.float32
BF16 = jnp.bfloat16


COST_SCALE = 1.0
COST = {
    "attend": 17.0,
    "asm_u": 4.0,
    "forward": 12.0,
    "back_ffn": 9.5,
    "grad_down": 4.7,
    "grad_up": 5.0,
    "back_attend": 16.5,
    "grad_qkvo": 9.5,
    "grad_tok": 7.9,
}


def dot(left, right):
    return jnp.dot(left, right, preferred_element_type=F32)


def dot_nt(left, right):
    return lax.dot_general(left, right, (((1,), (1,)), ((), ())), preferred_element_type=F32)


def dot_tn(left, right):
    return lax.dot_general(left, right, (((0,), (0,)), ((), ())), preferred_element_type=F32)


def call(body, name, place, inputs, outs, scratch=(), after=(), through=()):
    vmem = pl.BlockSpec(memory_space=pltpu.VMEM)
    any_place = pl.BlockSpec(memory_space=pl.ANY)
    count = 1 + len(inputs)
    skipped = count + len(after) + len(through)

    def run(*refs):
        own = skipped + len(outs)
        body(*refs[:count], *refs[skipped:own], *refs[own + len(through) :])

    return pl.pallas_call(
        run,
        name=name,
        out_shape=tuple(jax.ShapeDtypeStruct(s, t) for s, t in outs)
        + tuple(jax.ShapeDtypeStruct(a.shape, a.dtype) for a in through),
        in_specs=[pl.BlockSpec(memory_space=pltpu.SMEM)] + [vmem] * len(inputs) + [any_place] * (len(after) + len(through)),
        out_specs=tuple(vmem for _ in outs) + tuple(any_place for _ in through),
        input_output_aliases={count + len(after) + n: len(outs) + n for n in range(len(through))},
        scratch_shapes=list(scratch),
        compiler_params=pltpu.CompilerParams(vmem_limit_bytes=VMEM_BYTES),
        cost_estimate=pl.CostEstimate(
            flops=int(1.15e9 * COST_SCALE * COST.get(name, 2.5)), bytes_accessed=0, transcendentals=0
        ),
    )(place, *inputs, *after, *through)


def iota(shape, dim):
    return lax.broadcasted_iota(jnp.int32, shape, dim)


def sort_body(place, ids, tokens, cot, perm_out, pair_out, tok_out):
    rows = tokens.shape[0]
    id_j = jnp.broadcast_to(ids[...].astype(F32), (rows, rows))
    id_i = id_j.T
    same = jnp.where(id_i == id_j, 1.0, 0.0)
    count_i = jnp.sum(same, axis=1, keepdims=True)
    count_j = jnp.sum(same, axis=0, keepdims=True)
    i, j = iota((rows, rows), 0), iota((rows, rows), 1)
    equal = jnp.where((id_i == id_j) & (i < j), 1.0, 0.0)
    tie = jnp.where((count_i == count_j) & (id_i < id_j), 1.0, 0.0)
    larger = jnp.where(count_i > count_j, 1.0, 0.0)
    position = jnp.sum(equal + tie + larger, axis=0, keepdims=True)
    perm = jnp.where(i.astype(F32) == position, 1.0, 0.0).astype(BF16)
    perm_out[...] = perm
    tok = dot(perm, tokens[...]).astype(BF16)
    pair_out[0] = tok
    pair_out[1] = dot(perm, cot[...]).astype(BF16)
    tok_out[...] = tok


def pack_body(place, wq, wk, wv, wo, wup, *rest):
    vectors, b_up = rest[:8], rest[8]
    keep, send, rows8 = rest[9:]
    dev = place[3]

    def split(mine):
        other = 1 - mine
        for n, w in enumerate((wq, wk, wv, wo)):
            keep[n] = w[:, mine * HALF : (mine + 1) * HALF]
            send[n] = w[:, other * HALF : (other + 1) * HALF]
        for u in range(4):
            keep[4 + u] = wup[:, u * WIDTH + mine * HALF : u * WIDTH + (mine + 1) * HALF]
            send[4 + u] = wup[:, u * WIDTH + other * HALF : u * WIDTH + (other + 1) * HALF]

    on_core(place, split)
    for n, vector in enumerate(vectors):
        rows8[n : n + 1, :] = vector[...].astype(F32)
    spread = jnp.where(iota((SHARD, WIDTH), 1) == dev * SHARD + iota((SHARD, WIDTH), 0), 1.0, 0.0)
    eight = dot(rows8[...].astype(BF16), spread.astype(BF16))
    lane = lax.rem(dev, 8) * DOWN
    spread_up = jnp.where(iota((DOWN, WIDTH), 1) == lane + iota((DOWN, WIDTH), 0), 1.0, 0.0)
    one = dot(jnp.broadcast_to(b_up[...], (8, DOWN)), spread_up.astype(BF16))
    one = jnp.where(iota((8, WIDTH), 0) == dev // 8, one, 0.0)
    block = jnp.concatenate([eight, one, jnp.zeros((8, WIDTH), F32)], axis=0).astype(BF16)
    for n in range(2):
        part = block[:, n * HALF : (n + 1) * HALF]
        keep[8 + n] = part
        send[8 + n] = part


def merge_body(place, keep, recv, chunk_q):
    def fill(mine):
        even, odd = (keep, recv) if mine == 0 else (recv, keep)
        for n in range(3):
            chunk_q[n] = even[n]
            chunk_q[3 + n] = odd[n]

    on_core(place, fill)
    for n in range(2):
        chunk_q[6 + n] = (keep[8 + n].astype(F32) + recv[8 + n].astype(F32)).astype(BF16)


def z_slot(place, k):
    return lax.rem(place[2] + 4 - k, 4)


def zcat_q_body(place, own, r1, r2, r3, keep, recv, out, chunk_u):
    for k, part in enumerate((own, r1, r2, r3)):
        slot = z_slot(place, k) * 6
        for n in range(6):
            out[slot + n] = part[n]
    for n in (6, 7):
        total = own[n].astype(F32) + r1[n].astype(F32) + r2[n].astype(F32) + r3[n].astype(F32)
        out[18 + n] = total.astype(BF16)

    def fill(mine):
        even, odd = (keep, recv) if mine == 0 else (recv, keep)
        for n in range(5):
            chunk_u[n] = even[3 + n]
            chunk_u[5 + n] = odd[3 + n]

    on_core(place, fill)


def zcat_u_body(place, own, r1, r2, r3, out):
    for k, part in enumerate((own, r1, r2, r3)):
        slot = z_slot(place, k) * 10
        for n in range(10):
            out[slot + n] = part[n]


def pcat_body(place, own, r1, r2, r3, column):
    for r, part in enumerate((own, r1, r2, r3)):
        column[place[1] ^ r] = part[...]


def tcat_body(place, r1, r2, r3, three):
    for r, part in enumerate((r1, r2, r3)):
        three[r] = part[...]


def asm_u_body(place, p0, p1, p2, p3, wo, wup, slab):
    parts = (p0, p1, p2, p3)
    natural(place, parts, slab, 0, 5)
    wo[...] = slab[...].astype(BF16)
    for u in range(4):
        natural(place, parts, slab, 1 + u, 5)
        wup[:, u * HALF : (u + 1) * HALF] = slab[...].astype(BF16)


def natural(place, parts, scr, n, count):
    for r, part in enumerate(parts):
        base = (place[1] ^ r) * (8 * SHARD)
        for z in range(4):
            for c in range(2):
                row = pl.multiple_of(base + c * 4 * SHARD + z * SHARD, 8)
                scr[pl.ds(row, SHARD), :] = part[(z * 2 + c) * count + n].astype(F32)


def on_core(place, action):
    @pl.when(place[0] == 0)
    def _():
        action(0)

    @pl.when(place[0] == 1)
    def _():
        action(1)


def table_rows(tok_rows, n_col):
    long_rows = max(2 * 512, 64 * n_col) // n_col
    short_rows = 512 // n_col
    units = tok_rows // short_rows
    long_count = max(1, units // (2 * (long_rows // short_rows)))
    tables, start = [], 0
    for _ in range(long_count):
        tables.append((start, long_rows))
        start += long_rows
    while start < tok_rows:
        tables.append((start, short_rows))
        start += short_rows
    return tables


def attend_body(tables, place, *refs):
    same, pair_sib, three_sib, parts = refs[:4], refs[4], refs[5], refs[6:10]
    (wqkv, bias, tok, q_out, k_out, v_out, mixed_out, mixed_low, lse_out) = refs[10:19]
    slab, q3, k3, v3 = refs[19:]
    count, rows = tok.shape[:2]
    for n in range(3):
        natural(place, parts, slab, n, 3)
        wqkv[:, n * HALF : (n + 1) * HALF] = slab[...].astype(BF16)
    for n in range(2):
        total = sum(part[24 + n].astype(F32) for part in parts)
        bias[:, n * HALF : (n + 1) * HALF] = total
    for n, part in enumerate(same):
        tok[2 * n] = part[...]
        tok[2 * n + 1] = pair_sib[0] if n == 0 else three_sib[n - 1]
    k_all = dot(tok[...].reshape(count * rows, WIDTH), wqkv[:, HALF : 2 * HALF])
    k3[...] = k_all.astype(BF16).reshape(count, rows, HALF)

    def with_bias(c):
        q_bias = bias[0:1, c * HALF : (c + 1) * HALF]
        v_bias = bias[1:2, c * HALF : (c + 1) * HALF]
        q_all = dot(tok[0:2].reshape(2 * rows, WIDTH), wqkv[:, :HALF]) + q_bias
        q3[...] = q_all.astype(BF16).reshape(2, rows, HALF)
        v_all = dot(tok[...].reshape(count * rows, WIDTH), wqkv[:, 2 * HALF :]) + v_bias
        v3[...] = v_all.astype(BF16).reshape(count, rows, HALF)

    on_core(place, with_bias)
    q_out[...] = q3[...]
    k_out[...] = k3[...]
    v_out[...] = v3[...]
    for start, size in tables:
        lse = jnp.zeros((2 * size, 128), F32)
        for pair in range(3):
            lanes = slice(pair * 128, (pair + 1) * 128)
            qp = q3[:, start : start + size, lanes].reshape(2 * size, 128)
            kp = k3[:, start : start + size, lanes].reshape(count * size, 128)
            vp = v3[:, start : start + size, lanes].reshape(count * size, 128)
            low_half = iota(qp.shape, 1) < HD
            found = []
            for h in range(2):
                mine = low_half if h == 0 else jnp.logical_not(low_half)
                qm = jnp.where(mine, qp.astype(F32) * 0.125, 0.0).astype(BF16)
                scores = dot_nt(qm, kp)
                top = jnp.max(scores, axis=1, keepdims=True)
                expo = jnp.exp(scores - top)
                total = jnp.sum(expo, axis=1, keepdims=True)
                found.append(dot(expo.astype(BF16), vp) * (1.0 / total))
                lse = jnp.where(iota(lse.shape, 1) == pair * 2 + h, top + jnp.log(total), lse)
            mixed = jnp.where(low_half, found[0], found[1]).reshape(2, size, 128)
            mixed_out[:, start : start + size, lanes] = mixed
            mixed_low[:, start : start + size, lanes] = mixed.astype(BF16)
        lse_out[:, start : start + size, :] = lse.reshape(2, size, 128)


def norm_stats(values):
    center = values - jnp.mean(values, axis=1, keepdims=True)
    spread = jnp.mean(center * center, axis=1, keepdims=True)
    scale = lax.rsqrt(spread + NORM_EPS)
    return center * scale, scale


def norm_back(e, gain, vhat, scale):
    eg = e * gain
    mean_e = jnp.mean(eg, axis=1, keepdims=True)
    mean_ev = jnp.mean(eg * vhat, axis=1, keepdims=True)
    return scale * (eg - mean_e - vhat * mean_ev)


def flip(pair):
    return jnp.concatenate([pair[1], pair[0]], axis=0)


def forward_body(place, pair, pair_sib, mine, other, wo_mine, wo_other, bias, wup, *refs):
    d_parts = refs[:4]
    (partial, vhat_out, scale_out, normed_low, active, slope, wdown, mixed, wo) = refs[4:13]
    hidden = refs[13]
    for k, part in enumerate(d_parts):
        slot = z_slot(place, k)
        for y in range(4):
            wdown[y * 4 + slot] = part[y]
    rows = pair_sib.shape[1]

    def place_halves(c):
        mixed[:, c * HALF : (c + 1) * HALF] = mine[...].reshape(2 * rows, HALF)
        mixed[:, (1 - c) * HALF : (2 - c) * HALF] = flip(other)
        wo[:, c * HALF : (c + 1) * HALF] = wo_mine[...]
        wo[:, (1 - c) * HALF : (2 - c) * HALF] = wo_other[...]

    on_core(place, place_halves)
    hidden[...] = dot(mixed[...], wo[...]) + bias[2:3, :]
    hidden[:rows, :] += pair[0].astype(F32)
    hidden[rows:, :] += pair_sib[0].astype(F32)
    vhat, scale = norm_stats(hidden[...])
    vhat_out[...] = vhat
    scale_out[...] = scale
    normed_low[...] = (vhat * bias[4:5, :] + bias[5:6, :]).astype(BF16)

    def up(c):
        for u in range(4):
            b = bias[8 + u : 9 + u, c * HALF : (c + 1) * HALF]
            upper = dot(normed_low[...], wup[:, u * HALF : (u + 1) * HALF]) + b
            cdf = 0.5 * (1.0 + lax.erf(upper * 0.7071067811865476))
            pdf = jnp.exp(-0.5 * upper * upper) * 0.3989422804014327
            active[:, u * HALF : (u + 1) * HALF] = (upper * cdf).astype(BF16)
            slope[:, u * HALF : (u + 1) * HALF] = (cdf + upper * pdf).astype(BF16)

    on_core(place, up)
    partial[...] = dot(active[...], wdown[...].reshape(4 * HALF, WIDTH)).astype(BF16).reshape(2, rows, WIDTH)


def back_ffn_body(place, perm, mine, other, vhat1, bias, pair, pair_sib, slope, wup, wdown, *refs):
    layer_out, d_summed, d_down, d_upper, d_part, sums = refs
    rows = pair.shape[1]
    summed = vhat1[...] * bias[4:5, :] + bias[5:6, :] + bias[3:4, :]
    summed = summed + mine[...].astype(F32).reshape(2 * rows, WIDTH) + flip(other).astype(F32)
    vhat, scale = norm_stats(summed)
    gain = bias[6:7, :]
    result = (vhat[:rows] * gain + bias[7:8, :]).astype(BF16)
    layer_out[...] = dot_tn(perm[...], result).astype(BF16)
    e = jnp.concatenate([pair[1], pair_sib[1]], axis=0).astype(F32)
    sums[0:1, :] = jnp.sum(e * vhat, axis=0, keepdims=True)
    sums[1:2, :] = jnp.sum(e, axis=0, keepdims=True)
    grad = norm_back(e, gain, vhat, scale)
    d_summed[...] = grad
    low = grad.astype(BF16)
    d_down[...] = low
    sums[2:3, :] = jnp.sum(low.astype(F32), axis=0, keepdims=True)
    for u in range(4):
        d_active = dot_nt(d_down[...], wdown[u * 4 : (u + 1) * 4].reshape(HALF, WIDTH))
        part = (d_active * slope[:, u * HALF : (u + 1) * HALF].astype(F32)).astype(BF16)
        d_upper[:, u * HALF : (u + 1) * HALF] = part
        half = slice((u % 2) * HALF, (u % 2 + 1) * HALF)
        sums[3 + u // 2 : 4 + u // 2, half] = jnp.sum(part.astype(F32), axis=0, keepdims=True)
    sums[5:8, :] = jnp.zeros((3, WIDTH), F32)
    d_part[...] = dot_nt(d_upper[...], wup[...]).astype(BF16).reshape(2, rows, WIDTH)


def grad_down_body(place, active, d_down, out, scr):
    scr[...] = dot_tn(active[...], d_down[...])
    for z in range(4):
        for r in range(4):
            row = pl.multiple_of((place[1] ^ r) * (4 * DOWN) + z * DOWN, 8)
            out[z, r] = scr[pl.ds(row, DOWN), :].astype(BF16)


def cut_slabs(place, scr, outs, n, z_of):
    for r, out in enumerate(outs):
        base = (place[1] ^ r) * (8 * SHARD)
        for k in range(4):
            z = z_of(place[2], k)
            for c in range(2):
                row = pl.multiple_of(base + c * 4 * SHARD + z * SHARD, 8)
                out[k * 8 + c * 4 + n] = scr[pl.ds(row, SHARD), :].astype(BF16)


def shifted(z, k):
    return lax.rem(z + k, 4)


def grad_up_body(place, normed_low, d_upper, *refs):
    outs, scr = refs[:4], refs[4]
    for u in range(4):
        scr[...] = dot_tn(normed_low[...], d_upper[:, u * HALF : (u + 1) * HALF])
        cut_slabs(place, scr, outs, u, lambda z, k: z ^ k)


def back_attend_body(tables, place, d_summed, mine, other, vhat1, scale1, bias, wo, mixed, q3, k3, v3, lse, *refs):
    d_hidden_out, d_branch, dq_out, dk_out, dv_out, sums, dm3 = refs
    rows = d_hidden_out.shape[0]
    e = d_summed[...] + mine[...].astype(F32).reshape(2 * rows, WIDTH) + flip(other).astype(F32)
    vhat = vhat1[...]
    sums[0:1, :] = jnp.sum(e * vhat, axis=0, keepdims=True)
    sums[1:2, :] = jnp.sum(e, axis=0, keepdims=True)
    d_hidden = norm_back(e, bias[4:5, :], vhat, scale1[...])
    d_hidden_out[...] = d_hidden[:rows]
    low = d_hidden.astype(BF16)
    d_branch[...] = low
    sums[2:3, :] = jnp.sum(low.astype(F32), axis=0, keepdims=True)
    wo_rows = wo[pl.ds(pl.multiple_of(place[0] * HALF, HALF), HALF), :]
    dm3[...] = dot_nt(d_branch[...], wo_rows).astype(BF16).reshape(2, rows, HALF)
    count = k3.shape[0]
    for start, size in tables:
        for pair in range(3):
            lanes = slice(pair * 128, (pair + 1) * 128)
            qp = q3[:, start : start + size, lanes].reshape(2 * size, 128).astype(F32) * 0.125
            dp = dm3[:, start : start + size, lanes].reshape(2 * size, 128).astype(F32)
            mp = mixed[:, start : start + size, lanes].reshape(2 * size, 128)
            kp = k3[:, start : start + size, lanes].reshape(count * size, 128)
            vp = v3[:, start : start + size, lanes].reshape(count * size, 128)
            logs = lse[:, start : start + size, :].reshape(2 * size, 128)
            low_half = iota(qp.shape, 1) < HD
            found, d_key, d_value = [], None, None
            for h in range(2):
                mine_h = low_half if h == 0 else jnp.logical_not(low_half)
                qm = jnp.where(mine_h, qp, 0.0).astype(BF16)
                dmask = jnp.where(mine_h, dp, 0.0)
                delta = jnp.sum(dmask * mp, axis=1, keepdims=True)
                dm = dmask.astype(BF16)
                column = pair * 2 + h
                probs = jnp.exp(dot_nt(qm, kp) - logs[:, column : column + 1])
                part = dot_tn(probs.astype(BF16), dm)
                d_value = part if d_value is None else d_value + part
                d_scores = (probs * (dot_nt(dm, vp) - delta)).astype(BF16)
                found.append(dot(d_scores, kp))
                part = dot_tn(d_scores, qm)
                d_key = part if d_key is None else d_key + part
            d_query = jnp.where(low_half, found[0], found[1]) * 0.125
            dq_out[:, start : start + size, lanes] = d_query.astype(BF16).reshape(2, size, 128)
            dk_out[:, start : start + size, lanes] = d_key.astype(BF16).reshape(count, size, 128)
            dv_out[:, start : start + size, lanes] = d_value.astype(BF16).reshape(count, size, 128)
    sums[3:8, :] = jnp.zeros((5, WIDTH), F32)
    q_sum = jnp.sum(dq_out[...].reshape(2 * rows, HALF).astype(F32), axis=0, keepdims=True)
    v_sum = jnp.sum(dv_out[...].reshape(count * rows, HALF).astype(F32), axis=0, keepdims=True)

    def sides(c):
        sums[3:4, c * HALF : (c + 1) * HALF] = q_sum
        sums[4:5, c * HALF : (c + 1) * HALF] = v_sum

    on_core(place, sides)


def grad_qkvo_body(place, tok, dq, dk, dv, mixed, d_branch, sums_ffn, sums_attn, *refs):
    outs, scr, block = refs[:4], refs[4], refs[5]
    count, rows = tok.shape[:2]
    scr[...] = dot_tn(tok[:2].reshape(2 * rows, WIDTH), dq[...].reshape(2 * rows, HALF))
    cut_slabs(place, scr, outs, 0, shifted)
    every = tok[...].reshape(count * rows, WIDTH)
    scr[...] = dot_tn(every, dk[...].reshape(count * rows, HALF))
    cut_slabs(place, scr, outs, 1, shifted)
    scr[...] = dot_tn(every, dv[...].reshape(count * rows, HALF))
    cut_slabs(place, scr, outs, 2, shifted)

    def out_half(c):
        scr[...] = dot_tn(mixed[...], d_branch[:, c * HALF : (c + 1) * HALF])

    on_core(place, out_half)
    cut_slabs(place, scr, outs, 3, shifted)
    once = jnp.where(place[0] == 0, 1.0, 0.0)
    block[...] = jnp.zeros(block.shape, F32)
    block[0:2, :] = sums_attn[3:5, :]
    block[2:3, :] = sums_attn[2:3, :] * once
    block[3:4, :] = sums_ffn[2:3, :] * once
    block[4:6, :] = sums_attn[0:2, :] * once
    block[6:8, :] = sums_ffn[0:2, :] * once

    def up_rows(c):
        for u in range(4):
            half = sums_ffn[3 + u // 2 : 4 + u // 2, (u % 2) * HALF : (u % 2 + 1) * HALF]
            block[8 + u : 9 + u, c * HALF : (c + 1) * HALF] = half

    on_core(place, up_rows)
    for out in outs:
        for n in range(2):
            out[32 + n] = block[:, n * HALF : (n + 1) * HALF].astype(BF16)


def grad_tok_body(place, dq, dk, dv, wqkv, same, sib):
    rows = same.shape[1]
    count = dk.shape[0]
    for n in range(count):
        total = dot_nt(dk[n], wqkv[:, HALF : 2 * HALF]) + dot_nt(dv[n], wqkv[:, 2 * HALF :])
        if n < 2:
            total = total + dot_nt(dq[n], wqkv[:, :HALF])
        (same if n % 2 == 0 else sib)[n // 2] = total.astype(BF16)


def added(parts, index):
    total = parts[0][index].astype(F32)
    for part in parts[1:]:
        total = total + part[index].astype(F32)
    return total


def sum_up_body(place, own, r1, r2, r3, keep, send):
    for n in range(16):
        keep[n] = added((own, r1, r2, r3), n).astype(BF16)
        send[n] = added((own, r1, r2, r3), 16 + n).astype(BF16)


def mid_up_body(place, keep, recv, kept, sent):
    for n in range(8):
        kept[n] = added((keep, recv), n).astype(BF16)
        sent[n] = added((keep, recv), 8 + n).astype(BF16)


def sum_q_body(place, own, r1, r2, r3, *outs):
    parts = (own, r1, r2, r3)
    for k, out in enumerate(outs):
        for n in range(8):
            out[n] = added(parts, k * 8 + n).astype(BF16)
    for n in range(2):
        total = added(parts, 32 + n).astype(BF16)
        for out in outs:
            out[8 + n] = total


def sum_td_body(place, same, recv, down, keep_a, send_a, keep_b, send_b):
    rows, half = same.shape[1], keep_a.shape[1]
    for r in range(4):
        tok = (same[r].astype(F32) + recv[r].astype(F32)).astype(BF16)
        own = added(tuple(down.at[z] for z in range(4)), r).astype(BF16)
        (send_a if r % 2 else keep_a)[r // 2] = tok[:half]
        other = send_b if r >= 2 else keep_b
        other[r % 2, : rows - half, :] = tok[half:]
        other[r % 2, rows - half :, :] = own


def mid_td_body(place, keep_a, recv_a, keep_b, recv_b, kept_a, sent_a, kept_b, sent_b):
    kept_a[...] = added((keep_a, recv_a), 0).astype(BF16)
    sent_a[...] = added((keep_a, recv_a), 1).astype(BF16)
    kept_b[...] = added((keep_b, recv_b), 0).astype(BF16)
    sent_b[...] = added((keep_b, recv_b), 1).astype(BF16)


def last_td_body(place, perm, d_hidden, kept_a, recv_a, kept_b, recv_b, out, out_down):
    rows, half = d_hidden.shape[0], kept_a.shape[0]
    whole = slice(None)
    total_a, total_b = added((kept_a, recv_a), whole), added((kept_b, recv_b), whole)
    out_down[...] = total_b[rows - half :]
    total = d_hidden[...] + jnp.concatenate([total_a, total_b[: rows - half]], axis=0)
    high = total.astype(BF16)
    left = total - high.astype(F32)
    middle = left.astype(BF16)
    low = (left - middle.astype(F32)).astype(BF16)
    out[...] = dot_tn(perm[...], high) + dot_tn(perm[...], middle) + dot_tn(perm[...], low)


def sum_last_body(place, p0, p1, p2, p3, u0, u1, keep, send):
    parts, ups = (p0, p1, p2, p3), (u0, u1)

    def fill(mine):
        for n in range(4):
            keep[n] = added(parts, mine * 4 + n)
            send[n] = added(parts, (1 - mine) * 4 + n)
            keep[4 + n] = added(ups, mine * 4 + n)
            send[4 + n] = added(ups, (1 - mine) * 4 + n)

    on_core(place, fill)
    for n in (8, 9):
        total = added(parts, n)
        keep[n] = total
        send[n] = total


def last_body(place, keep, recv, gq, gk, gv, go, gup, vectors, ups):
    def fill(c):
        for n, out in enumerate((gq, gk, gv, go)):
            out[:, c * HALF : (c + 1) * HALF] = keep[n]
            out[:, (1 - c) * HALF : (2 - c) * HALF] = recv[n]
        for u in range(4):
            gup[:, u * WIDTH + c * HALF : u * WIDTH + (c + 1) * HALF] = keep[4 + u]
            gup[:, u * WIDTH + (1 - c) * HALF : u * WIDTH + (2 - c) * HALF] = recv[4 + u]

    on_core(place, fill)
    dev = place[3]
    total = jnp.concatenate([keep[8] + recv[8], keep[9] + recv[9]], axis=1)
    pick = jnp.where(iota((WIDTH, 128), 0) == dev * SHARD + iota((WIDTH, 128), 1), 1.0, 0.0)
    high = lax.Precision.HIGHEST
    vectors[...] = jnp.dot(total, pick, precision=high, preferred_element_type=F32)
    lane = lax.rem(dev, 8) * DOWN
    pick_up = jnp.where(iota((WIDTH, 128), 0) == lane + iota((WIDTH, 128), 1), 1.0, 0.0)
    rows = jnp.where(iota(total.shape, 0) == 8 + dev // 8, total, 0.0)
    row = jnp.broadcast_to(jnp.sum(rows, axis=0, keepdims=True), (8, WIDTH))
    ups[...] = jnp.dot(row, pick_up, precision=high, preferred_element_type=F32)


def fast_device(
    tokens,
    table_ids,
    w_query,
    w_key,
    w_value,
    w_out,
    w_up,
    w_down,
    b_query,
    b_value,
    b_out,
    b_up,
    b_down,
    gain_attn,
    shift_attn,
    gain_ffn,
    shift_ffn,
    cotangent,
):
    col, z = lax.axis_index("col"), lax.axis_index("seq")
    place = jnp.stack([col % 2, col // 2, z, col * 4 + z]).astype(jnp.int32)
    rows = tokens.shape[0]
    tables = table_rows(rows, 8)

    def swap(x):
        return lax.ppermute(x, "col", [(i, i ^ 1) for i in range(8)])

    def plane(x, r):
        return lax.ppermute(x, "col", [(i, i ^ (2 * r)) for i in range(8)])

    def shift(x, k):
        return lax.ppermute(x, "seq", [(i, (i + k) % 4) for i in range(4)])

    def planes(x):
        return (x, plane(x, 1), plane(x, 2), plane(x, 3))

    def ring(x):
        one = shift(x, 1)
        two = shift(one, 1)
        return (x, one, two, shift(two, 1))

    def exchange(x, k):
        return lax.ppermute(x, "seq", [(i, i ^ k) for i in range(4)])

    def slabs(count, kind=BF16):
        return ((count,) + SLAB, kind)

    vectors = (b_query, b_value, b_out, b_down, gain_attn, shift_attn, gain_ffn, shift_ffn)
    down_parts = planes(w_down)
    keep, send = call(
        pack_body,
        "pack",
        place,
        (w_query, w_key, w_value, w_out, w_up)
        + tuple(v.reshape(1, SHARD) for v in vectors)
        + (b_up.reshape(1, DOWN),),
        (slabs(10), slabs(10)),
        (pltpu.VMEM((8, SHARD), F32),),
    )
    perm, pair, tok_own = call(
        sort_body,
        "sort",
        place,
        (table_ids.reshape(1, rows), tokens, cotangent),
        (((rows, rows), BF16), ((2, rows, WIDTH), BF16), ((rows, WIDTH), BF16)),
        after=(send,),
    )
    tok_parts = planes(tok_own)
    recv = swap(send)
    (chunk_q,) = call(merge_body, "merge", place, (keep, recv), (slabs(8),), after=(tok_own,))
    pair_sib = swap(pair)
    (column_d,) = call(
        pcat_body, "pcat", place, down_parts, (((4, DOWN, WIDTH), BF16),), after=(chunk_q,)
    )
    plane_q, chunk_u = call(
        zcat_q_body,
        "zcat_q",
        place,
        ring(chunk_q) + (keep, recv),
        (slabs(26), slabs(10)),
        after=(column_d,),
    )
    q_parts = planes(plane_q)
    d_parts = ring(column_d)
    (three,) = call(
        tcat_body, "tcat", place, tok_parts[1:], (((3, rows, WIDTH), BF16),), after=(plane_q,)
    )
    three_sib = swap(three)
    (plane_u,) = call(zcat_u_body, "zcat_u", place, ring(chunk_u), (slabs(40),), after=(three,))
    u_parts = planes(plane_u)

    heads = ((2, rows, HALF), BF16)
    heads_all = ((8, rows, HALF), BF16)
    wqkv, bias, tok, q3, k3, v3, mixed3, mixed_low, lse = call(
        functools.partial(attend_body, tables),
        "attend",
        place,
        tok_parts + (pair_sib, three_sib) + q_parts,
        (
            ((WIDTH, 3 * HALF), BF16),
            ((SHARD, WIDTH), F32),
            ((8, rows, WIDTH), BF16),
            heads,
            heads_all,
            heads_all,
            ((2, rows, HALF), F32),
            heads,
            ((2, rows, 128), F32),
        ),
        (
            pltpu.VMEM((WIDTH, HALF), F32),
            pltpu.VMEM((2, rows, HALF), BF16),
            pltpu.VMEM((8, rows, HALF), BF16),
            pltpu.VMEM((8, rows, HALF), BF16),
        ),
        after=(plane_u,),
    )
    wo_mine, wup = call(
        asm_u_body,
        "asm_u",
        place,
        u_parts,
        (((WIDTH, HALF), BF16), ((WIDTH, 4 * HALF), BF16)),
        (pltpu.VMEM((WIDTH, HALF), F32),),
        after=(mixed_low,),
    )
    whole_pair = ((2, rows, WIDTH), BF16)
    full = (2 * rows, WIDTH)
    wide = ((2 * rows, 4 * HALF), BF16)
    partial, vhat, scale, normed_low, active, slope, wdown, mixed, wo = call(
        forward_body,
        "forward",
        place,
        (pair, pair_sib, mixed_low, swap(mixed_low), wo_mine, swap(wo_mine), bias, wup) + d_parts,
        (
            whole_pair,
            (full, F32),
            ((2 * rows, 1), F32),
            (full, BF16),
            wide,
            wide,
            ((16, DOWN, WIDTH), BF16),
            (full, BF16),
            ((WIDTH, WIDTH), BF16),
        ),
        (pltpu.VMEM(full, F32),),
    )
    layer_out, d_summed, d_down, d_upper, d_part, sums_ffn = call(
        back_ffn_body,
        "back_ffn",
        place,
        (perm, partial, swap(partial), vhat, bias, pair, pair_sib, slope, wup, wdown),
        (((rows, WIDTH), BF16), (full, F32), (full, BF16), wide, whole_pair, ((8, WIDTH), F32)),
    )
    d_part_other = swap(d_part)
    (g_down,) = call(
        grad_down_body,
        "grad_down",
        place,
        (active, d_down),
        (((4, 4, DOWN, WIDTH), BF16),),
        (pltpu.VMEM((4 * HALF, WIDTH), F32),),
    )
    g_up = call(
        grad_up_body,
        "grad_up",
        place,
        (normed_low, d_upper),
        (slabs(32),) * 4,
        (pltpu.VMEM((WIDTH, HALF), F32),),
        after=(g_down,),
    )
    d_hidden, d_branch, dq, dk, dv, sums_attn = call(
        functools.partial(back_attend_body, tables),
        "back_attend",
        place,
        (d_summed, d_part, d_part_other, vhat, scale, bias, wo, mixed3, q3, k3, v3, lse),
        (((rows, WIDTH), F32), (full, BF16), heads, heads_all, heads_all, ((8, WIDTH), F32)),
        (pltpu.VMEM((2, rows, HALF), BF16),),
        after=g_up,
    )
    g_q = call(
        grad_qkvo_body,
        "grad_qkvo",
        place,
        (tok, dq, dk, dv, mixed, d_branch, sums_ffn, sums_attn),
        (slabs(34),) * 4,
        (pltpu.VMEM((WIDTH, HALF), F32), pltpu.VMEM((SHARD, WIDTH), F32)),
    )
    quad = ((4, rows, WIDTH), BF16)
    same, sib = call(grad_tok_body, "grad_tok", place, (dq, dk, dv, wqkv), (quad, quad), after=g_q)
    sib = swap(sib)
    g_down = lax.all_to_all(g_down, "seq", 0, 0, tiled=True)
    g_up = (g_up[0],) + tuple(plane(g_up[r], r) for r in (1, 2, 3))
    keep_up, send_up, *g_q = call(
        sum_up_body, "sum_up", place, g_up, (slabs(16), slabs(16)), through=tuple(g_q)
    )
    g_q = (g_q[0],) + tuple(plane(g_q[r], r) for r in (1, 2, 3))
    kept_up, sent_up = call(
        mid_up_body, "mid_up", place, (keep_up, exchange(send_up, 2)), (slabs(8), slabs(8))
    )
    recv_up = exchange(sent_up, 1)
    s_q = call(sum_q_body, "sum_q", place, g_q, (slabs(10),) * 4, after=(sent_up,))
    half = ((rows + DOWN) // 2, WIDTH)
    two = ((2,) + half, BF16)
    keep_a, send_a, keep_b, send_b = call(
        sum_td_body, "sum_td", place, (same, sib, g_down), (two,) * 4, after=s_q
    )
    s_q = (s_q[0],) + tuple(shift(s_q[k], k) for k in (1, 2, 3))
    kept_a, sent_a, kept_b, sent_b = call(
        mid_td_body,
        "mid_td",
        place,
        (keep_a, plane(send_a, 1), keep_b, plane(send_b, 2)),
        ((half, BF16),) * 4,
    )
    recv_a, recv_b = plane(sent_a, 2), plane(sent_b, 1)
    kept, sent = call(
        sum_last_body,
        "sum_last",
        place,
        s_q + (kept_up, recv_up),
        (slabs(10, F32), slabs(10, F32)),
        after=(sent_a,),
    )
    grad_tokens, grad_down = call(
        last_td_body,
        "last_td",
        place,
        (perm, d_hidden, kept_a, recv_a, kept_b, recv_b),
        (((rows, WIDTH), F32), ((DOWN, WIDTH), F32)),
        after=(sent,),
    )
    row = ((SHARD, WIDTH), F32)
    gq, gk, gv, go, gup, small, ups = call(
        last_body,
        "last",
        place,
        (kept, swap(sent)),
        (row, row, row, row, ((SHARD, 4 * WIDTH), F32), ((SHARD, 128), F32), ((8, 128), F32)),
    )
    small = small[:, :SHARD]
    return (
        layer_out,
        grad_tokens,
        gq,
        gk,
        gv,
        go,
        gup,
        grad_down,
        small[0],
        small[1],
        small[2],
        ups[0, :DOWN],
        small[3],
        small[4],
        small[5],
        small[6],
        small[7],
    )


def solution(mesh):
    placed = (
        P(("col", "seq"), None),
        P(("col", "seq")),
        P(("col", "seq"), None),
        P(("col", "seq"), None),
        P(("col", "seq"), None),
        P(("col", "seq"), None),
        P(("col", "seq"), None),
        P(("col", "seq"), None),
        P(("col", "seq")),
        P(("col", "seq")),
        P(("col", "seq")),
        P(("col", "seq")),
        P(("col", "seq")),
        P(("col", "seq")),
        P(("col", "seq")),
        P(("col", "seq")),
        P(("col", "seq")),
        P(("col", "seq"), None),
    )
    fast = mesh.shape["col"] == 8 and mesh.shape["seq"] == 4
    return jax.shard_map(
        fast_device if fast else per_device,
        mesh=mesh,
        in_specs=placed,
        out_specs=(
            P(("col", "seq"), None),
            P(("col", "seq"), None),
            P(("col", "seq"), None),
            P(("col", "seq"), None),
            P(("col", "seq"), None),
            P(("col", "seq"), None),
            P(("col", "seq"), None),
            P(("col", "seq"), None),
            P(("col", "seq")),
            P(("col", "seq")),
            P(("col", "seq")),
            P(("col", "seq")),
            P(("col", "seq")),
            P(("col", "seq")),
            P(("col", "seq")),
            P(("col", "seq")),
            P(("col", "seq")),
        ),
        check_vma=False,
    )
```

```python
import functools

import jax
import jax.numpy as jnp
import numpy as np
from jax import lax
from jax.experimental import pallas as pl
from jax.experimental.pallas import tpu as pltpu
from jax.sharding import PartitionSpec as P

H = 12
HD = 64


NEG_BIG = -1e30
NORM_EPS = 1e-12
LOW_TYPE = jnp.bfloat16
FULL_TYPE = jnp.float32


def block_length(unit_rows):
    target = unit_rows * max(1, -(-512 // unit_rows))
    return target


def layer_norm(values, gain, shift):
    center = values - jnp.mean(values, axis=-1, keepdims=True)
    spread = jnp.mean(center * center, axis=-1, keepdims=True)
    return center * lax.rsqrt(spread + NORM_EPS) * gain + shift


def gelu_exact(values):
    return jax.nn.gelu(values, approximate=False)


def project(left, right, bias):
    return jnp.dot(left, right, preferred_element_type=FULL_TYPE) + bias.astype(FULL_TYPE)


def attend(running, query_heads, query_ids, key_slab, value_slab, key_ids):
    maxima, totals, weighted = running
    scores = (
        jnp.einsum("thd,shd->hts", query_heads, key_slab, preferred_element_type=FULL_TYPE) * 0.125
    )
    visible = (query_ids[:, None] == key_ids[None, :])[None]
    scores = jnp.where(visible, scores, NEG_BIG)
    new_max = jnp.maximum(maxima, jnp.max(scores, axis=2))
    rescale = jnp.exp(maxima - new_max)
    exponents = jnp.where(visible, jnp.exp(scores - new_max[:, :, None]), 0.0)
    totals = totals * rescale + jnp.sum(exponents, axis=2)
    weighted = weighted * rescale[:, :, None] + jnp.einsum(
        "hts,shd->htd", exponents.astype(LOW_TYPE), value_slab, preferred_element_type=FULL_TYPE
    )
    return (new_max, totals, weighted)


def grad_block(
    query_heads, dout_heads, log_totals, row_delta, query_ids, key_slab, value_slab, key_ids
):
    scores = (
        jnp.einsum("thd,shd->hts", query_heads, key_slab, preferred_element_type=FULL_TYPE) * 0.125
    )
    visible = (query_ids[:, None] == key_ids[None, :])[None]
    probabilities = jnp.where(visible, jnp.exp(scores - log_totals[:, :, None]), 0.0)
    grad_value = jnp.einsum(
        "hts,thd->shd", probabilities.astype(LOW_TYPE), dout_heads, preferred_element_type=FULL_TYPE
    )
    grad_probs = jnp.einsum(
        "thd,shd->hts", dout_heads, value_slab, preferred_element_type=FULL_TYPE
    )
    grad_scores = (probabilities * (grad_probs - row_delta[:, :, None])).astype(LOW_TYPE)
    grad_query = (
        jnp.einsum("hts,shd->thd", grad_scores, key_slab, preferred_element_type=FULL_TYPE) * 0.125
    )
    grad_key = (
        jnp.einsum("hts,thd->shd", grad_scores, query_heads, preferred_element_type=FULL_TYPE)
        * 0.125
    )
    return (grad_query, grad_key, grad_value)


def per_device(
    tokens,
    table_ids,
    w_query,
    w_key,
    w_value,
    w_out,
    w_up,
    w_down,
    b_query,
    b_value,
    b_out,
    b_up,
    b_down,
    gain_attn,
    shift_attn,
    gain_ffn,
    shift_ffn,
    cotangent,
):
    shards = (
        w_query,
        w_key,
        w_value,
        w_out,
        w_up,
        w_down,
        b_query,
        b_value,
        b_out,
        b_up,
        b_down,
        gain_attn,
        shift_attn,
        gain_ffn,
        shift_ffn,
    )
    gathered = (
        lax.all_gather(shards[0], ("col", "seq"), axis=0, tiled=True),
        lax.all_gather(shards[1], ("col", "seq"), axis=0, tiled=True),
        lax.all_gather(shards[2], ("col", "seq"), axis=0, tiled=True),
        lax.all_gather(shards[3], ("col", "seq"), axis=0, tiled=True),
        lax.all_gather(shards[4], ("col", "seq"), axis=0, tiled=True),
        lax.all_gather(shards[5], ("col", "seq"), axis=0, tiled=True),
        lax.all_gather(shards[6], ("col", "seq"), axis=0, tiled=True),
        lax.all_gather(shards[7], ("col", "seq"), axis=0, tiled=True),
        lax.all_gather(shards[8], ("col", "seq"), axis=0, tiled=True),
        lax.all_gather(shards[9], ("col", "seq"), axis=0, tiled=True),
        lax.all_gather(shards[10], ("col", "seq"), axis=0, tiled=True),
        lax.all_gather(shards[11], ("col", "seq"), axis=0, tiled=True),
        lax.all_gather(shards[12], ("col", "seq"), axis=0, tiled=True),
        lax.all_gather(shards[13], ("col", "seq"), axis=0, tiled=True),
        lax.all_gather(shards[14], ("col", "seq"), axis=0, tiled=True),
    )
    query_mat, key_mat, value_mat, out_mat, up_mat, down_mat = (
        gathered[0],
        gathered[1],
        gathered[2],
        gathered[3],
        gathered[4],
        gathered[5],
    )
    query_bias, value_bias, out_bias, up_bias, down_bias = (
        gathered[6],
        gathered[7],
        gathered[8],
        gathered[9],
        gathered[10],
    )
    attn_gain, attn_shift, ffn_gain, ffn_shift = (
        gathered[11],
        gathered[12],
        gathered[13],
        gathered[14],
    )
    tok_rows = tokens.shape[0]
    ids_all = lax.all_gather(table_ids, "col", axis=0, tiled=True)
    inputs = tokens.astype(FULL_TYPE)
    queries = project(tokens, query_mat, query_bias).astype(LOW_TYPE)
    keys = jnp.dot(tokens, key_mat, preferred_element_type=FULL_TYPE).astype(LOW_TYPE)
    values = project(tokens, value_mat, value_bias).astype(LOW_TYPE)
    query_heads = queries.reshape(tok_rows, H, HD)
    starting = (
        jnp.full((H, tok_rows), NEG_BIG, FULL_TYPE),
        jnp.zeros((H, tok_rows), FULL_TYPE),
        jnp.zeros((H, tok_rows, HD), FULL_TYPE),
    )
    running = starting
    key_rows = lax.all_gather(keys, "col", axis=0, tiled=True)
    value_rows = lax.all_gather(values, "col", axis=0, tiled=True)
    row_count = key_rows.shape[0]
    length = block_length(tok_rows)
    blocks = row_count // length

    def advance(current, pieces):
        return (attend(current, query_heads, table_ids, pieces[0], pieces[1], pieces[2]), None)

    running, _ = lax.scan(
        advance,
        running,
        (
            key_rows.reshape(blocks, length, H, HD),
            value_rows.reshape(blocks, length, H, HD),
            ids_all.reshape(blocks, length),
        ),
    )
    maxima, totals, weighted = running
    attn_heads = weighted / totals[:, :, None]
    log_totals = maxima + jnp.log(totals)
    attn_low = attn_heads.transpose(1, 0, 2).reshape(tok_rows, H * HD).astype(LOW_TYPE)
    hidden = inputs + project(attn_low, out_mat, out_bias)
    normed, norm_first = jax.vjp(
        layer_norm, hidden, attn_gain.astype(FULL_TYPE), attn_shift.astype(FULL_TYPE)
    )
    normed_low = normed.astype(LOW_TYPE)
    upper = project(normed_low, up_mat, up_bias)
    active, gelu_back = jax.vjp(gelu_exact, upper)
    active_low = active.astype(LOW_TYPE)
    summed = normed + project(active_low, down_mat, down_bias)
    result, norm_second = jax.vjp(
        layer_norm, summed, ffn_gain.astype(FULL_TYPE), ffn_shift.astype(FULL_TYPE)
    )
    again = (
        lax.all_gather(w_query, ("col", "seq"), axis=0, tiled=True),
        lax.all_gather(w_key, ("col", "seq"), axis=0, tiled=True),
        lax.all_gather(w_value, ("col", "seq"), axis=0, tiled=True),
        lax.all_gather(w_out, ("col", "seq"), axis=0, tiled=True),
        lax.all_gather(w_up, ("col", "seq"), axis=0, tiled=True),
        lax.all_gather(w_down, ("col", "seq"), axis=0, tiled=True),
    )
    query_mat, key_mat, value_mat, out_mat, up_mat, down_mat = (
        again[0],
        again[1],
        again[2],
        again[3],
        again[4],
        again[5],
    )
    d_summed, d_ffn_gain, d_ffn_shift = norm_second(cotangent.astype(FULL_TYPE))
    d_down = d_summed.astype(LOW_TYPE)
    grad_down = jnp.einsum("tf,td->fd", active_low, d_down, preferred_element_type=FULL_TYPE)
    d_active = jnp.einsum("td,fd->tf", d_down, down_mat, preferred_element_type=FULL_TYPE)
    d_upper = gelu_back(d_active)[0].astype(LOW_TYPE)
    grad_up = jnp.einsum("td,tf->df", normed_low, d_upper, preferred_element_type=FULL_TYPE)
    d_normed = d_summed + jnp.einsum("tf,df->td", d_upper, up_mat, preferred_element_type=FULL_TYPE)
    d_hidden, d_attn_gain, d_attn_shift = norm_first(d_normed)
    d_branch = d_hidden.astype(LOW_TYPE)
    grad_out = jnp.einsum("tc,td->cd", attn_low, d_branch, preferred_element_type=FULL_TYPE)
    d_attn = jnp.einsum("td,cd->tc", d_branch, out_mat, preferred_element_type=FULL_TYPE).astype(
        LOW_TYPE
    )
    dout_heads = d_attn.reshape(tok_rows, H, HD)
    row_delta = jnp.einsum("thd,htd->ht", dout_heads.astype(FULL_TYPE), attn_heads)
    key_all, value_all = (
        lax.all_gather(keys, "col", axis=0, tiled=True),
        lax.all_gather(values, "col", axis=0, tiled=True),
    )
    total_rows = key_all.shape[0]
    length = block_length(tok_rows)
    blocks = total_rows // length

    def key_pass(grad_sum, pieces):
        grad_query_part, grad_key_part, grad_value_part = grad_block(
            query_heads,
            dout_heads,
            log_totals,
            row_delta,
            table_ids,
            pieces[0],
            pieces[1],
            pieces[2],
        )
        return (grad_sum + grad_query_part, (grad_key_part, grad_value_part))

    query_sum, (key_parts, value_parts) = lax.scan(
        key_pass,
        jnp.zeros((tok_rows, H, HD), FULL_TYPE),
        (
            key_all.reshape(blocks, length, H, HD),
            value_all.reshape(blocks, length, H, HD),
            ids_all.reshape(blocks, length),
        ),
    )
    key_sum, value_sum = (
        lax.psum_scatter(
            key_parts.reshape(total_rows, H * HD).astype(jnp.bfloat16),
            "col",
            scatter_dimension=0,
            tiled=True,
        ).astype(jnp.float32),
        lax.psum_scatter(
            value_parts.reshape(total_rows, H * HD).astype(jnp.bfloat16),
            "col",
            scatter_dimension=0,
            tiled=True,
        ).astype(jnp.float32),
    )
    query_sum = query_sum.reshape(tok_rows, H * HD)
    query_low = query_sum.astype(LOW_TYPE)
    key_low = key_sum.astype(LOW_TYPE)
    value_low = value_sum.astype(LOW_TYPE)
    grad_query = jnp.einsum("tc,td->cd", tokens, query_low, preferred_element_type=FULL_TYPE)
    grad_key = jnp.einsum("tc,td->cd", tokens, key_low, preferred_element_type=FULL_TYPE)
    grad_value = jnp.einsum("tc,td->cd", tokens, value_low, preferred_element_type=FULL_TYPE)
    d_tokens = d_hidden + jnp.einsum(
        "td,cd->tc", query_low, query_mat, preferred_element_type=FULL_TYPE
    )
    d_tokens = d_tokens + jnp.einsum(
        "td,cd->tc", key_low, key_mat, preferred_element_type=FULL_TYPE
    )
    d_tokens = d_tokens + jnp.einsum(
        "td,cd->tc", value_low, value_mat, preferred_element_type=FULL_TYPE
    )
    sums_local = (
        grad_query,
        grad_key,
        grad_value,
        grad_out,
        grad_up,
        grad_down,
        jnp.sum(query_low.astype(FULL_TYPE), axis=0),
        jnp.sum(value_low.astype(FULL_TYPE), axis=0),
        jnp.sum(d_branch.astype(FULL_TYPE), axis=0),
        jnp.sum(d_upper.astype(FULL_TYPE), axis=0),
        jnp.sum(d_down.astype(FULL_TYPE), axis=0),
        d_attn_gain,
        d_attn_shift,
        d_ffn_gain,
        d_ffn_shift,
    )
    owned = (
        lax.psum_scatter(sums_local[0], ("col", "seq"), scatter_dimension=0, tiled=True),
        lax.psum_scatter(sums_local[1], ("col", "seq"), scatter_dimension=0, tiled=True),
        lax.psum_scatter(sums_local[2], ("col", "seq"), scatter_dimension=0, tiled=True),
        lax.psum_scatter(sums_local[3], ("col", "seq"), scatter_dimension=0, tiled=True),
        lax.psum_scatter(sums_local[4], ("col", "seq"), scatter_dimension=0, tiled=True),
        lax.psum_scatter(sums_local[5], ("col", "seq"), scatter_dimension=0, tiled=True),
        lax.psum_scatter(sums_local[6], ("col", "seq"), scatter_dimension=0, tiled=True),
        lax.psum_scatter(sums_local[7], ("col", "seq"), scatter_dimension=0, tiled=True),
        lax.psum_scatter(sums_local[8], ("col", "seq"), scatter_dimension=0, tiled=True),
        lax.psum_scatter(sums_local[9], ("col", "seq"), scatter_dimension=0, tiled=True),
        lax.psum_scatter(sums_local[10], ("col", "seq"), scatter_dimension=0, tiled=True),
        lax.psum_scatter(sums_local[11], ("col", "seq"), scatter_dimension=0, tiled=True),
        lax.psum_scatter(sums_local[12], ("col", "seq"), scatter_dimension=0, tiled=True),
        lax.psum_scatter(sums_local[13], ("col", "seq"), scatter_dimension=0, tiled=True),
        lax.psum_scatter(sums_local[14], ("col", "seq"), scatter_dimension=0, tiled=True),
    )
    return (result.astype(LOW_TYPE), d_tokens) + tuple(owned)


WIDTH = 768
HALF = WIDTH // 2
SHARD = 24
DOWN = 96
SLAB = (SHARD, HALF)
HEADS = 192
PIECE = (SHARD, 640)
BLOCK = (SHARD, 1024)
START_Q = 10 * HALF
CHUNK = (SHARD, START_Q + 5 * PIECE[1])
UNITS = ((slice(0, 128), 2), (slice(128, 192), 1))
VMEM_BYTES = 30 * 2**20
FULL_BYTES = 60 * 2**20
F32 = jnp.float32
BF16 = jnp.bfloat16


COST_SCALE = 10.0
COST = {
    "attend": 11.7,
    "asm_u": 2.5,
    "forward": 6.2,
    "back_ffn": 5.5,
    "grad_down": 2.2,
    "grad_up": 2.4,
    "back_attend": 11.7,
    "grad_qkvo": 5.2,
    "grad_tok": 4.3,
}


def dot(left, right):
    return jnp.dot(left, right, preferred_element_type=F32)


def dot_nt(left, right):
    return lax.dot_general(left, right, (((1,), (1,)), ((), ())), preferred_element_type=F32)


def dot_tn(left, right):
    return lax.dot_general(left, right, (((0,), (0,)), ((), ())), preferred_element_type=F32)


def call(body, name, place, inputs, outs, scratch=(), after=(), through=(), limit=VMEM_BYTES):
    vmem = pl.BlockSpec(memory_space=pltpu.VMEM)
    any_place = pl.BlockSpec(memory_space=pl.ANY)
    count = 1 + len(inputs)
    skipped = count + len(after) + len(through)

    def run(*refs):
        own = skipped + len(outs)
        body(*refs[:count], *refs[skipped:own], *refs[own + len(through) :])

    return pl.pallas_call(
        run,
        name=name,
        out_shape=tuple(jax.ShapeDtypeStruct(s, t) for s, t in outs)
        + tuple(jax.ShapeDtypeStruct(a.shape, a.dtype) for a in through),
        in_specs=[pl.BlockSpec(memory_space=pltpu.SMEM)] + [vmem] * len(inputs) + [any_place] * (len(after) + len(through)),
        out_specs=tuple(vmem for _ in outs) + tuple(any_place for _ in through),
        input_output_aliases={count + len(after) + n: len(outs) + n for n in range(len(through))},
        scratch_shapes=list(scratch),
        compiler_params=pltpu.CompilerParams(vmem_limit_bytes=limit),
        cost_estimate=pl.CostEstimate(
            flops=int(1.15e9 * COST_SCALE * COST.get(name, 1.3)), bytes_accessed=0, transcendentals=0
        ),
    )(place, *inputs, *after, *through)


def iota(shape, dim):
    return lax.broadcasted_iota(jnp.int32, shape, dim)


def sort_body(place, ids, tokens, cot, perm_out, pair_out, tok_out):
    rows = tokens.shape[0]
    id_j = jnp.broadcast_to(ids[...].astype(F32), (rows, rows))
    id_i = id_j.T
    same = jnp.where(id_i == id_j, 1.0, 0.0)
    count_i = jnp.sum(same, axis=1, keepdims=True)
    count_j = jnp.sum(same, axis=0, keepdims=True)
    i, j = iota((rows, rows), 0), iota((rows, rows), 1)
    equal = jnp.where((id_i == id_j) & (i < j), 1.0, 0.0)
    tie = jnp.where((count_i == count_j) & (id_i < id_j), 1.0, 0.0)
    larger = jnp.where(count_i > count_j, 1.0, 0.0)
    position = jnp.sum(equal + tie + larger, axis=0, keepdims=True)
    perm = jnp.where(i.astype(F32) == position, 1.0, 0.0).astype(BF16)
    perm_out[...] = perm
    tok = dot(perm, tokens[...]).astype(BF16)
    pair_out[0] = tok
    pair_out[1] = dot(perm, cot[...]).astype(BF16)
    tok_out[...] = tok


def fold(block):
    return jnp.concatenate([block[:, :HALF], block[:, HALF:]], axis=0)


def pack_body(place, wq, wk, wv, wo, wup, *rest):
    vectors, b_up = rest[:8], rest[8]
    parts, (keep, send) = rest[9:13], rest[13:15]
    rows8, pieces, block = rest[15:]
    dev = place[3]

    def split(mine):
        other = 1 - mine
        keep[0] = wo[:, mine * HALF : (mine + 1) * HALF]
        send[0] = wo[:, other * HALF : (other + 1) * HALF]
        for u in range(4):
            keep[1 + u] = wup[:, u * WIDTH + mine * HALF : u * WIDTH + (mine + 1) * HALF]
            send[1 + u] = wup[:, u * WIDTH + other * HALF : u * WIDTH + (other + 1) * HALF]

    on_core(place, split)
    for n, vector in enumerate(vectors):
        rows8[n : n + 1, :] = vector[...].astype(F32)
    spread = jnp.where(iota((SHARD, WIDTH), 1) == dev * SHARD + iota((SHARD, WIDTH), 0), 1.0, 0.0)
    eight = dot(rows8[...].astype(BF16), spread.astype(BF16))
    lane = lax.rem(dev, 8) * DOWN
    spread_up = jnp.where(iota((DOWN, WIDTH), 1) == lane + iota((DOWN, WIDTH), 0), 1.0, 0.0)
    one = dot(jnp.broadcast_to(b_up[...], (8, DOWN)), spread_up.astype(BF16))
    one = jnp.where(iota((8, WIDTH), 0) == dev // 8, one, 0.0)
    for n in range(2):
        lanes = slice(n * HALF, (n + 1) * HALF)
        block[n * 12 : n * 12 + 8, :] = eight[:, lanes]
        block[n * 12 + 8 : n * 12 + 12, :] = one[:4, lanes]
    for j in range(4):
        for n, w in enumerate((wq, wk, wv)):
            pieces[j, :, n * HEADS : (n + 1) * HEADS] = w[:, j * HEADS : (j + 1) * HEADS].astype(F32)
    for r, part in enumerate(parts):
        part[:, : 3 * HEADS] = pieces[place[1] ^ r].astype(BF16)
        part[:, 3 * HEADS : PIECE[1]] = jnp.zeros((SHARD, PIECE[1] - 3 * HEADS), BF16)
        part[:, PIECE[1] :] = block[...].astype(BF16)


def merge_body(place, keep, recv, q0, q1, q2, q3, chunk, slots):
    parts = (q0, q1, q2, q3)
    for r, part in enumerate(parts):
        slots[place[1] ^ r] = part[:, : PIECE[1]]
    for n in range(4):
        chunk[:, START_Q + n * PIECE[1] : START_Q + (n + 1) * PIECE[1]] = slots[n]
    total = sum(part[:, PIECE[1] :].astype(F32) for part in parts)
    total = jnp.concatenate([total, jnp.zeros((SHARD, PIECE[1] - HALF), F32)], axis=1)
    chunk[:, START_Q + 4 * PIECE[1] :] = total.astype(BF16)

    def fill(mine):
        even, odd = (keep, recv) if mine == 0 else (recv, keep)
        for n in range(5):
            chunk[:, n * HALF : (n + 1) * HALF] = even[n]
            chunk[:, (5 + n) * HALF : (6 + n) * HALF] = odd[n]

    on_core(place, fill)


def z_slot(place, k):
    return lax.rem(place[2] + 4 - k, 4)


def zcat_q_body(place, own, r1, r2, r3, out):
    parts = (own, r1, r2, r3)
    for k, part in enumerate(parts):
        slot = z_slot(place, k) * 4
        for n in range(4):
            out[slot + n] = part[n]
    out[16] = sum(part[4].astype(F32) for part in parts).astype(BF16)


def gate_body(place):
    pass


def zcat_body(place, own, r1, r2, r3, t1, t2, t3, plane_u, plane_q, three):
    parts = (own, r1, r2, r3)
    for k, part in enumerate(parts):
        slot = z_slot(place, k)
        for n in range(10):
            plane_u[slot * 10 + n] = part[:, n * HALF : (n + 1) * HALF]
        for n in range(4):
            plane_q[slot * 4 + n] = part[:, START_Q + n * PIECE[1] : START_Q + (n + 1) * PIECE[1]]
    plane_q[16] = sum(part[:, START_Q + 4 * PIECE[1] :].astype(F32) for part in parts).astype(BF16)
    for r, part in enumerate((t1, t2, t3)):
        three[r] = part[...]


def pcat_body(place, own, r1, r2, r3, column):
    for r, part in enumerate((own, r1, r2, r3)):
        column[place[1] ^ r] = part[...]


def asm_u_body(place, p0, p1, p2, p3, wo, wup, slab):
    parts = (p0, p1, p2, p3)
    natural(place, parts, slab, 0, 5)
    wo[...] = slab[...].astype(BF16)
    for u in range(4):
        natural(place, parts, slab, 1 + u, 5)
        wup[:, u * HALF : (u + 1) * HALF] = slab[...].astype(BF16)


def natural(place, parts, scr, n, count):
    for r, part in enumerate(parts):
        base = (place[1] ^ r) * (8 * SHARD)
        for z in range(4):
            for c in range(2):
                row = pl.multiple_of(base + c * 4 * SHARD + z * SHARD, 8)
                scr[pl.ds(row, SHARD), :] = part[(z * 2 + c) * count + n].astype(F32)


def on_core(place, action):
    @pl.when(place[0] == 0)
    def _():
        action(0)

    @pl.when(place[0] == 1)
    def _():
        action(1)


def table_rows(tok_rows, n_col):
    long_rows = max(2 * 512, 64 * n_col) // n_col
    short_rows = 512 // n_col
    units = tok_rows // short_rows
    long_count = max(1, units // (2 * (long_rows // short_rows)))
    tables, start = [], 0
    for _ in range(long_count):
        tables.append((start, long_rows))
        start += long_rows
    while start < tok_rows:
        tables.append((start, short_rows))
        start += short_rows
    return tables


def attend_body(tables, place, *refs):
    same, pair_sib, three_sib, mine_q, other_q = refs[:4], refs[4], refs[5], refs[6], refs[7]
    w3, bias, tok, q3, k3, v3, mixed_out = refs[8:15]
    mixed_low, lse_out, slab = refs[15:19], refs[19], refs[20]
    rows = tok.shape[1]

    def gather(mine):
        for c in range(2):
            source = mine_q if c == mine else other_q
            for z in range(4):
                for j in range(4):
                    row = j * 8 * SHARD + c * 4 * SHARD + z * SHARD
                    slab[row : row + SHARD, :] = source[z * 4 + j].astype(F32)

    on_core(place, gather)
    for n in range(3):
        w3[n] = slab[:, n * HEADS : (n + 1) * HEADS].astype(BF16)
    total = mine_q[16][:, :HALF].astype(F32) + other_q[16][:, :HALF].astype(F32)
    bias[:12, :HALF] = total[:12]
    bias[:12, HALF:] = total[12:]
    bias[12:, :] = jnp.zeros((4, WIDTH), F32)

    def own_columns(row):
        found = jnp.zeros((1, HEADS), F32)
        for j in range(4):
            part = bias[row : row + 1, j * HEADS : (j + 1) * HEADS]
            found = found + jnp.where(place[1] == j, part, 0.0)
        return found

    for n, part in enumerate(same):
        tok[n] = part[...]
        tok[4 + n] = pair_sib[0] if n == 0 else three_sib[n - 1]
    every = tok[...].reshape(8 * rows, WIDTH)
    k3[...] = dot(every, w3[1]).astype(BF16).reshape(8, rows, HEADS)
    v3[...] = (dot(every, w3[2]) + own_columns(1)).astype(BF16).reshape(8, rows, HEADS)
    queries = dot(tok[:4].reshape(4 * rows, WIDTH), w3[0]) + own_columns(0)
    q3[...] = queries.astype(BF16).reshape(4, rows, HEADS)
    for start, size in tables:
        lse = jnp.zeros((4 * size, 128), F32)
        for lanes, heads in UNITS:
            wide = lanes.stop - lanes.start
            qp = q3[:, start : start + size, lanes].reshape(4 * size, wide)
            kp = k3[:, start : start + size, lanes].reshape(8 * size, wide)
            vp = v3[:, start : start + size, lanes].reshape(8 * size, wide)
            low_half = iota(qp.shape, 1) < HD
            found = []
            for h in range(heads):
                qm = qp.astype(F32) * 0.125
                if heads == 2:
                    qm = jnp.where(low_half if h == 0 else jnp.logical_not(low_half), qm, 0.0)
                scores = dot_nt(qm.astype(BF16), kp)
                top = jnp.max(scores, axis=1, keepdims=True)
                expo = jnp.exp(scores - top)
                total = jnp.sum(expo, axis=1, keepdims=True)
                found.append(dot(expo.astype(BF16), vp) * (1.0 / total))
                column = lanes.start // HD + h
                lse = jnp.where(iota(lse.shape, 1) == column, top + jnp.log(total), lse)
            mixed = found[0] if heads == 1 else jnp.where(low_half, found[0], found[1])
            mixed = mixed.reshape(4, size, wide)
            mixed_out[:, start : start + size, lanes] = mixed
            for r, out in enumerate(mixed_low):
                out[start : start + size, lanes] = mixed[r].astype(BF16)
        lse_out[:, start : start + size, :] = lse.reshape(4, size, 128)


def mcat_body(place, own, r1, r2, r3, out, parts):
    for r, part in enumerate((own, r1, r2, r3)):
        parts[r] = part[...]
    for j in range(4):
        out[:, j * HEADS : (j + 1) * HEADS] = parts[place[1] ^ j]


def norm_stats(values):
    center = values - jnp.mean(values, axis=1, keepdims=True)
    spread = jnp.mean(center * center, axis=1, keepdims=True)
    scale = lax.rsqrt(spread + NORM_EPS)
    return center * scale, scale


def norm_back(e, gain, vhat, scale):
    eg = e * gain
    mean_e = jnp.mean(eg, axis=1, keepdims=True)
    mean_ev = jnp.mean(eg * vhat, axis=1, keepdims=True)
    return scale * (eg - mean_e - vhat * mean_ev)


def flip(pair):
    return jnp.concatenate([pair[1], pair[0]], axis=0)


def forward_body(place, pair, pair_sib, mine, other, wo_mine, wo_other, bias, wup, *refs):
    d_parts = refs[:4]
    (partial, vhat_out, scale_out, normed_low, active, slope, wdown, mixed, wo) = refs[4:13]
    hidden, upper, b_up = refs[13:]
    for k, part in enumerate(d_parts):
        slot = z_slot(place, k)
        for y in range(4):
            wdown[y * 4 + slot] = part[y]
    rows = pair_sib.shape[1]

    def place_halves(c):
        wo[:, c * HALF : (c + 1) * HALF] = wo_mine[...]
        wo[:, (1 - c) * HALF : (2 - c) * HALF] = wo_other[...]

    on_core(place, place_halves)
    mixed[:rows, :] = mine[...]
    mixed[rows:, :] = other[...]
    hidden[...] = dot(mixed[...], wo[...]) + bias[2:3, :]
    hidden[:rows, :] += pair[0].astype(F32)
    hidden[rows:, :] += pair_sib[0].astype(F32)
    vhat, scale = norm_stats(hidden[...])
    vhat_out[...] = vhat
    scale_out[...] = jnp.broadcast_to(scale, scale_out.shape)
    normed_low[...] = (vhat * bias[4:5, :] + bias[5:6, :]).astype(BF16)

    def bias_half(c):
        for u in range(4):
            b_up[:, u * HALF : (u + 1) * HALF] = bias[8 + u : 9 + u, c * HALF : (c + 1) * HALF]

    on_core(place, bias_half)
    upper[...] = dot(normed_low[...], wup[...])

    def gelu_rows(step, carry):
        block = pl.ds(pl.multiple_of(step * 16, 16), 16)
        x = upper[block, :] + b_up[...]
        cdf = 0.5 * (1.0 + lax.erf(x * 0.7071067811865476))
        pdf = jnp.exp(-0.5 * x * x) * 0.3989422804014327
        active[block, :] = (x * cdf).astype(BF16)
        slope[block, :] = (cdf + x * pdf).astype(BF16)
        return carry

    lax.fori_loop(0, upper.shape[0] // 16, gelu_rows, 0)
    partial[...] = dot(active[...], wdown[...].reshape(4 * HALF, WIDTH)).astype(BF16).reshape(2, rows, WIDTH)


def back_ffn_body(place, perm, mine, other, vhat1, bias, pair, pair_sib, slope, wup, wdown, *refs):
    layer_out, d_summed, d_down, d_upper, d_part, sums = refs
    rows = pair.shape[1]
    summed = vhat1[...] * bias[4:5, :] + bias[5:6, :] + bias[3:4, :]
    summed = summed + mine[...].astype(F32).reshape(2 * rows, WIDTH) + flip(other).astype(F32)
    vhat, scale = norm_stats(summed)
    gain = bias[6:7, :]
    result = (vhat[:rows] * gain + bias[7:8, :]).astype(BF16)
    layer_out[...] = dot_tn(perm[...], result).astype(BF16)
    e = jnp.concatenate([pair[1], pair_sib[1]], axis=0).astype(F32)
    sums[0:1, :] = jnp.sum(e * vhat, axis=0, keepdims=True)
    sums[1:2, :] = jnp.sum(e, axis=0, keepdims=True)
    grad = norm_back(e, gain, vhat, scale)
    d_summed[...] = grad
    low = grad.astype(BF16)
    d_down[...] = low
    sums[2:3, :] = jnp.sum(low.astype(F32), axis=0, keepdims=True)
    for u in range(4):
        d_active = dot_nt(d_down[...], wdown[u * 4 : (u + 1) * 4].reshape(HALF, WIDTH))
        part = (d_active * slope[:, u * HALF : (u + 1) * HALF].astype(F32)).astype(BF16)
        d_upper[:, u * HALF : (u + 1) * HALF] = part
        half = slice((u % 2) * HALF, (u % 2 + 1) * HALF)
        sums[3 + u // 2 : 4 + u // 2, half] = jnp.sum(part.astype(F32), axis=0, keepdims=True)
    sums[5:8, :] = jnp.zeros((3, WIDTH), F32)
    d_part[...] = dot_nt(d_upper[...], wup[...]).astype(BF16).reshape(2, rows, WIDTH)


def grad_down_body(place, active, d_down, *refs):
    outs, scr = refs[:4], refs[4]
    scr[...] = dot_tn(active[...], d_down[...])
    for k, out in enumerate(outs):
        z = z_slot(place, k)
        for r in range(4):
            row = pl.multiple_of((place[1] ^ r) * (4 * DOWN) + z * DOWN, 8)
            out[r] = scr[pl.ds(row, DOWN), :].astype(BF16)


def ring_down_body(place, recv, own, out):
    out[...] = (recv[...].astype(F32) + own[...].astype(F32)).astype(BF16)


def grad_up_body(place, normed_low, d_upper, mixed, d_branch, *refs):
    outs, scr = refs[:4], refs[4]

    def cut_slabs(n):
        for r, out in enumerate(outs):
            base = (place[1] ^ r) * (8 * SHARD)
            for k in range(4):
                for c in range(2):
                    row = pl.multiple_of(base + c * 4 * SHARD + (place[2] ^ k) * SHARD, 8)
                    out[(k * 2 + c) * 5 + n] = scr[pl.ds(row, SHARD), :].astype(BF16)

    def out_half(c):
        scr[...] = dot_tn(mixed[...], d_branch[:, c * HALF : (c + 1) * HALF])

    on_core(place, out_half)
    cut_slabs(0)
    for u in range(4):
        scr[...] = dot_tn(normed_low[...], d_upper[:, u * HALF : (u + 1) * HALF])
        cut_slabs(1 + u)


def back_norm_body(place, d_summed, mine, other, vhat1, scale1, bias, wo, d_hidden_out, d_branch, *refs):
    d_mixed, sums = refs[:4], refs[4]
    rows = d_hidden_out.shape[0]
    e = d_summed[...] + mine[...].astype(F32).reshape(2 * rows, WIDTH) + flip(other).astype(F32)
    vhat = vhat1[...]
    sums[0:1, :] = jnp.sum(e * vhat, axis=0, keepdims=True)
    sums[1:2, :] = jnp.sum(e, axis=0, keepdims=True)
    d_hidden = norm_back(e, bias[4:5, :], vhat, scale1[:, 0:1])
    d_hidden_out[...] = d_hidden[:rows]
    low = d_hidden.astype(BF16)
    d_branch[...] = low
    sums[2:3, :] = jnp.sum(low.astype(F32), axis=0, keepdims=True)
    sums[3:8, :] = jnp.zeros((5, WIDTH), F32)
    for r, out in enumerate(d_mixed):
        row = pl.multiple_of((place[1] ^ r) * HEADS, 64)
        out[...] = dot_nt(d_branch[:rows, :], wo[pl.ds(row, HEADS), :]).astype(BF16)


def back_attend_body(tables, place, d0, d1, d2, d3, mixed, q3, k3, v3, lse, dq_out, dk_out, dv_out, sums, dm3):
    rows = d0.shape[0]
    for r, part in enumerate((d0, d1, d2, d3)):
        dm3[r] = part[...]
    for start, size in tables:
        logs = lse[:, start : start + size, :].reshape(4 * size, 128)
        for lanes, heads in UNITS:
            wide = lanes.stop - lanes.start
            qp = q3[:, start : start + size, lanes].reshape(4 * size, wide).astype(F32) * 0.125
            dp = dm3[:, start : start + size, lanes].reshape(4 * size, wide).astype(F32)
            mp = mixed[:, start : start + size, lanes].reshape(4 * size, wide)
            kp = k3[:, start : start + size, lanes].reshape(8 * size, wide)
            vp = v3[:, start : start + size, lanes].reshape(8 * size, wide)
            low_half = iota(qp.shape, 1) < HD
            found, d_key, d_value = [], None, None
            for h in range(heads):
                qm, dmask = qp, dp
                if heads == 2:
                    mine_h = low_half if h == 0 else jnp.logical_not(low_half)
                    qm, dmask = jnp.where(mine_h, qp, 0.0), jnp.where(mine_h, dp, 0.0)
                delta = jnp.sum(dmask * mp, axis=1, keepdims=True)
                qm, dm = qm.astype(BF16), dmask.astype(BF16)
                column = lanes.start // HD + h
                probs = jnp.exp(dot_nt(qm, kp) - logs[:, column : column + 1])
                part = dot_tn(probs.astype(BF16), dm)
                d_value = part if d_value is None else d_value + part
                d_scores = (probs * (dot_nt(dm, vp) - delta)).astype(BF16)
                found.append(dot(d_scores, kp))
                part = dot_tn(d_scores, qm)
                d_key = part if d_key is None else d_key + part
            d_query = found[0] if heads == 1 else jnp.where(low_half, found[0], found[1])
            d_query = (d_query * 0.125).astype(BF16)
            dq_out[:, start : start + size, lanes] = d_query.reshape(4, size, wide)
            dk_out[:, start : start + size, lanes] = d_key.astype(BF16).reshape(8, size, wide)
            dv_out[:, start : start + size, lanes] = d_value.astype(BF16).reshape(8, size, wide)
    q_sum = jnp.sum(dq_out[...].reshape(4 * rows, HEADS).astype(F32), axis=0, keepdims=True)
    v_sum = jnp.sum(dv_out[...].reshape(8 * rows, HEADS).astype(F32), axis=0, keepdims=True)
    for j in range(4):
        mine = place[1] == j
        sums[0:1, j * HEADS : (j + 1) * HEADS] = jnp.where(mine, q_sum, 0.0)
        sums[1:2, j * HEADS : (j + 1) * HEADS] = jnp.where(mine, v_sum, 0.0)
    sums[2:8, :] = jnp.zeros((6, WIDTH), F32)


def grad_qkv_body(place, tok, dq, dk, dv, sums_ffn, sums_norm, sums_attn, keep, send, scr, block):
    rows = tok.shape[1]
    every = tok[...].reshape(8 * rows, WIDTH)
    scr[:, :HEADS] = dot_tn(tok[:4].reshape(4 * rows, WIDTH), dq[...].reshape(4 * rows, HEADS))
    scr[:, HEADS : 2 * HEADS] = dot_tn(every, dk[...].reshape(8 * rows, HEADS))
    scr[:, 2 * HEADS : 3 * HEADS] = dot_tn(every, dv[...].reshape(8 * rows, HEADS))
    scr[:, 3 * HEADS :] = jnp.zeros((WIDTH, PIECE[1] - 3 * HEADS), F32)
    for k in range(4):
        z = place[2] ^ k
        for r in range(4):
            base = (place[1] ^ r) * (8 * SHARD) + z * SHARD
            for core, out in ((place[0], keep), (1 - place[0], send)):
                row = pl.multiple_of(base + core * (4 * SHARD), 8)
                out[k * 4 + r] = scr[pl.ds(row, SHARD), :].astype(BF16)
    once = jnp.where(place[0] == 0, 1.0, 0.0)
    block[...] = jnp.zeros(block.shape, F32)
    block[0:2, :] = sums_attn[0:2, :]
    block[2:3, :] = sums_norm[2:3, :] * once
    block[3:4, :] = sums_ffn[2:3, :] * once
    block[4:6, :] = sums_norm[0:2, :] * once
    block[6:8, :] = sums_ffn[0:2, :] * once

    def up_rows(c):
        for u in range(4):
            half = sums_ffn[3 + u // 2 : 4 + u // 2, (u % 2) * HALF : (u % 2 + 1) * HALF]
            block[8 + u : 9 + u, c * HALF : (c + 1) * HALF] = half

    on_core(place, up_rows)
    folded = jnp.concatenate([block[:12, :HALF], block[:12, HALF:]], axis=0)
    folded = jnp.concatenate([folded, jnp.zeros((SHARD, PIECE[1] - HALF), F32)], axis=1).astype(BF16)
    keep[16] = folded
    send[16] = folded


def grad_tok_body(place, dq, dk, dv, w3, same, sib):
    rows = same.shape[1]
    for n in range(2):
        keys = dk[4 * n : 4 * n + 4].reshape(4 * rows, HEADS)
        values = dv[4 * n : 4 * n + 4].reshape(4 * rows, HEADS)
        total = dot_nt(keys, w3[1]) + dot_nt(values, w3[2])
        if n == 0:
            total = total + dot_nt(dq[...].reshape(4 * rows, HEADS), w3[0])
        (same, sib)[n][...] = total.astype(BF16).reshape(4, rows, WIDTH)


def added(parts, index):
    total = parts[0][index].astype(F32)
    for part in parts[1:]:
        total = total + part[index].astype(F32)
    return total


def sum_up_body(place, own, r1, r2, r3, keep, send):
    for n in range(20):
        keep[n] = added((own, r1, r2, r3), n).astype(BF16)
        send[n] = added((own, r1, r2, r3), 20 + n).astype(BF16)


def mid_up_body(place, keep, recv, kept, sent):
    for n in range(10):
        kept[n] = added((keep, recv), n).astype(BF16)
        sent[n] = added((keep, recv), 10 + n).astype(BF16)


def sum_core_body(place, keep, recv, keep_z, send_z):
    total = added((keep, recv), 16).astype(BF16)
    for out, k in ((keep_z, 0), (send_z, 2)):
        for n in range(8):
            out[n] = added((keep, recv), k * 4 + n).astype(BF16)
        out[8] = total


def mid_q_body(place, keep, recv, kept, sent):
    total = added((keep, recv), 8).astype(BF16)
    for out, k in ((kept, 0), (sent, 1)):
        for n in range(4):
            out[n] = added((keep, recv), k * 4 + n).astype(BF16)
        out[4] = total


def sum_q_body(place, own, recv, *outs):
    parts = (own, recv)
    total = added(parts, 4)[:, :HALF].astype(BF16)
    for r, out in enumerate(outs):
        out[:, : PIECE[1]] = added(parts, r).astype(BF16)
        out[:, PIECE[1] :] = total


def last_q_body(place, own, r1, r2, r3, gq, gk, gv, vectors, ups, pieces):
    parts = (own, r1, r2, r3)
    for r, part in enumerate(parts):
        pieces[r] = part[:, : PIECE[1]].astype(F32)
    for j in range(4):
        piece = pieces[place[1] ^ j]
        for n, out in enumerate((gq, gk, gv)):
            out[:, j * HEADS : (j + 1) * HEADS] = piece[:, n * HEADS : (n + 1) * HEADS]
    block = sum(part[:, PIECE[1] :].astype(F32) for part in parts)
    total = jnp.concatenate([block[:12], block[12:]], axis=1)
    dev = place[3]
    high = lax.Precision.HIGHEST
    pick = jnp.where(iota((WIDTH, 128), 0) == dev * SHARD + iota((WIDTH, 128), 1), 1.0, 0.0)
    vectors[...] = jnp.dot(total, pick, precision=high, preferred_element_type=F32)
    lane = lax.rem(dev, 8) * DOWN
    pick_up = jnp.where(iota((WIDTH, 128), 0) == lane + iota((WIDTH, 128), 1), 1.0, 0.0)
    rows = jnp.where(iota(total.shape, 0) == 8 + dev // 8, total, 0.0)
    row = jnp.broadcast_to(jnp.sum(rows, axis=0, keepdims=True), (8, WIDTH))
    ups[...] = jnp.dot(row, pick_up, precision=high, preferred_element_type=F32)


def sum_td_body(place, same, recv, d0, d1, keep_a, send_a, keep_b, send_b):
    rows, half = same.shape[1], keep_a.shape[1]
    for r in range(4):
        tok = (same[r].astype(F32) + recv[r].astype(F32)).astype(BF16)
        own = added((d0, d1), r).astype(BF16)
        (send_a if r % 2 else keep_a)[r // 2] = tok[:half]
        other = send_b if r >= 2 else keep_b
        other[r % 2, : rows - half, :] = tok[half:]
        other[r % 2, rows - half :, :] = own


def mid_td_body(place, keep_a, recv_a, keep_b, recv_b, kept_a, sent_a, kept_b, sent_b):
    kept_a[...] = added((keep_a, recv_a), 0).astype(BF16)
    sent_a[...] = added((keep_a, recv_a), 1).astype(BF16)
    kept_b[...] = added((keep_b, recv_b), 0).astype(BF16)
    sent_b[...] = added((keep_b, recv_b), 1).astype(BF16)


def last_td_body(place, perm, d_hidden, kept_a, recv_a, kept_b, recv_b, out, out_down):
    rows, half = d_hidden.shape[0], kept_a.shape[0]
    whole = slice(None)
    total_a, total_b = added((kept_a, recv_a), whole), added((kept_b, recv_b), whole)
    out_down[...] = total_b[rows - half :]
    total = d_hidden[...] + jnp.concatenate([total_a, total_b[: rows - half]], axis=0)
    high = total.astype(BF16)
    left = total - high.astype(F32)
    middle = left.astype(BF16)
    low = (left - middle.astype(F32)).astype(BF16)
    out[...] = dot_tn(perm[...], high) + dot_tn(perm[...], middle) + dot_tn(perm[...], low)


def sum_last_body(place, u0, u1, keep, send):
    def fill(mine):
        for n in range(5):
            keep[n] = added((u0, u1), mine * 5 + n)
            send[n] = added((u0, u1), (1 - mine) * 5 + n)

    on_core(place, fill)


def last_up_body(place, keep, recv, go, gup):
    def fill(c):
        go[:, c * HALF : (c + 1) * HALF] = keep[0]
        go[:, (1 - c) * HALF : (2 - c) * HALF] = recv[0]
        for u in range(4):
            gup[:, u * WIDTH + c * HALF : u * WIDTH + (c + 1) * HALF] = keep[1 + u]
            gup[:, u * WIDTH + (1 - c) * HALF : u * WIDTH + (2 - c) * HALF] = recv[1 + u]

    on_core(place, fill)


def fast_device(
    tokens,
    table_ids,
    w_query,
    w_key,
    w_value,
    w_out,
    w_up,
    w_down,
    b_query,
    b_value,
    b_out,
    b_up,
    b_down,
    gain_attn,
    shift_attn,
    gain_ffn,
    shift_ffn,
    cotangent,
):
    col, z = lax.axis_index("col"), lax.axis_index("seq")
    place = jnp.stack([col % 2, col // 2, z, col * 4 + z]).astype(jnp.int32)
    rows = tokens.shape[0]
    tables = table_rows(rows, 8)

    def swap(x):
        return lax.ppermute(x, "col", [(i, i ^ 1) for i in range(8)])

    def plane(x, r):
        return lax.ppermute(x, "col", [(i, i ^ (2 * r)) for i in range(8)])

    def shift(x, k):
        return lax.ppermute(x, "seq", [(i, (i + k) % 4) for i in range(4)])

    def planes(x):
        return (x, plane(x, 1), plane(x, 2), plane(x, 3))

    def exchanged(parts):
        return (parts[0],) + tuple(plane(parts[r], r) for r in (1, 2, 3))

    def ring(x):
        one = shift(x, 1)
        two = shift(one, 1)
        return (x, one, two, shift(two, 1))

    def exchange(x, k):
        return lax.ppermute(x, "seq", [(i, i ^ k) for i in range(4)])

    def slabs(count, kind=BF16):
        return ((count,) + SLAB, kind)

    vectors = (b_query, b_value, b_out, b_down, gain_attn, shift_attn, gain_ffn, shift_ffn)
    block = (BLOCK, BF16)
    *q_out, keep_u, send_u = call(
        pack_body,
        "pack",
        place,
        (w_query, w_key, w_value, w_out, w_up)
        + tuple(v.reshape(1, SHARD) for v in vectors)
        + (b_up.reshape(1, DOWN),),
        (block,) * 4 + (slabs(5), slabs(5)),
        (
            pltpu.VMEM((8, SHARD), F32),
            pltpu.VMEM((4, SHARD, 3 * HEADS), F32),
            pltpu.VMEM(SLAB, F32),
        ),
        limit=FULL_BYTES,
    )
    q_in = exchanged(q_out)
    recv_u = swap(send_u)
    perm, pair, tok_own = call(
        sort_body,
        "sort",
        place,
        (table_ids.reshape(1, rows), tokens, cotangent),
        (((rows, rows), BF16), ((2, rows, WIDTH), BF16), ((rows, WIDTH), BF16)),
        after=(send_u,),
        limit=FULL_BYTES,
    )
    chunk, w_down = call(
        merge_body,
        "merge",
        place,
        (keep_u, recv_u) + q_in,
        ((CHUNK, BF16),),
        (pltpu.VMEM((4,) + PIECE, BF16),),
        after=(tok_own,),
        through=(w_down,),
    )
    column_d, one, tok_own, pair = call(
        pcat_body,
        "pcat",
        place,
        planes(w_down),
        (((4, DOWN, WIDTH), BF16),),
        through=(shift(chunk, 1), tok_own, pair),
    )
    two, tok_x, tok_y, pair_sib, column_d = call(
        gate_body,
        "gate",
        place,
        (),
        (),
        through=(shift(one, 1), plane(tok_own, 1), plane(tok_own, 2), swap(pair), column_d),
    )
    tok_parts = (tok_own, tok_x, tok_y, plane(tok_x, 2))
    plane_u, plane_q, three, column_d = call(
        zcat_body,
        "zcat",
        place,
        (chunk, one, two, shift(two, 1)) + tok_parts[1:],
        (slabs(40), ((17,) + PIECE, BF16), ((3, rows, WIDTH), BF16)),
        through=(column_d,),
    )
    three_sib = swap(three)
    other_q = swap(plane_q)
    u_parts = planes(plane_u)
    d_one = shift(column_d, 1)

    heads = ((4, rows, HEADS), BF16)
    heads_all = ((8, rows, HEADS), BF16)
    piece = ((rows, HEADS), BF16)
    w3, bias, tok, q3, k3, v3, mixed3, *mixed_low, lse = call(
        functools.partial(attend_body, tables),
        "attend",
        place,
        tok_parts + (pair_sib, three_sib, plane_q, other_q),
        (
            ((3, WIDTH, HEADS), BF16),
            ((16, WIDTH), F32),
            ((8, rows, WIDTH), BF16),
            heads,
            heads_all,
            heads_all,
            ((4, rows, HEADS), F32),
            piece,
            piece,
            piece,
            piece,
            ((4, rows, 128), F32),
        ),
        (pltpu.VMEM((WIDTH, PIECE[1]), F32),),
        after=(plane_u,),
    )
    (d_one,) = call(gate_body, "gate_d", place, (), (), after=(lse,), through=(d_one,))
    d_two = shift(d_one, 1)
    d_parts = (column_d, d_one, d_two, shift(d_two, 1))
    wo_mine, wup, *mixed_low = call(
        asm_u_body,
        "asm_u",
        place,
        u_parts,
        (((WIDTH, HALF), BF16), ((WIDTH, 4 * HALF), BF16)),
        (pltpu.VMEM((WIDTH, HALF), F32),),
        after=(lse,),
        through=tuple(mixed_low),
    )
    (mixed_own,) = call(
        mcat_body,
        "mcat",
        place,
        exchanged(mixed_low),
        (((rows, WIDTH), BF16),),
        (pltpu.VMEM((4, rows, HEADS), BF16),),
    )
    whole_pair = ((2, rows, WIDTH), BF16)
    full = (2 * rows, WIDTH)
    wide = ((2 * rows, 4 * HALF), BF16)
    partial, vhat, scale, normed_low, active, slope, wdown, mixed, wo = call(
        forward_body,
        "forward",
        place,
        (pair, pair_sib, mixed_own, swap(mixed_own), wo_mine, swap(wo_mine), bias, wup) + d_parts,
        (
            whole_pair,
            (full, F32),
            ((2 * rows, 128), F32),
            (full, BF16),
            wide,
            wide,
            ((16, DOWN, WIDTH), BF16),
            (full, BF16),
            ((WIDTH, WIDTH), BF16),
        ),
        (pltpu.VMEM(full, F32), pltpu.VMEM(wide[0], F32), pltpu.VMEM((1, 4 * HALF), F32)),
    )
    layer_out, d_summed, d_down, d_upper, d_part, sums_ffn = call(
        back_ffn_body,
        "back_ffn",
        place,
        (perm, partial, swap(partial), vhat, bias, pair, pair_sib, slope, wup, wdown),
        (((rows, WIDTH), BF16), (full, F32), (full, BF16), wide, whole_pair, ((8, WIDTH), F32)),
    )
    d_part_other = swap(d_part)
    column = ((4, DOWN, WIDTH), BF16)
    g_down = call(
        grad_down_body,
        "grad_down",
        place,
        (active, d_down),
        (column,) * 4,
        (pltpu.VMEM((4 * HALF, WIDTH), F32),),
    )
    down_one = shift(g_down[1], 1)
    d_hidden, d_branch, *d_mixed, sums_norm = call(
        back_norm_body,
        "back_norm",
        place,
        (d_summed, d_part, d_part_other, vhat, scale, bias, wo),
        (((rows, WIDTH), F32), (full, BF16), piece, piece, piece, piece, ((8, WIDTH), F32)),
        after=(g_down[1],),
    )
    d_mixed = exchanged(d_mixed)
    g_up = call(
        grad_up_body,
        "grad_up",
        place,
        (normed_low, d_upper, mixed, d_branch),
        (slabs(40),) * 4,
        (pltpu.VMEM((WIDTH, HALF), F32),),
    )
    g_up_in = exchanged(g_up)
    (down_src,) = call(
        ring_down_body, "ring_down_1", place, (down_one, g_down[2]), (column,), after=(g_up[1],)
    )
    down_two = shift(down_src, 1)
    dq, dk, dv, sums_attn = call(
        functools.partial(back_attend_body, tables),
        "back_attend",
        place,
        d_mixed + (mixed3, q3, k3, v3, lse),
        (heads, heads_all, heads_all, ((8, WIDTH), F32)),
        (pltpu.VMEM((4, rows, HEADS), BF16),),
        after=(down_src,),
    )
    keep_q, send_q = call(
        grad_qkv_body,
        "grad_qkv",
        place,
        (tok, dq, dk, dv, sums_ffn, sums_norm, sums_attn),
        (((17,) + PIECE, BF16),) * 2,
        (pltpu.VMEM((WIDTH, PIECE[1]), F32), pltpu.VMEM((16, WIDTH), F32)),
    )
    recv_q = swap(send_q)
    quad = ((4, rows, WIDTH), BF16)
    same, sib = call(
        grad_tok_body, "grad_tok", place, (dq, dk, dv, w3), (quad, quad), after=(send_q,)
    )
    (down_src,) = call(
        ring_down_body, "ring_down_2", place, (down_two, g_down[3]), (column,), after=(sib,)
    )
    sib = swap(sib)
    down_three = shift(down_src, 1)
    two_q = ((9,) + PIECE, BF16)
    keep_z, send_z = call(
        sum_core_body, "sum_core", place, (keep_q, recv_q), (two_q,) * 2, after=(down_src,)
    )
    recv_z = exchange(send_z, 2)
    keep_up, send_up = call(
        sum_up_body, "sum_up", place, g_up_in, (slabs(20), slabs(20)), after=(send_z,)
    )
    recv_up = exchange(send_up, 2)
    one_q = ((5,) + PIECE, BF16)
    half = ((rows + DOWN) // 2, WIDTH)
    two = ((2,) + half, BF16)
    keep_a, send_a, keep_b, send_b = call(
        sum_td_body, "sum_td", place, (same, sib, g_down[0], down_three), (two,) * 4, after=(send_up,)
    )
    recv_a, recv_b = plane(send_a, 1), plane(send_b, 2)
    kept_z, sent_z = call(
        mid_q_body, "mid_q", place, (keep_z, recv_z), (one_q,) * 2, after=(send_a,)
    )
    z_q = (kept_z, exchange(sent_z, 1))
    kept_up, sent_up = call(
        mid_up_body, "mid_up", place, (keep_up, recv_up), (slabs(10), slabs(10)), after=(sent_z,)
    )
    recv_up = exchange(sent_up, 1)
    p_q = call(sum_q_body, "sum_q", place, z_q, (block,) * 4, after=(sent_up,))
    kept_a, sent_a, kept_b, sent_b = call(
        mid_td_body, "mid_td", place, (keep_a, recv_a, keep_b, recv_b), ((half, BF16),) * 4
    )
    recv_a, recv_b = plane(sent_a, 2), plane(sent_b, 1)
    row = ((SHARD, WIDTH), F32)
    gq, gk, gv, small, ups = call(
        last_q_body,
        "last_q",
        place,
        exchanged(p_q),
        (row, row, row, ((12, 128), F32), ((8, 128), F32)),
        (pltpu.VMEM((4,) + PIECE, F32),),
    )
    kept, sent = call(
        sum_last_body, "sum_last", place, (kept_up, recv_up), (slabs(5, F32), slabs(5, F32))
    )
    go, gup = call(
        last_up_body, "last_up", place, (kept, swap(sent)), (row, ((SHARD, 4 * WIDTH), F32))
    )
    grad_tokens, grad_down = call(
        last_td_body,
        "last_td",
        place,
        (perm, d_hidden, kept_a, recv_a, kept_b, recv_b),
        (((rows, WIDTH), F32), ((DOWN, WIDTH), F32)),
        after=(gup,),
    )
    small = small[:, :SHARD]
    return (
        layer_out,
        grad_tokens,
        gq,
        gk,
        gv,
        go,
        gup,
        grad_down,
        small[0],
        small[1],
        small[2],
        ups[0, :DOWN],
        small[3],
        small[4],
        small[5],
        small[6],
        small[7],
    )


def solution(mesh):
    placed = (
        P(("col", "seq"), None),
        P(("col", "seq")),
        P(("col", "seq"), None),
        P(("col", "seq"), None),
        P(("col", "seq"), None),
        P(("col", "seq"), None),
        P(("col", "seq"), None),
        P(("col", "seq"), None),
        P(("col", "seq")),
        P(("col", "seq")),
        P(("col", "seq")),
        P(("col", "seq")),
        P(("col", "seq")),
        P(("col", "seq")),
        P(("col", "seq")),
        P(("col", "seq")),
        P(("col", "seq")),
        P(("col", "seq"), None),
    )
    fast = mesh.shape["col"] == 8 and mesh.shape["seq"] == 4
    return jax.shard_map(
        fast_device if fast else per_device,
        mesh=mesh,
        in_specs=placed,
        out_specs=(
            P(("col", "seq"), None),
            P(("col", "seq"), None),
            P(("col", "seq"), None),
            P(("col", "seq"), None),
            P(("col", "seq"), None),
            P(("col", "seq"), None),
            P(("col", "seq"), None),
            P(("col", "seq"), None),
            P(("col", "seq")),
            P(("col", "seq")),
            P(("col", "seq")),
            P(("col", "seq")),
            P(("col", "seq")),
            P(("col", "seq")),
            P(("col", "seq")),
            P(("col", "seq")),
            P(("col", "seq")),
        ),
        check_vma=False,
    )
```

```python
import functools

import jax
import jax.numpy as jnp
import numpy as np
from jax import lax
from jax.experimental import pallas as pl
from jax.experimental.pallas import tpu as pltpu
from jax.sharding import PartitionSpec as P

H = 12
HD = 64


NEG_BIG = -1e30
NORM_EPS = 1e-12
LOW_TYPE = jnp.bfloat16
FULL_TYPE = jnp.float32


def block_length(unit_rows):
    target = unit_rows * max(1, -(-512 // unit_rows))
    return target


def layer_norm(values, gain, shift):
    center = values - jnp.mean(values, axis=-1, keepdims=True)
    spread = jnp.mean(center * center, axis=-1, keepdims=True)
    return center * lax.rsqrt(spread + NORM_EPS) * gain + shift


def gelu_exact(values):
    return jax.nn.gelu(values, approximate=False)


def project(left, right, bias):
    return jnp.dot(left, right, preferred_element_type=FULL_TYPE) + bias.astype(FULL_TYPE)


def attend(running, query_heads, query_ids, key_slab, value_slab, key_ids):
    maxima, totals, weighted = running
    scores = (
        jnp.einsum("thd,shd->hts", query_heads, key_slab, preferred_element_type=FULL_TYPE) * 0.125
    )
    visible = (query_ids[:, None] == key_ids[None, :])[None]
    scores = jnp.where(visible, scores, NEG_BIG)
    new_max = jnp.maximum(maxima, jnp.max(scores, axis=2))
    rescale = jnp.exp(maxima - new_max)
    exponents = jnp.where(visible, jnp.exp(scores - new_max[:, :, None]), 0.0)
    totals = totals * rescale + jnp.sum(exponents, axis=2)
    weighted = weighted * rescale[:, :, None] + jnp.einsum(
        "hts,shd->htd", exponents.astype(LOW_TYPE), value_slab, preferred_element_type=FULL_TYPE
    )
    return (new_max, totals, weighted)


def grad_block(
    query_heads, dout_heads, log_totals, row_delta, query_ids, key_slab, value_slab, key_ids
):
    scores = (
        jnp.einsum("thd,shd->hts", query_heads, key_slab, preferred_element_type=FULL_TYPE) * 0.125
    )
    visible = (query_ids[:, None] == key_ids[None, :])[None]
    probabilities = jnp.where(visible, jnp.exp(scores - log_totals[:, :, None]), 0.0)
    grad_value = jnp.einsum(
        "hts,thd->shd", probabilities.astype(LOW_TYPE), dout_heads, preferred_element_type=FULL_TYPE
    )
    grad_probs = jnp.einsum(
        "thd,shd->hts", dout_heads, value_slab, preferred_element_type=FULL_TYPE
    )
    grad_scores = (probabilities * (grad_probs - row_delta[:, :, None])).astype(LOW_TYPE)
    grad_query = (
        jnp.einsum("hts,shd->thd", grad_scores, key_slab, preferred_element_type=FULL_TYPE) * 0.125
    )
    grad_key = (
        jnp.einsum("hts,thd->shd", grad_scores, query_heads, preferred_element_type=FULL_TYPE)
        * 0.125
    )
    return (grad_query, grad_key, grad_value)


def per_device(
    tokens,
    table_ids,
    w_query,
    w_key,
    w_value,
    w_out,
    w_up,
    w_down,
    b_query,
    b_value,
    b_out,
    b_up,
    b_down,
    gain_attn,
    shift_attn,
    gain_ffn,
    shift_ffn,
    cotangent,
):
    shards = (
        w_query,
        w_key,
        w_value,
        w_out,
        w_up,
        w_down,
        b_query,
        b_value,
        b_out,
        b_up,
        b_down,
        gain_attn,
        shift_attn,
        gain_ffn,
        shift_ffn,
    )
    gathered = (
        lax.all_gather(shards[0], ("col", "seq"), axis=0, tiled=True),
        lax.all_gather(shards[1], ("col", "seq"), axis=0, tiled=True),
        lax.all_gather(shards[2], ("col", "seq"), axis=0, tiled=True),
        lax.all_gather(shards[3], ("col", "seq"), axis=0, tiled=True),
        lax.all_gather(shards[4], ("col", "seq"), axis=0, tiled=True),
        lax.all_gather(shards[5], ("col", "seq"), axis=0, tiled=True),
        lax.all_gather(shards[6], ("col", "seq"), axis=0, tiled=True),
        lax.all_gather(shards[7], ("col", "seq"), axis=0, tiled=True),
        lax.all_gather(shards[8], ("col", "seq"), axis=0, tiled=True),
        lax.all_gather(shards[9], ("col", "seq"), axis=0, tiled=True),
        lax.all_gather(shards[10], ("col", "seq"), axis=0, tiled=True),
        lax.all_gather(shards[11], ("col", "seq"), axis=0, tiled=True),
        lax.all_gather(shards[12], ("col", "seq"), axis=0, tiled=True),
        lax.all_gather(shards[13], ("col", "seq"), axis=0, tiled=True),
        lax.all_gather(shards[14], ("col", "seq"), axis=0, tiled=True),
    )
    query_mat, key_mat, value_mat, out_mat, up_mat, down_mat = (
        gathered[0],
        gathered[1],
        gathered[2],
        gathered[3],
        gathered[4],
        gathered[5],
    )
    query_bias, value_bias, out_bias, up_bias, down_bias = (
        gathered[6],
        gathered[7],
        gathered[8],
        gathered[9],
        gathered[10],
    )
    attn_gain, attn_shift, ffn_gain, ffn_shift = (
        gathered[11],
        gathered[12],
        gathered[13],
        gathered[14],
    )
    tok_rows = tokens.shape[0]
    ids_all = lax.all_gather(table_ids, "col", axis=0, tiled=True)
    inputs = tokens.astype(FULL_TYPE)
    queries = project(tokens, query_mat, query_bias).astype(LOW_TYPE)
    keys = jnp.dot(tokens, key_mat, preferred_element_type=FULL_TYPE).astype(LOW_TYPE)
    values = project(tokens, value_mat, value_bias).astype(LOW_TYPE)
    query_heads = queries.reshape(tok_rows, H, HD)
    starting = (
        jnp.full((H, tok_rows), NEG_BIG, FULL_TYPE),
        jnp.zeros((H, tok_rows), FULL_TYPE),
        jnp.zeros((H, tok_rows, HD), FULL_TYPE),
    )
    running = starting
    key_rows = lax.all_gather(keys, "col", axis=0, tiled=True)
    value_rows = lax.all_gather(values, "col", axis=0, tiled=True)
    row_count = key_rows.shape[0]
    length = block_length(tok_rows)
    blocks = row_count // length

    def advance(current, pieces):
        return (attend(current, query_heads, table_ids, pieces[0], pieces[1], pieces[2]), None)

    running, _ = lax.scan(
        advance,
        running,
        (
            key_rows.reshape(blocks, length, H, HD),
            value_rows.reshape(blocks, length, H, HD),
            ids_all.reshape(blocks, length),
        ),
    )
    maxima, totals, weighted = running
    attn_heads = weighted / totals[:, :, None]
    log_totals = maxima + jnp.log(totals)
    attn_low = attn_heads.transpose(1, 0, 2).reshape(tok_rows, H * HD).astype(LOW_TYPE)
    hidden = inputs + project(attn_low, out_mat, out_bias)
    normed, norm_first = jax.vjp(
        layer_norm, hidden, attn_gain.astype(FULL_TYPE), attn_shift.astype(FULL_TYPE)
    )
    normed_low = normed.astype(LOW_TYPE)
    upper = project(normed_low, up_mat, up_bias)
    active, gelu_back = jax.vjp(gelu_exact, upper)
    active_low = active.astype(LOW_TYPE)
    summed = normed + project(active_low, down_mat, down_bias)
    result, norm_second = jax.vjp(
        layer_norm, summed, ffn_gain.astype(FULL_TYPE), ffn_shift.astype(FULL_TYPE)
    )
    again = (
        lax.all_gather(w_query, ("col", "seq"), axis=0, tiled=True),
        lax.all_gather(w_key, ("col", "seq"), axis=0, tiled=True),
        lax.all_gather(w_value, ("col", "seq"), axis=0, tiled=True),
        lax.all_gather(w_out, ("col", "seq"), axis=0, tiled=True),
        lax.all_gather(w_up, ("col", "seq"), axis=0, tiled=True),
        lax.all_gather(w_down, ("col", "seq"), axis=0, tiled=True),
    )
    query_mat, key_mat, value_mat, out_mat, up_mat, down_mat = (
        again[0],
        again[1],
        again[2],
        again[3],
        again[4],
        again[5],
    )
    d_summed, d_ffn_gain, d_ffn_shift = norm_second(cotangent.astype(FULL_TYPE))
    d_down = d_summed.astype(LOW_TYPE)
    grad_down = jnp.einsum("tf,td->fd", active_low, d_down, preferred_element_type=FULL_TYPE)
    d_active = jnp.einsum("td,fd->tf", d_down, down_mat, preferred_element_type=FULL_TYPE)
    d_upper = gelu_back(d_active)[0].astype(LOW_TYPE)
    grad_up = jnp.einsum("td,tf->df", normed_low, d_upper, preferred_element_type=FULL_TYPE)
    d_normed = d_summed + jnp.einsum("tf,df->td", d_upper, up_mat, preferred_element_type=FULL_TYPE)
    d_hidden, d_attn_gain, d_attn_shift = norm_first(d_normed)
    d_branch = d_hidden.astype(LOW_TYPE)
    grad_out = jnp.einsum("tc,td->cd", attn_low, d_branch, preferred_element_type=FULL_TYPE)
    d_attn = jnp.einsum("td,cd->tc", d_branch, out_mat, preferred_element_type=FULL_TYPE).astype(
        LOW_TYPE
    )
    dout_heads = d_attn.reshape(tok_rows, H, HD)
    row_delta = jnp.einsum("thd,htd->ht", dout_heads.astype(FULL_TYPE), attn_heads)
    key_all, value_all = (
        lax.all_gather(keys, "col", axis=0, tiled=True),
        lax.all_gather(values, "col", axis=0, tiled=True),
    )
    total_rows = key_all.shape[0]
    length = block_length(tok_rows)
    blocks = total_rows // length

    def key_pass(grad_sum, pieces):
        grad_query_part, grad_key_part, grad_value_part = grad_block(
            query_heads,
            dout_heads,
            log_totals,
            row_delta,
            table_ids,
            pieces[0],
            pieces[1],
            pieces[2],
        )
        return (grad_sum + grad_query_part, (grad_key_part, grad_value_part))

    query_sum, (key_parts, value_parts) = lax.scan(
        key_pass,
        jnp.zeros((tok_rows, H, HD), FULL_TYPE),
        (
            key_all.reshape(blocks, length, H, HD),
            value_all.reshape(blocks, length, H, HD),
            ids_all.reshape(blocks, length),
        ),
    )
    key_sum, value_sum = (
        lax.psum_scatter(
            key_parts.reshape(total_rows, H * HD).astype(jnp.bfloat16),
            "col",
            scatter_dimension=0,
            tiled=True,
        ).astype(jnp.float32),
        lax.psum_scatter(
            value_parts.reshape(total_rows, H * HD).astype(jnp.bfloat16),
            "col",
            scatter_dimension=0,
            tiled=True,
        ).astype(jnp.float32),
    )
    query_sum = query_sum.reshape(tok_rows, H * HD)
    query_low = query_sum.astype(LOW_TYPE)
    key_low = key_sum.astype(LOW_TYPE)
    value_low = value_sum.astype(LOW_TYPE)
    grad_query = jnp.einsum("tc,td->cd", tokens, query_low, preferred_element_type=FULL_TYPE)
    grad_key = jnp.einsum("tc,td->cd", tokens, key_low, preferred_element_type=FULL_TYPE)
    grad_value = jnp.einsum("tc,td->cd", tokens, value_low, preferred_element_type=FULL_TYPE)
    d_tokens = d_hidden + jnp.einsum(
        "td,cd->tc", query_low, query_mat, preferred_element_type=FULL_TYPE
    )
    d_tokens = d_tokens + jnp.einsum(
        "td,cd->tc", key_low, key_mat, preferred_element_type=FULL_TYPE
    )
    d_tokens = d_tokens + jnp.einsum(
        "td,cd->tc", value_low, value_mat, preferred_element_type=FULL_TYPE
    )
    sums_local = (
        grad_query,
        grad_key,
        grad_value,
        grad_out,
        grad_up,
        grad_down,
        jnp.sum(query_low.astype(FULL_TYPE), axis=0),
        jnp.sum(value_low.astype(FULL_TYPE), axis=0),
        jnp.sum(d_branch.astype(FULL_TYPE), axis=0),
        jnp.sum(d_upper.astype(FULL_TYPE), axis=0),
        jnp.sum(d_down.astype(FULL_TYPE), axis=0),
        d_attn_gain,
        d_attn_shift,
        d_ffn_gain,
        d_ffn_shift,
    )
    owned = (
        lax.psum_scatter(sums_local[0], ("col", "seq"), scatter_dimension=0, tiled=True),
        lax.psum_scatter(sums_local[1], ("col", "seq"), scatter_dimension=0, tiled=True),
        lax.psum_scatter(sums_local[2], ("col", "seq"), scatter_dimension=0, tiled=True),
        lax.psum_scatter(sums_local[3], ("col", "seq"), scatter_dimension=0, tiled=True),
        lax.psum_scatter(sums_local[4], ("col", "seq"), scatter_dimension=0, tiled=True),
        lax.psum_scatter(sums_local[5], ("col", "seq"), scatter_dimension=0, tiled=True),
        lax.psum_scatter(sums_local[6], ("col", "seq"), scatter_dimension=0, tiled=True),
        lax.psum_scatter(sums_local[7], ("col", "seq"), scatter_dimension=0, tiled=True),
        lax.psum_scatter(sums_local[8], ("col", "seq"), scatter_dimension=0, tiled=True),
        lax.psum_scatter(sums_local[9], ("col", "seq"), scatter_dimension=0, tiled=True),
        lax.psum_scatter(sums_local[10], ("col", "seq"), scatter_dimension=0, tiled=True),
        lax.psum_scatter(sums_local[11], ("col", "seq"), scatter_dimension=0, tiled=True),
        lax.psum_scatter(sums_local[12], ("col", "seq"), scatter_dimension=0, tiled=True),
        lax.psum_scatter(sums_local[13], ("col", "seq"), scatter_dimension=0, tiled=True),
        lax.psum_scatter(sums_local[14], ("col", "seq"), scatter_dimension=0, tiled=True),
    )
    return (result.astype(LOW_TYPE), d_tokens) + tuple(owned)


WIDTH = 768
HALF = WIDTH // 2
SHARD = 24
DOWN = 96
SLAB = (SHARD, HALF)
HEADS = 192
PIECE = (SHARD, 640)
BLOCK = (SHARD, 1024)
START_Q = 10 * HALF
CHUNK = (SHARD, START_Q + 5 * PIECE[1])
UNITS = ((slice(0, 128), 2), (slice(128, 192), 1))
VMEM_BYTES = 30 * 2**20
FULL_BYTES = 60 * 2**20
F32 = jnp.float32
BF16 = jnp.bfloat16


COST_SCALE = 10.0
COST = {
    "attend": 11.7,
    "asm_u": 2.5,
    "forward": 5.5,
    "down": 2.0,
    "back_ffn": 5.5,
    "grad_down": 2.2,
    "grad_up": 2.4,
    "back_attend": 11.7,
    "grad_qkvo": 5.2,
    "grad_tok": 4.3,
}


def dot(left, right):
    return jnp.dot(left, right, preferred_element_type=F32)


def dot_nt(left, right):
    return lax.dot_general(left, right, (((1,), (1,)), ((), ())), preferred_element_type=F32)


def dot_tn(left, right):
    return lax.dot_general(left, right, (((0,), (0,)), ((), ())), preferred_element_type=F32)


def call(body, name, place, inputs, outs, scratch=(), after=(), through=(), limit=VMEM_BYTES):
    vmem = pl.BlockSpec(memory_space=pltpu.VMEM)
    any_place = pl.BlockSpec(memory_space=pl.ANY)
    count = 1 + len(inputs)
    skipped = count + len(after) + len(through)

    def run(*refs):
        own = skipped + len(outs)
        body(*refs[:count], *refs[skipped:own], *refs[own + len(through) :])

    return pl.pallas_call(
        run,
        name=name,
        out_shape=tuple(jax.ShapeDtypeStruct(s, t) for s, t in outs)
        + tuple(jax.ShapeDtypeStruct(a.shape, a.dtype) for a in through),
        in_specs=[pl.BlockSpec(memory_space=pltpu.SMEM)] + [vmem] * len(inputs) + [any_place] * (len(after) + len(through)),
        out_specs=tuple(vmem for _ in outs) + tuple(any_place for _ in through),
        input_output_aliases={count + len(after) + n: len(outs) + n for n in range(len(through))},
        scratch_shapes=list(scratch),
        compiler_params=pltpu.CompilerParams(vmem_limit_bytes=limit),
        cost_estimate=pl.CostEstimate(
            flops=int(1.15e9 * COST_SCALE * COST.get(name, 1.3)), bytes_accessed=0, transcendentals=0
        ),
    )(place, *inputs, *after, *through)


def iota(shape, dim):
    return lax.broadcasted_iota(jnp.int32, shape, dim)


def sort_body(place, ids, tokens, cot, perm_out, pair_out, tok_out):
    rows = tokens.shape[0]
    id_j = jnp.broadcast_to(ids[...].astype(F32), (rows, rows))
    id_i = id_j.T
    same = jnp.where(id_i == id_j, 1.0, 0.0)
    count_i = jnp.sum(same, axis=1, keepdims=True)
    count_j = jnp.sum(same, axis=0, keepdims=True)
    i, j = iota((rows, rows), 0), iota((rows, rows), 1)
    equal = jnp.where((id_i == id_j) & (i < j), 1.0, 0.0)
    tie = jnp.where((count_i == count_j) & (id_i < id_j), 1.0, 0.0)
    larger = jnp.where(count_i > count_j, 1.0, 0.0)
    position = jnp.sum(equal + tie + larger, axis=0, keepdims=True)
    perm = jnp.where(i.astype(F32) == position, 1.0, 0.0).astype(BF16)
    perm_out[...] = perm
    tok = dot(perm, tokens[...]).astype(BF16)
    pair_out[0] = tok
    pair_out[1] = dot(perm, cot[...]).astype(BF16)
    tok_out[...] = tok


def fold(block):
    return jnp.concatenate([block[:, :HALF], block[:, HALF:]], axis=0)


def pack_body(place, w_down, wq, wk, wv, wo, wup, *rest):
    vectors, b_up = rest[:8], rest[8]
    parts, (keep, send, down_out) = rest[9:13], rest[13:16]
    rows8, pieces, block = rest[16:]
    down_out[...] = w_down[...]
    dev = place[3]

    def split(mine):
        other = 1 - mine
        keep[0] = wo[:, mine * HALF : (mine + 1) * HALF]
        send[0] = wo[:, other * HALF : (other + 1) * HALF]
        for u in range(4):
            keep[1 + u] = wup[:, u * WIDTH + mine * HALF : u * WIDTH + (mine + 1) * HALF]
            send[1 + u] = wup[:, u * WIDTH + other * HALF : u * WIDTH + (other + 1) * HALF]

    on_core(place, split)
    for n, vector in enumerate(vectors):
        rows8[n : n + 1, :] = vector[...].astype(F32)
    spread = jnp.where(iota((SHARD, WIDTH), 1) == dev * SHARD + iota((SHARD, WIDTH), 0), 1.0, 0.0)
    eight = dot(rows8[...].astype(BF16), spread.astype(BF16))
    lane = lax.rem(dev, 8) * DOWN
    spread_up = jnp.where(iota((DOWN, WIDTH), 1) == lane + iota((DOWN, WIDTH), 0), 1.0, 0.0)
    one = dot(jnp.broadcast_to(b_up[...], (8, DOWN)), spread_up.astype(BF16))
    one = jnp.where(iota((8, WIDTH), 0) == dev // 8, one, 0.0)
    for n in range(2):
        lanes = slice(n * HALF, (n + 1) * HALF)
        block[n * 12 : n * 12 + 8, :] = eight[:, lanes]
        block[n * 12 + 8 : n * 12 + 12, :] = one[:4, lanes]
    for j in range(4):
        for n, w in enumerate((wq, wk, wv)):
            pieces[j, :, n * HEADS : (n + 1) * HEADS] = w[:, j * HEADS : (j + 1) * HEADS].astype(F32)
    for r, part in enumerate(parts):
        part[:, : 3 * HEADS] = pieces[place[1] ^ r].astype(BF16)
        part[:, 3 * HEADS : PIECE[1]] = jnp.zeros((SHARD, PIECE[1] - 3 * HEADS), BF16)
        part[:, PIECE[1] :] = block[...].astype(BF16)


def merge_body(place, keep, recv, q0, q1, q2, q3, chunk, slots):
    parts = (q0, q1, q2, q3)
    for r, part in enumerate(parts):
        slots[place[1] ^ r] = part[:, : PIECE[1]]
    for n in range(4):
        chunk[:, START_Q + n * PIECE[1] : START_Q + (n + 1) * PIECE[1]] = slots[n]
    total = sum(part[:, PIECE[1] :].astype(F32) for part in parts)
    total = jnp.concatenate([total, jnp.zeros((SHARD, PIECE[1] - HALF), F32)], axis=1)
    chunk[:, START_Q + 4 * PIECE[1] :] = total.astype(BF16)

    def fill(mine):
        even, odd = (keep, recv) if mine == 0 else (recv, keep)
        for n in range(5):
            chunk[:, n * HALF : (n + 1) * HALF] = even[n]
            chunk[:, (5 + n) * HALF : (6 + n) * HALF] = odd[n]

    on_core(place, fill)


def z_slot(place, k):
    return lax.rem(place[2] + 4 - k, 4)


def zcat_q_body(place, own, r1, r2, r3, out):
    parts = (own, r1, r2, r3)
    for k, part in enumerate(parts):
        slot = z_slot(place, k) * 4
        for n in range(4):
            out[slot + n] = part[n]
    out[16] = sum(part[4].astype(F32) for part in parts).astype(BF16)


def gate_body(place):
    pass


def zcat_body(place, own, r1, r2, r3, t1, t2, t3, plane_u, plane_q, three):
    parts = (own, r1, r2, r3)
    for k, part in enumerate(parts):
        slot = z_slot(place, k)
        for n in range(10):
            plane_u[slot * 10 + n] = part[:, n * HALF : (n + 1) * HALF]
        for n in range(4):
            plane_q[slot * 4 + n] = part[:, START_Q + n * PIECE[1] : START_Q + (n + 1) * PIECE[1]]
    plane_q[16] = sum(part[:, START_Q + 4 * PIECE[1] :].astype(F32) for part in parts).astype(BF16)
    for r, part in enumerate((t1, t2, t3)):
        three[r] = part[...]


def pcat_body(place, own, r1, r2, r3, column):
    for r, part in enumerate((own, r1, r2, r3)):
        column[place[1] ^ r] = part[...]


def ucut_body(place, from_x, from_y, half_x, half_y):
    half_x[...] = from_x[:20]
    half_y[...] = from_y[20:]


def asm_u_body(place, own, from_x, from_y, low, high, wo, wup, slab):
    parts = (own, from_x, from_y, (low, high))
    natural(place, parts, slab, 0, 5)
    wo[...] = slab[...].astype(BF16)
    for u in range(4):
        natural(place, parts, slab, 1 + u, 5)
        wup[:, u * HALF : (u + 1) * HALF] = slab[...].astype(BF16)


def natural(place, parts, scr, n, count):
    for r, part in enumerate(parts):
        base = (place[1] ^ r) * (8 * SHARD)
        for z in range(4):
            for c in range(2):
                row = pl.multiple_of(base + c * 4 * SHARD + z * SHARD, 8)
                source, index = part, (z * 2 + c) * count + n
                if isinstance(part, tuple):
                    source, index = part[z // 2], index - (z // 2) * 4 * count
                scr[pl.ds(row, SHARD), :] = source[index].astype(F32)


def on_core(place, action):
    @pl.when(place[0] == 0)
    def _():
        action(0)

    @pl.when(place[0] == 1)
    def _():
        action(1)


def table_rows(tok_rows, n_col):
    long_rows = max(2 * 512, 64 * n_col) // n_col
    short_rows = 512 // n_col
    units = tok_rows // short_rows
    long_count = max(1, units // (2 * (long_rows // short_rows)))
    tables, start = [], 0
    for _ in range(long_count):
        tables.append((start, long_rows))
        start += long_rows
    while start < tok_rows:
        tables.append((start, short_rows))
        start += short_rows
    return tables


def attend_body(tables, place, *refs):
    same, pair_sib, three_sib, mine_q, other_q = refs[:4], refs[4], refs[5], refs[6], refs[7]
    w3, bias, tok, q3, k3, v3, mixed_out = refs[8:15]
    mixed_low, lse_out, slab = refs[15:19], refs[19], refs[20]
    rows = tok.shape[1]

    def gather(mine):
        for c in range(2):
            source = mine_q if c == mine else other_q
            for z in range(4):
                for j in range(4):
                    row = j * 8 * SHARD + c * 4 * SHARD + z * SHARD
                    slab[row : row + SHARD, :] = source[z * 4 + j].astype(F32)

    on_core(place, gather)
    for n in range(3):
        w3[n] = slab[:, n * HEADS : (n + 1) * HEADS].astype(BF16)
    total = mine_q[16][:, :HALF].astype(F32) + other_q[16][:, :HALF].astype(F32)
    bias[:12, :HALF] = total[:12]
    bias[:12, HALF:] = total[12:]
    bias[12:, :] = jnp.zeros((4, WIDTH), F32)

    def own_columns(row):
        found = jnp.zeros((1, HEADS), F32)
        for j in range(4):
            part = bias[row : row + 1, j * HEADS : (j + 1) * HEADS]
            found = found + jnp.where(place[1] == j, part, 0.0)
        return found

    for n, part in enumerate(same):
        tok[n] = part[...]
        tok[4 + n] = pair_sib[0] if n == 0 else three_sib[n - 1]
    every = tok[...].reshape(8 * rows, WIDTH)
    k3[...] = dot(every, w3[1]).astype(BF16).reshape(8, rows, HEADS)
    v3[...] = (dot(every, w3[2]) + own_columns(1)).astype(BF16).reshape(8, rows, HEADS)
    queries = dot(tok[:4].reshape(4 * rows, WIDTH), w3[0]) + own_columns(0)
    q3[...] = queries.astype(BF16).reshape(4, rows, HEADS)
    for start, size in tables:
        lse = jnp.zeros((4 * size, 128), F32)
        for lanes, heads in UNITS:
            wide = lanes.stop - lanes.start
            qp = q3[:, start : start + size, lanes].reshape(4 * size, wide)
            kp = k3[:, start : start + size, lanes].reshape(8 * size, wide)
            vp = v3[:, start : start + size, lanes].reshape(8 * size, wide)
            low_half = iota(qp.shape, 1) < HD
            found = []
            for h in range(heads):
                qm = qp.astype(F32) * 0.125
                if heads == 2:
                    qm = jnp.where(low_half if h == 0 else jnp.logical_not(low_half), qm, 0.0)
                scores = dot_nt(qm.astype(BF16), kp)
                top = jnp.max(scores, axis=1, keepdims=True)
                expo = jnp.exp(scores - top)
                total = jnp.sum(expo, axis=1, keepdims=True)
                found.append(dot(expo.astype(BF16), vp) * (1.0 / total))
                column = lanes.start // HD + h
                lse = jnp.where(iota(lse.shape, 1) == column, top + jnp.log(total), lse)
            mixed = found[0] if heads == 1 else jnp.where(low_half, found[0], found[1])
            mixed = mixed.reshape(4, size, wide)
            mixed_out[:, start : start + size, lanes] = mixed
            for r, out in enumerate(mixed_low):
                out[start : start + size, lanes] = mixed[r].astype(BF16)
        lse_out[:, start : start + size, :] = lse.reshape(4, size, 128)


def mcat_body(place, own, r1, r2, r3, out, parts):
    for r, part in enumerate((own, r1, r2, r3)):
        parts[r] = part[...]
    for j in range(4):
        out[:, j * HEADS : (j + 1) * HEADS] = parts[place[1] ^ j]


def norm_stats(values):
    center = values - jnp.mean(values, axis=1, keepdims=True)
    spread = jnp.mean(center * center, axis=1, keepdims=True)
    scale = lax.rsqrt(spread + NORM_EPS)
    return center * scale, scale


def norm_back(e, gain, vhat, scale):
    eg = e * gain
    mean_e = jnp.mean(eg, axis=1, keepdims=True)
    mean_ev = jnp.mean(eg * vhat, axis=1, keepdims=True)
    return scale * (eg - mean_e - vhat * mean_ev)


def flip(pair):
    return jnp.concatenate([pair[1], pair[0]], axis=0)


def forward_body(place, pair, pair_sib, mine, other, wo_mine, wo_other, bias, wup, *refs):
    vhat_out, scale_out, normed_low, active, slope, mixed, wo = refs[:7]
    hidden, upper, b_up = refs[7:]
    rows = pair_sib.shape[1]

    def place_halves(c):
        wo[:, c * HALF : (c + 1) * HALF] = wo_mine[...]
        wo[:, (1 - c) * HALF : (2 - c) * HALF] = wo_other[...]

    on_core(place, place_halves)
    mixed[:rows, :] = mine[...]
    mixed[rows:, :] = other[...]
    hidden[...] = dot(mixed[...], wo[...]) + bias[2:3, :]
    hidden[:rows, :] += pair[0].astype(F32)
    hidden[rows:, :] += pair_sib[0].astype(F32)
    vhat, scale = norm_stats(hidden[...])
    vhat_out[...] = vhat
    scale_out[...] = jnp.broadcast_to(scale, scale_out.shape)
    normed_low[...] = (vhat * bias[4:5, :] + bias[5:6, :]).astype(BF16)

    def bias_half(c):
        for u in range(4):
            b_up[:, u * HALF : (u + 1) * HALF] = bias[8 + u : 9 + u, c * HALF : (c + 1) * HALF]

    on_core(place, bias_half)
    upper[...] = dot(normed_low[...], wup[...])

    def gelu_rows(step, carry):
        block = pl.ds(pl.multiple_of(step * 16, 16), 16)
        x = upper[block, :] + b_up[...]
        cdf = 0.5 * (1.0 + lax.erf(x * 0.7071067811865476))
        pdf = jnp.exp(-0.5 * x * x) * 0.3989422804014327
        active[block, :] = (x * cdf).astype(BF16)
        slope[block, :] = (cdf + x * pdf).astype(BF16)
        return carry

    lax.fori_loop(0, upper.shape[0] // 16, gelu_rows, 0)

def down_body(place, active, p0, p1, p2, p3, partial, wdown):
    for k, part in enumerate((p0, p1, p2, p3)):
        slot = z_slot(place, k)
        for y in range(4):
            wdown[y * 4 + slot] = part[y]
    total = dot(active[...], wdown[...].reshape(4 * HALF, WIDTH))
    partial[...] = total.astype(BF16).reshape(partial.shape)


def back_ffn_body(place, perm, mine, other, vhat1, bias, pair, pair_sib, slope, wup, wdown, *refs):
    layer_out, d_summed, d_down, d_upper, d_part, sums = refs
    rows = pair.shape[1]
    summed = vhat1[...] * bias[4:5, :] + bias[5:6, :] + bias[3:4, :]
    summed = summed + mine[...].astype(F32).reshape(2 * rows, WIDTH) + flip(other).astype(F32)
    vhat, scale = norm_stats(summed)
    gain = bias[6:7, :]
    result = (vhat[:rows] * gain + bias[7:8, :]).astype(BF16)
    layer_out[...] = dot_tn(perm[...], result).astype(BF16)
    e = jnp.concatenate([pair[1], pair_sib[1]], axis=0).astype(F32)
    sums[0:1, :] = jnp.sum(e * vhat, axis=0, keepdims=True)
    sums[1:2, :] = jnp.sum(e, axis=0, keepdims=True)
    grad = norm_back(e, gain, vhat, scale)
    d_summed[...] = grad
    low = grad.astype(BF16)
    d_down[...] = low
    sums[2:3, :] = jnp.sum(low.astype(F32), axis=0, keepdims=True)
    for u in range(4):
        d_active = dot_nt(d_down[...], wdown[u * 4 : (u + 1) * 4].reshape(HALF, WIDTH))
        part = (d_active * slope[:, u * HALF : (u + 1) * HALF].astype(F32)).astype(BF16)
        d_upper[:, u * HALF : (u + 1) * HALF] = part
        half = slice((u % 2) * HALF, (u % 2 + 1) * HALF)
        sums[3 + u // 2 : 4 + u // 2, half] = jnp.sum(part.astype(F32), axis=0, keepdims=True)
    sums[5:8, :] = jnp.zeros((3, WIDTH), F32)
    d_part[...] = dot_nt(d_upper[...], wup[...]).astype(BF16).reshape(2, rows, WIDTH)


def grad_down_body(place, active, d_down, *refs):
    outs, scr = refs[:4], refs[4]
    scr[...] = dot_tn(active[...], d_down[...])
    for k, out in enumerate(outs):
        z = z_slot(place, k)
        for r in range(4):
            row = pl.multiple_of((place[1] ^ r) * (4 * DOWN) + z * DOWN, 8)
            out[r] = scr[pl.ds(row, DOWN), :].astype(BF16)


def ring_down_body(place, recv, own, out):
    out[...] = (recv[...].astype(F32) + own[...].astype(F32)).astype(BF16)


def grad_up_body(place, normed_low, d_upper, mixed, d_branch, *refs):
    outs, scr = refs[:4], refs[4]

    keep_a, send_a, keep_b, send_b = outs

    def cut_slabs(n):
        for r in range(4):
            base = (place[1] ^ r) * (8 * SHARD)
            for k in range(4):
                out = (send_b if r >= 2 else keep_b) if k % 2 else (send_a if r % 2 else keep_a)
                pair = r % 2 if k % 2 else r // 2
                for c in range(2):
                    row = pl.multiple_of(base + c * 4 * SHARD + (place[2] ^ k) * SHARD, 8)
                    slab = scr[pl.ds(row, SHARD), :].astype(BF16)
                    out[pair * 20 + ((k // 2) * 2 + c) * 5 + n] = slab

    def out_half(c):
        scr[...] = dot_tn(mixed[...], d_branch[:, c * HALF : (c + 1) * HALF])

    on_core(place, out_half)
    cut_slabs(0)
    for u in range(4):
        scr[...] = dot_tn(normed_low[...], d_upper[:, u * HALF : (u + 1) * HALF])
        cut_slabs(1 + u)


def back_norm_body(place, d_summed, mine, other, vhat1, scale1, bias, wo, d_hidden_out, d_branch, *refs):
    d_mixed, sums = refs[:4], refs[4]
    rows = d_hidden_out.shape[0]
    e = d_summed[...] + mine[...].astype(F32).reshape(2 * rows, WIDTH) + flip(other).astype(F32)
    vhat = vhat1[...]
    sums[0:1, :] = jnp.sum(e * vhat, axis=0, keepdims=True)
    sums[1:2, :] = jnp.sum(e, axis=0, keepdims=True)
    d_hidden = norm_back(e, bias[4:5, :], vhat, scale1[:, 0:1])
    d_hidden_out[...] = d_hidden[:rows]
    low = d_hidden.astype(BF16)
    d_branch[...] = low
    sums[2:3, :] = jnp.sum(low.astype(F32), axis=0, keepdims=True)
    sums[3:8, :] = jnp.zeros((5, WIDTH), F32)
    for r, out in enumerate(d_mixed):
        row = pl.multiple_of((place[1] ^ r) * HEADS, 64)
        out[...] = dot_nt(d_branch[:rows, :], wo[pl.ds(row, HEADS), :]).astype(BF16)


def back_attend_body(tables, place, d0, d1, d2, d3, mixed, q3, k3, v3, lse, dq_out, dk_out, dv_out, sums, dm3):
    rows = d0.shape[0]
    for r, part in enumerate((d0, d1, d2, d3)):
        dm3[r] = part[...]
    for start, size in tables:
        logs = lse[:, start : start + size, :].reshape(4 * size, 128)
        for lanes, heads in UNITS:
            wide = lanes.stop - lanes.start
            qp = q3[:, start : start + size, lanes].reshape(4 * size, wide).astype(F32) * 0.125
            dp = dm3[:, start : start + size, lanes].reshape(4 * size, wide).astype(F32)
            mp = mixed[:, start : start + size, lanes].reshape(4 * size, wide)
            kp = k3[:, start : start + size, lanes].reshape(8 * size, wide)
            vp = v3[:, start : start + size, lanes].reshape(8 * size, wide)
            low_half = iota(qp.shape, 1) < HD
            found, d_key, d_value = [], None, None
            for h in range(heads):
                qm, dmask = qp, dp
                if heads == 2:
                    mine_h = low_half if h == 0 else jnp.logical_not(low_half)
                    qm, dmask = jnp.where(mine_h, qp, 0.0), jnp.where(mine_h, dp, 0.0)
                delta = jnp.sum(dmask * mp, axis=1, keepdims=True)
                qm, dm = qm.astype(BF16), dmask.astype(BF16)
                column = lanes.start // HD + h
                probs = jnp.exp(dot_nt(qm, kp) - logs[:, column : column + 1])
                part = dot_tn(probs.astype(BF16), dm)
                d_value = part if d_value is None else d_value + part
                d_scores = (probs * (dot_nt(dm, vp) - delta)).astype(BF16)
                found.append(dot(d_scores, kp))
                part = dot_tn(d_scores, qm)
                d_key = part if d_key is None else d_key + part
            d_query = found[0] if heads == 1 else jnp.where(low_half, found[0], found[1])
            d_query = (d_query * 0.125).astype(BF16)
            dq_out[:, start : start + size, lanes] = d_query.reshape(4, size, wide)
            dk_out[:, start : start + size, lanes] = d_key.astype(BF16).reshape(8, size, wide)
            dv_out[:, start : start + size, lanes] = d_value.astype(BF16).reshape(8, size, wide)
    q_sum = jnp.sum(dq_out[...].reshape(4 * rows, HEADS).astype(F32), axis=0, keepdims=True)
    v_sum = jnp.sum(dv_out[...].reshape(8 * rows, HEADS).astype(F32), axis=0, keepdims=True)
    for j in range(4):
        mine = place[1] == j
        sums[0:1, j * HEADS : (j + 1) * HEADS] = jnp.where(mine, q_sum, 0.0)
        sums[1:2, j * HEADS : (j + 1) * HEADS] = jnp.where(mine, v_sum, 0.0)
    sums[2:8, :] = jnp.zeros((6, WIDTH), F32)


def grad_qkv_body(place, tok, dq, dk, dv, sums_ffn, sums_norm, sums_attn, keep, send, scr, block):
    rows = tok.shape[1]
    every = tok[...].reshape(8 * rows, WIDTH)
    scr[:, :HEADS] = dot_tn(tok[:4].reshape(4 * rows, WIDTH), dq[...].reshape(4 * rows, HEADS))
    scr[:, HEADS : 2 * HEADS] = dot_tn(every, dk[...].reshape(8 * rows, HEADS))
    scr[:, 2 * HEADS : 3 * HEADS] = dot_tn(every, dv[...].reshape(8 * rows, HEADS))
    scr[:, 3 * HEADS :] = jnp.zeros((WIDTH, PIECE[1] - 3 * HEADS), F32)
    for k in range(4):
        z = place[2] ^ k
        for r in range(4):
            base = (place[1] ^ r) * (8 * SHARD) + z * SHARD
            for core, out in ((place[0], keep), (1 - place[0], send)):
                row = pl.multiple_of(base + core * (4 * SHARD), 8)
                out[k * 4 + r] = scr[pl.ds(row, SHARD), :].astype(BF16)
    once = jnp.where(place[0] == 0, 1.0, 0.0)
    block[...] = jnp.zeros(block.shape, F32)
    block[0:2, :] = sums_attn[0:2, :]
    block[2:3, :] = sums_norm[2:3, :] * once
    block[3:4, :] = sums_ffn[2:3, :] * once
    block[4:6, :] = sums_norm[0:2, :] * once
    block[6:8, :] = sums_ffn[0:2, :] * once

    def up_rows(c):
        for u in range(4):
            half = sums_ffn[3 + u // 2 : 4 + u // 2, (u % 2) * HALF : (u % 2 + 1) * HALF]
            block[8 + u : 9 + u, c * HALF : (c + 1) * HALF] = half

    on_core(place, up_rows)
    folded = jnp.concatenate([block[:12, :HALF], block[:12, HALF:]], axis=0)
    folded = jnp.concatenate([folded, jnp.zeros((SHARD, PIECE[1] - HALF), F32)], axis=1).astype(BF16)
    keep[16] = folded
    send[16] = folded


def grad_tok_body(place, dq, dk, dv, w3, same, sib):
    rows = same.shape[1]
    for n in range(2):
        keys = dk[4 * n : 4 * n + 4].reshape(4 * rows, HEADS)
        values = dv[4 * n : 4 * n + 4].reshape(4 * rows, HEADS)
        total = dot_nt(keys, w3[1]) + dot_nt(values, w3[2])
        if n == 0:
            total = total + dot_nt(dq[...].reshape(4 * rows, HEADS), w3[0])
        (same, sib)[n][...] = total.astype(BF16).reshape(4, rows, WIDTH)


def added(parts, index):
    total = parts[0][index].astype(F32)
    for part in parts[1:]:
        total = total + part[index].astype(F32)
    return total


def half_up_body(place, keep_a, recv_a, keep_b, recv_b, kept_a, sent_a, kept_b, sent_b):
    for keep, recv, kept, sent in ((keep_a, recv_a, kept_a, sent_a), (keep_b, recv_b, kept_b, sent_b)):
        for n in range(20):
            kept[n] = added((keep, recv), n).astype(BF16)
            sent[n] = added((keep, recv), 20 + n).astype(BF16)


def sum_up_body(place, kept_a, recv_a, kept_b, recv_b, keep, send):
    for n in range(20):
        keep[n] = added((kept_a, recv_a), n).astype(BF16)
        send[n] = added((kept_b, recv_b), n).astype(BF16)


def mid_up_body(place, keep, recv, kept, sent):
    for n in range(10):
        kept[n] = added((keep, recv), n).astype(BF16)
        sent[n] = added((keep, recv), 10 + n).astype(BF16)


def sum_core_body(place, keep, recv, keep_z, send_z):
    total = added((keep, recv), 16).astype(BF16)
    for first, out in enumerate((keep_z, send_z)):
        for n in range(8):
            out[n] = added((keep, recv), (first + 2 * (n // 4)) * 4 + n % 4).astype(BF16)
        out[8] = total


def mid_q_body(place, keep, recv, kept, sent):
    total = added((keep, recv), 8).astype(BF16)
    for out, k in ((kept, 0), (sent, 1)):
        for n in range(4):
            out[n] = added((keep, recv), k * 4 + n).astype(BF16)
        out[4] = total


def sum_q_body(place, own, recv, *outs):
    parts = (own, recv)
    total = added(parts, 4)[:, :HALF].astype(BF16)
    for r, out in enumerate(outs):
        out[:, : PIECE[1]] = added(parts, r).astype(BF16)
        out[:, PIECE[1] :] = total


def last_q_body(place, own, r1, r2, r3, gq, gk, gv, vectors, ups, pieces):
    parts = (own, r1, r2, r3)
    for r, part in enumerate(parts):
        pieces[r] = part[:, : PIECE[1]].astype(F32)
    for j in range(4):
        piece = pieces[place[1] ^ j]
        for n, out in enumerate((gq, gk, gv)):
            out[:, j * HEADS : (j + 1) * HEADS] = piece[:, n * HEADS : (n + 1) * HEADS]
    block = sum(part[:, PIECE[1] :].astype(F32) for part in parts)
    total = jnp.concatenate([block[:12], block[12:]], axis=1)
    dev = place[3]
    high = lax.Precision.HIGHEST
    pick = jnp.where(iota((WIDTH, 128), 0) == dev * SHARD + iota((WIDTH, 128), 1), 1.0, 0.0)
    vectors[...] = jnp.dot(total, pick, precision=high, preferred_element_type=F32)
    lane = lax.rem(dev, 8) * DOWN
    pick_up = jnp.where(iota((WIDTH, 128), 0) == lane + iota((WIDTH, 128), 1), 1.0, 0.0)
    rows = jnp.where(iota(total.shape, 0) == 8 + dev // 8, total, 0.0)
    row = jnp.broadcast_to(jnp.sum(rows, axis=0, keepdims=True), (8, WIDTH))
    ups[...] = jnp.dot(row, pick_up, precision=high, preferred_element_type=F32)


def sum_td_body(place, same, recv, d0, d1, d3, keep_a, send_a, keep_b, send_b):
    rows, half = same.shape[1], keep_a.shape[1]
    for r in range(4):
        tok = (same[r].astype(F32) + recv[r].astype(F32)).astype(BF16)
        own = added((d0, d1, d3), r).astype(BF16)
        (send_a if r % 2 else keep_a)[r // 2] = tok[:half]
        other = send_b if r >= 2 else keep_b
        other[r % 2, : rows - half, :] = tok[half:]
        other[r % 2, rows - half :, :] = own


def mid_td_body(place, keep_a, recv_a, keep_b, recv_b, kept_a, sent_a, kept_b, sent_b):
    kept_a[...] = added((keep_a, recv_a), 0).astype(BF16)
    sent_a[...] = added((keep_a, recv_a), 1).astype(BF16)
    kept_b[...] = added((keep_b, recv_b), 0).astype(BF16)
    sent_b[...] = added((keep_b, recv_b), 1).astype(BF16)


def last_td_body(place, perm, d_hidden, kept_a, recv_a, kept_b, recv_b, out, out_down):
    rows, half = d_hidden.shape[0], kept_a.shape[0]
    whole = slice(None)
    total_a, total_b = added((kept_a, recv_a), whole), added((kept_b, recv_b), whole)
    out_down[...] = total_b[rows - half :]
    total = d_hidden[...] + jnp.concatenate([total_a, total_b[: rows - half]], axis=0)
    high = total.astype(BF16)
    left = total - high.astype(F32)
    middle = left.astype(BF16)
    low = (left - middle.astype(F32)).astype(BF16)
    out[...] = dot_tn(perm[...], high) + dot_tn(perm[...], middle) + dot_tn(perm[...], low)


def sum_last_body(place, u0, u1, keep, send):
    def fill(mine):
        for n in range(5):
            keep[n] = added((u0, u1), mine * 5 + n)
            send[n] = added((u0, u1), (1 - mine) * 5 + n)

    on_core(place, fill)


def last_up_body(place, keep, recv, go, gup):
    def fill(c):
        go[:, c * HALF : (c + 1) * HALF] = keep[0]
        go[:, (1 - c) * HALF : (2 - c) * HALF] = recv[0]
        for u in range(4):
            gup[:, u * WIDTH + c * HALF : u * WIDTH + (c + 1) * HALF] = keep[1 + u]
            gup[:, u * WIDTH + (1 - c) * HALF : u * WIDTH + (2 - c) * HALF] = recv[1 + u]

    on_core(place, fill)


def fast_device(
    tokens,
    table_ids,
    w_query,
    w_key,
    w_value,
    w_out,
    w_up,
    w_down,
    b_query,
    b_value,
    b_out,
    b_up,
    b_down,
    gain_attn,
    shift_attn,
    gain_ffn,
    shift_ffn,
    cotangent,
):
    col, z = lax.axis_index("col"), lax.axis_index("seq")
    place = jnp.stack([col % 2, col // 2, z, col * 4 + z]).astype(jnp.int32)
    rows = tokens.shape[0]
    tables = table_rows(rows, 8)

    def swap(x):
        return lax.ppermute(x, "col", [(i, i ^ 1) for i in range(8)])

    def plane(x, r):
        return lax.ppermute(x, "col", [(i, i ^ (2 * r)) for i in range(8)])

    def shift(x, k):
        return lax.ppermute(x, "seq", [(i, (i + k) % 4) for i in range(4)])

    def planes(x):
        return (x, plane(x, 1), plane(x, 2), plane(x, 3))

    def exchanged(parts):
        return (parts[0],) + tuple(plane(parts[r], r) for r in (1, 2, 3))

    def ring(x):
        one = shift(x, 1)
        two = shift(one, 1)
        return (x, one, two, shift(two, 1))

    def exchange(x, k):
        return lax.ppermute(x, "seq", [(i, i ^ k) for i in range(4)])

    def slabs(count, kind=BF16):
        return ((count,) + SLAB, kind)

    vectors = (b_query, b_value, b_out, b_down, gain_attn, shift_attn, gain_ffn, shift_ffn)
    block = (BLOCK, BF16)
    *q_out, keep_u, send_u, w_down = call(
        pack_body,
        "pack",
        place,
        (w_down, w_query, w_key, w_value, w_out, w_up)
        + tuple(v.reshape(1, SHARD) for v in vectors)
        + (b_up.reshape(1, DOWN),),
        (block,) * 4 + (slabs(5), slabs(5), ((DOWN, WIDTH), BF16)),
        (
            pltpu.VMEM((8, SHARD), F32),
            pltpu.VMEM((4, SHARD, 3 * HEADS), F32),
            pltpu.VMEM(SLAB, F32),
        ),
        limit=FULL_BYTES,
    )
    q_in = exchanged(q_out)
    recv_u = swap(send_u)
    perm, pair, tok_own = call(
        sort_body,
        "sort",
        place,
        (table_ids.reshape(1, rows), tokens, cotangent),
        (((rows, rows), BF16), ((2, rows, WIDTH), BF16), ((rows, WIDTH), BF16)),
        after=(send_u,),
        limit=FULL_BYTES,
    )
    chunk, w_down = call(
        merge_body,
        "merge",
        place,
        (keep_u, recv_u) + q_in,
        ((CHUNK, BF16),),
        (pltpu.VMEM((4,) + PIECE, BF16),),
        after=(tok_own,),
        through=(w_down,),
    )
    column_d, one, tok_own, pair = call(
        pcat_body,
        "pcat",
        place,
        planes(w_down),
        (((4, DOWN, WIDTH), BF16),),
        through=(shift(chunk, 1), tok_own, pair),
    )
    two, tok_x, tok_y, pair_sib, column_d = call(
        gate_body,
        "gate",
        place,
        (),
        (),
        through=(shift(one, 1), plane(tok_own, 1), plane(tok_own, 2), swap(pair), column_d),
    )
    tok_parts = (tok_own, tok_x, tok_y, plane(tok_x, 2))
    plane_u, plane_q, three, column_d = call(
        zcat_body,
        "zcat",
        place,
        (chunk, one, two, shift(two, 1)) + tok_parts[1:],
        (slabs(40), ((17,) + PIECE, BF16), ((3, rows, WIDTH), BF16)),
        through=(column_d,),
    )
    three_sib = swap(three)
    other_q = swap(plane_q)
    u_x, u_y = plane(plane_u, 1), plane(plane_u, 2)
    d_one = shift(column_d, 1)

    heads = ((4, rows, HEADS), BF16)
    heads_all = ((8, rows, HEADS), BF16)
    piece = ((rows, HEADS), BF16)
    w3, bias, tok, q3, k3, v3, mixed3, *mixed_low, lse = call(
        functools.partial(attend_body, tables),
        "attend",
        place,
        tok_parts + (pair_sib, three_sib, plane_q, other_q),
        (
            ((3, WIDTH, HEADS), BF16),
            ((16, WIDTH), F32),
            ((8, rows, WIDTH), BF16),
            heads,
            heads_all,
            heads_all,
            ((4, rows, HEADS), F32),
            piece,
            piece,
            piece,
            piece,
            ((4, rows, 128), F32),
        ),
        (pltpu.VMEM((WIDTH, PIECE[1]), F32),),
        after=(plane_u,),
    )
    half_x, half_y, d_one = call(
        ucut_body, "ucut", place, (u_x, u_y), (slabs(20), slabs(20)), after=(lse,), through=(d_one,)
    )
    d_two = shift(d_one, 1)
    d_parts = (column_d, d_one, d_two, shift(d_two, 1))
    wo_mine, wup, *mixed_low = call(
        asm_u_body,
        "asm_u",
        place,
        (plane_u, u_x, u_y, plane(half_x, 2), plane(half_y, 1)),
        (((WIDTH, HALF), BF16), ((WIDTH, 4 * HALF), BF16)),
        (pltpu.VMEM((WIDTH, HALF), F32),),
        after=(half_x,),
        through=tuple(mixed_low),
    )
    (mixed_own,) = call(
        mcat_body,
        "mcat",
        place,
        exchanged(mixed_low),
        (((rows, WIDTH), BF16),),
        (pltpu.VMEM((4, rows, HEADS), BF16),),
        after=(d_two,),
    )
    whole_pair = ((2, rows, WIDTH), BF16)
    full = (2 * rows, WIDTH)
    wide = ((2 * rows, 4 * HALF), BF16)
    vhat, scale, normed_low, active, slope, mixed, wo = call(
        forward_body,
        "forward",
        place,
        (pair, pair_sib, mixed_own, swap(mixed_own), wo_mine, swap(wo_mine), bias, wup),
        (
            (full, F32),
            ((2 * rows, 128), F32),
            (full, BF16),
            wide,
            wide,
            (full, BF16),
            ((WIDTH, WIDTH), BF16),
        ),
        (pltpu.VMEM(full, F32), pltpu.VMEM(wide[0], F32), pltpu.VMEM((1, 4 * HALF), F32)),
    )
    partial, wdown = call(
        down_body, "down", place, (active,) + d_parts, (whole_pair, ((16, DOWN, WIDTH), BF16))
    )
    layer_out, d_summed, d_down, d_upper, d_part, sums_ffn = call(
        back_ffn_body,
        "back_ffn",
        place,
        (perm, partial, swap(partial), vhat, bias, pair, pair_sib, slope, wup, wdown),
        (((rows, WIDTH), BF16), (full, F32), (full, BF16), wide, whole_pair, ((8, WIDTH), F32)),
    )
    d_part_other = swap(d_part)
    column = ((4, DOWN, WIDTH), BF16)
    g_down = call(
        grad_down_body,
        "grad_down",
        place,
        (active, d_down),
        (column,) * 4,
        (pltpu.VMEM((4 * HALF, WIDTH), F32),),
    )
    down_two, down_three = shift(g_down[2], 1), shift(g_down[1], 3)
    d_hidden, d_branch, *d_mixed, sums_norm = call(
        back_norm_body,
        "back_norm",
        place,
        (d_summed, d_part, d_part_other, vhat, scale, bias, wo),
        (((rows, WIDTH), F32), (full, BF16), piece, piece, piece, piece, ((8, WIDTH), F32)),
        after=(g_down[2],),
    )
    d_mixed = exchanged(d_mixed)
    g_up = call(
        grad_up_body,
        "grad_up",
        place,
        (normed_low, d_upper, mixed, d_branch),
        (slabs(40),) * 4,
        (pltpu.VMEM((WIDTH, HALF), F32),),
    )
    up_a, up_b = plane(g_up[1], 1), plane(g_up[3], 2)
    dq, dk, dv, sums_attn = call(
        functools.partial(back_attend_body, tables),
        "back_attend",
        place,
        d_mixed + (mixed3, q3, k3, v3, lse),
        (heads, heads_all, heads_all, ((8, WIDTH), F32)),
        (pltpu.VMEM((4, rows, HEADS), BF16),),
        after=(g_up[1],),
    )
    keep_q, send_q = call(
        grad_qkv_body,
        "grad_qkv",
        place,
        (tok, dq, dk, dv, sums_ffn, sums_norm, sums_attn),
        (((17,) + PIECE, BF16),) * 2,
        (pltpu.VMEM((WIDTH, PIECE[1]), F32), pltpu.VMEM((16, WIDTH), F32)),
    )
    recv_q = swap(send_q)
    quad = ((4, rows, WIDTH), BF16)
    same, sib = call(
        grad_tok_body, "grad_tok", place, (dq, dk, dv, w3), (quad, quad), after=(send_q,)
    )
    (down_src,) = call(
        ring_down_body, "ring_down", place, (down_two, g_down[3]), (column,), after=(sib,)
    )
    sib = swap(sib)
    down_one = shift(down_src, 1)
    kept_a, sent_a, kept_b, sent_b = call(
        half_up_body,
        "half_up",
        place,
        (g_up[0], up_a, g_up[2], up_b),
        (slabs(20),) * 4,
        after=(down_src,),
    )
    up_a, up_b = plane(sent_a, 2), plane(sent_b, 1)
    two_q = ((9,) + PIECE, BF16)
    keep_z, send_z = call(
        sum_core_body, "sum_core", place, (keep_q, recv_q), (two_q,) * 2, after=(sent_a,)
    )
    recv_z = exchange(send_z, 1)
    keep_up, send_up = call(
        sum_up_body,
        "sum_up",
        place,
        (kept_a, up_a, kept_b, up_b),
        (slabs(20), slabs(20)),
        after=(send_z,),
    )
    recv_up = exchange(send_up, 1)
    one_q = ((5,) + PIECE, BF16)
    half = ((rows + DOWN) // 2, WIDTH)
    two = ((2,) + half, BF16)
    keep_a, send_a, keep_b, send_b = call(
        sum_td_body, "sum_td", place, (same, sib, g_down[0], down_one, down_three), (two,) * 4, after=(send_up,)
    )
    recv_a, recv_b = plane(send_a, 1), plane(send_b, 2)
    kept_z, sent_z = call(
        mid_q_body, "mid_q", place, (keep_z, recv_z), (one_q,) * 2, after=(send_a,)
    )
    z_q = (kept_z, exchange(sent_z, 2))
    kept_a, sent_a, kept_b, sent_b = call(
        mid_td_body, "mid_td", place, (keep_a, recv_a, keep_b, recv_b), ((half, BF16),) * 4, after=(sent_z,)
    )
    recv_a, recv_b = plane(sent_a, 2), plane(sent_b, 1)
    kept_up, sent_up = call(
        mid_up_body, "mid_up", place, (keep_up, recv_up), (slabs(10), slabs(10)), after=(sent_a,)
    )
    recv_up = exchange(sent_up, 2)
    p_q = call(sum_q_body, "sum_q", place, z_q, (block,) * 4, after=(sent_up,))
    row = ((SHARD, WIDTH), F32)
    gq, gk, gv, small, ups = call(
        last_q_body,
        "last_q",
        place,
        exchanged(p_q),
        (row, row, row, ((12, 128), F32), ((8, 128), F32)),
        (pltpu.VMEM((4,) + PIECE, F32),),
    )
    kept, sent = call(
        sum_last_body, "sum_last", place, (kept_up, recv_up), (slabs(5, F32), slabs(5, F32))
    )
    go, gup = call(
        last_up_body, "last_up", place, (kept, swap(sent)), (row, ((SHARD, 4 * WIDTH), F32))
    )
    grad_tokens, grad_down = call(
        last_td_body,
        "last_td",
        place,
        (perm, d_hidden, kept_a, recv_a, kept_b, recv_b),
        (((rows, WIDTH), F32), ((DOWN, WIDTH), F32)),
        after=(gup,),
    )
    small = small[:, :SHARD]
    return (
        layer_out,
        grad_tokens,
        gq,
        gk,
        gv,
        go,
        gup,
        grad_down,
        small[0],
        small[1],
        small[2],
        ups[0, :DOWN],
        small[3],
        small[4],
        small[5],
        small[6],
        small[7],
    )


def solution(mesh):
    placed = (
        P(("col", "seq"), None),
        P(("col", "seq")),
        P(("col", "seq"), None),
        P(("col", "seq"), None),
        P(("col", "seq"), None),
        P(("col", "seq"), None),
        P(("col", "seq"), None),
        P(("col", "seq"), None),
        P(("col", "seq")),
        P(("col", "seq")),
        P(("col", "seq")),
        P(("col", "seq")),
        P(("col", "seq")),
        P(("col", "seq")),
        P(("col", "seq")),
        P(("col", "seq")),
        P(("col", "seq")),
        P(("col", "seq"), None),
    )
    fast = mesh.shape["col"] == 8 and mesh.shape["seq"] == 4
    return jax.shard_map(
        fast_device if fast else per_device,
        mesh=mesh,
        in_specs=placed,
        out_specs=(
            P(("col", "seq"), None),
            P(("col", "seq"), None),
            P(("col", "seq"), None),
            P(("col", "seq"), None),
            P(("col", "seq"), None),
            P(("col", "seq"), None),
            P(("col", "seq"), None),
            P(("col", "seq"), None),
            P(("col", "seq")),
            P(("col", "seq")),
            P(("col", "seq")),
            P(("col", "seq")),
            P(("col", "seq")),
            P(("col", "seq")),
            P(("col", "seq")),
            P(("col", "seq")),
            P(("col", "seq")),
        ),
        check_vma=False,
    )
```

```python
import functools

import jax
import jax.numpy as jnp
import numpy as np
from jax import lax
from jax.experimental import pallas as pl
from jax.experimental.pallas import tpu as pltpu
from jax.sharding import PartitionSpec as P

H = 12
HD = 64


NEG_BIG = -1e30
NORM_EPS = 1e-12
LOW_TYPE = jnp.bfloat16
FULL_TYPE = jnp.float32


def block_length(unit_rows):
    target = unit_rows * max(1, -(-512 // unit_rows))
    return target


def layer_norm(values, gain, shift):
    center = values - jnp.mean(values, axis=-1, keepdims=True)
    spread = jnp.mean(center * center, axis=-1, keepdims=True)
    return center * lax.rsqrt(spread + NORM_EPS) * gain + shift


def gelu_exact(values):
    return jax.nn.gelu(values, approximate=False)


def project(left, right, bias):
    return jnp.dot(left, right, preferred_element_type=FULL_TYPE) + bias.astype(FULL_TYPE)


def attend(running, query_heads, query_ids, key_slab, value_slab, key_ids):
    maxima, totals, weighted = running
    scores = (
        jnp.einsum("thd,shd->hts", query_heads, key_slab, preferred_element_type=FULL_TYPE) * 0.125
    )
    visible = (query_ids[:, None] == key_ids[None, :])[None]
    scores = jnp.where(visible, scores, NEG_BIG)
    new_max = jnp.maximum(maxima, jnp.max(scores, axis=2))
    rescale = jnp.exp(maxima - new_max)
    exponents = jnp.where(visible, jnp.exp(scores - new_max[:, :, None]), 0.0)
    totals = totals * rescale + jnp.sum(exponents, axis=2)
    weighted = weighted * rescale[:, :, None] + jnp.einsum(
        "hts,shd->htd", exponents.astype(LOW_TYPE), value_slab, preferred_element_type=FULL_TYPE
    )
    return (new_max, totals, weighted)


def grad_block(
    query_heads, dout_heads, log_totals, row_delta, query_ids, key_slab, value_slab, key_ids
):
    scores = (
        jnp.einsum("thd,shd->hts", query_heads, key_slab, preferred_element_type=FULL_TYPE) * 0.125
    )
    visible = (query_ids[:, None] == key_ids[None, :])[None]
    probabilities = jnp.where(visible, jnp.exp(scores - log_totals[:, :, None]), 0.0)
    grad_value = jnp.einsum(
        "hts,thd->shd", probabilities.astype(LOW_TYPE), dout_heads, preferred_element_type=FULL_TYPE
    )
    grad_probs = jnp.einsum(
        "thd,shd->hts", dout_heads, value_slab, preferred_element_type=FULL_TYPE
    )
    grad_scores = (probabilities * (grad_probs - row_delta[:, :, None])).astype(LOW_TYPE)
    grad_query = (
        jnp.einsum("hts,shd->thd", grad_scores, key_slab, preferred_element_type=FULL_TYPE) * 0.125
    )
    grad_key = (
        jnp.einsum("hts,thd->shd", grad_scores, query_heads, preferred_element_type=FULL_TYPE)
        * 0.125
    )
    return (grad_query, grad_key, grad_value)


def per_device(
    tokens,
    table_ids,
    w_query,
    w_key,
    w_value,
    w_out,
    w_up,
    w_down,
    b_query,
    b_value,
    b_out,
    b_up,
    b_down,
    gain_attn,
    shift_attn,
    gain_ffn,
    shift_ffn,
    cotangent,
):
    shards = (
        w_query,
        w_key,
        w_value,
        w_out,
        w_up,
        w_down,
        b_query,
        b_value,
        b_out,
        b_up,
        b_down,
        gain_attn,
        shift_attn,
        gain_ffn,
        shift_ffn,
    )
    gathered = (
        lax.all_gather(shards[0], ("col", "seq"), axis=0, tiled=True),
        lax.all_gather(shards[1], ("col", "seq"), axis=0, tiled=True),
        lax.all_gather(shards[2], ("col", "seq"), axis=0, tiled=True),
        lax.all_gather(shards[3], ("col", "seq"), axis=0, tiled=True),
        lax.all_gather(shards[4], ("col", "seq"), axis=0, tiled=True),
        lax.all_gather(shards[5], ("col", "seq"), axis=0, tiled=True),
        lax.all_gather(shards[6], ("col", "seq"), axis=0, tiled=True),
        lax.all_gather(shards[7], ("col", "seq"), axis=0, tiled=True),
        lax.all_gather(shards[8], ("col", "seq"), axis=0, tiled=True),
        lax.all_gather(shards[9], ("col", "seq"), axis=0, tiled=True),
        lax.all_gather(shards[10], ("col", "seq"), axis=0, tiled=True),
        lax.all_gather(shards[11], ("col", "seq"), axis=0, tiled=True),
        lax.all_gather(shards[12], ("col", "seq"), axis=0, tiled=True),
        lax.all_gather(shards[13], ("col", "seq"), axis=0, tiled=True),
        lax.all_gather(shards[14], ("col", "seq"), axis=0, tiled=True),
    )
    query_mat, key_mat, value_mat, out_mat, up_mat, down_mat = (
        gathered[0],
        gathered[1],
        gathered[2],
        gathered[3],
        gathered[4],
        gathered[5],
    )
    query_bias, value_bias, out_bias, up_bias, down_bias = (
        gathered[6],
        gathered[7],
        gathered[8],
        gathered[9],
        gathered[10],
    )
    attn_gain, attn_shift, ffn_gain, ffn_shift = (
        gathered[11],
        gathered[12],
        gathered[13],
        gathered[14],
    )
    tok_rows = tokens.shape[0]
    ids_all = lax.all_gather(table_ids, "col", axis=0, tiled=True)
    inputs = tokens.astype(FULL_TYPE)
    queries = project(tokens, query_mat, query_bias).astype(LOW_TYPE)
    keys = jnp.dot(tokens, key_mat, preferred_element_type=FULL_TYPE).astype(LOW_TYPE)
    values = project(tokens, value_mat, value_bias).astype(LOW_TYPE)
    query_heads = queries.reshape(tok_rows, H, HD)
    starting = (
        jnp.full((H, tok_rows), NEG_BIG, FULL_TYPE),
        jnp.zeros((H, tok_rows), FULL_TYPE),
        jnp.zeros((H, tok_rows, HD), FULL_TYPE),
    )
    running = starting
    key_rows = lax.all_gather(keys, "col", axis=0, tiled=True)
    value_rows = lax.all_gather(values, "col", axis=0, tiled=True)
    row_count = key_rows.shape[0]
    length = block_length(tok_rows)
    blocks = row_count // length

    def advance(current, pieces):
        return (attend(current, query_heads, table_ids, pieces[0], pieces[1], pieces[2]), None)

    running, _ = lax.scan(
        advance,
        running,
        (
            key_rows.reshape(blocks, length, H, HD),
            value_rows.reshape(blocks, length, H, HD),
            ids_all.reshape(blocks, length),
        ),
    )
    maxima, totals, weighted = running
    attn_heads = weighted / totals[:, :, None]
    log_totals = maxima + jnp.log(totals)
    attn_low = attn_heads.transpose(1, 0, 2).reshape(tok_rows, H * HD).astype(LOW_TYPE)
    hidden = inputs + project(attn_low, out_mat, out_bias)
    normed, norm_first = jax.vjp(
        layer_norm, hidden, attn_gain.astype(FULL_TYPE), attn_shift.astype(FULL_TYPE)
    )
    normed_low = normed.astype(LOW_TYPE)
    upper = project(normed_low, up_mat, up_bias)
    active, gelu_back = jax.vjp(gelu_exact, upper)
    active_low = active.astype(LOW_TYPE)
    summed = normed + project(active_low, down_mat, down_bias)
    result, norm_second = jax.vjp(
        layer_norm, summed, ffn_gain.astype(FULL_TYPE), ffn_shift.astype(FULL_TYPE)
    )
    again = (
        lax.all_gather(w_query, ("col", "seq"), axis=0, tiled=True),
        lax.all_gather(w_key, ("col", "seq"), axis=0, tiled=True),
        lax.all_gather(w_value, ("col", "seq"), axis=0, tiled=True),
        lax.all_gather(w_out, ("col", "seq"), axis=0, tiled=True),
        lax.all_gather(w_up, ("col", "seq"), axis=0, tiled=True),
        lax.all_gather(w_down, ("col", "seq"), axis=0, tiled=True),
    )
    query_mat, key_mat, value_mat, out_mat, up_mat, down_mat = (
        again[0],
        again[1],
        again[2],
        again[3],
        again[4],
        again[5],
    )
    d_summed, d_ffn_gain, d_ffn_shift = norm_second(cotangent.astype(FULL_TYPE))
    d_down = d_summed.astype(LOW_TYPE)
    grad_down = jnp.einsum("tf,td->fd", active_low, d_down, preferred_element_type=FULL_TYPE)
    d_active = jnp.einsum("td,fd->tf", d_down, down_mat, preferred_element_type=FULL_TYPE)
    d_upper = gelu_back(d_active)[0].astype(LOW_TYPE)
    grad_up = jnp.einsum("td,tf->df", normed_low, d_upper, preferred_element_type=FULL_TYPE)
    d_normed = d_summed + jnp.einsum("tf,df->td", d_upper, up_mat, preferred_element_type=FULL_TYPE)
    d_hidden, d_attn_gain, d_attn_shift = norm_first(d_normed)
    d_branch = d_hidden.astype(LOW_TYPE)
    grad_out = jnp.einsum("tc,td->cd", attn_low, d_branch, preferred_element_type=FULL_TYPE)
    d_attn = jnp.einsum("td,cd->tc", d_branch, out_mat, preferred_element_type=FULL_TYPE).astype(
        LOW_TYPE
    )
    dout_heads = d_attn.reshape(tok_rows, H, HD)
    row_delta = jnp.einsum("thd,htd->ht", dout_heads.astype(FULL_TYPE), attn_heads)
    key_all, value_all = (
        lax.all_gather(keys, "col", axis=0, tiled=True),
        lax.all_gather(values, "col", axis=0, tiled=True),
    )
    total_rows = key_all.shape[0]
    length = block_length(tok_rows)
    blocks = total_rows // length

    def key_pass(grad_sum, pieces):
        grad_query_part, grad_key_part, grad_value_part = grad_block(
            query_heads,
            dout_heads,
            log_totals,
            row_delta,
            table_ids,
            pieces[0],
            pieces[1],
            pieces[2],
        )
        return (grad_sum + grad_query_part, (grad_key_part, grad_value_part))

    query_sum, (key_parts, value_parts) = lax.scan(
        key_pass,
        jnp.zeros((tok_rows, H, HD), FULL_TYPE),
        (
            key_all.reshape(blocks, length, H, HD),
            value_all.reshape(blocks, length, H, HD),
            ids_all.reshape(blocks, length),
        ),
    )
    key_sum, value_sum = (
        lax.psum_scatter(
            key_parts.reshape(total_rows, H * HD).astype(jnp.bfloat16),
            "col",
            scatter_dimension=0,
            tiled=True,
        ).astype(jnp.float32),
        lax.psum_scatter(
            value_parts.reshape(total_rows, H * HD).astype(jnp.bfloat16),
            "col",
            scatter_dimension=0,
            tiled=True,
        ).astype(jnp.float32),
    )
    query_sum = query_sum.reshape(tok_rows, H * HD)
    query_low = query_sum.astype(LOW_TYPE)
    key_low = key_sum.astype(LOW_TYPE)
    value_low = value_sum.astype(LOW_TYPE)
    grad_query = jnp.einsum("tc,td->cd", tokens, query_low, preferred_element_type=FULL_TYPE)
    grad_key = jnp.einsum("tc,td->cd", tokens, key_low, preferred_element_type=FULL_TYPE)
    grad_value = jnp.einsum("tc,td->cd", tokens, value_low, preferred_element_type=FULL_TYPE)
    d_tokens = d_hidden + jnp.einsum(
        "td,cd->tc", query_low, query_mat, preferred_element_type=FULL_TYPE
    )
    d_tokens = d_tokens + jnp.einsum(
        "td,cd->tc", key_low, key_mat, preferred_element_type=FULL_TYPE
    )
    d_tokens = d_tokens + jnp.einsum(
        "td,cd->tc", value_low, value_mat, preferred_element_type=FULL_TYPE
    )
    sums_local = (
        grad_query,
        grad_key,
        grad_value,
        grad_out,
        grad_up,
        grad_down,
        jnp.sum(query_low.astype(FULL_TYPE), axis=0),
        jnp.sum(value_low.astype(FULL_TYPE), axis=0),
        jnp.sum(d_branch.astype(FULL_TYPE), axis=0),
        jnp.sum(d_upper.astype(FULL_TYPE), axis=0),
        jnp.sum(d_down.astype(FULL_TYPE), axis=0),
        d_attn_gain,
        d_attn_shift,
        d_ffn_gain,
        d_ffn_shift,
    )
    owned = (
        lax.psum_scatter(sums_local[0], ("col", "seq"), scatter_dimension=0, tiled=True),
        lax.psum_scatter(sums_local[1], ("col", "seq"), scatter_dimension=0, tiled=True),
        lax.psum_scatter(sums_local[2], ("col", "seq"), scatter_dimension=0, tiled=True),
        lax.psum_scatter(sums_local[3], ("col", "seq"), scatter_dimension=0, tiled=True),
        lax.psum_scatter(sums_local[4], ("col", "seq"), scatter_dimension=0, tiled=True),
        lax.psum_scatter(sums_local[5], ("col", "seq"), scatter_dimension=0, tiled=True),
        lax.psum_scatter(sums_local[6], ("col", "seq"), scatter_dimension=0, tiled=True),
        lax.psum_scatter(sums_local[7], ("col", "seq"), scatter_dimension=0, tiled=True),
        lax.psum_scatter(sums_local[8], ("col", "seq"), scatter_dimension=0, tiled=True),
        lax.psum_scatter(sums_local[9], ("col", "seq"), scatter_dimension=0, tiled=True),
        lax.psum_scatter(sums_local[10], ("col", "seq"), scatter_dimension=0, tiled=True),
        lax.psum_scatter(sums_local[11], ("col", "seq"), scatter_dimension=0, tiled=True),
        lax.psum_scatter(sums_local[12], ("col", "seq"), scatter_dimension=0, tiled=True),
        lax.psum_scatter(sums_local[13], ("col", "seq"), scatter_dimension=0, tiled=True),
        lax.psum_scatter(sums_local[14], ("col", "seq"), scatter_dimension=0, tiled=True),
    )
    return (result.astype(LOW_TYPE), d_tokens) + tuple(owned)


WIDTH = 768
HALF = WIDTH // 2
SHARD = 24
DOWN = 96
SLAB = (SHARD, HALF)
HEADS = 192
PIECE = (SHARD, 640)
BLOCK = (SHARD, 1024)
START_Q = 10 * HALF
CHUNK = (SHARD, START_Q + 5 * PIECE[1])
KEYS = slice(0, 192)
VALUES = slice(256, 448)
BOTH = 512
UNITS = ((slice(0, 128), 2), (slice(128, 192), 1))
VMEM_BYTES = 30 * 2**20
FULL_BYTES = 60 * 2**20
F32 = jnp.float32
BF16 = jnp.bfloat16


COST_SCALE = 10.0
COST = {
    "attend": 11.7,
    "asm_u": 2.5,
    "forward": 5.5,
    "down": 2.0,
    "back_ffn": 5.5,
    "grad_down": 2.2,
    "grad_up": 2.4,
    "back_attend": 11.7,
    "grad_qkvo": 5.2,
    "grad_tok": 4.3,
}


def dot(left, right):
    return jnp.dot(left, right, preferred_element_type=F32)


def dot_nt(left, right):
    return lax.dot_general(left, right, (((1,), (1,)), ((), ())), preferred_element_type=F32)


def dot_tn(left, right):
    return lax.dot_general(left, right, (((0,), (0,)), ((), ())), preferred_element_type=F32)


def call(body, name, place, inputs, outs, scratch=(), after=(), through=(), limit=VMEM_BYTES):
    vmem = pl.BlockSpec(memory_space=pltpu.VMEM)
    any_place = pl.BlockSpec(memory_space=pl.ANY)
    count = 1 + len(inputs)
    skipped = count + len(after) + len(through)

    def run(*refs):
        own = skipped + len(outs)
        body(*refs[:count], *refs[skipped:own], *refs[own + len(through) :])

    return pl.pallas_call(
        run,
        name=name,
        out_shape=tuple(jax.ShapeDtypeStruct(s, t) for s, t in outs)
        + tuple(jax.ShapeDtypeStruct(a.shape, a.dtype) for a in through),
        in_specs=[pl.BlockSpec(memory_space=pltpu.SMEM)] + [vmem] * len(inputs) + [any_place] * (len(after) + len(through)),
        out_specs=tuple(vmem for _ in outs) + tuple(any_place for _ in through),
        input_output_aliases={count + len(after) + n: len(outs) + n for n in range(len(through))},
        scratch_shapes=list(scratch),
        compiler_params=pltpu.CompilerParams(vmem_limit_bytes=limit),
        cost_estimate=pl.CostEstimate(
            flops=int(1.15e9 * COST_SCALE * COST.get(name, 1.3)), bytes_accessed=0, transcendentals=0
        ),
    )(place, *inputs, *after, *through)


def iota(shape, dim):
    return lax.broadcasted_iota(jnp.int32, shape, dim)


def sort_body(place, ids, tokens, cot, perm_out, pair_out, tok_out):
    rows = tokens.shape[0]
    id_j = jnp.broadcast_to(ids[...].astype(F32), (rows, rows))
    id_i = id_j.T
    same = jnp.where(id_i == id_j, 1.0, 0.0)
    count_i = jnp.sum(same, axis=1, keepdims=True)
    count_j = jnp.sum(same, axis=0, keepdims=True)
    i, j = iota((rows, rows), 0), iota((rows, rows), 1)
    equal = jnp.where((id_i == id_j) & (i < j), 1.0, 0.0)
    tie = jnp.where((count_i == count_j) & (id_i < id_j), 1.0, 0.0)
    larger = jnp.where(count_i > count_j, 1.0, 0.0)
    position = jnp.sum(equal + tie + larger, axis=0, keepdims=True)
    perm = jnp.where(i.astype(F32) == position, 1.0, 0.0).astype(BF16)
    perm_out[...] = perm
    tok = dot(perm, tokens[...]).astype(BF16)
    pair_out[0] = tok
    pair_out[1] = dot(perm, cot[...]).astype(BF16)
    tok_out[...] = tok


def fold(block):
    return jnp.concatenate([block[:, :HALF], block[:, HALF:]], axis=0)


def pack_body(place, w_down, wq, wk, wv, wo, wup, *rest):
    vectors, b_up = rest[:8], rest[8]
    parts, (keep, send, down_out) = rest[9:13], rest[13:16]
    rows8, pieces, block = rest[16:]
    down_out[...] = w_down[...]
    dev = place[3]

    def split(mine):
        other = 1 - mine
        keep[0] = wo[:, mine * HALF : (mine + 1) * HALF]
        send[0] = wo[:, other * HALF : (other + 1) * HALF]
        for u in range(4):
            keep[1 + u] = wup[:, u * WIDTH + mine * HALF : u * WIDTH + (mine + 1) * HALF]
            send[1 + u] = wup[:, u * WIDTH + other * HALF : u * WIDTH + (other + 1) * HALF]

    on_core(place, split)
    for n, vector in enumerate(vectors):
        rows8[n : n + 1, :] = vector[...].astype(F32)
    spread = jnp.where(iota((SHARD, WIDTH), 1) == dev * SHARD + iota((SHARD, WIDTH), 0), 1.0, 0.0)
    eight = dot(rows8[...].astype(BF16), spread.astype(BF16))
    lane = lax.rem(dev, 8) * DOWN
    spread_up = jnp.where(iota((DOWN, WIDTH), 1) == lane + iota((DOWN, WIDTH), 0), 1.0, 0.0)
    one = dot(jnp.broadcast_to(b_up[...], (8, DOWN)), spread_up.astype(BF16))
    one = jnp.where(iota((8, WIDTH), 0) == dev // 8, one, 0.0)
    for n in range(2):
        lanes = slice(n * HALF, (n + 1) * HALF)
        block[n * 12 : n * 12 + 8, :] = eight[:, lanes]
        block[n * 12 + 8 : n * 12 + 12, :] = one[:4, lanes]
    for j in range(4):
        for n, w in enumerate((wq, wk, wv)):
            pieces[j, :, n * HEADS : (n + 1) * HEADS] = w[:, j * HEADS : (j + 1) * HEADS].astype(F32)
    for r, part in enumerate(parts):
        part[:, : 3 * HEADS] = pieces[place[1] ^ r].astype(BF16)
        part[:, 3 * HEADS : PIECE[1]] = jnp.zeros((SHARD, PIECE[1] - 3 * HEADS), BF16)
        part[:, PIECE[1] :] = block[...].astype(BF16)


def merge_body(place, keep, recv, q0, q1, q2, q3, chunk, slots):
    parts = (q0, q1, q2, q3)
    for r, part in enumerate(parts):
        slots[place[1] ^ r] = part[:, : PIECE[1]]
    for n in range(4):
        chunk[:, START_Q + n * PIECE[1] : START_Q + (n + 1) * PIECE[1]] = slots[n]
    total = sum(part[:, PIECE[1] :].astype(F32) for part in parts)
    total = jnp.concatenate([total, jnp.zeros((SHARD, PIECE[1] - HALF), F32)], axis=1)
    chunk[:, START_Q + 4 * PIECE[1] :] = total.astype(BF16)

    def fill(mine):
        even, odd = (keep, recv) if mine == 0 else (recv, keep)
        for n in range(5):
            chunk[:, n * HALF : (n + 1) * HALF] = even[n]
            chunk[:, (5 + n) * HALF : (6 + n) * HALF] = odd[n]

    on_core(place, fill)


def z_slot(place, k):
    return lax.rem(place[2] + 4 - k, 4)


def zcat_q_body(place, own, r1, r2, r3, out):
    parts = (own, r1, r2, r3)
    for k, part in enumerate(parts):
        slot = z_slot(place, k) * 4
        for n in range(4):
            out[slot + n] = part[n]
    out[16] = sum(part[4].astype(F32) for part in parts).astype(BF16)


def gate_body(place):
    pass


def zcat_body(place, own, r1, r2, r3, t1, t2, t3, plane_u, plane_q, three):
    parts = (own, r1, r2, r3)
    for k, part in enumerate(parts):
        slot = z_slot(place, k)
        for n in range(10):
            plane_u[slot * 10 + n] = part[:, n * HALF : (n + 1) * HALF]
        for n in range(4):
            plane_q[slot * 4 + n] = part[:, START_Q + n * PIECE[1] : START_Q + (n + 1) * PIECE[1]]
    plane_q[16] = sum(part[:, START_Q + 4 * PIECE[1] :].astype(F32) for part in parts).astype(BF16)
    for r, part in enumerate((t1, t2, t3)):
        three[r] = part[...]


def pcat_body(place, own, r1, r2, r3, column):
    for r, part in enumerate((own, r1, r2, r3)):
        column[place[1] ^ r] = part[...]


def ucut_body(place, from_x, from_y, half_x, half_y):
    half_x[...] = from_x[:20]
    half_y[...] = from_y[20:]


def asm_u_body(place, own, from_x, from_y, low, high, wo, wup, slab):
    parts = (own, from_x, from_y, (low, high))
    natural(place, parts, slab, 0, 5)
    wo[...] = slab[...].astype(BF16)
    for u in range(4):
        natural(place, parts, slab, 1 + u, 5)
        wup[:, u * HALF : (u + 1) * HALF] = slab[...].astype(BF16)


def natural(place, parts, scr, n, count):
    for r, part in enumerate(parts):
        base = (place[1] ^ r) * (8 * SHARD)
        for z in range(4):
            for c in range(2):
                row = pl.multiple_of(base + c * 4 * SHARD + z * SHARD, 8)
                source, index = part, (z * 2 + c) * count + n
                if isinstance(part, tuple):
                    source, index = part[z // 2], index - (z // 2) * 4 * count
                scr[pl.ds(row, SHARD), :] = source[index].astype(F32)


def on_core(place, action):
    @pl.when(place[0] == 0)
    def _():
        action(0)

    @pl.when(place[0] == 1)
    def _():
        action(1)


def table_rows(tok_rows, n_col):
    long_rows = max(2 * 512, 64 * n_col) // n_col
    short_rows = 512 // n_col
    units = tok_rows // short_rows
    long_count = max(1, units // (2 * (long_rows // short_rows)))
    tables, start = [], 0
    for _ in range(long_count):
        tables.append((start, long_rows))
        start += long_rows
    while start < tok_rows:
        tables.append((start, short_rows))
        start += short_rows
    return tables


def attend_body(tables, place, *refs):
    same, pair_sib, three_sib, mine_q, other_q = refs[:4], refs[4], refs[5], refs[6], refs[7]
    wq, wkv, bias, tok, q3, k3, v3, mixed_out = refs[8:16]
    mixed_low, lse_out, slab = refs[16:20], refs[20], refs[21]
    rows = tok.shape[1]

    def gather(mine):
        for c in range(2):
            source = mine_q if c == mine else other_q
            for z in range(4):
                for j in range(4):
                    row = j * 8 * SHARD + c * 4 * SHARD + z * SHARD
                    slab[row : row + SHARD, :] = source[z * 4 + j].astype(F32)

    on_core(place, gather)
    wq[...] = slab[:, :HEADS].astype(BF16)
    wkv[...] = jnp.zeros(wkv.shape, BF16)
    wkv[:, KEYS] = slab[:, HEADS : 2 * HEADS].astype(BF16)
    wkv[:, VALUES] = slab[:, 2 * HEADS : 3 * HEADS].astype(BF16)
    total = mine_q[16][:, :HALF].astype(F32) + other_q[16][:, :HALF].astype(F32)
    bias[:12, :HALF] = total[:12]
    bias[:12, HALF:] = total[12:]
    bias[12:, :] = jnp.zeros((4, WIDTH), F32)

    def own_columns(row):
        found = jnp.zeros((1, HEADS), F32)
        for j in range(4):
            part = bias[row : row + 1, j * HEADS : (j + 1) * HEADS]
            found = found + jnp.where(place[1] == j, part, 0.0)
        return found

    for n, part in enumerate(same):
        tok[n] = part[...]
        tok[4 + n] = pair_sib[0] if n == 0 else three_sib[n - 1]
    every = tok[...].reshape(8 * rows, WIDTH)
    both = dot(every, wkv[...])
    k3[...] = both[:, KEYS].astype(BF16).reshape(8, rows, HEADS)
    v3[...] = (both[:, VALUES] + own_columns(1)).astype(BF16).reshape(8, rows, HEADS)
    queries = dot(tok[:4].reshape(4 * rows, WIDTH), wq[...]) + own_columns(0)
    q3[...] = queries.astype(BF16).reshape(4, rows, HEADS)
    for start, size in tables:
        lse = jnp.zeros((4 * size, 128), F32)
        for lanes, heads in UNITS:
            wide = lanes.stop - lanes.start
            qp = q3[:, start : start + size, lanes].reshape(4 * size, wide)
            kp = k3[:, start : start + size, lanes].reshape(8 * size, wide)
            vp = v3[:, start : start + size, lanes].reshape(8 * size, wide)
            low_half = iota(qp.shape, 1) < HD
            found = []
            for h in range(heads):
                qm = qp.astype(F32) * 0.125
                if heads == 2:
                    qm = jnp.where(low_half if h == 0 else jnp.logical_not(low_half), qm, 0.0)
                scores = dot_nt(qm.astype(BF16), kp)
                top = jnp.max(scores, axis=1, keepdims=True)
                expo = jnp.exp(scores - top)
                total = jnp.sum(expo, axis=1, keepdims=True)
                found.append(dot(expo.astype(BF16), vp) * (1.0 / total))
                column = lanes.start // HD + h
                lse = jnp.where(iota(lse.shape, 1) == column, top + jnp.log(total), lse)
            mixed = found[0] if heads == 1 else jnp.where(low_half, found[0], found[1])
            mixed = mixed.reshape(4, size, wide)
            mixed_out[:, start : start + size, lanes] = mixed
            for r, out in enumerate(mixed_low):
                out[start : start + size, lanes] = mixed[r].astype(BF16)
        lse_out[:, start : start + size, :] = lse.reshape(4, size, 128)


def mcat_body(place, own, r1, r2, r3, out, parts):
    for r, part in enumerate((own, r1, r2, r3)):
        parts[r] = part[...]
    for j in range(4):
        out[:, j * HEADS : (j + 1) * HEADS] = parts[place[1] ^ j]


def norm_stats(values):
    center = values - jnp.mean(values, axis=1, keepdims=True)
    spread = jnp.mean(center * center, axis=1, keepdims=True)
    scale = lax.rsqrt(spread + NORM_EPS)
    return center * scale, scale


def norm_back(e, gain, vhat, scale):
    eg = e * gain
    mean_e = jnp.mean(eg, axis=1, keepdims=True)
    mean_ev = jnp.mean(eg * vhat, axis=1, keepdims=True)
    return scale * (eg - mean_e - vhat * mean_ev)


def flip(pair):
    return jnp.concatenate([pair[1], pair[0]], axis=0)


def forward_body(place, pair, pair_sib, mine, other, wo_mine, wo_other, bias, wup, *refs):
    vhat_out, scale_out, normed_low, active, slope, mixed, wo = refs[:7]
    hidden, upper, b_up = refs[7:]
    rows = pair_sib.shape[1]

    def place_halves(c):
        wo[:, c * HALF : (c + 1) * HALF] = wo_mine[...]
        wo[:, (1 - c) * HALF : (2 - c) * HALF] = wo_other[...]

    on_core(place, place_halves)
    mixed[:rows, :] = mine[...]
    mixed[rows:, :] = other[...]
    hidden[...] = dot(mixed[...], wo[...]) + bias[2:3, :]
    hidden[:rows, :] += pair[0].astype(F32)
    hidden[rows:, :] += pair_sib[0].astype(F32)
    vhat, scale = norm_stats(hidden[...])
    vhat_out[...] = vhat
    scale_out[...] = jnp.broadcast_to(scale, scale_out.shape)
    normed_low[...] = (vhat * bias[4:5, :] + bias[5:6, :]).astype(BF16)

    def bias_half(c):
        for u in range(4):
            b_up[:, u * HALF : (u + 1) * HALF] = bias[8 + u : 9 + u, c * HALF : (c + 1) * HALF]

    on_core(place, bias_half)
    upper[...] = dot(normed_low[...], wup[...])

    def gelu_rows(step, carry):
        block = pl.ds(pl.multiple_of(step * 16, 16), 16)
        x = upper[block, :] + b_up[...]
        cdf = 0.5 * (1.0 + lax.erf(x * 0.7071067811865476))
        pdf = jnp.exp(-0.5 * x * x) * 0.3989422804014327
        active[block, :] = (x * cdf).astype(BF16)
        slope[block, :] = (cdf + x * pdf).astype(BF16)
        return carry

    lax.fori_loop(0, upper.shape[0] // 16, gelu_rows, 0)

def down_body(place, active, p0, p1, p2, p3, partial, wdown):
    for k, part in enumerate((p0, p1, p2, p3)):
        slot = z_slot(place, k)
        for y in range(4):
            wdown[y * 4 + slot] = part[y]
    total = dot(active[...], wdown[...].reshape(4 * HALF, WIDTH))
    partial[...] = total.astype(BF16).reshape(partial.shape)


def back_ffn_body(place, perm, mine, other, vhat1, bias, pair, pair_sib, slope, wup, wdown, *refs):
    layer_out, d_summed, d_down, d_upper, d_part, sums = refs
    rows = pair.shape[1]
    summed = vhat1[...] * bias[4:5, :] + bias[5:6, :] + bias[3:4, :]
    summed = summed + mine[...].astype(F32).reshape(2 * rows, WIDTH) + flip(other).astype(F32)
    vhat, scale = norm_stats(summed)
    gain = bias[6:7, :]
    result = (vhat[:rows] * gain + bias[7:8, :]).astype(BF16)
    layer_out[...] = dot_tn(perm[...], result).astype(BF16)
    e = jnp.concatenate([pair[1], pair_sib[1]], axis=0).astype(F32)
    sums[0:1, :] = jnp.sum(e * vhat, axis=0, keepdims=True)
    sums[1:2, :] = jnp.sum(e, axis=0, keepdims=True)
    grad = norm_back(e, gain, vhat, scale)
    d_summed[...] = grad
    low = grad.astype(BF16)
    d_down[...] = low
    sums[2:3, :] = jnp.sum(low.astype(F32), axis=0, keepdims=True)
    for u in range(4):
        d_active = dot_nt(d_down[...], wdown[u * 4 : (u + 1) * 4].reshape(HALF, WIDTH))
        part = (d_active * slope[:, u * HALF : (u + 1) * HALF].astype(F32)).astype(BF16)
        d_upper[:, u * HALF : (u + 1) * HALF] = part
        half = slice((u % 2) * HALF, (u % 2 + 1) * HALF)
        sums[3 + u // 2 : 4 + u // 2, half] = jnp.sum(part.astype(F32), axis=0, keepdims=True)
    sums[5:8, :] = jnp.zeros((3, WIDTH), F32)
    d_part[...] = dot_nt(d_upper[...], wup[...]).astype(BF16).reshape(2, rows, WIDTH)


def grad_down_body(place, active, d_down, *refs):
    outs, scr = refs[:4], refs[4]
    scr[...] = dot_tn(active[...], d_down[...])
    for k, out in enumerate(outs):
        z = z_slot(place, k)
        for r in range(4):
            row = pl.multiple_of((place[1] ^ r) * (4 * DOWN) + z * DOWN, 8)
            out[r] = scr[pl.ds(row, DOWN), :].astype(BF16)


def ring_down_body(place, recv, own, out):
    out[...] = (recv[...].astype(F32) + own[...].astype(F32)).astype(BF16)


def grad_up_body(place, normed_low, d_upper, mixed, d_branch, *refs):
    (keep_a, send_a, keep_b, send_b), scr, scr_up = refs[:4], refs[4], refs[5]

    def out_half(c):
        scr[...] = dot_tn(mixed[...], d_branch[:, c * HALF : (c + 1) * HALF])

    on_core(place, out_half)
    scr_up[...] = dot_tn(normed_low[...], d_upper[...])
    for r in range(4):
        base = (place[1] ^ r) * (8 * SHARD)
        for k in range(4):
            out = (send_b if r >= 2 else keep_b) if k % 2 else (send_a if r % 2 else keep_a)
            pair = r % 2 if k % 2 else r // 2
            for c in range(2):
                row = pl.multiple_of(base + c * 4 * SHARD + (place[2] ^ k) * SHARD, 8)
                first = pair * 20 + ((k // 2) * 2 + c) * 5
                out[first] = scr[pl.ds(row, SHARD), :].astype(BF16)
                for u in range(4):
                    slab = scr_up[pl.ds(row, SHARD), u * HALF : (u + 1) * HALF]
                    out[first + 1 + u] = slab.astype(BF16)


def back_norm_body(place, d_summed, mine, other, vhat1, scale1, bias, wo, d_hidden_out, d_branch, *refs):
    d_mixed, sums = refs[:4], refs[4]
    rows = d_hidden_out.shape[0]
    e = d_summed[...] + mine[...].astype(F32).reshape(2 * rows, WIDTH) + flip(other).astype(F32)
    vhat = vhat1[...]
    sums[0:1, :] = jnp.sum(e * vhat, axis=0, keepdims=True)
    sums[1:2, :] = jnp.sum(e, axis=0, keepdims=True)
    d_hidden = norm_back(e, bias[4:5, :], vhat, scale1[:, 0:1])
    d_hidden_out[...] = d_hidden[:rows]
    low = d_hidden.astype(BF16)
    d_branch[...] = low
    sums[2:3, :] = jnp.sum(low.astype(F32), axis=0, keepdims=True)
    sums[3:8, :] = jnp.zeros((5, WIDTH), F32)
    for r, out in enumerate(d_mixed):
        row = pl.multiple_of((place[1] ^ r) * HEADS, 64)
        out[...] = dot_nt(d_branch[:rows, :], wo[pl.ds(row, HEADS), :]).astype(BF16)


def back_attend_body(tables, place, d0, d1, d2, d3, mixed, q3, k3, v3, lse, dq_out, dkv_out, sums, dm3):
    rows = d0.shape[0]
    for r, part in enumerate((d0, d1, d2, d3)):
        dm3[r] = part[...]
    pad = jnp.zeros((8, rows, BOTH // 2 - HEADS), BF16)
    dkv_out[:, :, HEADS : BOTH // 2] = pad
    dkv_out[:, :, BOTH // 2 + HEADS :] = pad
    for start, size in tables:
        logs = lse[:, start : start + size, :].reshape(4 * size, 128)
        for lanes, heads in UNITS:
            wide = lanes.stop - lanes.start
            qp = q3[:, start : start + size, lanes].reshape(4 * size, wide).astype(F32) * 0.125
            dp = dm3[:, start : start + size, lanes].reshape(4 * size, wide).astype(F32)
            mp = mixed[:, start : start + size, lanes].reshape(4 * size, wide)
            kp = k3[:, start : start + size, lanes].reshape(8 * size, wide)
            vp = v3[:, start : start + size, lanes].reshape(8 * size, wide)
            low_half = iota(qp.shape, 1) < HD
            found, d_key, d_value = [], None, None
            for h in range(heads):
                qm, dmask = qp, dp
                if heads == 2:
                    mine_h = low_half if h == 0 else jnp.logical_not(low_half)
                    qm, dmask = jnp.where(mine_h, qp, 0.0), jnp.where(mine_h, dp, 0.0)
                delta = jnp.sum(dmask * mp, axis=1, keepdims=True)
                qm, dm = qm.astype(BF16), dmask.astype(BF16)
                column = lanes.start // HD + h
                probs = jnp.exp(dot_nt(qm, kp) - logs[:, column : column + 1])
                part = dot_tn(probs.astype(BF16), dm)
                d_value = part if d_value is None else d_value + part
                d_scores = (probs * (dot_nt(dm, vp) - delta)).astype(BF16)
                found.append(dot(d_scores, kp))
                part = dot_tn(d_scores, qm)
                d_key = part if d_key is None else d_key + part
            d_query = found[0] if heads == 1 else jnp.where(low_half, found[0], found[1])
            d_query = (d_query * 0.125).astype(BF16)
            dq_out[:, start : start + size, lanes] = d_query.reshape(4, size, wide)
            dkv_out[:, start : start + size, lanes] = d_key.astype(BF16).reshape(8, size, wide)
            moved = slice(VALUES.start + lanes.start, VALUES.start + lanes.stop)
            dkv_out[:, start : start + size, moved] = d_value.astype(BF16).reshape(8, size, wide)
    q_sum = jnp.sum(dq_out[...].reshape(4 * rows, HEADS).astype(F32), axis=0, keepdims=True)
    v_sum = jnp.sum(dkv_out[:, :, VALUES].reshape(8 * rows, HEADS).astype(F32), axis=0, keepdims=True)
    for j in range(4):
        mine = place[1] == j
        sums[0:1, j * HEADS : (j + 1) * HEADS] = jnp.where(mine, q_sum, 0.0)
        sums[1:2, j * HEADS : (j + 1) * HEADS] = jnp.where(mine, v_sum, 0.0)
    sums[2:8, :] = jnp.zeros((6, WIDTH), F32)


def grad_qkv_body(place, tok, dq, dkv, sums_ffn, sums_norm, sums_attn, keep, send, scr, block):
    rows = tok.shape[1]
    every = tok[...].reshape(8 * rows, WIDTH)
    scr[:, :HEADS] = dot_tn(tok[:4].reshape(4 * rows, WIDTH), dq[...].reshape(4 * rows, HEADS))
    both = dot_tn(every, dkv[...].reshape(8 * rows, BOTH))
    scr[:, HEADS : 2 * HEADS] = both[:, KEYS]
    scr[:, 2 * HEADS : 3 * HEADS] = both[:, VALUES]
    scr[:, 3 * HEADS :] = jnp.zeros((WIDTH, PIECE[1] - 3 * HEADS), F32)
    for k in range(4):
        z = place[2] ^ k
        for r in range(4):
            base = (place[1] ^ r) * (8 * SHARD) + z * SHARD
            for core, out in ((place[0], keep), (1 - place[0], send)):
                row = pl.multiple_of(base + core * (4 * SHARD), 8)
                out[k * 4 + r] = scr[pl.ds(row, SHARD), :].astype(BF16)
    once = jnp.where(place[0] == 0, 1.0, 0.0)
    block[...] = jnp.zeros(block.shape, F32)
    block[0:2, :] = sums_attn[0:2, :]
    block[2:3, :] = sums_norm[2:3, :] * once
    block[3:4, :] = sums_ffn[2:3, :] * once
    block[4:6, :] = sums_norm[0:2, :] * once
    block[6:8, :] = sums_ffn[0:2, :] * once

    def up_rows(c):
        for u in range(4):
            half = sums_ffn[3 + u // 2 : 4 + u // 2, (u % 2) * HALF : (u % 2 + 1) * HALF]
            block[8 + u : 9 + u, c * HALF : (c + 1) * HALF] = half

    on_core(place, up_rows)
    folded = jnp.concatenate([block[:12, :HALF], block[:12, HALF:]], axis=0)
    folded = jnp.concatenate([folded, jnp.zeros((SHARD, PIECE[1] - HALF), F32)], axis=1).astype(BF16)
    keep[16] = folded
    send[16] = folded


def grad_tok_body(place, dq, dkv, wq, wkv, same, sib):
    rows = same.shape[1]
    for n, out in enumerate((same, sib)):
        total = dot_nt(dkv[4 * n : 4 * n + 4].reshape(4 * rows, BOTH), wkv[...])
        if n == 0:
            total = total + dot_nt(dq[...].reshape(4 * rows, HEADS), wq[...])
        out[...] = total.astype(BF16).reshape(4, rows, WIDTH)


def added(parts, index):
    total = parts[0][index].astype(F32)
    for part in parts[1:]:
        total = total + part[index].astype(F32)
    return total


def half_up_body(place, keep_a, recv_a, keep_b, recv_b, kept_a, sent_a, kept_b, sent_b):
    for keep, recv, kept, sent in ((keep_a, recv_a, kept_a, sent_a), (keep_b, recv_b, kept_b, sent_b)):
        for n in range(20):
            kept[n] = added((keep, recv), n).astype(BF16)
            sent[n] = added((keep, recv), 20 + n).astype(BF16)


def sum_up_body(place, kept_a, recv_a, kept_b, recv_b, keep, send):
    for n in range(20):
        keep[n] = added((kept_a, recv_a), n).astype(BF16)
        send[n] = added((kept_b, recv_b), n).astype(BF16)


def mid_up_body(place, keep, recv, kept, sent):
    for n in range(10):
        kept[n] = added((keep, recv), n).astype(BF16)
        sent[n] = added((keep, recv), 10 + n).astype(BF16)


def sum_core_body(place, keep, recv, keep_z, send_z):
    total = added((keep, recv), 16).astype(BF16)
    for first, out in enumerate((keep_z, send_z)):
        for n in range(8):
            out[n] = added((keep, recv), (first + 2 * (n // 4)) * 4 + n % 4).astype(BF16)
        out[8] = total


def mid_q_body(place, keep, recv, kept, sent):
    total = added((keep, recv), 8).astype(BF16)
    for out, k in ((kept, 0), (sent, 1)):
        for n in range(4):
            out[n] = added((keep, recv), k * 4 + n).astype(BF16)
        out[4] = total


def sum_q_body(place, own, recv, *outs):
    parts = (own, recv)
    total = added(parts, 4)[:, :HALF].astype(BF16)
    for r, out in enumerate(outs):
        out[:, : PIECE[1]] = added(parts, r).astype(BF16)
        out[:, PIECE[1] :] = total


def last_q_body(place, own, r1, r2, r3, gq, gk, gv, vectors, ups, pieces):
    parts = (own, r1, r2, r3)
    for r, part in enumerate(parts):
        pieces[r] = part[:, : PIECE[1]].astype(F32)
    for j in range(4):
        piece = pieces[place[1] ^ j]
        for n, out in enumerate((gq, gk, gv)):
            out[:, j * HEADS : (j + 1) * HEADS] = piece[:, n * HEADS : (n + 1) * HEADS]
    block = sum(part[:, PIECE[1] :].astype(F32) for part in parts)
    total = jnp.concatenate([block[:12], block[12:]], axis=1)
    dev = place[3]
    high = lax.Precision.HIGHEST
    pick = jnp.where(iota((WIDTH, 128), 0) == dev * SHARD + iota((WIDTH, 128), 1), 1.0, 0.0)
    vectors[...] = jnp.dot(total, pick, precision=high, preferred_element_type=F32)
    lane = lax.rem(dev, 8) * DOWN
    pick_up = jnp.where(iota((WIDTH, 128), 0) == lane + iota((WIDTH, 128), 1), 1.0, 0.0)
    rows = jnp.where(iota(total.shape, 0) == 8 + dev // 8, total, 0.0)
    row = jnp.broadcast_to(jnp.sum(rows, axis=0, keepdims=True), (8, WIDTH))
    ups[...] = jnp.dot(row, pick_up, precision=high, preferred_element_type=F32)


def sum_td_body(place, same, recv, d0, d1, d3, keep_a, send_a, keep_b, send_b):
    rows, half = same.shape[1], keep_a.shape[1]
    for r in range(4):
        tok = (same[r].astype(F32) + recv[r].astype(F32)).astype(BF16)
        own = added((d0, d1, d3), r).astype(BF16)
        (send_a if r % 2 else keep_a)[r // 2] = tok[:half]
        other = send_b if r >= 2 else keep_b
        other[r % 2, : rows - half, :] = tok[half:]
        other[r % 2, rows - half :, :] = own


def mid_td_body(place, keep_a, recv_a, keep_b, recv_b, kept_a, sent_a, kept_b, sent_b):
    kept_a[...] = added((keep_a, recv_a), 0).astype(BF16)
    sent_a[...] = added((keep_a, recv_a), 1).astype(BF16)
    kept_b[...] = added((keep_b, recv_b), 0).astype(BF16)
    sent_b[...] = added((keep_b, recv_b), 1).astype(BF16)


def last_td_body(place, perm, d_hidden, kept_a, recv_a, kept_b, recv_b, out, out_down):
    rows, half = d_hidden.shape[0], kept_a.shape[0]
    whole = slice(None)
    total_a, total_b = added((kept_a, recv_a), whole), added((kept_b, recv_b), whole)
    out_down[...] = total_b[rows - half :]
    total = d_hidden[...] + jnp.concatenate([total_a, total_b[: rows - half]], axis=0)
    high = total.astype(BF16)
    left = total - high.astype(F32)
    middle = left.astype(BF16)
    low = (left - middle.astype(F32)).astype(BF16)
    out[...] = dot_tn(perm[...], high) + dot_tn(perm[...], middle) + dot_tn(perm[...], low)


def sum_last_body(place, u0, u1, keep, send):
    def fill(mine):
        for n in range(5):
            keep[n] = added((u0, u1), mine * 5 + n)
            send[n] = added((u0, u1), (1 - mine) * 5 + n)

    on_core(place, fill)


def last_up_body(place, keep, recv, go, gup):
    def fill(c):
        go[:, c * HALF : (c + 1) * HALF] = keep[0]
        go[:, (1 - c) * HALF : (2 - c) * HALF] = recv[0]
        for u in range(4):
            gup[:, u * WIDTH + c * HALF : u * WIDTH + (c + 1) * HALF] = keep[1 + u]
            gup[:, u * WIDTH + (1 - c) * HALF : u * WIDTH + (2 - c) * HALF] = recv[1 + u]

    on_core(place, fill)


def fast_device(
    tokens,
    table_ids,
    w_query,
    w_key,
    w_value,
    w_out,
    w_up,
    w_down,
    b_query,
    b_value,
    b_out,
    b_up,
    b_down,
    gain_attn,
    shift_attn,
    gain_ffn,
    shift_ffn,
    cotangent,
):
    col, z = lax.axis_index("col"), lax.axis_index("seq")
    place = jnp.stack([col % 2, col // 2, z, col * 4 + z]).astype(jnp.int32)
    rows = tokens.shape[0]
    tables = table_rows(rows, 8)

    def swap(x):
        return lax.ppermute(x, "col", [(i, i ^ 1) for i in range(8)])

    def plane(x, r):
        return lax.ppermute(x, "col", [(i, i ^ (2 * r)) for i in range(8)])

    def shift(x, k):
        return lax.ppermute(x, "seq", [(i, (i + k) % 4) for i in range(4)])

    def planes(x):
        return (x, plane(x, 1), plane(x, 2), plane(x, 3))

    def exchanged(parts):
        return (parts[0],) + tuple(plane(parts[r], r) for r in (1, 2, 3))

    def ring(x):
        one = shift(x, 1)
        two = shift(one, 1)
        return (x, one, two, shift(two, 1))

    def exchange(x, k):
        return lax.ppermute(x, "seq", [(i, i ^ k) for i in range(4)])

    def slabs(count, kind=BF16):
        return ((count,) + SLAB, kind)

    vectors = (b_query, b_value, b_out, b_down, gain_attn, shift_attn, gain_ffn, shift_ffn)
    block = (BLOCK, BF16)
    *q_out, keep_u, send_u, w_down = call(
        pack_body,
        "pack",
        place,
        (w_down, w_query, w_key, w_value, w_out, w_up)
        + tuple(v.reshape(1, SHARD) for v in vectors)
        + (b_up.reshape(1, DOWN),),
        (block,) * 4 + (slabs(5), slabs(5), ((DOWN, WIDTH), BF16)),
        (
            pltpu.VMEM((8, SHARD), F32),
            pltpu.VMEM((4, SHARD, 3 * HEADS), F32),
            pltpu.VMEM(SLAB, F32),
        ),
        limit=FULL_BYTES,
    )
    q_in = exchanged(q_out)
    recv_u = swap(send_u)
    perm, pair, tok_own = call(
        sort_body,
        "sort",
        place,
        (table_ids.reshape(1, rows), tokens, cotangent),
        (((rows, rows), BF16), ((2, rows, WIDTH), BF16), ((rows, WIDTH), BF16)),
        after=(send_u,),
        limit=FULL_BYTES,
    )
    chunk, w_down = call(
        merge_body,
        "merge",
        place,
        (keep_u, recv_u) + q_in,
        ((CHUNK, BF16),),
        (pltpu.VMEM((4,) + PIECE, BF16),),
        after=(tok_own,),
        through=(w_down,),
    )
    column_d, one, tok_own, pair = call(
        pcat_body,
        "pcat",
        place,
        planes(w_down),
        (((4, DOWN, WIDTH), BF16),),
        through=(shift(chunk, 1), tok_own, pair),
    )
    two, tok_x, tok_y, pair_sib, column_d = call(
        gate_body,
        "gate",
        place,
        (),
        (),
        through=(shift(one, 1), plane(tok_own, 1), plane(tok_own, 2), swap(pair), column_d),
    )
    tok_parts = (tok_own, tok_x, tok_y, plane(tok_x, 2))
    plane_u, plane_q, three, column_d = call(
        zcat_body,
        "zcat",
        place,
        (chunk, one, two, shift(two, 1)) + tok_parts[1:],
        (slabs(40), ((17,) + PIECE, BF16), ((3, rows, WIDTH), BF16)),
        through=(column_d,),
    )
    three_sib = swap(three)
    other_q = swap(plane_q)
    u_x, u_y = plane(plane_u, 1), plane(plane_u, 2)
    d_one = shift(column_d, 1)

    heads = ((4, rows, HEADS), BF16)
    heads_all = ((8, rows, HEADS), BF16)
    piece = ((rows, HEADS), BF16)
    wq, wkv, bias, tok, q3, k3, v3, mixed3, *mixed_low, lse = call(
        functools.partial(attend_body, tables),
        "attend",
        place,
        tok_parts + (pair_sib, three_sib, plane_q, other_q),
        (
            ((WIDTH, HEADS), BF16),
            ((WIDTH, BOTH), BF16),
            ((16, WIDTH), F32),
            ((8, rows, WIDTH), BF16),
            heads,
            heads_all,
            heads_all,
            ((4, rows, HEADS), F32),
            piece,
            piece,
            piece,
            piece,
            ((4, rows, 128), F32),
        ),
        (pltpu.VMEM((WIDTH, PIECE[1]), F32),),
        after=(plane_u,),
    )
    half_x, half_y, d_one = call(
        ucut_body, "ucut", place, (u_x, u_y), (slabs(20), slabs(20)), after=(lse,), through=(d_one,)
    )
    d_two = shift(d_one, 1)
    wo_mine, wup, column_d, *mixed_low = call(
        asm_u_body,
        "asm_u",
        place,
        (plane_u, u_x, u_y, plane(half_x, 2), plane(half_y, 1)),
        (((WIDTH, HALF), BF16), ((WIDTH, 4 * HALF), BF16)),
        (pltpu.VMEM((WIDTH, HALF), F32),),
        after=(half_x,),
        through=(column_d,) + tuple(mixed_low),
    )
    d_parts = (column_d, d_one, d_two, shift(column_d, 3))
    (mixed_own,) = call(
        mcat_body,
        "mcat",
        place,
        exchanged(mixed_low),
        (((rows, WIDTH), BF16),),
        (pltpu.VMEM((4, rows, HEADS), BF16),),
        after=(d_two,),
    )
    whole_pair = ((2, rows, WIDTH), BF16)
    full = (2 * rows, WIDTH)
    wide = ((2 * rows, 4 * HALF), BF16)
    vhat, scale, normed_low, active, slope, mixed, wo = call(
        forward_body,
        "forward",
        place,
        (pair, pair_sib, mixed_own, swap(mixed_own), wo_mine, swap(wo_mine), bias, wup),
        (
            (full, F32),
            ((2 * rows, 128), F32),
            (full, BF16),
            wide,
            wide,
            (full, BF16),
            ((WIDTH, WIDTH), BF16),
        ),
        (pltpu.VMEM(full, F32), pltpu.VMEM(wide[0], F32), pltpu.VMEM((1, 4 * HALF), F32)),
    )
    partial, wdown = call(
        down_body, "down", place, (active,) + d_parts, (whole_pair, ((16, DOWN, WIDTH), BF16))
    )
    layer_out, d_summed, d_down, d_upper, d_part, sums_ffn = call(
        back_ffn_body,
        "back_ffn",
        place,
        (perm, partial, swap(partial), vhat, bias, pair, pair_sib, slope, wup, wdown),
        (((rows, WIDTH), BF16), (full, F32), (full, BF16), wide, whole_pair, ((8, WIDTH), F32)),
    )
    d_part_other = swap(d_part)
    column = ((4, DOWN, WIDTH), BF16)
    g_down = call(
        grad_down_body,
        "grad_down",
        place,
        (active, d_down),
        (column,) * 4,
        (pltpu.VMEM((4 * HALF, WIDTH), F32),),
    )
    down_two, down_three = shift(g_down[2], 1), shift(g_down[1], 3)
    d_hidden, d_branch, *d_mixed, sums_norm = call(
        back_norm_body,
        "back_norm",
        place,
        (d_summed, d_part, d_part_other, vhat, scale, bias, wo),
        (((rows, WIDTH), F32), (full, BF16), piece, piece, piece, piece, ((8, WIDTH), F32)),
        after=(g_down[2],),
    )
    d_mixed = exchanged(d_mixed)
    g_up = call(
        grad_up_body,
        "grad_up",
        place,
        (normed_low, d_upper, mixed, d_branch),
        (slabs(40),) * 4,
        (pltpu.VMEM((WIDTH, HALF), F32), pltpu.VMEM((WIDTH, 4 * HALF), F32)),
    )
    up_a, up_b = plane(g_up[1], 1), plane(g_up[3], 2)
    dq, dkv, sums_attn = call(
        functools.partial(back_attend_body, tables),
        "back_attend",
        place,
        d_mixed + (mixed3, q3, k3, v3, lse),
        (heads, ((8, rows, BOTH), BF16), ((8, WIDTH), F32)),
        (pltpu.VMEM((4, rows, HEADS), BF16),),
        after=(g_up[1],),
    )
    keep_q, send_q = call(
        grad_qkv_body,
        "grad_qkv",
        place,
        (tok, dq, dkv, sums_ffn, sums_norm, sums_attn),
        (((17,) + PIECE, BF16),) * 2,
        (pltpu.VMEM((WIDTH, PIECE[1]), F32), pltpu.VMEM((16, WIDTH), F32)),
    )
    recv_q = swap(send_q)
    quad = ((4, rows, WIDTH), BF16)
    same, sib = call(
        grad_tok_body, "grad_tok", place, (dq, dkv, wq, wkv), (quad, quad), after=(send_q,)
    )
    (down_src,) = call(
        ring_down_body, "ring_down", place, (down_two, g_down[3]), (column,), after=(sib,)
    )
    sib = swap(sib)
    down_one = shift(down_src, 1)
    kept_a, sent_a, kept_b, sent_b = call(
        half_up_body,
        "half_up",
        place,
        (g_up[0], up_a, g_up[2], up_b),
        (slabs(20),) * 4,
        after=(down_src,),
    )
    up_a, up_b = plane(sent_a, 2), plane(sent_b, 1)
    two_q = ((9,) + PIECE, BF16)
    keep_z, send_z = call(
        sum_core_body, "sum_core", place, (keep_q, recv_q), (two_q,) * 2, after=(sent_a,)
    )
    recv_z = exchange(send_z, 1)
    keep_up, send_up = call(
        sum_up_body,
        "sum_up",
        place,
        (kept_a, up_a, kept_b, up_b),
        (slabs(20), slabs(20)),
        after=(send_z,),
    )
    recv_up = exchange(send_up, 1)
    one_q = ((5,) + PIECE, BF16)
    half = ((rows + DOWN) // 2, WIDTH)
    two = ((2,) + half, BF16)
    keep_a, send_a, keep_b, send_b = call(
        sum_td_body, "sum_td", place, (same, sib, g_down[0], down_one, down_three), (two,) * 4, after=(send_up,)
    )
    recv_a, recv_b = plane(send_a, 1), plane(send_b, 2)
    kept_z, sent_z = call(
        mid_q_body, "mid_q", place, (keep_z, recv_z), (one_q,) * 2, after=(send_a,)
    )
    z_q = (kept_z, exchange(sent_z, 2))
    kept_a, sent_a, kept_b, sent_b = call(
        mid_td_body, "mid_td", place, (keep_a, recv_a, keep_b, recv_b), ((half, BF16),) * 4, after=(sent_z,)
    )
    recv_a, recv_b = plane(sent_a, 2), plane(sent_b, 1)
    kept_up, sent_up = call(
        mid_up_body, "mid_up", place, (keep_up, recv_up), (slabs(10), slabs(10)), after=(sent_a,)
    )
    recv_up = exchange(sent_up, 2)
    p_q = call(sum_q_body, "sum_q", place, z_q, (block,) * 4, after=(sent_up,))
    row = ((SHARD, WIDTH), F32)
    gq, gk, gv, small, ups = call(
        last_q_body,
        "last_q",
        place,
        exchanged(p_q),
        (row, row, row, ((12, 128), F32), ((8, 128), F32)),
        (pltpu.VMEM((4,) + PIECE, F32),),
    )
    kept, sent = call(
        sum_last_body, "sum_last", place, (kept_up, recv_up), (slabs(5, F32), slabs(5, F32))
    )
    grad_tokens, grad_down = call(
        last_td_body,
        "last_td",
        place,
        (perm, d_hidden, kept_a, recv_a, kept_b, recv_b),
        (((rows, WIDTH), F32), ((DOWN, WIDTH), F32)),
        after=(sent,),
    )
    go, gup = call(
        last_up_body, "last_up", place, (kept, swap(sent)), (row, ((SHARD, 4 * WIDTH), F32)), after=(grad_down,), limit=FULL_BYTES
    )
    small = small[:, :SHARD]
    return (
        layer_out,
        grad_tokens,
        gq,
        gk,
        gv,
        go,
        gup,
        grad_down,
        small[0],
        small[1],
        small[2],
        ups[0, :DOWN],
        small[3],
        small[4],
        small[5],
        small[6],
        small[7],
    )


def solution(mesh):
    placed = (
        P(("col", "seq"), None),
        P(("col", "seq")),
        P(("col", "seq"), None),
        P(("col", "seq"), None),
        P(("col", "seq"), None),
        P(("col", "seq"), None),
        P(("col", "seq"), None),
        P(("col", "seq"), None),
        P(("col", "seq")),
        P(("col", "seq")),
        P(("col", "seq")),
        P(("col", "seq")),
        P(("col", "seq")),
        P(("col", "seq")),
        P(("col", "seq")),
        P(("col", "seq")),
        P(("col", "seq")),
        P(("col", "seq"), None),
    )
    fast = mesh.shape["col"] == 8 and mesh.shape["seq"] == 4
    return jax.shard_map(
        fast_device if fast else per_device,
        mesh=mesh,
        in_specs=placed,
        out_specs=(
            P(("col", "seq"), None),
            P(("col", "seq"), None),
            P(("col", "seq"), None),
            P(("col", "seq"), None),
            P(("col", "seq"), None),
            P(("col", "seq"), None),
            P(("col", "seq"), None),
            P(("col", "seq"), None),
            P(("col", "seq")),
            P(("col", "seq")),
            P(("col", "seq")),
            P(("col", "seq")),
            P(("col", "seq")),
            P(("col", "seq")),
            P(("col", "seq")),
            P(("col", "seq")),
            P(("col", "seq")),
        ),
        check_vma=False,
    )
```

```python
import functools

import jax
import jax.numpy as jnp
import numpy as np
from jax import lax
from jax.experimental import pallas as pl
from jax.experimental.pallas import tpu as pltpu
from jax.sharding import PartitionSpec as P

H = 12
HD = 64


NEG_BIG = -1e30
NORM_EPS = 1e-12
LOW_TYPE = jnp.bfloat16
FULL_TYPE = jnp.float32


def block_length(unit_rows):
    target = unit_rows * max(1, -(-512 // unit_rows))
    return target


def layer_norm(values, gain, shift):
    center = values - jnp.mean(values, axis=-1, keepdims=True)
    spread = jnp.mean(center * center, axis=-1, keepdims=True)
    return center * lax.rsqrt(spread + NORM_EPS) * gain + shift


def gelu_exact(values):
    return jax.nn.gelu(values, approximate=False)


def project(left, right, bias):
    return jnp.dot(left, right, preferred_element_type=FULL_TYPE) + bias.astype(FULL_TYPE)


def attend(running, query_heads, query_ids, key_slab, value_slab, key_ids):
    maxima, totals, weighted = running
    scores = (
        jnp.einsum("thd,shd->hts", query_heads, key_slab, preferred_element_type=FULL_TYPE) * 0.125
    )
    visible = (query_ids[:, None] == key_ids[None, :])[None]
    scores = jnp.where(visible, scores, NEG_BIG)
    new_max = jnp.maximum(maxima, jnp.max(scores, axis=2))
    rescale = jnp.exp(maxima - new_max)
    exponents = jnp.where(visible, jnp.exp(scores - new_max[:, :, None]), 0.0)
    totals = totals * rescale + jnp.sum(exponents, axis=2)
    weighted = weighted * rescale[:, :, None] + jnp.einsum(
        "hts,shd->htd", exponents.astype(LOW_TYPE), value_slab, preferred_element_type=FULL_TYPE
    )
    return (new_max, totals, weighted)


def grad_block(
    query_heads, dout_heads, log_totals, row_delta, query_ids, key_slab, value_slab, key_ids
):
    scores = (
        jnp.einsum("thd,shd->hts", query_heads, key_slab, preferred_element_type=FULL_TYPE) * 0.125
    )
    visible = (query_ids[:, None] == key_ids[None, :])[None]
    probabilities = jnp.where(visible, jnp.exp(scores - log_totals[:, :, None]), 0.0)
    grad_value = jnp.einsum(
        "hts,thd->shd", probabilities.astype(LOW_TYPE), dout_heads, preferred_element_type=FULL_TYPE
    )
    grad_probs = jnp.einsum(
        "thd,shd->hts", dout_heads, value_slab, preferred_element_type=FULL_TYPE
    )
    grad_scores = (probabilities * (grad_probs - row_delta[:, :, None])).astype(LOW_TYPE)
    grad_query = (
        jnp.einsum("hts,shd->thd", grad_scores, key_slab, preferred_element_type=FULL_TYPE) * 0.125
    )
    grad_key = (
        jnp.einsum("hts,thd->shd", grad_scores, query_heads, preferred_element_type=FULL_TYPE)
        * 0.125
    )
    return (grad_query, grad_key, grad_value)


def per_device(
    tokens,
    table_ids,
    w_query,
    w_key,
    w_value,
    w_out,
    w_up,
    w_down,
    b_query,
    b_value,
    b_out,
    b_up,
    b_down,
    gain_attn,
    shift_attn,
    gain_ffn,
    shift_ffn,
    cotangent,
):
    shards = (
        w_query,
        w_key,
        w_value,
        w_out,
        w_up,
        w_down,
        b_query,
        b_value,
        b_out,
        b_up,
        b_down,
        gain_attn,
        shift_attn,
        gain_ffn,
        shift_ffn,
    )
    gathered = (
        lax.all_gather(shards[0], ("col", "seq"), axis=0, tiled=True),
        lax.all_gather(shards[1], ("col", "seq"), axis=0, tiled=True),
        lax.all_gather(shards[2], ("col", "seq"), axis=0, tiled=True),
        lax.all_gather(shards[3], ("col", "seq"), axis=0, tiled=True),
        lax.all_gather(shards[4], ("col", "seq"), axis=0, tiled=True),
        lax.all_gather(shards[5], ("col", "seq"), axis=0, tiled=True),
        lax.all_gather(shards[6], ("col", "seq"), axis=0, tiled=True),
        lax.all_gather(shards[7], ("col", "seq"), axis=0, tiled=True),
        lax.all_gather(shards[8], ("col", "seq"), axis=0, tiled=True),
        lax.all_gather(shards[9], ("col", "seq"), axis=0, tiled=True),
        lax.all_gather(shards[10], ("col", "seq"), axis=0, tiled=True),
        lax.all_gather(shards[11], ("col", "seq"), axis=0, tiled=True),
        lax.all_gather(shards[12], ("col", "seq"), axis=0, tiled=True),
        lax.all_gather(shards[13], ("col", "seq"), axis=0, tiled=True),
        lax.all_gather(shards[14], ("col", "seq"), axis=0, tiled=True),
    )
    query_mat, key_mat, value_mat, out_mat, up_mat, down_mat = (
        gathered[0],
        gathered[1],
        gathered[2],
        gathered[3],
        gathered[4],
        gathered[5],
    )
    query_bias, value_bias, out_bias, up_bias, down_bias = (
        gathered[6],
        gathered[7],
        gathered[8],
        gathered[9],
        gathered[10],
    )
    attn_gain, attn_shift, ffn_gain, ffn_shift = (
        gathered[11],
        gathered[12],
        gathered[13],
        gathered[14],
    )
    tok_rows = tokens.shape[0]
    ids_all = lax.all_gather(table_ids, "col", axis=0, tiled=True)
    inputs = tokens.astype(FULL_TYPE)
    queries = project(tokens, query_mat, query_bias).astype(LOW_TYPE)
    keys = jnp.dot(tokens, key_mat, preferred_element_type=FULL_TYPE).astype(LOW_TYPE)
    values = project(tokens, value_mat, value_bias).astype(LOW_TYPE)
    query_heads = queries.reshape(tok_rows, H, HD)
    starting = (
        jnp.full((H, tok_rows), NEG_BIG, FULL_TYPE),
        jnp.zeros((H, tok_rows), FULL_TYPE),
        jnp.zeros((H, tok_rows, HD), FULL_TYPE),
    )
    running = starting
    key_rows = lax.all_gather(keys, "col", axis=0, tiled=True)
    value_rows = lax.all_gather(values, "col", axis=0, tiled=True)
    row_count = key_rows.shape[0]
    length = block_length(tok_rows)
    blocks = row_count // length

    def advance(current, pieces):
        return (attend(current, query_heads, table_ids, pieces[0], pieces[1], pieces[2]), None)

    running, _ = lax.scan(
        advance,
        running,
        (
            key_rows.reshape(blocks, length, H, HD),
            value_rows.reshape(blocks, length, H, HD),
            ids_all.reshape(blocks, length),
        ),
    )
    maxima, totals, weighted = running
    attn_heads = weighted / totals[:, :, None]
    log_totals = maxima + jnp.log(totals)
    attn_low = attn_heads.transpose(1, 0, 2).reshape(tok_rows, H * HD).astype(LOW_TYPE)
    hidden = inputs + project(attn_low, out_mat, out_bias)
    normed, norm_first = jax.vjp(
        layer_norm, hidden, attn_gain.astype(FULL_TYPE), attn_shift.astype(FULL_TYPE)
    )
    normed_low = normed.astype(LOW_TYPE)
    upper = project(normed_low, up_mat, up_bias)
    active, gelu_back = jax.vjp(gelu_exact, upper)
    active_low = active.astype(LOW_TYPE)
    summed = normed + project(active_low, down_mat, down_bias)
    result, norm_second = jax.vjp(
        layer_norm, summed, ffn_gain.astype(FULL_TYPE), ffn_shift.astype(FULL_TYPE)
    )
    again = (
        lax.all_gather(w_query, ("col", "seq"), axis=0, tiled=True),
        lax.all_gather(w_key, ("col", "seq"), axis=0, tiled=True),
        lax.all_gather(w_value, ("col", "seq"), axis=0, tiled=True),
        lax.all_gather(w_out, ("col", "seq"), axis=0, tiled=True),
        lax.all_gather(w_up, ("col", "seq"), axis=0, tiled=True),
        lax.all_gather(w_down, ("col", "seq"), axis=0, tiled=True),
    )
    query_mat, key_mat, value_mat, out_mat, up_mat, down_mat = (
        again[0],
        again[1],
        again[2],
        again[3],
        again[4],
        again[5],
    )
    d_summed, d_ffn_gain, d_ffn_shift = norm_second(cotangent.astype(FULL_TYPE))
    d_down = d_summed.astype(LOW_TYPE)
    grad_down = jnp.einsum("tf,td->fd", active_low, d_down, preferred_element_type=FULL_TYPE)
    d_active = jnp.einsum("td,fd->tf", d_down, down_mat, preferred_element_type=FULL_TYPE)
    d_upper = gelu_back(d_active)[0].astype(LOW_TYPE)
    grad_up = jnp.einsum("td,tf->df", normed_low, d_upper, preferred_element_type=FULL_TYPE)
    d_normed = d_summed + jnp.einsum("tf,df->td", d_upper, up_mat, preferred_element_type=FULL_TYPE)
    d_hidden, d_attn_gain, d_attn_shift = norm_first(d_normed)
    d_branch = d_hidden.astype(LOW_TYPE)
    grad_out = jnp.einsum("tc,td->cd", attn_low, d_branch, preferred_element_type=FULL_TYPE)
    d_attn = jnp.einsum("td,cd->tc", d_branch, out_mat, preferred_element_type=FULL_TYPE).astype(
        LOW_TYPE
    )
    dout_heads = d_attn.reshape(tok_rows, H, HD)
    row_delta = jnp.einsum("thd,htd->ht", dout_heads.astype(FULL_TYPE), attn_heads)
    key_all, value_all = (
        lax.all_gather(keys, "col", axis=0, tiled=True),
        lax.all_gather(values, "col", axis=0, tiled=True),
    )
    total_rows = key_all.shape[0]
    length = block_length(tok_rows)
    blocks = total_rows // length

    def key_pass(grad_sum, pieces):
        grad_query_part, grad_key_part, grad_value_part = grad_block(
            query_heads,
            dout_heads,
            log_totals,
            row_delta,
            table_ids,
            pieces[0],
            pieces[1],
            pieces[2],
        )
        return (grad_sum + grad_query_part, (grad_key_part, grad_value_part))

    query_sum, (key_parts, value_parts) = lax.scan(
        key_pass,
        jnp.zeros((tok_rows, H, HD), FULL_TYPE),
        (
            key_all.reshape(blocks, length, H, HD),
            value_all.reshape(blocks, length, H, HD),
            ids_all.reshape(blocks, length),
        ),
    )
    key_sum, value_sum = (
        lax.psum_scatter(
            key_parts.reshape(total_rows, H * HD).astype(jnp.bfloat16),
            "col",
            scatter_dimension=0,
            tiled=True,
        ).astype(jnp.float32),
        lax.psum_scatter(
            value_parts.reshape(total_rows, H * HD).astype(jnp.bfloat16),
            "col",
            scatter_dimension=0,
            tiled=True,
        ).astype(jnp.float32),
    )
    query_sum = query_sum.reshape(tok_rows, H * HD)
    query_low = query_sum.astype(LOW_TYPE)
    key_low = key_sum.astype(LOW_TYPE)
    value_low = value_sum.astype(LOW_TYPE)
    grad_query = jnp.einsum("tc,td->cd", tokens, query_low, preferred_element_type=FULL_TYPE)
    grad_key = jnp.einsum("tc,td->cd", tokens, key_low, preferred_element_type=FULL_TYPE)
    grad_value = jnp.einsum("tc,td->cd", tokens, value_low, preferred_element_type=FULL_TYPE)
    d_tokens = d_hidden + jnp.einsum(
        "td,cd->tc", query_low, query_mat, preferred_element_type=FULL_TYPE
    )
    d_tokens = d_tokens + jnp.einsum(
        "td,cd->tc", key_low, key_mat, preferred_element_type=FULL_TYPE
    )
    d_tokens = d_tokens + jnp.einsum(
        "td,cd->tc", value_low, value_mat, preferred_element_type=FULL_TYPE
    )
    sums_local = (
        grad_query,
        grad_key,
        grad_value,
        grad_out,
        grad_up,
        grad_down,
        jnp.sum(query_low.astype(FULL_TYPE), axis=0),
        jnp.sum(value_low.astype(FULL_TYPE), axis=0),
        jnp.sum(d_branch.astype(FULL_TYPE), axis=0),
        jnp.sum(d_upper.astype(FULL_TYPE), axis=0),
        jnp.sum(d_down.astype(FULL_TYPE), axis=0),
        d_attn_gain,
        d_attn_shift,
        d_ffn_gain,
        d_ffn_shift,
    )
    owned = (
        lax.psum_scatter(sums_local[0], ("col", "seq"), scatter_dimension=0, tiled=True),
        lax.psum_scatter(sums_local[1], ("col", "seq"), scatter_dimension=0, tiled=True),
        lax.psum_scatter(sums_local[2], ("col", "seq"), scatter_dimension=0, tiled=True),
        lax.psum_scatter(sums_local[3], ("col", "seq"), scatter_dimension=0, tiled=True),
        lax.psum_scatter(sums_local[4], ("col", "seq"), scatter_dimension=0, tiled=True),
        lax.psum_scatter(sums_local[5], ("col", "seq"), scatter_dimension=0, tiled=True),
        lax.psum_scatter(sums_local[6], ("col", "seq"), scatter_dimension=0, tiled=True),
        lax.psum_scatter(sums_local[7], ("col", "seq"), scatter_dimension=0, tiled=True),
        lax.psum_scatter(sums_local[8], ("col", "seq"), scatter_dimension=0, tiled=True),
        lax.psum_scatter(sums_local[9], ("col", "seq"), scatter_dimension=0, tiled=True),
        lax.psum_scatter(sums_local[10], ("col", "seq"), scatter_dimension=0, tiled=True),
        lax.psum_scatter(sums_local[11], ("col", "seq"), scatter_dimension=0, tiled=True),
        lax.psum_scatter(sums_local[12], ("col", "seq"), scatter_dimension=0, tiled=True),
        lax.psum_scatter(sums_local[13], ("col", "seq"), scatter_dimension=0, tiled=True),
        lax.psum_scatter(sums_local[14], ("col", "seq"), scatter_dimension=0, tiled=True),
    )
    return (result.astype(LOW_TYPE), d_tokens) + tuple(owned)


WIDTH = 768
HALF = WIDTH // 2
SHARD = 24
DOWN = 96
SLAB = (SHARD, HALF)
HEADS = 192
PIECE = (SHARD, 640)
BLOCK = (SHARD, 1024)
START_Q = 10 * HALF
CHUNK = (SHARD, START_Q + 5 * PIECE[1])
KEYS = slice(0, 192)
VALUES = slice(256, 448)
BOTH = 512
UNITS = ((slice(0, 128), 2), (slice(128, 192), 1))
VMEM_BYTES = 30 * 2**20
FULL_BYTES = 60 * 2**20
F32 = jnp.float32
BF16 = jnp.bfloat16


COST_SCALE = 10.0
COST = {
    "attend": 11.7,
    "asm_u": 2.5,
    "forward": 5.5,
    "down": 2.0,
    "back_ffn": 5.5,
    "grad_down": 2.2,
    "grad_up": 2.4,
    "back_attend": 11.7,
    "grad_qkvo": 5.2,
    "grad_tok": 4.3,
}


def dot(left, right):
    return jnp.dot(left, right, preferred_element_type=F32)


def dot_nt(left, right):
    return lax.dot_general(left, right, (((1,), (1,)), ((), ())), preferred_element_type=F32)


def dot_tn(left, right):
    return lax.dot_general(left, right, (((0,), (0,)), ((), ())), preferred_element_type=F32)


def call(body, name, place, inputs, outs, scratch=(), after=(), through=(), limit=VMEM_BYTES):
    vmem = pl.BlockSpec(memory_space=pltpu.VMEM)
    any_place = pl.BlockSpec(memory_space=pl.ANY)
    count = 1 + len(inputs)
    skipped = count + len(after) + len(through)

    def run(*refs):
        own = skipped + len(outs)
        body(*refs[:count], *refs[skipped:own], *refs[own + len(through) :])

    return pl.pallas_call(
        run,
        name=name,
        out_shape=tuple(jax.ShapeDtypeStruct(s, t) for s, t in outs)
        + tuple(jax.ShapeDtypeStruct(a.shape, a.dtype) for a in through),
        in_specs=[pl.BlockSpec(memory_space=pltpu.SMEM)] + [vmem] * len(inputs) + [any_place] * (len(after) + len(through)),
        out_specs=tuple(vmem for _ in outs) + tuple(any_place for _ in through),
        input_output_aliases={count + len(after) + n: len(outs) + n for n in range(len(through))},
        scratch_shapes=list(scratch),
        compiler_params=pltpu.CompilerParams(vmem_limit_bytes=limit),
        cost_estimate=pl.CostEstimate(
            flops=int(1.15e9 * COST_SCALE * COST.get(name, 1.3)), bytes_accessed=0, transcendentals=0
        ),
    )(place, *inputs, *after, *through)


def iota(shape, dim):
    return lax.broadcasted_iota(jnp.int32, shape, dim)


def sort_body(place, ids, tokens, cot, perm_out, pair_out, tok_out):
    rows = tokens.shape[0]
    id_j = jnp.broadcast_to(ids[...].astype(F32), (rows, rows))
    id_i = id_j.T
    same = jnp.where(id_i == id_j, 1.0, 0.0)
    count_i = jnp.sum(same, axis=1, keepdims=True)
    count_j = jnp.sum(same, axis=0, keepdims=True)
    i, j = iota((rows, rows), 0), iota((rows, rows), 1)
    equal = jnp.where((id_i == id_j) & (i < j), 1.0, 0.0)
    tie = jnp.where((count_i == count_j) & (id_i < id_j), 1.0, 0.0)
    larger = jnp.where(count_i > count_j, 1.0, 0.0)
    position = jnp.sum(equal + tie + larger, axis=0, keepdims=True)
    perm = jnp.where(i.astype(F32) == position, 1.0, 0.0).astype(BF16)
    perm_out[...] = perm
    tok = dot(perm, tokens[...]).astype(BF16)
    pair_out[0] = tok
    pair_out[1] = dot(perm, cot[...]).astype(BF16)
    tok_out[...] = tok


def fold(block):
    return jnp.concatenate([block[:, :HALF], block[:, HALF:]], axis=0)


def pack_body(place, w_down, wq, wk, wv, wo, wup, *rest):
    vectors, b_up = rest[:8], rest[8]
    parts, (keep, send, down_out) = rest[9:13], rest[13:16]
    rows8, pieces, block = rest[16:]
    down_out[...] = w_down[...]
    dev = place[3]

    def split(mine):
        other = 1 - mine
        keep[0] = wo[:, mine * HALF : (mine + 1) * HALF]
        send[0] = wo[:, other * HALF : (other + 1) * HALF]
        for u in range(4):
            keep[1 + u] = wup[:, u * WIDTH + mine * HALF : u * WIDTH + (mine + 1) * HALF]
            send[1 + u] = wup[:, u * WIDTH + other * HALF : u * WIDTH + (other + 1) * HALF]

    on_core(place, split)
    for n, vector in enumerate(vectors):
        rows8[n : n + 1, :] = vector[...].astype(F32)
    spread = jnp.where(iota((SHARD, WIDTH), 1) == dev * SHARD + iota((SHARD, WIDTH), 0), 1.0, 0.0)
    eight = dot(rows8[...].astype(BF16), spread.astype(BF16))
    lane = lax.rem(dev, 8) * DOWN
    spread_up = jnp.where(iota((DOWN, WIDTH), 1) == lane + iota((DOWN, WIDTH), 0), 1.0, 0.0)
    one = dot(jnp.broadcast_to(b_up[...], (8, DOWN)), spread_up.astype(BF16))
    one = jnp.where(iota((8, WIDTH), 0) == dev // 8, one, 0.0)
    for n in range(2):
        lanes = slice(n * HALF, (n + 1) * HALF)
        block[n * 12 : n * 12 + 8, :] = eight[:, lanes]
        block[n * 12 + 8 : n * 12 + 12, :] = one[:4, lanes]
    for j in range(4):
        for n, w in enumerate((wq, wk, wv)):
            pieces[j, :, n * HEADS : (n + 1) * HEADS] = w[:, j * HEADS : (j + 1) * HEADS].astype(F32)
    for r, part in enumerate(parts):
        part[:, : 3 * HEADS] = pieces[place[1] ^ r].astype(BF16)
        part[:, 3 * HEADS : PIECE[1]] = jnp.zeros((SHARD, PIECE[1] - 3 * HEADS), BF16)
        part[:, PIECE[1] :] = block[...].astype(BF16)


def merge_body(place, keep, recv, q0, q1, q2, q3, chunk, slots):
    parts = (q0, q1, q2, q3)
    for r, part in enumerate(parts):
        slots[place[1] ^ r] = part[:, : PIECE[1]]
    for n in range(4):
        chunk[:, START_Q + n * PIECE[1] : START_Q + (n + 1) * PIECE[1]] = slots[n]
    total = sum(part[:, PIECE[1] :].astype(F32) for part in parts)
    total = jnp.concatenate([total, jnp.zeros((SHARD, PIECE[1] - HALF), F32)], axis=1)
    chunk[:, START_Q + 4 * PIECE[1] :] = total.astype(BF16)

    def fill(mine):
        even, odd = (keep, recv) if mine == 0 else (recv, keep)
        for n in range(5):
            chunk[:, n * HALF : (n + 1) * HALF] = even[n]
            chunk[:, (5 + n) * HALF : (6 + n) * HALF] = odd[n]

    on_core(place, fill)


def z_slot(place, k):
    return lax.rem(place[2] + 4 - k, 4)


def zcat_q_body(place, own, r1, r2, r3, out):
    parts = (own, r1, r2, r3)
    for k, part in enumerate(parts):
        slot = z_slot(place, k) * 4
        for n in range(4):
            out[slot + n] = part[n]
    out[16] = sum(part[4].astype(F32) for part in parts).astype(BF16)


def gate_body(place):
    pass


def zcat_body(place, own, r1, r2, r3, t1, t2, t3, plane_u, plane_q, three):
    parts = (own, r1, r2, r3)
    for k, part in enumerate(parts):
        slot = z_slot(place, k)
        for n in range(10):
            plane_u[slot * 10 + n] = part[:, n * HALF : (n + 1) * HALF]
        for n in range(4):
            plane_q[slot * 4 + n] = part[:, START_Q + n * PIECE[1] : START_Q + (n + 1) * PIECE[1]]
    plane_q[16] = sum(part[:, START_Q + 4 * PIECE[1] :].astype(F32) for part in parts).astype(BF16)
    for r, part in enumerate((t1, t2, t3)):
        three[r] = part[...]


def pcat_body(place, own, r1, r2, r3, column):
    for r, part in enumerate((own, r1, r2, r3)):
        column[place[1] ^ r] = part[...]


def ucut_body(place, from_x, from_y, half_x, half_y):
    half_x[...] = from_x[:20]
    half_y[...] = from_y[20:]


def asm_u_body(place, own, from_x, from_y, low, high, wo, wup, slab):
    parts = (own, from_x, from_y, (low, high))
    natural(place, parts, slab, 0, 5)
    wo[...] = slab[...].astype(BF16)
    for u in range(4):
        natural(place, parts, slab, 1 + u, 5)
        wup[:, u * HALF : (u + 1) * HALF] = slab[...].astype(BF16)


def natural(place, parts, scr, n, count):
    for r, part in enumerate(parts):
        base = (place[1] ^ r) * (8 * SHARD)
        for z in range(4):
            for c in range(2):
                row = pl.multiple_of(base + c * 4 * SHARD + z * SHARD, 8)
                source, index = part, (z * 2 + c) * count + n
                if isinstance(part, tuple):
                    source, index = part[z // 2], index - (z // 2) * 4 * count
                scr[pl.ds(row, SHARD), :] = source[index].astype(F32)


def on_core(place, action):
    @pl.when(place[0] == 0)
    def _():
        action(0)

    @pl.when(place[0] == 1)
    def _():
        action(1)


def table_rows(tok_rows, n_col):
    long_rows = max(2 * 512, 64 * n_col) // n_col
    short_rows = 512 // n_col
    units = tok_rows // short_rows
    long_count = max(1, units // (2 * (long_rows // short_rows)))
    tables, start = [], 0
    for _ in range(long_count):
        tables.append((start, long_rows))
        start += long_rows
    while start < tok_rows:
        tables.append((start, short_rows))
        start += short_rows
    return tables


def attend_body(tables, place, *refs):
    same, pair_sib, three_sib, mine_q, other_q = refs[:4], refs[4], refs[5], refs[6], refs[7]
    wq, wkv, bias, tok, q3, k3, v3, mixed_out = refs[8:16]
    mixed_low, lse_out, slab = refs[16:20], refs[20], refs[21]
    rows = tok.shape[1]

    def gather(mine):
        for c in range(2):
            source = mine_q if c == mine else other_q
            for z in range(4):
                for j in range(4):
                    row = j * 8 * SHARD + c * 4 * SHARD + z * SHARD
                    slab[row : row + SHARD, :] = source[z * 4 + j].astype(F32)

    on_core(place, gather)
    wq[...] = slab[:, :HEADS].astype(BF16)
    wkv[...] = jnp.zeros(wkv.shape, BF16)
    wkv[:, KEYS] = slab[:, HEADS : 2 * HEADS].astype(BF16)
    wkv[:, VALUES] = slab[:, 2 * HEADS : 3 * HEADS].astype(BF16)
    total = mine_q[16][:, :HALF].astype(F32) + other_q[16][:, :HALF].astype(F32)
    bias[:12, :HALF] = total[:12]
    bias[:12, HALF:] = total[12:]
    bias[12:, :] = jnp.zeros((4, WIDTH), F32)

    def own_columns(row):
        found = jnp.zeros((1, HEADS), F32)
        for j in range(4):
            part = bias[row : row + 1, j * HEADS : (j + 1) * HEADS]
            found = found + jnp.where(place[1] == j, part, 0.0)
        return found

    for n, part in enumerate(same):
        tok[n] = part[...]
        tok[4 + n] = pair_sib[0] if n == 0 else three_sib[n - 1]
    every = tok[...].reshape(8 * rows, WIDTH)
    both = dot(every, wkv[...])
    k3[...] = both[:, KEYS].astype(BF16).reshape(8, rows, HEADS)
    v3[...] = (both[:, VALUES] + own_columns(1)).astype(BF16).reshape(8, rows, HEADS)
    queries = dot(tok[:4].reshape(4 * rows, WIDTH), wq[...]) + own_columns(0)
    q3[...] = queries.astype(BF16).reshape(4, rows, HEADS)
    for start, size in tables:
        lse = jnp.zeros((4 * size, 128), F32)
        for lanes, heads in UNITS:
            wide = lanes.stop - lanes.start
            qp = q3[:, start : start + size, lanes].reshape(4 * size, wide)
            kp = k3[:, start : start + size, lanes].reshape(8 * size, wide)
            vp = v3[:, start : start + size, lanes].reshape(8 * size, wide)
            low_half = iota(qp.shape, 1) < HD
            found = []
            for h in range(heads):
                qm = qp.astype(F32) * 0.125
                if heads == 2:
                    qm = jnp.where(low_half if h == 0 else jnp.logical_not(low_half), qm, 0.0)
                scores = dot_nt(qm.astype(BF16), kp)
                top = jnp.max(scores, axis=1, keepdims=True)
                expo = jnp.exp(scores - top)
                total = jnp.sum(expo, axis=1, keepdims=True)
                found.append(dot(expo.astype(BF16), vp) * (1.0 / total))
                column = lanes.start // HD + h
                lse = jnp.where(iota(lse.shape, 1) == column, top + jnp.log(total), lse)
            mixed = found[0] if heads == 1 else jnp.where(low_half, found[0], found[1])
            mixed = mixed.reshape(4, size, wide)
            mixed_out[:, start : start + size, lanes] = mixed
            for r, out in enumerate(mixed_low):
                out[start : start + size, lanes] = mixed[r].astype(BF16)
        lse_out[:, start : start + size, :] = lse.reshape(4, size, 128)


def mcat_body(place, own, r1, r2, r3, out, parts):
    for r, part in enumerate((own, r1, r2, r3)):
        parts[r] = part[...]
    for j in range(4):
        out[:, j * HEADS : (j + 1) * HEADS] = parts[place[1] ^ j]


def norm_stats(values):
    center = values - jnp.mean(values, axis=1, keepdims=True)
    spread = jnp.mean(center * center, axis=1, keepdims=True)
    scale = lax.rsqrt(spread + NORM_EPS)
    return center * scale, scale


def norm_back(e, gain, vhat, scale):
    eg = e * gain
    mean_e = jnp.mean(eg, axis=1, keepdims=True)
    mean_ev = jnp.mean(eg * vhat, axis=1, keepdims=True)
    return scale * (eg - mean_e - vhat * mean_ev)


def flip(pair):
    return jnp.concatenate([pair[1], pair[0]], axis=0)


def forward_body(place, pair, pair_sib, mine, other, wo_mine, wo_other, bias, wup, *refs):
    vhat_out, scale_out, normed_low, active, slope, mixed, wo = refs[:7]
    hidden, upper, b_up = refs[7:]
    rows = pair_sib.shape[1]

    def place_halves(c):
        wo[:, c * HALF : (c + 1) * HALF] = wo_mine[...]
        wo[:, (1 - c) * HALF : (2 - c) * HALF] = wo_other[...]

    on_core(place, place_halves)
    mixed[:rows, :] = mine[...]
    mixed[rows:, :] = other[...]
    hidden[...] = dot(mixed[...], wo[...]) + bias[2:3, :]
    hidden[:rows, :] += pair[0].astype(F32)
    hidden[rows:, :] += pair_sib[0].astype(F32)
    vhat, scale = norm_stats(hidden[...])
    vhat_out[...] = vhat
    scale_out[...] = jnp.broadcast_to(scale, scale_out.shape)
    normed_low[...] = (vhat * bias[4:5, :] + bias[5:6, :]).astype(BF16)

    def bias_half(c):
        for u in range(4):
            b_up[:, u * HALF : (u + 1) * HALF] = bias[8 + u : 9 + u, c * HALF : (c + 1) * HALF]

    on_core(place, bias_half)
    upper[...] = dot(normed_low[...], wup[...])

    def gelu_rows(step, carry):
        block = pl.ds(pl.multiple_of(step * 16, 16), 16)
        x = upper[block, :] + b_up[...]
        cdf = 0.5 * (1.0 + lax.erf(x * 0.7071067811865476))
        pdf = jnp.exp(-0.5 * x * x) * 0.3989422804014327
        active[block, :] = (x * cdf).astype(BF16)
        slope[block, :] = (cdf + x * pdf).astype(BF16)
        return carry

    lax.fori_loop(0, upper.shape[0] // 16, gelu_rows, 0)

def down_body(place, active, p0, p1, p2, p3, partial, wdown):
    for k, part in enumerate((p0, p1, p2, p3)):
        slot = z_slot(place, k)
        for y in range(4):
            wdown[y * 4 + slot] = part[y]
    total = dot(active[...], wdown[...].reshape(4 * HALF, WIDTH))
    partial[...] = total.astype(BF16).reshape(partial.shape)


def back_ffn_body(place, perm, mine, other, vhat1, bias, pair, pair_sib, slope, wup, wdown, *refs):
    layer_out, d_summed, d_down, d_upper, d_part, sums = refs
    rows = pair.shape[1]
    summed = vhat1[...] * bias[4:5, :] + bias[5:6, :] + bias[3:4, :]
    summed = summed + mine[...].astype(F32).reshape(2 * rows, WIDTH) + flip(other).astype(F32)
    vhat, scale = norm_stats(summed)
    gain = bias[6:7, :]
    result = (vhat[:rows] * gain + bias[7:8, :]).astype(BF16)
    layer_out[...] = dot_tn(perm[...], result).astype(BF16)
    e = jnp.concatenate([pair[1], pair_sib[1]], axis=0).astype(F32)
    sums[0:1, :] = jnp.sum(e * vhat, axis=0, keepdims=True)
    sums[1:2, :] = jnp.sum(e, axis=0, keepdims=True)
    grad = norm_back(e, gain, vhat, scale)
    d_summed[...] = grad
    low = grad.astype(BF16)
    d_down[...] = low
    sums[2:3, :] = jnp.sum(low.astype(F32), axis=0, keepdims=True)
    for u in range(4):
        d_active = dot_nt(d_down[...], wdown[u * 4 : (u + 1) * 4].reshape(HALF, WIDTH))
        part = (d_active * slope[:, u * HALF : (u + 1) * HALF].astype(F32)).astype(BF16)
        d_upper[:, u * HALF : (u + 1) * HALF] = part
        half = slice((u % 2) * HALF, (u % 2 + 1) * HALF)
        sums[3 + u // 2 : 4 + u // 2, half] = jnp.sum(part.astype(F32), axis=0, keepdims=True)
    sums[5:8, :] = jnp.zeros((3, WIDTH), F32)
    d_part[...] = dot_nt(d_upper[...], wup[...]).astype(BF16).reshape(2, rows, WIDTH)


def grad_down_body(place, active, d_down, *refs):
    outs, scr = refs[:4], refs[4]
    scr[...] = dot_tn(active[...], d_down[...])
    for k, out in enumerate(outs):
        z = z_slot(place, k)
        for r in range(4):
            row = pl.multiple_of((place[1] ^ r) * (4 * DOWN) + z * DOWN, 8)
            out[r] = scr[pl.ds(row, DOWN), :].astype(BF16)


def ring_down_body(place, recv, own, out):
    out[...] = (recv[...].astype(F32) + own[...].astype(F32)).astype(BF16)


def grad_up_body(place, normed_low, d_upper, mixed, d_branch, *refs):
    (keep_a, send_a, keep_b, send_b), scr, scr_up = refs[:4], refs[4], refs[5]

    def out_half(c):
        scr[...] = dot_tn(mixed[...], d_branch[:, c * HALF : (c + 1) * HALF])

    on_core(place, out_half)
    scr_up[...] = dot_tn(normed_low[...], d_upper[...])
    for r in range(4):
        base = (place[1] ^ r) * (8 * SHARD)
        for k in range(4):
            out = (send_b if r >= 2 else keep_b) if k % 2 else (send_a if r % 2 else keep_a)
            pair = r % 2 if k % 2 else r // 2
            for c in range(2):
                row = pl.multiple_of(base + c * 4 * SHARD + (place[2] ^ k) * SHARD, 8)
                first = pair * 20 + ((k // 2) * 2 + c) * 5
                out[first] = scr[pl.ds(row, SHARD), :].astype(BF16)
                for u in range(4):
                    slab = scr_up[pl.ds(row, SHARD), u * HALF : (u + 1) * HALF]
                    out[first + 1 + u] = slab.astype(BF16)


def back_norm_body(place, d_summed, mine, other, vhat1, scale1, bias, wo, d_hidden_out, d_branch, *refs):
    d_mixed, sums = refs[:4], refs[4]
    rows = d_hidden_out.shape[0]
    e = d_summed[...] + mine[...].astype(F32).reshape(2 * rows, WIDTH) + flip(other).astype(F32)
    vhat = vhat1[...]
    sums[0:1, :] = jnp.sum(e * vhat, axis=0, keepdims=True)
    sums[1:2, :] = jnp.sum(e, axis=0, keepdims=True)
    d_hidden = norm_back(e, bias[4:5, :], vhat, scale1[:, 0:1])
    d_hidden_out[...] = d_hidden[:rows]
    low = d_hidden.astype(BF16)
    d_branch[...] = low
    sums[2:3, :] = jnp.sum(low.astype(F32), axis=0, keepdims=True)
    sums[3:8, :] = jnp.zeros((5, WIDTH), F32)
    for r, out in enumerate(d_mixed):
        row = pl.multiple_of((place[1] ^ r) * HEADS, 64)
        out[...] = dot_nt(d_branch[:rows, :], wo[pl.ds(row, HEADS), :]).astype(BF16)


def back_attend_body(tables, place, d0, d1, d2, d3, mixed, q3, k3, v3, lse, dq_out, dkv_out, sums, dm3):
    rows = d0.shape[0]
    for r, part in enumerate((d0, d1, d2, d3)):
        dm3[r] = part[...]
    pad = jnp.zeros((8, rows, BOTH // 2 - HEADS), BF16)
    dkv_out[:, :, HEADS : BOTH // 2] = pad
    dkv_out[:, :, BOTH // 2 + HEADS :] = pad
    for start, size in tables:
        logs = lse[:, start : start + size, :].reshape(4 * size, 128)
        for lanes, heads in UNITS:
            wide = lanes.stop - lanes.start
            qp = q3[:, start : start + size, lanes].reshape(4 * size, wide).astype(F32) * 0.125
            dp = dm3[:, start : start + size, lanes].reshape(4 * size, wide).astype(F32)
            mp = mixed[:, start : start + size, lanes].reshape(4 * size, wide)
            kp = k3[:, start : start + size, lanes].reshape(8 * size, wide)
            vp = v3[:, start : start + size, lanes].reshape(8 * size, wide)
            low_half = iota(qp.shape, 1) < HD
            found, d_key, d_value = [], None, None
            for h in range(heads):
                qm, dmask = qp, dp
                if heads == 2:
                    mine_h = low_half if h == 0 else jnp.logical_not(low_half)
                    qm, dmask = jnp.where(mine_h, qp, 0.0), jnp.where(mine_h, dp, 0.0)
                delta = jnp.sum(dmask * mp, axis=1, keepdims=True)
                qm, dm = qm.astype(BF16), dmask.astype(BF16)
                column = lanes.start // HD + h
                probs = jnp.exp(dot_nt(qm, kp) - logs[:, column : column + 1])
                part = dot_tn(probs.astype(BF16), dm)
                d_value = part if d_value is None else d_value + part
                d_scores = (probs * (dot_nt(dm, vp) - delta)).astype(BF16)
                found.append(dot(d_scores, kp))
                part = dot_tn(d_scores, qm)
                d_key = part if d_key is None else d_key + part
            d_query = found[0] if heads == 1 else jnp.where(low_half, found[0], found[1])
            d_query = (d_query * 0.125).astype(BF16)
            dq_out[:, start : start + size, lanes] = d_query.reshape(4, size, wide)
            dkv_out[:, start : start + size, lanes] = d_key.astype(BF16).reshape(8, size, wide)
            moved = slice(VALUES.start + lanes.start, VALUES.start + lanes.stop)
            dkv_out[:, start : start + size, moved] = d_value.astype(BF16).reshape(8, size, wide)
    q_sum = jnp.sum(dq_out[...].reshape(4 * rows, HEADS).astype(F32), axis=0, keepdims=True)
    v_sum = jnp.sum(dkv_out[:, :, VALUES].reshape(8 * rows, HEADS).astype(F32), axis=0, keepdims=True)
    for j in range(4):
        mine = place[1] == j
        sums[0:1, j * HEADS : (j + 1) * HEADS] = jnp.where(mine, q_sum, 0.0)
        sums[1:2, j * HEADS : (j + 1) * HEADS] = jnp.where(mine, v_sum, 0.0)
    sums[2:8, :] = jnp.zeros((6, WIDTH), F32)


def grad_qkv_body(place, tok, dq, dkv, sums_ffn, sums_norm, sums_attn, keep, send, scr, block):
    rows = tok.shape[1]
    every = tok[...].reshape(8 * rows, WIDTH)
    scr[:, :HEADS] = dot_tn(tok[:4].reshape(4 * rows, WIDTH), dq[...].reshape(4 * rows, HEADS))
    both = dot_tn(every, dkv[...].reshape(8 * rows, BOTH))
    scr[:, HEADS : 2 * HEADS] = both[:, KEYS]
    scr[:, 2 * HEADS : 3 * HEADS] = both[:, VALUES]
    scr[:, 3 * HEADS :] = jnp.zeros((WIDTH, PIECE[1] - 3 * HEADS), F32)
    for k in range(4):
        z = place[2] ^ k
        for r in range(4):
            base = (place[1] ^ r) * (8 * SHARD) + z * SHARD
            for core, out in ((place[0], keep), (1 - place[0], send)):
                row = pl.multiple_of(base + core * (4 * SHARD), 8)
                out[k * 4 + r] = scr[pl.ds(row, SHARD), :].astype(BF16)
    once = jnp.where(place[0] == 0, 1.0, 0.0)
    block[...] = jnp.zeros(block.shape, F32)
    block[0:2, :] = sums_attn[0:2, :]
    block[2:3, :] = sums_norm[2:3, :] * once
    block[3:4, :] = sums_ffn[2:3, :] * once
    block[4:6, :] = sums_norm[0:2, :] * once
    block[6:8, :] = sums_ffn[0:2, :] * once

    def up_rows(c):
        for u in range(4):
            half = sums_ffn[3 + u // 2 : 4 + u // 2, (u % 2) * HALF : (u % 2 + 1) * HALF]
            block[8 + u : 9 + u, c * HALF : (c + 1) * HALF] = half

    on_core(place, up_rows)
    folded = jnp.concatenate([block[:12, :HALF], block[:12, HALF:]], axis=0)
    folded = jnp.concatenate([folded, jnp.zeros((SHARD, PIECE[1] - HALF), F32)], axis=1).astype(BF16)
    keep[16] = folded
    send[16] = folded


def grad_tok_body(place, dq, dkv, wq, wkv, same, sib):
    rows = same.shape[1]
    for n, out in enumerate((same, sib)):
        total = dot_nt(dkv[4 * n : 4 * n + 4].reshape(4 * rows, BOTH), wkv[...])
        if n == 0:
            total = total + dot_nt(dq[...].reshape(4 * rows, HEADS), wq[...])
        out[...] = total.astype(BF16).reshape(4, rows, WIDTH)


def added(parts, index):
    total = parts[0][index].astype(F32)
    for part in parts[1:]:
        total = total + part[index].astype(F32)
    return total


def half_up_body(place, keep_a, recv_a, keep_b, recv_b, kept_a, sent_a, kept_b, sent_b):
    for keep, recv, kept, sent in ((keep_a, recv_a, kept_a, sent_a), (keep_b, recv_b, kept_b, sent_b)):
        for n in range(20):
            kept[n] = added((keep, recv), n).astype(BF16)
            sent[n] = added((keep, recv), 20 + n).astype(BF16)


def sum_up_body(place, kept_a, recv_a, kept_b, recv_b, keep, send):
    for n in range(20):
        keep[n] = added((kept_a, recv_a), n).astype(BF16)
        send[n] = added((kept_b, recv_b), n).astype(BF16)


def mid_up_body(place, keep, recv, kept, sent):
    for n in range(10):
        kept[n] = added((keep, recv), n).astype(BF16)
        sent[n] = added((keep, recv), 10 + n).astype(BF16)


def sum_core_body(place, keep, recv, keep_z, send_z):
    total = added((keep, recv), 16).astype(BF16)
    for first, out in enumerate((keep_z, send_z)):
        for n in range(8):
            out[n] = added((keep, recv), (first + 2 * (n // 4)) * 4 + n % 4).astype(BF16)
        out[8] = total


def mid_q_body(place, keep, recv, kept, sent):
    total = added((keep, recv), 8).astype(BF16)
    for out, k in ((kept, 0), (sent, 1)):
        for n in range(4):
            out[n] = added((keep, recv), k * 4 + n).astype(BF16)
        out[4] = total


def sum_q_body(place, own, recv, *outs):
    parts = (own, recv)
    total = added(parts, 4)[:, :HALF].astype(BF16)
    for r, out in enumerate(outs):
        out[:, : PIECE[1]] = added(parts, r).astype(BF16)
        out[:, PIECE[1] :] = total


def last_q_body(place, own, r1, r2, r3, gq, gk, gv, vectors, ups, pieces):
    parts = (own, r1, r2, r3)
    for r, part in enumerate(parts):
        pieces[r] = part[:, : PIECE[1]].astype(F32)
    for j in range(4):
        piece = pieces[place[1] ^ j]
        for n, out in enumerate((gq, gk, gv)):
            out[:, j * HEADS : (j + 1) * HEADS] = piece[:, n * HEADS : (n + 1) * HEADS]
    block = sum(part[:, PIECE[1] :].astype(F32) for part in parts)
    total = jnp.concatenate([block[:12], block[12:]], axis=1)
    dev = place[3]
    high = lax.Precision.HIGHEST
    pick = jnp.where(iota((WIDTH, 128), 0) == dev * SHARD + iota((WIDTH, 128), 1), 1.0, 0.0)
    vectors[...] = jnp.dot(total, pick, precision=high, preferred_element_type=F32)
    lane = lax.rem(dev, 8) * DOWN
    pick_up = jnp.where(iota((WIDTH, 128), 0) == lane + iota((WIDTH, 128), 1), 1.0, 0.0)
    rows = jnp.where(iota(total.shape, 0) == 8 + dev // 8, total, 0.0)
    row = jnp.broadcast_to(jnp.sum(rows, axis=0, keepdims=True), (8, WIDTH))
    ups[...] = jnp.dot(row, pick_up, precision=high, preferred_element_type=F32)


def sum_td_body(place, same, recv, d0, d1, d3, keep_a, send_a, keep_b, send_b):
    rows, half = same.shape[1], keep_a.shape[1]
    for r in range(4):
        tok = (same[r].astype(F32) + recv[r].astype(F32)).astype(BF16)
        own = added((d0, d1, d3), r).astype(BF16)
        (send_a if r % 2 else keep_a)[r // 2] = tok[:half]
        other = send_b if r >= 2 else keep_b
        other[r % 2, : rows - half, :] = tok[half:]
        other[r % 2, rows - half :, :] = own


def mid_td_body(place, keep_a, recv_a, keep_b, recv_b, kept_a, sent_a, kept_b, sent_b):
    kept_a[...] = added((keep_a, recv_a), 0).astype(BF16)
    sent_a[...] = added((keep_a, recv_a), 1).astype(BF16)
    kept_b[...] = added((keep_b, recv_b), 0).astype(BF16)
    sent_b[...] = added((keep_b, recv_b), 1).astype(BF16)


def last_td_body(place, perm, d_hidden, kept_a, recv_a, kept_b, recv_b, out, out_down):
    rows, half = d_hidden.shape[0], kept_a.shape[0]
    whole = slice(None)
    total_a, total_b = added((kept_a, recv_a), whole), added((kept_b, recv_b), whole)
    out_down[...] = total_b[rows - half :]
    total = d_hidden[...] + jnp.concatenate([total_a, total_b[: rows - half]], axis=0)
    high = total.astype(BF16)
    left = total - high.astype(F32)
    middle = left.astype(BF16)
    low = (left - middle.astype(F32)).astype(BF16)
    out[...] = dot_tn(perm[...], high) + dot_tn(perm[...], middle) + dot_tn(perm[...], low)


def sum_last_body(place, u0, u1, keep, send):
    def fill(mine):
        for n in range(5):
            keep[n] = added((u0, u1), mine * 5 + n)
            send[n] = added((u0, u1), (1 - mine) * 5 + n)

    on_core(place, fill)


def last_up_body(place, keep, recv, go, gup):
    def fill(c):
        go[:, c * HALF : (c + 1) * HALF] = keep[0]
        go[:, (1 - c) * HALF : (2 - c) * HALF] = recv[0]
        for u in range(4):
            gup[:, u * WIDTH + c * HALF : u * WIDTH + (c + 1) * HALF] = keep[1 + u]
            gup[:, u * WIDTH + (1 - c) * HALF : u * WIDTH + (2 - c) * HALF] = recv[1 + u]

    on_core(place, fill)


def fast_device(
    tokens,
    table_ids,
    w_query,
    w_key,
    w_value,
    w_out,
    w_up,
    w_down,
    b_query,
    b_value,
    b_out,
    b_up,
    b_down,
    gain_attn,
    shift_attn,
    gain_ffn,
    shift_ffn,
    cotangent,
):
    col, z = lax.axis_index("col"), lax.axis_index("seq")
    place = jnp.stack([col % 2, col // 2, z, col * 4 + z]).astype(jnp.int32)
    rows = tokens.shape[0]
    tables = table_rows(rows, 8)

    def swap(x):
        return lax.ppermute(x, "col", [(i, i ^ 1) for i in range(8)])

    def plane(x, r):
        return lax.ppermute(x, "col", [(i, i ^ (2 * r)) for i in range(8)])

    def shift(x, k):
        return lax.ppermute(x, "seq", [(i, (i + k) % 4) for i in range(4)])

    def planes(x):
        return (x, plane(x, 1), plane(x, 2), plane(x, 3))

    def exchanged(parts):
        return (parts[0],) + tuple(plane(parts[r], r) for r in (1, 2, 3))

    def ring(x):
        one = shift(x, 1)
        two = shift(one, 1)
        return (x, one, two, shift(two, 1))

    def exchange(x, k):
        return lax.ppermute(x, "seq", [(i, i ^ k) for i in range(4)])

    def slabs(count, kind=BF16):
        return ((count,) + SLAB, kind)

    vectors = (b_query, b_value, b_out, b_down, gain_attn, shift_attn, gain_ffn, shift_ffn)
    block = (BLOCK, BF16)
    *q_out, keep_u, send_u, w_down = call(
        pack_body,
        "pack",
        place,
        (w_down, w_query, w_key, w_value, w_out, w_up)
        + tuple(v.reshape(1, SHARD) for v in vectors)
        + (b_up.reshape(1, DOWN),),
        (block,) * 4 + (slabs(5), slabs(5), ((DOWN, WIDTH), BF16)),
        (
            pltpu.VMEM((8, SHARD), F32),
            pltpu.VMEM((4, SHARD, 3 * HEADS), F32),
            pltpu.VMEM(SLAB, F32),
        ),
        limit=FULL_BYTES,
    )
    q_in = exchanged(q_out)
    recv_u = swap(send_u)
    perm, pair, tok_own = call(
        sort_body,
        "sort",
        place,
        (table_ids.reshape(1, rows), tokens, cotangent),
        (((rows, rows), BF16), ((2, rows, WIDTH), BF16), ((rows, WIDTH), BF16)),
        after=(send_u,),
        limit=FULL_BYTES,
    )
    chunk, w_down, tok_own, pair = call(
        merge_body,
        "merge",
        place,
        (keep_u, recv_u) + q_in,
        ((CHUNK, BF16),),
        (pltpu.VMEM((4,) + PIECE, BF16),),
        through=(w_down, tok_own, pair),
    )
    column_d, one = call(
        pcat_body,
        "pcat",
        place,
        planes(w_down),
        (((4, DOWN, WIDTH), BF16),),
        through=(shift(chunk, 1),),
    )
    two, tok_x, tok_y, pair_sib, column_d = call(
        gate_body,
        "gate",
        place,
        (),
        (),
        through=(shift(one, 1), plane(tok_own, 1), plane(tok_own, 2), swap(pair), column_d),
    )
    tok_parts = (tok_own, tok_x, tok_y, plane(tok_x, 2))
    plane_u, plane_q, three, column_d = call(
        zcat_body,
        "zcat",
        place,
        (chunk, one, two, shift(two, 1)) + tok_parts[1:],
        (slabs(40), ((17,) + PIECE, BF16), ((3, rows, WIDTH), BF16)),
        through=(column_d,),
    )
    three_sib = swap(three)
    other_q = swap(plane_q)
    u_x, u_y = plane(plane_u, 1), plane(plane_u, 2)
    d_one = shift(column_d, 1)

    heads = ((4, rows, HEADS), BF16)
    heads_all = ((8, rows, HEADS), BF16)
    piece = ((rows, HEADS), BF16)
    wq, wkv, bias, tok, q3, k3, v3, mixed3, *mixed_low, lse = call(
        functools.partial(attend_body, tables),
        "attend",
        place,
        tok_parts + (pair_sib, three_sib, plane_q, other_q),
        (
            ((WIDTH, HEADS), BF16),
            ((WIDTH, BOTH), BF16),
            ((16, WIDTH), F32),
            ((8, rows, WIDTH), BF16),
            heads,
            heads_all,
            heads_all,
            ((4, rows, HEADS), F32),
            piece,
            piece,
            piece,
            piece,
            ((4, rows, 128), F32),
        ),
        (pltpu.VMEM((WIDTH, PIECE[1]), F32),),
        after=(plane_u,),
    )
    half_x, half_y, d_one = call(
        ucut_body, "ucut", place, (u_x, u_y), (slabs(20), slabs(20)), after=(lse,), through=(d_one,)
    )
    d_two = shift(d_one, 1)
    wo_mine, wup, column_d, *mixed_low = call(
        asm_u_body,
        "asm_u",
        place,
        (plane_u, u_x, u_y, plane(half_x, 2), plane(half_y, 1)),
        (((WIDTH, HALF), BF16), ((WIDTH, 4 * HALF), BF16)),
        (pltpu.VMEM((WIDTH, HALF), F32),),
        after=(half_x,),
        through=(column_d,) + tuple(mixed_low),
    )
    d_parts = (column_d, d_one, d_two, shift(column_d, 3))
    (mixed_own,) = call(
        mcat_body,
        "mcat",
        place,
        exchanged(mixed_low),
        (((rows, WIDTH), BF16),),
        (pltpu.VMEM((4, rows, HEADS), BF16),),
        after=(d_two,),
    )
    whole_pair = ((2, rows, WIDTH), BF16)
    full = (2 * rows, WIDTH)
    wide = ((2 * rows, 4 * HALF), BF16)
    vhat, scale, normed_low, active, slope, mixed, wo = call(
        forward_body,
        "forward",
        place,
        (pair, pair_sib, mixed_own, swap(mixed_own), wo_mine, swap(wo_mine), bias, wup),
        (
            (full, F32),
            ((2 * rows, 128), F32),
            (full, BF16),
            wide,
            wide,
            (full, BF16),
            ((WIDTH, WIDTH), BF16),
        ),
        (pltpu.VMEM(full, F32), pltpu.VMEM(wide[0], F32), pltpu.VMEM((1, 4 * HALF), F32)),
    )
    partial, wdown = call(
        down_body, "down", place, (active,) + d_parts, (whole_pair, ((16, DOWN, WIDTH), BF16))
    )
    layer_out, d_summed, d_down, d_upper, d_part, sums_ffn = call(
        back_ffn_body,
        "back_ffn",
        place,
        (perm, partial, swap(partial), vhat, bias, pair, pair_sib, slope, wup, wdown),
        (((rows, WIDTH), BF16), (full, F32), (full, BF16), wide, whole_pair, ((8, WIDTH), F32)),
    )
    d_part_other = swap(d_part)
    column = ((4, DOWN, WIDTH), BF16)
    g_down = call(
        grad_down_body,
        "grad_down",
        place,
        (active, d_down),
        (column,) * 4,
        (pltpu.VMEM((4 * HALF, WIDTH), F32),),
    )
    down_two, down_three = shift(g_down[2], 1), shift(g_down[1], 3)
    d_hidden, d_branch, *d_mixed, sums_norm = call(
        back_norm_body,
        "back_norm",
        place,
        (d_summed, d_part, d_part_other, vhat, scale, bias, wo),
        (((rows, WIDTH), F32), (full, BF16), piece, piece, piece, piece, ((8, WIDTH), F32)),
        after=(g_down[2],),
    )
    d_mixed = exchanged(d_mixed)
    g_up = call(
        grad_up_body,
        "grad_up",
        place,
        (normed_low, d_upper, mixed, d_branch),
        (slabs(40),) * 4,
        (pltpu.VMEM((WIDTH, HALF), F32), pltpu.VMEM((WIDTH, 4 * HALF), F32)),
    )
    up_a, up_b = plane(g_up[1], 1), plane(g_up[3], 2)
    dq, dkv, sums_attn = call(
        functools.partial(back_attend_body, tables),
        "back_attend",
        place,
        d_mixed + (mixed3, q3, k3, v3, lse),
        (heads, ((8, rows, BOTH), BF16), ((8, WIDTH), F32)),
        (pltpu.VMEM((4, rows, HEADS), BF16),),
        after=(g_up[1],),
    )
    keep_q, send_q = call(
        grad_qkv_body,
        "grad_qkv",
        place,
        (tok, dq, dkv, sums_ffn, sums_norm, sums_attn),
        (((17,) + PIECE, BF16),) * 2,
        (pltpu.VMEM((WIDTH, PIECE[1]), F32), pltpu.VMEM((16, WIDTH), F32)),
    )
    recv_q = swap(send_q)
    quad = ((4, rows, WIDTH), BF16)
    same, sib = call(
        grad_tok_body, "grad_tok", place, (dq, dkv, wq, wkv), (quad, quad), after=(send_q,)
    )
    (down_src,) = call(
        ring_down_body, "ring_down", place, (down_two, g_down[3]), (column,), after=(sib,)
    )
    sib = swap(sib)
    down_one = shift(down_src, 1)
    kept_a, sent_a, kept_b, sent_b = call(
        half_up_body,
        "half_up",
        place,
        (g_up[0], up_a, g_up[2], up_b),
        (slabs(20),) * 4,
        after=(down_src,),
    )
    up_a, up_b = plane(sent_a, 2), plane(sent_b, 1)
    two_q = ((9,) + PIECE, BF16)
    keep_z, send_z = call(
        sum_core_body, "sum_core", place, (keep_q, recv_q), (two_q,) * 2, after=(sent_a,)
    )
    recv_z = exchange(send_z, 1)
    keep_up, send_up = call(
        sum_up_body,
        "sum_up",
        place,
        (kept_a, up_a, kept_b, up_b),
        (slabs(20), slabs(20)),
        after=(send_z,),
    )
    recv_up = exchange(send_up, 1)
    one_q = ((5,) + PIECE, BF16)
    half = ((rows + DOWN) // 2, WIDTH)
    two = ((2,) + half, BF16)
    keep_a, send_a, keep_b, send_b = call(
        sum_td_body, "sum_td", place, (same, sib, g_down[0], down_one, down_three), (two,) * 4, after=(send_up,)
    )
    recv_a, recv_b = plane(send_a, 1), plane(send_b, 2)
    kept_z, sent_z = call(
        mid_q_body, "mid_q", place, (keep_z, recv_z), (one_q,) * 2, after=(send_a,)
    )
    z_q = (kept_z, exchange(sent_z, 2))
    kept_a, sent_a, kept_b, sent_b = call(
        mid_td_body, "mid_td", place, (keep_a, recv_a, keep_b, recv_b), ((half, BF16),) * 4, after=(sent_z,)
    )
    recv_a, recv_b = plane(sent_a, 2), plane(sent_b, 1)
    kept_up, sent_up = call(
        mid_up_body, "mid_up", place, (keep_up, recv_up), (slabs(10), slabs(10)), after=(sent_a,)
    )
    recv_up = exchange(sent_up, 2)
    p_q = call(sum_q_body, "sum_q", place, z_q, (block,) * 4, after=(sent_up,))
    row = ((SHARD, WIDTH), F32)
    gq, gk, gv, small, ups = call(
        last_q_body,
        "last_q",
        place,
        exchanged(p_q),
        (row, row, row, ((12, 128), F32), ((8, 128), F32)),
        (pltpu.VMEM((4,) + PIECE, F32),),
    )
    kept, sent = call(
        sum_last_body, "sum_last", place, (kept_up, recv_up), (slabs(5, F32), slabs(5, F32))
    )
    grad_tokens, grad_down = call(
        last_td_body,
        "last_td",
        place,
        (perm, d_hidden, kept_a, recv_a, kept_b, recv_b),
        (((rows, WIDTH), F32), ((DOWN, WIDTH), F32)),
        after=(sent,),
    )
    go, gup = call(
        last_up_body, "last_up", place, (kept, swap(sent)), (row, ((SHARD, 4 * WIDTH), F32)), after=(grad_down,), limit=FULL_BYTES
    )
    small = small[:, :SHARD]
    return (
        layer_out,
        grad_tokens,
        gq,
        gk,
        gv,
        go,
        gup,
        grad_down,
        small[0],
        small[1],
        small[2],
        ups[0, :DOWN],
        small[3],
        small[4],
        small[5],
        small[6],
        small[7],
    )


def solution(mesh):
    placed = (
        P(("col", "seq"), None),
        P(("col", "seq")),
        P(("col", "seq"), None),
        P(("col", "seq"), None),
        P(("col", "seq"), None),
        P(("col", "seq"), None),
        P(("col", "seq"), None),
        P(("col", "seq"), None),
        P(("col", "seq")),
        P(("col", "seq")),
        P(("col", "seq")),
        P(("col", "seq")),
        P(("col", "seq")),
        P(("col", "seq")),
        P(("col", "seq")),
        P(("col", "seq")),
        P(("col", "seq")),
        P(("col", "seq"), None),
    )
    fast = mesh.shape["col"] == 8 and mesh.shape["seq"] == 4
    return jax.shard_map(
        fast_device if fast else per_device,
        mesh=mesh,
        in_specs=placed,
        out_specs=(
            P(("col", "seq"), None),
            P(("col", "seq"), None),
            P(("col", "seq"), None),
            P(("col", "seq"), None),
            P(("col", "seq"), None),
            P(("col", "seq"), None),
            P(("col", "seq"), None),
            P(("col", "seq"), None),
            P(("col", "seq")),
            P(("col", "seq")),
            P(("col", "seq")),
            P(("col", "seq")),
            P(("col", "seq")),
            P(("col", "seq")),
            P(("col", "seq")),
            P(("col", "seq")),
            P(("col", "seq")),
        ),
        check_vma=False,
    )
```

```python
import functools

import jax
import jax.numpy as jnp
import numpy as np
from jax import lax
from jax.experimental import pallas as pl
from jax.experimental.pallas import tpu as pltpu
from jax.sharding import PartitionSpec as P

H = 12
HD = 64


NEG_BIG = -1e30
NORM_EPS = 1e-12
LOW_TYPE = jnp.bfloat16
FULL_TYPE = jnp.float32


def block_length(unit_rows):
    target = unit_rows * max(1, -(-512 // unit_rows))
    return target


def layer_norm(values, gain, shift):
    center = values - jnp.mean(values, axis=-1, keepdims=True)
    spread = jnp.mean(center * center, axis=-1, keepdims=True)
    return center * lax.rsqrt(spread + NORM_EPS) * gain + shift


def gelu_exact(values):
    return jax.nn.gelu(values, approximate=False)


def project(left, right, bias):
    return jnp.dot(left, right, preferred_element_type=FULL_TYPE) + bias.astype(FULL_TYPE)


def attend(running, query_heads, query_ids, key_slab, value_slab, key_ids):
    maxima, totals, weighted = running
    scores = (
        jnp.einsum("thd,shd->hts", query_heads, key_slab, preferred_element_type=FULL_TYPE) * 0.125
    )
    visible = (query_ids[:, None] == key_ids[None, :])[None]
    scores = jnp.where(visible, scores, NEG_BIG)
    new_max = jnp.maximum(maxima, jnp.max(scores, axis=2))
    rescale = jnp.exp(maxima - new_max)
    exponents = jnp.where(visible, jnp.exp(scores - new_max[:, :, None]), 0.0)
    totals = totals * rescale + jnp.sum(exponents, axis=2)
    weighted = weighted * rescale[:, :, None] + jnp.einsum(
        "hts,shd->htd", exponents.astype(LOW_TYPE), value_slab, preferred_element_type=FULL_TYPE
    )
    return (new_max, totals, weighted)


def grad_block(
    query_heads, dout_heads, log_totals, row_delta, query_ids, key_slab, value_slab, key_ids
):
    scores = (
        jnp.einsum("thd,shd->hts", query_heads, key_slab, preferred_element_type=FULL_TYPE) * 0.125
    )
    visible = (query_ids[:, None] == key_ids[None, :])[None]
    probabilities = jnp.where(visible, jnp.exp(scores - log_totals[:, :, None]), 0.0)
    grad_value = jnp.einsum(
        "hts,thd->shd", probabilities.astype(LOW_TYPE), dout_heads, preferred_element_type=FULL_TYPE
    )
    grad_probs = jnp.einsum(
        "thd,shd->hts", dout_heads, value_slab, preferred_element_type=FULL_TYPE
    )
    grad_scores = (probabilities * (grad_probs - row_delta[:, :, None])).astype(LOW_TYPE)
    grad_query = (
        jnp.einsum("hts,shd->thd", grad_scores, key_slab, preferred_element_type=FULL_TYPE) * 0.125
    )
    grad_key = (
        jnp.einsum("hts,thd->shd", grad_scores, query_heads, preferred_element_type=FULL_TYPE)
        * 0.125
    )
    return (grad_query, grad_key, grad_value)


def per_device(
    tokens,
    table_ids,
    w_query,
    w_key,
    w_value,
    w_out,
    w_up,
    w_down,
    b_query,
    b_value,
    b_out,
    b_up,
    b_down,
    gain_attn,
    shift_attn,
    gain_ffn,
    shift_ffn,
    cotangent,
):
    shards = (
        w_query,
        w_key,
        w_value,
        w_out,
        w_up,
        w_down,
        b_query,
        b_value,
        b_out,
        b_up,
        b_down,
        gain_attn,
        shift_attn,
        gain_ffn,
        shift_ffn,
    )
    gathered = (
        lax.all_gather(shards[0], ("col", "seq"), axis=0, tiled=True),
        lax.all_gather(shards[1], ("col", "seq"), axis=0, tiled=True),
        lax.all_gather(shards[2], ("col", "seq"), axis=0, tiled=True),
        lax.all_gather(shards[3], ("col", "seq"), axis=0, tiled=True),
        lax.all_gather(shards[4], ("col", "seq"), axis=0, tiled=True),
        lax.all_gather(shards[5], ("col", "seq"), axis=0, tiled=True),
        lax.all_gather(shards[6], ("col", "seq"), axis=0, tiled=True),
        lax.all_gather(shards[7], ("col", "seq"), axis=0, tiled=True),
        lax.all_gather(shards[8], ("col", "seq"), axis=0, tiled=True),
        lax.all_gather(shards[9], ("col", "seq"), axis=0, tiled=True),
        lax.all_gather(shards[10], ("col", "seq"), axis=0, tiled=True),
        lax.all_gather(shards[11], ("col", "seq"), axis=0, tiled=True),
        lax.all_gather(shards[12], ("col", "seq"), axis=0, tiled=True),
        lax.all_gather(shards[13], ("col", "seq"), axis=0, tiled=True),
        lax.all_gather(shards[14], ("col", "seq"), axis=0, tiled=True),
    )
    query_mat, key_mat, value_mat, out_mat, up_mat, down_mat = (
        gathered[0],
        gathered[1],
        gathered[2],
        gathered[3],
        gathered[4],
        gathered[5],
    )
    query_bias, value_bias, out_bias, up_bias, down_bias = (
        gathered[6],
        gathered[7],
        gathered[8],
        gathered[9],
        gathered[10],
    )
    attn_gain, attn_shift, ffn_gain, ffn_shift = (
        gathered[11],
        gathered[12],
        gathered[13],
        gathered[14],
    )
    tok_rows = tokens.shape[0]
    ids_all = lax.all_gather(table_ids, "col", axis=0, tiled=True)
    inputs = tokens.astype(FULL_TYPE)
    queries = project(tokens, query_mat, query_bias).astype(LOW_TYPE)
    keys = jnp.dot(tokens, key_mat, preferred_element_type=FULL_TYPE).astype(LOW_TYPE)
    values = project(tokens, value_mat, value_bias).astype(LOW_TYPE)
    query_heads = queries.reshape(tok_rows, H, HD)
    starting = (
        jnp.full((H, tok_rows), NEG_BIG, FULL_TYPE),
        jnp.zeros((H, tok_rows), FULL_TYPE),
        jnp.zeros((H, tok_rows, HD), FULL_TYPE),
    )
    running = starting
    key_rows = lax.all_gather(keys, "col", axis=0, tiled=True)
    value_rows = lax.all_gather(values, "col", axis=0, tiled=True)
    row_count = key_rows.shape[0]
    length = block_length(tok_rows)
    blocks = row_count // length

    def advance(current, pieces):
        return (attend(current, query_heads, table_ids, pieces[0], pieces[1], pieces[2]), None)

    running, _ = lax.scan(
        advance,
        running,
        (
            key_rows.reshape(blocks, length, H, HD),
            value_rows.reshape(blocks, length, H, HD),
            ids_all.reshape(blocks, length),
        ),
    )
    maxima, totals, weighted = running
    attn_heads = weighted / totals[:, :, None]
    log_totals = maxima + jnp.log(totals)
    attn_low = attn_heads.transpose(1, 0, 2).reshape(tok_rows, H * HD).astype(LOW_TYPE)
    hidden = inputs + project(attn_low, out_mat, out_bias)
    normed, norm_first = jax.vjp(
        layer_norm, hidden, attn_gain.astype(FULL_TYPE), attn_shift.astype(FULL_TYPE)
    )
    normed_low = normed.astype(LOW_TYPE)
    upper = project(normed_low, up_mat, up_bias)
    active, gelu_back = jax.vjp(gelu_exact, upper)
    active_low = active.astype(LOW_TYPE)
    summed = normed + project(active_low, down_mat, down_bias)
    result, norm_second = jax.vjp(
        layer_norm, summed, ffn_gain.astype(FULL_TYPE), ffn_shift.astype(FULL_TYPE)
    )
    again = (
        lax.all_gather(w_query, ("col", "seq"), axis=0, tiled=True),
        lax.all_gather(w_key, ("col", "seq"), axis=0, tiled=True),
        lax.all_gather(w_value, ("col", "seq"), axis=0, tiled=True),
        lax.all_gather(w_out, ("col", "seq"), axis=0, tiled=True),
        lax.all_gather(w_up, ("col", "seq"), axis=0, tiled=True),
        lax.all_gather(w_down, ("col", "seq"), axis=0, tiled=True),
    )
    query_mat, key_mat, value_mat, out_mat, up_mat, down_mat = (
        again[0],
        again[1],
        again[2],
        again[3],
        again[4],
        again[5],
    )
    d_summed, d_ffn_gain, d_ffn_shift = norm_second(cotangent.astype(FULL_TYPE))
    d_down = d_summed.astype(LOW_TYPE)
    grad_down = jnp.einsum("tf,td->fd", active_low, d_down, preferred_element_type=FULL_TYPE)
    d_active = jnp.einsum("td,fd->tf", d_down, down_mat, preferred_element_type=FULL_TYPE)
    d_upper = gelu_back(d_active)[0].astype(LOW_TYPE)
    grad_up = jnp.einsum("td,tf->df", normed_low, d_upper, preferred_element_type=FULL_TYPE)
    d_normed = d_summed + jnp.einsum("tf,df->td", d_upper, up_mat, preferred_element_type=FULL_TYPE)
    d_hidden, d_attn_gain, d_attn_shift = norm_first(d_normed)
    d_branch = d_hidden.astype(LOW_TYPE)
    grad_out = jnp.einsum("tc,td->cd", attn_low, d_branch, preferred_element_type=FULL_TYPE)
    d_attn = jnp.einsum("td,cd->tc", d_branch, out_mat, preferred_element_type=FULL_TYPE).astype(
        LOW_TYPE
    )
    dout_heads = d_attn.reshape(tok_rows, H, HD)
    row_delta = jnp.einsum("thd,htd->ht", dout_heads.astype(FULL_TYPE), attn_heads)
    key_all, value_all = (
        lax.all_gather(keys, "col", axis=0, tiled=True),
        lax.all_gather(values, "col", axis=0, tiled=True),
    )
    total_rows = key_all.shape[0]
    length = block_length(tok_rows)
    blocks = total_rows // length

    def key_pass(grad_sum, pieces):
        grad_query_part, grad_key_part, grad_value_part = grad_block(
            query_heads,
            dout_heads,
            log_totals,
            row_delta,
            table_ids,
            pieces[0],
            pieces[1],
            pieces[2],
        )
        return (grad_sum + grad_query_part, (grad_key_part, grad_value_part))

    query_sum, (key_parts, value_parts) = lax.scan(
        key_pass,
        jnp.zeros((tok_rows, H, HD), FULL_TYPE),
        (
            key_all.reshape(blocks, length, H, HD),
            value_all.reshape(blocks, length, H, HD),
            ids_all.reshape(blocks, length),
        ),
    )
    key_sum, value_sum = (
        lax.psum_scatter(
            key_parts.reshape(total_rows, H * HD).astype(jnp.bfloat16),
            "col",
            scatter_dimension=0,
            tiled=True,
        ).astype(jnp.float32),
        lax.psum_scatter(
            value_parts.reshape(total_rows, H * HD).astype(jnp.bfloat16),
            "col",
            scatter_dimension=0,
            tiled=True,
        ).astype(jnp.float32),
    )
    query_sum = query_sum.reshape(tok_rows, H * HD)
    query_low = query_sum.astype(LOW_TYPE)
    key_low = key_sum.astype(LOW_TYPE)
    value_low = value_sum.astype(LOW_TYPE)
    grad_query = jnp.einsum("tc,td->cd", tokens, query_low, preferred_element_type=FULL_TYPE)
    grad_key = jnp.einsum("tc,td->cd", tokens, key_low, preferred_element_type=FULL_TYPE)
    grad_value = jnp.einsum("tc,td->cd", tokens, value_low, preferred_element_type=FULL_TYPE)
    d_tokens = d_hidden + jnp.einsum(
        "td,cd->tc", query_low, query_mat, preferred_element_type=FULL_TYPE
    )
    d_tokens = d_tokens + jnp.einsum(
        "td,cd->tc", key_low, key_mat, preferred_element_type=FULL_TYPE
    )
    d_tokens = d_tokens + jnp.einsum(
        "td,cd->tc", value_low, value_mat, preferred_element_type=FULL_TYPE
    )
    sums_local = (
        grad_query,
        grad_key,
        grad_value,
        grad_out,
        grad_up,
        grad_down,
        jnp.sum(query_low.astype(FULL_TYPE), axis=0),
        jnp.sum(value_low.astype(FULL_TYPE), axis=0),
        jnp.sum(d_branch.astype(FULL_TYPE), axis=0),
        jnp.sum(d_upper.astype(FULL_TYPE), axis=0),
        jnp.sum(d_down.astype(FULL_TYPE), axis=0),
        d_attn_gain,
        d_attn_shift,
        d_ffn_gain,
        d_ffn_shift,
    )
    owned = (
        lax.psum_scatter(sums_local[0], ("col", "seq"), scatter_dimension=0, tiled=True),
        lax.psum_scatter(sums_local[1], ("col", "seq"), scatter_dimension=0, tiled=True),
        lax.psum_scatter(sums_local[2], ("col", "seq"), scatter_dimension=0, tiled=True),
        lax.psum_scatter(sums_local[3], ("col", "seq"), scatter_dimension=0, tiled=True),
        lax.psum_scatter(sums_local[4], ("col", "seq"), scatter_dimension=0, tiled=True),
        lax.psum_scatter(sums_local[5], ("col", "seq"), scatter_dimension=0, tiled=True),
        lax.psum_scatter(sums_local[6], ("col", "seq"), scatter_dimension=0, tiled=True),
        lax.psum_scatter(sums_local[7], ("col", "seq"), scatter_dimension=0, tiled=True),
        lax.psum_scatter(sums_local[8], ("col", "seq"), scatter_dimension=0, tiled=True),
        lax.psum_scatter(sums_local[9], ("col", "seq"), scatter_dimension=0, tiled=True),
        lax.psum_scatter(sums_local[10], ("col", "seq"), scatter_dimension=0, tiled=True),
        lax.psum_scatter(sums_local[11], ("col", "seq"), scatter_dimension=0, tiled=True),
        lax.psum_scatter(sums_local[12], ("col", "seq"), scatter_dimension=0, tiled=True),
        lax.psum_scatter(sums_local[13], ("col", "seq"), scatter_dimension=0, tiled=True),
        lax.psum_scatter(sums_local[14], ("col", "seq"), scatter_dimension=0, tiled=True),
    )
    return (result.astype(LOW_TYPE), d_tokens) + tuple(owned)


WIDTH = 768
HALF = WIDTH // 2
SHARD = 24
DOWN = 96
SLAB = (SHARD, HALF)
HEADS = 192
PIECE = (SHARD, 640)
BLOCK = (SHARD, 1024)
START_Q = 10 * HALF
CHUNK = (SHARD, START_Q + 5 * PIECE[1])
KEYS = slice(0, 192)
VALUES = slice(256, 448)
BOTH = 512
UNITS = ((slice(0, 128), 2), (slice(128, 192), 1))
VMEM_BYTES = 30 * 2**20
FULL_BYTES = 60 * 2**20
F32 = jnp.float32
BF16 = jnp.bfloat16


COST_SCALE = 10.0
COST = {
    "attend": 11.7,
    "asm_u": 2.5,
    "forward": 5.5,
    "down": 2.0,
    "back_ffn": 5.5,
    "grad_down": 2.2,
    "grad_up": 2.4,
    "back_attend": 11.7,
    "grad_qkvo": 5.2,
    "grad_tok": 4.3,
}


def dot(left, right):
    return jnp.dot(left, right, preferred_element_type=F32)


def dot_nt(left, right):
    return lax.dot_general(left, right, (((1,), (1,)), ((), ())), preferred_element_type=F32)


def dot_tn(left, right):
    return lax.dot_general(left, right, (((0,), (0,)), ((), ())), preferred_element_type=F32)


def call(body, name, place, inputs, outs, scratch=(), after=(), through=(), limit=VMEM_BYTES):
    vmem = pl.BlockSpec(memory_space=pltpu.VMEM)
    any_place = pl.BlockSpec(memory_space=pl.ANY)
    count = 1 + len(inputs)
    skipped = count + len(after) + len(through)

    def run(*refs):
        own = skipped + len(outs)
        body(*refs[:count], *refs[skipped:own], *refs[own + len(through) :])

    return pl.pallas_call(
        run,
        name=name,
        out_shape=tuple(jax.ShapeDtypeStruct(s, t) for s, t in outs)
        + tuple(jax.ShapeDtypeStruct(a.shape, a.dtype) for a in through),
        in_specs=[pl.BlockSpec(memory_space=pltpu.SMEM)] + [vmem] * len(inputs) + [any_place] * (len(after) + len(through)),
        out_specs=tuple(vmem for _ in outs) + tuple(any_place for _ in through),
        input_output_aliases={count + len(after) + n: len(outs) + n for n in range(len(through))},
        scratch_shapes=list(scratch),
        compiler_params=pltpu.CompilerParams(vmem_limit_bytes=limit),
        cost_estimate=pl.CostEstimate(
            flops=int(1.15e9 * COST_SCALE * COST.get(name, 1.3)), bytes_accessed=0, transcendentals=0
        ),
    )(place, *inputs, *after, *through)


def iota(shape, dim):
    return lax.broadcasted_iota(jnp.int32, shape, dim)


def sort_body(place, ids, tokens, cot, perm_out, pair_out, tok_out):
    rows = tokens.shape[0]
    id_j = jnp.broadcast_to(ids[...].astype(F32), (rows, rows))
    id_i = id_j.T
    same = jnp.where(id_i == id_j, 1.0, 0.0)
    count_i = jnp.sum(same, axis=1, keepdims=True)
    count_j = jnp.sum(same, axis=0, keepdims=True)
    i, j = iota((rows, rows), 0), iota((rows, rows), 1)
    equal = jnp.where((id_i == id_j) & (i < j), 1.0, 0.0)
    tie = jnp.where((count_i == count_j) & (id_i < id_j), 1.0, 0.0)
    larger = jnp.where(count_i > count_j, 1.0, 0.0)
    position = jnp.sum(equal + tie + larger, axis=0, keepdims=True)
    perm = jnp.where(i.astype(F32) == position, 1.0, 0.0).astype(BF16)
    perm_out[...] = perm
    tok = dot(perm, tokens[...]).astype(BF16)
    pair_out[0] = tok
    pair_out[1] = dot(perm, cot[...]).astype(BF16)
    tok_out[...] = tok


def fold(block):
    return jnp.concatenate([block[:, :HALF], block[:, HALF:]], axis=0)


def pack_body(place, w_down, wq, wk, wv, wo, wup, *rest):
    vectors, b_up = rest[:8], rest[8]
    parts, (keep, send, down_out) = rest[9:13], rest[13:16]
    rows8, pieces, block = rest[16:]
    down_out[...] = w_down[...]
    dev = place[3]

    def split(mine):
        other = 1 - mine
        keep[0] = wo[:, mine * HALF : (mine + 1) * HALF]
        send[0] = wo[:, other * HALF : (other + 1) * HALF]
        for u in range(4):
            keep[1 + u] = wup[:, u * WIDTH + mine * HALF : u * WIDTH + (mine + 1) * HALF]
            send[1 + u] = wup[:, u * WIDTH + other * HALF : u * WIDTH + (other + 1) * HALF]

    on_core(place, split)
    for n, vector in enumerate(vectors):
        rows8[n : n + 1, :] = vector[...].astype(F32)
    spread = jnp.where(iota((SHARD, WIDTH), 1) == dev * SHARD + iota((SHARD, WIDTH), 0), 1.0, 0.0)
    eight = dot(rows8[...].astype(BF16), spread.astype(BF16))
    lane = lax.rem(dev, 8) * DOWN
    spread_up = jnp.where(iota((DOWN, WIDTH), 1) == lane + iota((DOWN, WIDTH), 0), 1.0, 0.0)
    one = dot(jnp.broadcast_to(b_up[...], (8, DOWN)), spread_up.astype(BF16))
    one = jnp.where(iota((8, WIDTH), 0) == dev // 8, one, 0.0)
    for n in range(2):
        lanes = slice(n * HALF, (n + 1) * HALF)
        block[n * 12 : n * 12 + 8, :] = eight[:, lanes]
        block[n * 12 + 8 : n * 12 + 12, :] = one[:4, lanes]
    for j in range(4):
        for n, w in enumerate((wq, wk, wv)):
            pieces[j, :, n * HEADS : (n + 1) * HEADS] = w[:, j * HEADS : (j + 1) * HEADS].astype(F32)
    for r, part in enumerate(parts):
        part[:, : 3 * HEADS] = pieces[place[1] ^ r].astype(BF16)
        part[:, 3 * HEADS : PIECE[1]] = jnp.zeros((SHARD, PIECE[1] - 3 * HEADS), BF16)
        part[:, PIECE[1] :] = block[...].astype(BF16)


def merge_body(place, keep, recv, q0, q1, q2, q3, chunk, slots):
    parts = (q0, q1, q2, q3)
    for r, part in enumerate(parts):
        slots[place[1] ^ r] = part[:, : PIECE[1]]
    for n in range(4):
        chunk[:, START_Q + n * PIECE[1] : START_Q + (n + 1) * PIECE[1]] = slots[n]
    total = sum(part[:, PIECE[1] :].astype(F32) for part in parts)
    total = jnp.concatenate([total, jnp.zeros((SHARD, PIECE[1] - HALF), F32)], axis=1)
    chunk[:, START_Q + 4 * PIECE[1] :] = total.astype(BF16)

    def fill(mine):
        even, odd = (keep, recv) if mine == 0 else (recv, keep)
        for n in range(5):
            chunk[:, n * HALF : (n + 1) * HALF] = even[n]
            chunk[:, (5 + n) * HALF : (6 + n) * HALF] = odd[n]

    on_core(place, fill)


def z_slot(place, k):
    return lax.rem(place[2] + 4 - k, 4)


def zcat_q_body(place, own, r1, r2, r3, out):
    parts = (own, r1, r2, r3)
    for k, part in enumerate(parts):
        slot = z_slot(place, k) * 4
        for n in range(4):
            out[slot + n] = part[n]
    out[16] = sum(part[4].astype(F32) for part in parts).astype(BF16)


def gate_body(place):
    pass


def zcat_body(place, own, r1, r2, r3, t1, t2, t3, plane_u, plane_q, three):
    parts = (own, r1, r2, r3)
    for k, part in enumerate(parts):
        slot = z_slot(place, k)
        for n in range(10):
            plane_u[slot * 10 + n] = part[:, n * HALF : (n + 1) * HALF]
        for n in range(4):
            plane_q[slot * 4 + n] = part[:, START_Q + n * PIECE[1] : START_Q + (n + 1) * PIECE[1]]
    plane_q[16] = sum(part[:, START_Q + 4 * PIECE[1] :].astype(F32) for part in parts).astype(BF16)
    for r, part in enumerate((t1, t2, t3)):
        three[r] = part[...]


def pcat_body(place, own, r1, r2, r3, column):
    for r, part in enumerate((own, r1, r2, r3)):
        column[place[1] ^ r] = part[...]


def ucut_body(place, from_x, from_y, half_x, half_y):
    half_x[...] = from_x[:20]
    half_y[...] = from_y[20:]


def asm_u_body(place, own, from_x, from_y, low, high, wo, wup, slab):
    parts = (own, from_x, from_y, (low, high))
    natural(place, parts, slab, 0, 5)
    wo[...] = slab[...].astype(BF16)
    for u in range(4):
        natural(place, parts, slab, 1 + u, 5)
        wup[:, u * HALF : (u + 1) * HALF] = slab[...].astype(BF16)


def natural(place, parts, scr, n, count):
    for r, part in enumerate(parts):
        base = (place[1] ^ r) * (8 * SHARD)
        for z in range(4):
            for c in range(2):
                row = pl.multiple_of(base + c * 4 * SHARD + z * SHARD, 8)
                source, index = part, (z * 2 + c) * count + n
                if isinstance(part, tuple):
                    source, index = part[z // 2], index - (z // 2) * 4 * count
                scr[pl.ds(row, SHARD), :] = source[index].astype(F32)


def on_core(place, action):
    @pl.when(place[0] == 0)
    def _():
        action(0)

    @pl.when(place[0] == 1)
    def _():
        action(1)


def table_rows(tok_rows, n_col):
    long_rows = max(2 * 512, 64 * n_col) // n_col
    short_rows = 512 // n_col
    units = tok_rows // short_rows
    long_count = max(1, units // (2 * (long_rows // short_rows)))
    tables, start = [], 0
    for _ in range(long_count):
        tables.append((start, long_rows))
        start += long_rows
    while start < tok_rows:
        tables.append((start, short_rows))
        start += short_rows
    return tables


def attend_body(tables, place, *refs):
    same, pair_sib, three_sib, mine_q, other_q = refs[:4], refs[4], refs[5], refs[6], refs[7]
    wq, wkv, bias, tok, q3, k3, v3, mixed_out = refs[8:16]
    mixed_low, lse_out, slab = refs[16:20], refs[20], refs[21]
    rows = tok.shape[1]

    def gather(mine):
        for c in range(2):
            source = mine_q if c == mine else other_q
            for z in range(4):
                for j in range(4):
                    row = j * 8 * SHARD + c * 4 * SHARD + z * SHARD
                    slab[row : row + SHARD, :] = source[z * 4 + j].astype(F32)

    on_core(place, gather)
    wq[...] = slab[:, :HEADS].astype(BF16)
    wkv[...] = jnp.zeros(wkv.shape, BF16)
    wkv[:, KEYS] = slab[:, HEADS : 2 * HEADS].astype(BF16)
    wkv[:, VALUES] = slab[:, 2 * HEADS : 3 * HEADS].astype(BF16)
    total = mine_q[16][:, :HALF].astype(F32) + other_q[16][:, :HALF].astype(F32)
    bias[:12, :HALF] = total[:12]
    bias[:12, HALF:] = total[12:]
    bias[12:, :] = jnp.zeros((4, WIDTH), F32)

    def own_columns(row):
        found = jnp.zeros((1, HEADS), F32)
        for j in range(4):
            part = bias[row : row + 1, j * HEADS : (j + 1) * HEADS]
            found = found + jnp.where(place[1] == j, part, 0.0)
        return found

    for n, part in enumerate(same):
        tok[n] = part[...]
        tok[4 + n] = pair_sib[0] if n == 0 else three_sib[n - 1]
    every = tok[...].reshape(8 * rows, WIDTH)
    both = dot(every, wkv[...])
    k3[...] = both[:, KEYS].astype(BF16).reshape(8, rows, HEADS)
    v3[...] = (both[:, VALUES] + own_columns(1)).astype(BF16).reshape(8, rows, HEADS)
    queries = dot(tok[:4].reshape(4 * rows, WIDTH), wq[...]) + own_columns(0)
    q3[...] = queries.astype(BF16).reshape(4, rows, HEADS)
    for start, size in tables:
        lse = jnp.zeros((4 * size, 128), F32)
        for lanes, heads in UNITS:
            wide = lanes.stop - lanes.start
            qp = q3[:, start : start + size, lanes].reshape(4 * size, wide)
            kp = k3[:, start : start + size, lanes].reshape(8 * size, wide)
            vp = v3[:, start : start + size, lanes].reshape(8 * size, wide)
            low_half = iota(qp.shape, 1) < HD
            found = []
            for h in range(heads):
                qm = qp.astype(F32) * 0.125
                if heads == 2:
                    qm = jnp.where(low_half if h == 0 else jnp.logical_not(low_half), qm, 0.0)
                scores = dot_nt(qm.astype(BF16), kp)
                top = jnp.max(scores, axis=1, keepdims=True)
                expo = jnp.exp(scores - top)
                total = jnp.sum(expo, axis=1, keepdims=True)
                found.append(dot(expo.astype(BF16), vp) * (1.0 / total))
                column = lanes.start // HD + h
                lse = jnp.where(iota(lse.shape, 1) == column, top + jnp.log(total), lse)
            mixed = found[0] if heads == 1 else jnp.where(low_half, found[0], found[1])
            mixed = mixed.reshape(4, size, wide)
            mixed_out[:, start : start + size, lanes] = mixed
            for r, out in enumerate(mixed_low):
                out[start : start + size, lanes] = mixed[r].astype(BF16)
        lse_out[:, start : start + size, :] = lse.reshape(4, size, 128)


def mcat_body(place, own, r1, r2, r3, out, parts):
    for r, part in enumerate((own, r1, r2, r3)):
        parts[r] = part[...]
    for j in range(4):
        out[:, j * HEADS : (j + 1) * HEADS] = parts[place[1] ^ j]


def norm_stats(values):
    center = values - jnp.mean(values, axis=1, keepdims=True)
    spread = jnp.mean(center * center, axis=1, keepdims=True)
    scale = lax.rsqrt(spread + NORM_EPS)
    return center * scale, scale


def norm_back(e, gain, vhat, scale):
    eg = e * gain
    mean_e = jnp.mean(eg, axis=1, keepdims=True)
    mean_ev = jnp.mean(eg * vhat, axis=1, keepdims=True)
    return scale * (eg - mean_e - vhat * mean_ev)


def flip(pair):
    return jnp.concatenate([pair[1], pair[0]], axis=0)


def forward_body(place, pair, pair_sib, mine, other, wo_mine, wo_other, bias, wup, *refs):
    vhat_out, scale_out, normed_low, active, slope, mixed, wo = refs[:7]
    hidden, upper, b_up = refs[7:]
    rows = pair_sib.shape[1]

    def place_halves(c):
        wo[:, c * HALF : (c + 1) * HALF] = wo_mine[...]
        wo[:, (1 - c) * HALF : (2 - c) * HALF] = wo_other[...]

    on_core(place, place_halves)
    mixed[:rows, :] = mine[...]
    mixed[rows:, :] = other[...]
    hidden[...] = dot(mixed[...], wo[...]) + bias[2:3, :]
    hidden[:rows, :] += pair[0].astype(F32)
    hidden[rows:, :] += pair_sib[0].astype(F32)
    vhat, scale = norm_stats(hidden[...])
    vhat_out[...] = vhat
    scale_out[...] = jnp.broadcast_to(scale, scale_out.shape)
    normed_low[...] = (vhat * bias[4:5, :] + bias[5:6, :]).astype(BF16)

    def bias_half(c):
        for u in range(4):
            b_up[:, u * HALF : (u + 1) * HALF] = bias[8 + u : 9 + u, c * HALF : (c + 1) * HALF]

    on_core(place, bias_half)
    upper[...] = dot(normed_low[...], wup[...])

    def gelu_rows(step, carry):
        block = pl.ds(pl.multiple_of(step * 16, 16), 16)
        x = upper[block, :] + b_up[...]
        cdf = 0.5 * (1.0 + lax.erf(x * 0.7071067811865476))
        pdf = jnp.exp(-0.5 * x * x) * 0.3989422804014327
        active[block, :] = (x * cdf).astype(BF16)
        slope[block, :] = (cdf + x * pdf).astype(BF16)
        return carry

    lax.fori_loop(0, upper.shape[0] // 16, gelu_rows, 0)

def down_body(place, active, p0, p1, p2, p3, partial, wdown):
    for k, part in enumerate((p0, p1, p2, p3)):
        slot = z_slot(place, k)
        for y in range(4):
            wdown[y * 4 + slot] = part[y]
    total = dot(active[...], wdown[...].reshape(4 * HALF, WIDTH))
    partial[...] = total.astype(BF16).reshape(partial.shape)


def back_ffn_body(place, perm, mine, other, vhat1, bias, pair, pair_sib, slope, wup, wdown, *refs):
    layer_out, d_summed, d_down, d_upper, d_part, sums = refs
    rows = pair.shape[1]
    summed = vhat1[...] * bias[4:5, :] + bias[5:6, :] + bias[3:4, :]
    summed = summed + mine[...].astype(F32).reshape(2 * rows, WIDTH) + flip(other).astype(F32)
    vhat, scale = norm_stats(summed)
    gain = bias[6:7, :]
    result = (vhat[:rows] * gain + bias[7:8, :]).astype(BF16)
    layer_out[...] = dot_tn(perm[...], result).astype(BF16)
    e = jnp.concatenate([pair[1], pair_sib[1]], axis=0).astype(F32)
    sums[0:1, :] = jnp.sum(e * vhat, axis=0, keepdims=True)
    sums[1:2, :] = jnp.sum(e, axis=0, keepdims=True)
    grad = norm_back(e, gain, vhat, scale)
    d_summed[...] = grad
    low = grad.astype(BF16)
    d_down[...] = low
    sums[2:3, :] = jnp.sum(low.astype(F32), axis=0, keepdims=True)
    for u in range(4):
        d_active = dot_nt(d_down[...], wdown[u * 4 : (u + 1) * 4].reshape(HALF, WIDTH))
        part = (d_active * slope[:, u * HALF : (u + 1) * HALF].astype(F32)).astype(BF16)
        d_upper[:, u * HALF : (u + 1) * HALF] = part
        half = slice((u % 2) * HALF, (u % 2 + 1) * HALF)
        sums[3 + u // 2 : 4 + u // 2, half] = jnp.sum(part.astype(F32), axis=0, keepdims=True)
    sums[5:8, :] = jnp.zeros((3, WIDTH), F32)
    d_part[...] = dot_nt(d_upper[...], wup[...]).astype(BF16).reshape(2, rows, WIDTH)


def grad_down_body(place, active, d_down, *refs):
    outs, scr = refs[:4], refs[4]
    scr[...] = dot_tn(active[...], d_down[...])
    for k, out in enumerate(outs):
        z = z_slot(place, k)
        for r in range(4):
            row = pl.multiple_of((place[1] ^ r) * (4 * DOWN) + z * DOWN, 8)
            out[r] = scr[pl.ds(row, DOWN), :].astype(BF16)


def ring_down_body(place, recv, own, out):
    out[...] = (recv[...].astype(F32) + own[...].astype(F32)).astype(BF16)


def grad_up_body(place, normed_low, d_upper, mixed, d_branch, *refs):
    (keep_a, send_a, keep_b, send_b), scr, scr_up = refs[:4], refs[4], refs[5]

    def out_half(c):
        scr[...] = dot_tn(mixed[...], d_branch[:, c * HALF : (c + 1) * HALF])

    on_core(place, out_half)
    scr_up[...] = dot_tn(normed_low[...], d_upper[...])
    for r in range(4):
        base = (place[1] ^ r) * (8 * SHARD)
        for k in range(4):
            out = (send_b if r >= 2 else keep_b) if k % 2 else (send_a if r % 2 else keep_a)
            pair = r % 2 if k % 2 else r // 2
            for c in range(2):
                row = pl.multiple_of(base + c * 4 * SHARD + (place[2] ^ k) * SHARD, 8)
                first = pair * 20 + ((k // 2) * 2 + c) * 5
                out[first] = scr[pl.ds(row, SHARD), :].astype(BF16)
                for u in range(4):
                    slab = scr_up[pl.ds(row, SHARD), u * HALF : (u + 1) * HALF]
                    out[first + 1 + u] = slab.astype(BF16)


def back_norm_body(place, d_summed, mine, other, vhat1, scale1, bias, wo, d_hidden_out, d_branch, *refs):
    d_mixed, sums = refs[:4], refs[4]
    rows = d_hidden_out.shape[0]
    e = d_summed[...] + mine[...].astype(F32).reshape(2 * rows, WIDTH) + flip(other).astype(F32)
    vhat = vhat1[...]
    sums[0:1, :] = jnp.sum(e * vhat, axis=0, keepdims=True)
    sums[1:2, :] = jnp.sum(e, axis=0, keepdims=True)
    d_hidden = norm_back(e, bias[4:5, :], vhat, scale1[:, 0:1])
    d_hidden_out[...] = d_hidden[:rows]
    low = d_hidden.astype(BF16)
    d_branch[...] = low
    sums[2:3, :] = jnp.sum(low.astype(F32), axis=0, keepdims=True)
    sums[3:8, :] = jnp.zeros((5, WIDTH), F32)
    for r, out in enumerate(d_mixed):
        row = pl.multiple_of((place[1] ^ r) * HEADS, 64)
        out[...] = dot_nt(d_branch[:rows, :], wo[pl.ds(row, HEADS), :]).astype(BF16)


def back_attend_body(tables, place, d0, d1, d2, d3, mixed, q3, k3, v3, lse, dq_out, dkv_out, sums, dm3):
    rows = d0.shape[0]
    for r, part in enumerate((d0, d1, d2, d3)):
        dm3[r] = part[...]
    pad = jnp.zeros((8, rows, BOTH // 2 - HEADS), BF16)
    dkv_out[:, :, HEADS : BOTH // 2] = pad
    dkv_out[:, :, BOTH // 2 + HEADS :] = pad
    for start, size in tables:
        logs = lse[:, start : start + size, :].reshape(4 * size, 128)
        for lanes, heads in UNITS:
            wide = lanes.stop - lanes.start
            qp = q3[:, start : start + size, lanes].reshape(4 * size, wide).astype(F32) * 0.125
            dp = dm3[:, start : start + size, lanes].reshape(4 * size, wide).astype(F32)
            mp = mixed[:, start : start + size, lanes].reshape(4 * size, wide)
            kp = k3[:, start : start + size, lanes].reshape(8 * size, wide)
            vp = v3[:, start : start + size, lanes].reshape(8 * size, wide)
            low_half = iota(qp.shape, 1) < HD
            found, d_key, d_value = [], None, None
            for h in range(heads):
                qm, dmask = qp, dp
                if heads == 2:
                    mine_h = low_half if h == 0 else jnp.logical_not(low_half)
                    qm, dmask = jnp.where(mine_h, qp, 0.0), jnp.where(mine_h, dp, 0.0)
                delta = jnp.sum(dmask * mp, axis=1, keepdims=True)
                qm, dm = qm.astype(BF16), dmask.astype(BF16)
                column = lanes.start // HD + h
                probs = jnp.exp(dot_nt(qm, kp) - logs[:, column : column + 1])
                part = dot_tn(probs.astype(BF16), dm)
                d_value = part if d_value is None else d_value + part
                d_scores = (probs * (dot_nt(dm, vp) - delta)).astype(BF16)
                found.append(dot(d_scores, kp))
                part = dot_tn(d_scores, qm)
                d_key = part if d_key is None else d_key + part
            d_query = found[0] if heads == 1 else jnp.where(low_half, found[0], found[1])
            d_query = (d_query * 0.125).astype(BF16)
            dq_out[:, start : start + size, lanes] = d_query.reshape(4, size, wide)
            dkv_out[:, start : start + size, lanes] = d_key.astype(BF16).reshape(8, size, wide)
            moved = slice(VALUES.start + lanes.start, VALUES.start + lanes.stop)
            dkv_out[:, start : start + size, moved] = d_value.astype(BF16).reshape(8, size, wide)
    q_sum = jnp.sum(dq_out[...].reshape(4 * rows, HEADS).astype(F32), axis=0, keepdims=True)
    v_sum = jnp.sum(dkv_out[:, :, VALUES].reshape(8 * rows, HEADS).astype(F32), axis=0, keepdims=True)
    for j in range(4):
        mine = place[1] == j
        sums[0:1, j * HEADS : (j + 1) * HEADS] = jnp.where(mine, q_sum, 0.0)
        sums[1:2, j * HEADS : (j + 1) * HEADS] = jnp.where(mine, v_sum, 0.0)
    sums[2:8, :] = jnp.zeros((6, WIDTH), F32)


def grad_qkv_body(place, tok, dq, dkv, sums_ffn, sums_norm, sums_attn, keep, send, scr, block):
    rows = tok.shape[1]
    every = tok[...].reshape(8 * rows, WIDTH)
    scr[:, :HEADS] = dot_tn(tok[:4].reshape(4 * rows, WIDTH), dq[...].reshape(4 * rows, HEADS))
    both = dot_tn(every, dkv[...].reshape(8 * rows, BOTH))
    scr[:, HEADS : 2 * HEADS] = both[:, KEYS]
    scr[:, 2 * HEADS : 3 * HEADS] = both[:, VALUES]
    scr[:, 3 * HEADS :] = jnp.zeros((WIDTH, PIECE[1] - 3 * HEADS), F32)
    for k in range(4):
        z = place[2] ^ k
        for r in range(4):
            base = (place[1] ^ r) * (8 * SHARD) + z * SHARD
            for core, out in ((place[0], keep), (1 - place[0], send)):
                row = pl.multiple_of(base + core * (4 * SHARD), 8)
                out[k * 4 + r] = scr[pl.ds(row, SHARD), :].astype(BF16)
    once = jnp.where(place[0] == 0, 1.0, 0.0)
    block[...] = jnp.zeros(block.shape, F32)
    block[0:2, :] = sums_attn[0:2, :]
    block[2:3, :] = sums_norm[2:3, :] * once
    block[3:4, :] = sums_ffn[2:3, :] * once
    block[4:6, :] = sums_norm[0:2, :] * once
    block[6:8, :] = sums_ffn[0:2, :] * once

    def up_rows(c):
        for u in range(4):
            half = sums_ffn[3 + u // 2 : 4 + u // 2, (u % 2) * HALF : (u % 2 + 1) * HALF]
            block[8 + u : 9 + u, c * HALF : (c + 1) * HALF] = half

    on_core(place, up_rows)
    folded = jnp.concatenate([block[:12, :HALF], block[:12, HALF:]], axis=0)
    folded = jnp.concatenate([folded, jnp.zeros((SHARD, PIECE[1] - HALF), F32)], axis=1).astype(BF16)
    keep[16] = folded
    send[16] = folded


def grad_tok_body(place, dq, dkv, wq, wkv, same, sib):
    rows = same.shape[1]
    for n, out in enumerate((same, sib)):
        total = dot_nt(dkv[4 * n : 4 * n + 4].reshape(4 * rows, BOTH), wkv[...])
        if n == 0:
            total = total + dot_nt(dq[...].reshape(4 * rows, HEADS), wq[...])
        out[...] = total.astype(BF16).reshape(4, rows, WIDTH)


def added(parts, index):
    total = parts[0][index].astype(F32)
    for part in parts[1:]:
        total = total + part[index].astype(F32)
    return total


def half_up_body(place, keep_a, recv_a, keep_b, recv_b, kept_a, sent_a, kept_b, sent_b):
    for keep, recv, kept, sent in ((keep_a, recv_a, kept_a, sent_a), (keep_b, recv_b, kept_b, sent_b)):
        for n in range(20):
            kept[n] = added((keep, recv), n).astype(BF16)
            sent[n] = added((keep, recv), 20 + n).astype(BF16)


def sum_up_body(place, kept_a, recv_a, kept_b, recv_b, keep, send):
    for n in range(20):
        keep[n] = added((kept_a, recv_a), n).astype(BF16)
        send[n] = added((kept_b, recv_b), n).astype(BF16)


def mid_up_body(place, keep, recv, kept, sent):
    for n in range(10):
        kept[n] = added((keep, recv), n).astype(BF16)
        sent[n] = added((keep, recv), 10 + n).astype(BF16)


def sum_core_body(place, keep, recv, keep_z, send_z):
    total = added((keep, recv), 16).astype(BF16)
    for first, out in enumerate((keep_z, send_z)):
        for n in range(8):
            out[n] = added((keep, recv), (first + 2 * (n // 4)) * 4 + n % 4).astype(BF16)
        out[8] = total


def mid_q_body(place, keep, recv, kept, sent):
    total = added((keep, recv), 8).astype(BF16)
    for out, k in ((kept, 0), (sent, 1)):
        for n in range(4):
            out[n] = added((keep, recv), k * 4 + n).astype(BF16)
        out[4] = total


def sum_q_body(place, own, recv, *outs):
    parts = (own, recv)
    total = added(parts, 4)[:, :HALF].astype(BF16)
    for r, out in enumerate(outs):
        out[:, : PIECE[1]] = added(parts, r).astype(BF16)
        out[:, PIECE[1] :] = total


def last_q_body(place, own, r1, r2, r3, gq, gk, gv, vectors, ups, pieces):
    parts = (own, r1, r2, r3)
    for r, part in enumerate(parts):
        pieces[r] = part[:, : PIECE[1]].astype(F32)
    for j in range(4):
        piece = pieces[place[1] ^ j]
        for n, out in enumerate((gq, gk, gv)):
            out[:, j * HEADS : (j + 1) * HEADS] = piece[:, n * HEADS : (n + 1) * HEADS]
    block = sum(part[:, PIECE[1] :].astype(F32) for part in parts)
    total = jnp.concatenate([block[:12], block[12:]], axis=1)
    dev = place[3]
    high = lax.Precision.HIGHEST
    pick = jnp.where(iota((WIDTH, 128), 0) == dev * SHARD + iota((WIDTH, 128), 1), 1.0, 0.0)
    vectors[...] = jnp.dot(total, pick, precision=high, preferred_element_type=F32)
    lane = lax.rem(dev, 8) * DOWN
    pick_up = jnp.where(iota((WIDTH, 128), 0) == lane + iota((WIDTH, 128), 1), 1.0, 0.0)
    rows = jnp.where(iota(total.shape, 0) == 8 + dev // 8, total, 0.0)
    row = jnp.broadcast_to(jnp.sum(rows, axis=0, keepdims=True), (8, WIDTH))
    ups[...] = jnp.dot(row, pick_up, precision=high, preferred_element_type=F32)


def sum_td_body(place, same, recv, d0, d1, d3, keep_a, send_a, keep_b, send_b):
    rows, half = same.shape[1], keep_a.shape[1]
    for r in range(4):
        tok = (same[r].astype(F32) + recv[r].astype(F32)).astype(BF16)
        own = added((d0, d1, d3), r).astype(BF16)
        (send_a if r % 2 else keep_a)[r // 2] = tok[:half]
        other = send_b if r >= 2 else keep_b
        other[r % 2, : rows - half, :] = tok[half:]
        other[r % 2, rows - half :, :] = own


def mid_td_body(place, keep_a, recv_a, keep_b, recv_b, kept_a, sent_a, kept_b, sent_b):
    kept_a[...] = added((keep_a, recv_a), 0).astype(BF16)
    sent_a[...] = added((keep_a, recv_a), 1).astype(BF16)
    kept_b[...] = added((keep_b, recv_b), 0).astype(BF16)
    sent_b[...] = added((keep_b, recv_b), 1).astype(BF16)


def last_td_body(place, perm, d_hidden, kept_a, recv_a, kept_b, recv_b, out, out_down):
    rows, half = d_hidden.shape[0], kept_a.shape[0]
    whole = slice(None)
    total_a, total_b = added((kept_a, recv_a), whole), added((kept_b, recv_b), whole)
    out_down[...] = total_b[rows - half :]
    total = d_hidden[...] + jnp.concatenate([total_a, total_b[: rows - half]], axis=0)
    high = total.astype(BF16)
    left = total - high.astype(F32)
    middle = left.astype(BF16)
    low = (left - middle.astype(F32)).astype(BF16)
    out[...] = dot_tn(perm[...], high) + dot_tn(perm[...], middle) + dot_tn(perm[...], low)


def sum_last_body(place, u0, u1, keep, send):
    def fill(mine):
        for n in range(5):
            keep[n] = added((u0, u1), mine * 5 + n)
            send[n] = added((u0, u1), (1 - mine) * 5 + n)

    on_core(place, fill)


def last_up_body(place, keep, recv, go, gup):
    def fill(c):
        go[:, c * HALF : (c + 1) * HALF] = keep[0]
        go[:, (1 - c) * HALF : (2 - c) * HALF] = recv[0]
        for u in range(4):
            gup[:, u * WIDTH + c * HALF : u * WIDTH + (c + 1) * HALF] = keep[1 + u]
            gup[:, u * WIDTH + (1 - c) * HALF : u * WIDTH + (2 - c) * HALF] = recv[1 + u]

    on_core(place, fill)


def fast_device(
    tokens,
    table_ids,
    w_query,
    w_key,
    w_value,
    w_out,
    w_up,
    w_down,
    b_query,
    b_value,
    b_out,
    b_up,
    b_down,
    gain_attn,
    shift_attn,
    gain_ffn,
    shift_ffn,
    cotangent,
):
    col, z = lax.axis_index("col"), lax.axis_index("seq")
    place = jnp.stack([col % 2, col // 2, z, col * 4 + z]).astype(jnp.int32)
    rows = tokens.shape[0]
    tables = table_rows(rows, 8)

    def swap(x):
        return lax.ppermute(x, "col", [(i, i ^ 1) for i in range(8)])

    def plane(x, r):
        return lax.ppermute(x, "col", [(i, i ^ (2 * r)) for i in range(8)])

    def shift(x, k):
        return lax.ppermute(x, "seq", [(i, (i + k) % 4) for i in range(4)])

    def planes(x):
        return (x, plane(x, 1), plane(x, 2), plane(x, 3))

    def exchanged(parts):
        return (parts[0],) + tuple(plane(parts[r], r) for r in (1, 2, 3))

    def ring(x):
        one = shift(x, 1)
        two = shift(one, 1)
        return (x, one, two, shift(two, 1))

    def exchange(x, k):
        return lax.ppermute(x, "seq", [(i, i ^ k) for i in range(4)])

    def slabs(count, kind=BF16):
        return ((count,) + SLAB, kind)

    vectors = (b_query, b_value, b_out, b_down, gain_attn, shift_attn, gain_ffn, shift_ffn)
    block = (BLOCK, BF16)
    *q_out, keep_u, send_u, w_down = call(
        pack_body,
        "pack",
        place,
        (w_down, w_query, w_key, w_value, w_out, w_up)
        + tuple(v.reshape(1, SHARD) for v in vectors)
        + (b_up.reshape(1, DOWN),),
        (block,) * 4 + (slabs(5), slabs(5), ((DOWN, WIDTH), BF16)),
        (
            pltpu.VMEM((8, SHARD), F32),
            pltpu.VMEM((4, SHARD, 3 * HEADS), F32),
            pltpu.VMEM(SLAB, F32),
        ),
        limit=FULL_BYTES,
    )
    q_in = exchanged(q_out)
    recv_u = swap(send_u)
    perm, pair, tok_own = call(
        sort_body,
        "sort",
        place,
        (table_ids.reshape(1, rows), tokens, cotangent),
        (((rows, rows), BF16), ((2, rows, WIDTH), BF16), ((rows, WIDTH), BF16)),
        after=(send_u,),
        limit=FULL_BYTES,
    )
    chunk, w_down, tok_own, pair = call(
        merge_body,
        "merge",
        place,
        (keep_u, recv_u) + q_in,
        ((CHUNK, BF16),),
        (pltpu.VMEM((4,) + PIECE, BF16),),
        through=(w_down, tok_own, pair),
    )
    column_d, one = call(
        pcat_body,
        "pcat",
        place,
        planes(w_down),
        (((4, DOWN, WIDTH), BF16),),
        through=(shift(chunk, 1),),
    )
    tok_x, tok_y = plane(tok_own, 1), plane(tok_own, 2)
    two, pair_sib, column_d = call(
        gate_body,
        "gate",
        place,
        (),
        (),
        through=(shift(one, 1), swap(pair), column_d),
    )
    tok_parts = (tok_own, tok_x, tok_y, plane(tok_x, 2))
    plane_u, plane_q, three, column_d = call(
        zcat_body,
        "zcat",
        place,
        (chunk, one, two, shift(two, 1)) + tok_parts[1:],
        (slabs(40), ((17,) + PIECE, BF16), ((3, rows, WIDTH), BF16)),
        through=(column_d,),
    )
    three_sib = swap(three)
    other_q = swap(plane_q)
    u_x, u_y = plane(plane_u, 1), plane(plane_u, 2)
    d_one = shift(column_d, 1)

    heads = ((4, rows, HEADS), BF16)
    heads_all = ((8, rows, HEADS), BF16)
    piece = ((rows, HEADS), BF16)
    wq, wkv, bias, tok, q3, k3, v3, mixed3, *mixed_low, lse = call(
        functools.partial(attend_body, tables),
        "attend",
        place,
        tok_parts + (pair_sib, three_sib, plane_q, other_q),
        (
            ((WIDTH, HEADS), BF16),
            ((WIDTH, BOTH), BF16),
            ((16, WIDTH), F32),
            ((8, rows, WIDTH), BF16),
            heads,
            heads_all,
            heads_all,
            ((4, rows, HEADS), F32),
            piece,
            piece,
            piece,
            piece,
            ((4, rows, 128), F32),
        ),
        (pltpu.VMEM((WIDTH, PIECE[1]), F32),),
        after=(plane_u,),
    )
    half_x, half_y, d_one = call(
        ucut_body, "ucut", place, (u_x, u_y), (slabs(20), slabs(20)), after=(lse,), through=(d_one,)
    )
    d_two = shift(d_one, 1)
    wo_mine, wup, column_d, *mixed_low = call(
        asm_u_body,
        "asm_u",
        place,
        (plane_u, u_x, u_y, plane(half_x, 2), plane(half_y, 1)),
        (((WIDTH, HALF), BF16), ((WIDTH, 4 * HALF), BF16)),
        (pltpu.VMEM((WIDTH, HALF), F32),),
        after=(half_x,),
        through=(column_d,) + tuple(mixed_low),
    )
    d_parts = (column_d, d_one, d_two, shift(column_d, 3))
    (mixed_own,) = call(
        mcat_body,
        "mcat",
        place,
        exchanged(mixed_low),
        (((rows, WIDTH), BF16),),
        (pltpu.VMEM((4, rows, HEADS), BF16),),
        after=(d_two,),
    )
    whole_pair = ((2, rows, WIDTH), BF16)
    full = (2 * rows, WIDTH)
    wide = ((2 * rows, 4 * HALF), BF16)
    vhat, scale, normed_low, active, slope, mixed, wo = call(
        forward_body,
        "forward",
        place,
        (pair, pair_sib, mixed_own, swap(mixed_own), wo_mine, swap(wo_mine), bias, wup),
        (
            (full, F32),
            ((2 * rows, 128), F32),
            (full, BF16),
            wide,
            wide,
            (full, BF16),
            ((WIDTH, WIDTH), BF16),
        ),
        (pltpu.VMEM(full, F32), pltpu.VMEM(wide[0], F32), pltpu.VMEM((1, 4 * HALF), F32)),
    )
    partial, wdown = call(
        down_body, "down", place, (active,) + d_parts, (whole_pair, ((16, DOWN, WIDTH), BF16))
    )
    layer_out, d_summed, d_down, d_upper, d_part, sums_ffn = call(
        back_ffn_body,
        "back_ffn",
        place,
        (perm, partial, swap(partial), vhat, bias, pair, pair_sib, slope, wup, wdown),
        (((rows, WIDTH), BF16), (full, F32), (full, BF16), wide, whole_pair, ((8, WIDTH), F32)),
    )
    d_part_other = swap(d_part)
    column = ((4, DOWN, WIDTH), BF16)
    g_down = call(
        grad_down_body,
        "grad_down",
        place,
        (active, d_down),
        (column,) * 4,
        (pltpu.VMEM((4 * HALF, WIDTH), F32),),
    )
    down_two, down_three = shift(g_down[2], 1), shift(g_down[1], 3)
    d_hidden, d_branch, *d_mixed, sums_norm = call(
        back_norm_body,
        "back_norm",
        place,
        (d_summed, d_part, d_part_other, vhat, scale, bias, wo),
        (((rows, WIDTH), F32), (full, BF16), piece, piece, piece, piece, ((8, WIDTH), F32)),
        after=(g_down[2],),
    )
    d_mixed = exchanged(d_mixed)
    g_up = call(
        grad_up_body,
        "grad_up",
        place,
        (normed_low, d_upper, mixed, d_branch),
        (slabs(40),) * 4,
        (pltpu.VMEM((WIDTH, HALF), F32), pltpu.VMEM((WIDTH, 4 * HALF), F32)),
    )
    up_a, up_b = plane(g_up[1], 1), plane(g_up[3], 2)
    dq, dkv, sums_attn = call(
        functools.partial(back_attend_body, tables),
        "back_attend",
        place,
        d_mixed + (mixed3, q3, k3, v3, lse),
        (heads, ((8, rows, BOTH), BF16), ((8, WIDTH), F32)),
        (pltpu.VMEM((4, rows, HEADS), BF16),),
        after=(g_up[1],),
    )
    keep_q, send_q = call(
        grad_qkv_body,
        "grad_qkv",
        place,
        (tok, dq, dkv, sums_ffn, sums_norm, sums_attn),
        (((17,) + PIECE, BF16),) * 2,
        (pltpu.VMEM((WIDTH, PIECE[1]), F32), pltpu.VMEM((16, WIDTH), F32)),
    )
    recv_q = swap(send_q)
    quad = ((4, rows, WIDTH), BF16)
    same, sib = call(
        grad_tok_body, "grad_tok", place, (dq, dkv, wq, wkv), (quad, quad), after=(send_q,)
    )
    (down_src,) = call(
        ring_down_body, "ring_down", place, (down_two, g_down[3]), (column,), after=(sib,)
    )
    sib = swap(sib)
    down_one = shift(down_src, 1)
    kept_a, sent_a, kept_b, sent_b = call(
        half_up_body,
        "half_up",
        place,
        (g_up[0], up_a, g_up[2], up_b),
        (slabs(20),) * 4,
        after=(down_src,),
    )
    up_a, up_b = plane(sent_a, 2), plane(sent_b, 1)
    two_q = ((9,) + PIECE, BF16)
    keep_z, send_z = call(
        sum_core_body, "sum_core", place, (keep_q, recv_q), (two_q,) * 2, after=(sent_a,)
    )
    recv_z = exchange(send_z, 1)
    keep_up, send_up = call(
        sum_up_body,
        "sum_up",
        place,
        (kept_a, up_a, kept_b, up_b),
        (slabs(20), slabs(20)),
        after=(send_z,),
    )
    recv_up = exchange(send_up, 1)
    one_q = ((5,) + PIECE, BF16)
    half = ((rows + DOWN) // 2, WIDTH)
    two = ((2,) + half, BF16)
    keep_a, send_a, keep_b, send_b = call(
        sum_td_body, "sum_td", place, (same, sib, g_down[0], down_one, down_three), (two,) * 4, after=(send_up,)
    )
    recv_a, recv_b = plane(send_a, 1), plane(send_b, 2)
    kept_z, sent_z = call(
        mid_q_body, "mid_q", place, (keep_z, recv_z), (one_q,) * 2, after=(send_a,)
    )
    z_q = (kept_z, exchange(sent_z, 2))
    kept_a, sent_a, kept_b, sent_b = call(
        mid_td_body, "mid_td", place, (keep_a, recv_a, keep_b, recv_b), ((half, BF16),) * 4, after=(sent_z,)
    )
    recv_a, recv_b = plane(sent_a, 2), plane(sent_b, 1)
    kept_up, sent_up = call(
        mid_up_body, "mid_up", place, (keep_up, recv_up), (slabs(10), slabs(10)), after=(sent_a,)
    )
    recv_up = exchange(sent_up, 2)
    p_q = call(sum_q_body, "sum_q", place, z_q, (block,) * 4, after=(sent_up,))
    row = ((SHARD, WIDTH), F32)
    gq, gk, gv, small, ups = call(
        last_q_body,
        "last_q",
        place,
        exchanged(p_q),
        (row, row, row, ((12, 128), F32), ((8, 128), F32)),
        (pltpu.VMEM((4,) + PIECE, F32),),
    )
    kept, sent = call(
        sum_last_body, "sum_last", place, (kept_up, recv_up), (slabs(5, F32), slabs(5, F32))
    )
    grad_tokens, grad_down = call(
        last_td_body,
        "last_td",
        place,
        (perm, d_hidden, kept_a, recv_a, kept_b, recv_b),
        (((rows, WIDTH), F32), ((DOWN, WIDTH), F32)),
        after=(sent,),
    )
    go, gup = call(
        last_up_body, "last_up", place, (kept, swap(sent)), (row, ((SHARD, 4 * WIDTH), F32)), after=(grad_down,), limit=FULL_BYTES
    )
    small = small[:, :SHARD]
    return (
        layer_out,
        grad_tokens,
        gq,
        gk,
        gv,
        go,
        gup,
        grad_down,
        small[0],
        small[1],
        small[2],
        ups[0, :DOWN],
        small[3],
        small[4],
        small[5],
        small[6],
        small[7],
    )


def solution(mesh):
    placed = (
        P(("col", "seq"), None),
        P(("col", "seq")),
        P(("col", "seq"), None),
        P(("col", "seq"), None),
        P(("col", "seq"), None),
        P(("col", "seq"), None),
        P(("col", "seq"), None),
        P(("col", "seq"), None),
        P(("col", "seq")),
        P(("col", "seq")),
        P(("col", "seq")),
        P(("col", "seq")),
        P(("col", "seq")),
        P(("col", "seq")),
        P(("col", "seq")),
        P(("col", "seq")),
        P(("col", "seq")),
        P(("col", "seq"), None),
    )
    fast = mesh.shape["col"] == 8 and mesh.shape["seq"] == 4
    return jax.shard_map(
        fast_device if fast else per_device,
        mesh=mesh,
        in_specs=placed,
        out_specs=(
            P(("col", "seq"), None),
            P(("col", "seq"), None),
            P(("col", "seq"), None),
            P(("col", "seq"), None),
            P(("col", "seq"), None),
            P(("col", "seq"), None),
            P(("col", "seq"), None),
            P(("col", "seq"), None),
            P(("col", "seq")),
            P(("col", "seq")),
            P(("col", "seq")),
            P(("col", "seq")),
            P(("col", "seq")),
            P(("col", "seq")),
            P(("col", "seq")),
            P(("col", "seq")),
            P(("col", "seq")),
        ),
        check_vma=False,
    )
```
